32 devices in a mesh: fsdp: 4 (over z), ctx: 4 (over y, x), tp: 2 (over core).
Axes of the slice: x: 2, y: 2, z: 4, core: 2. Of those that a mesh axis runs over, the one named last changes fastest.
Arguments:
- tokens: bfloat16 [8, 1152, 1536], P('fsdp', 'ctx')
- positions: int32 [8, 1152], P('fsdp', 'ctx'), may hold values from 0 to 3456, as said below
- valid: int32 [8, 1152], P('fsdp', 'ctx'), may hold values from 0 to 1, as said below
- piece_starts: int32 [8, 2], P('fsdp'), may hold values from 0 to 896, as said below
- d_out: bfloat16 [8, 1152, 1536], P('fsdp', 'ctx'), may hold values from -6 to 6
- attn_gain: bfloat16 [2, 1536], P(None, 'fsdp'), may hold values from 0.5 to 1.5
- w_query: bfloat16 [2, 1536, 1536], P(None, 'fsdp', 'tp'), may hold values from -0.15625 to 0.15625
- w_key: bfloat16 [2, 1536, 768], P(None, 'fsdp', 'tp'), may hold values from -0.15625 to 0.15625
- w_value: bfloat16 [2, 1536, 768], P(None, 'fsdp', 'tp'), may hold values from -0.15625 to 0.15625
- w_out: bfloat16 [2, 1536, 1536], P(None, 'tp', 'fsdp'), may hold values from -1.25 to 1.25
- mlp_gain: bfloat16 [2, 1536], P(None, 'fsdp'), may hold values from 0.5 to 1.5
- w_gate: bfloat16 [2, 1536, 4096], P(None, 'fsdp', 'tp'), may hold values from -0.15625 to 0.15625
- w_up: bfloat16 [2, 1536, 4096], P(None, 'fsdp', 'tp'), may hold values from -0.15625 to 0.15625
- w_down: bfloat16 [2, 4096, 1536], P(None, 'tp', 'fsdp'), may hold values from -0.09375 to 0.09375
Outputs:
- output: bfloat16 [8, 1152, 1536], P('fsdp', 'ctx')
- input_grad: float32 [8, 1152, 1536], P('fsdp', 'ctx')
- g_attn_gain: float32 [2, 1536], P(None, 'fsdp')
- g_w_query: float32 [2, 1536, 1536], P(None, 'fsdp', 'tp')
- g_w_key: float32 [2, 1536, 768], P(None, 'fsdp', 'tp')
- g_w_value: float32 [2, 1536, 768], P(None, 'fsdp', 'tp')
- g_w_out: float32 [2, 1536, 1536], P(None, 'tp', 'fsdp')
- g_mlp_gain: float32 [2, 1536], P(None, 'fsdp')
- g_w_gate: float32 [2, 1536, 4096], P(None, 'fsdp', 'tp')
- g_w_up: float32 [2, 1536, 4096], P(None, 'fsdp', 'tp')
- g_w_down: float32 [2, 4096, 1536], P(None, 'tp', 'fsdp')
- rms_stats: float32 [2, 3], replicated
The draws below stay inside these ranges and needn't reach their ends.
Inputs may be any that keep to these rules, and one draw needn't show every extreme that they name: Each sequence's positions rise by 1 or 2 from token to token and start at most 2305. The first token of every sequence is valid. `piece_starts`: piece k of a sequence starts between k * (576) and (k + 1) * 576 - 256, so that pieces never intersect.
All inputs are finite; a program needn't handle non-finite values.
Results may differ from the reference program's by a relative error of at most 0.033.
Values may be sent and summed in bfloat16 or wider, within the bound.
A program may use at most 320 MiB of HBM per device.

```python
import jax
import jax.numpy as jnp
from jax import lax

D = 1536
HEADS = 16
KV_HEADS = 8
HEAD_DIM = 96
FF = 4096
LAYERS = 2
LEN = 1152
PIECE_LEN = 256
PIECES = 2
SEQUENCES = 8


def draw_tokens(key, part):
    key = jax.random.fold_in(key, 11)
    shape_all = (SEQUENCES, LEN, D)
    base_vals = jax.random.normal(key, shape_all, jnp.float32)
    pos_scale = 0.5 + (jnp.arange(LEN, dtype=jnp.float32) + 0.5) / LEN
    seq_scale = 0.5 + (jnp.arange(SEQUENCES, dtype=jnp.float32) + 0.5) / SEQUENCES
    scaled = base_vals * seq_scale[:, None, None] * pos_scale[None, :, None]
    return scaled.astype(jnp.bfloat16)


def draw_positions(key, part):
    key = jax.random.fold_in(key, 12)
    key_offset, key_steps, key_pick = jax.random.split(key, 3)
    offsets = jax.random.randint(key_offset, (SEQUENCES,), 0, LEN, dtype=jnp.int32)
    increments = jax.random.randint(key_steps, (SEQUENCES, LEN), 1, 3, dtype=jnp.int32)
    relative = jnp.cumsum(increments, axis=1) - increments[:, :1]
    span_end = relative[:, -1]
    chosen = jax.random.randint(key_pick, (), 0, SEQUENCES, dtype=jnp.int32)
    seq_rows = jnp.arange(SEQUENCES, dtype=jnp.int32)
    offsets = jnp.where(seq_rows == chosen, 3 * LEN - span_end, offsets)
    offsets = jnp.where(seq_rows == (chosen + 1) % SEQUENCES, 0, offsets)
    return (offsets[:, None] + relative).astype(jnp.int32)


def draw_valid(key, part):
    key = jax.random.fold_in(key, 13)
    coin_draws = jax.random.randint(key, (SEQUENCES, LEN), 0, LEN, dtype=jnp.int32)
    tok_index = jnp.arange(LEN, dtype=jnp.int32)[None, :]
    keep_token = coin_draws >= 4 * tok_index // 5
    leading = tok_index == 0
    return jnp.where(leading | keep_token, 1, 0).astype(jnp.int32)


def draw_piece_starts(key, part):
    key = jax.random.fold_in(key, 14)
    key_offs, key_pick = jax.random.split(key)
    seg_len = LEN // PIECES
    offsets = jax.random.randint(key_offs, (SEQUENCES, PIECES), 0, seg_len - PIECE_LEN + 1, dtype=jnp.int32)
    chosen = jax.random.randint(key_pick, (), 0, SEQUENCES, dtype=jnp.int32)
    seq_rows = jnp.arange(SEQUENCES, dtype=jnp.int32)[:, None]
    piece_cols = jnp.arange(PIECES, dtype=jnp.int32)[None, :]
    offsets = jnp.where((seq_rows == chosen) & (piece_cols == PIECES - 1), seg_len - PIECE_LEN, offsets)
    offsets = jnp.where((seq_rows == (chosen + 1) % SEQUENCES) & (piece_cols == 0), 0, offsets)
    return (piece_cols * seg_len + offsets).astype(jnp.int32)


def steps_of(own_key, shape, cuts, smallest, high):
    gain = 1.0
    for position, shards_of in cuts:
        draws = jax.random.uniform(jax.random.fold_in(jax.random.fold_in(own_key, 6), position), (shards_of,), jnp.float32, smallest / len(cuts), high / len(cuts))
        gain = gain * jnp.repeat(jnp.exp(draws), shape[position] // shards_of).reshape((-1,) + (1,) * (len(shape) - 1 - position))
    return gain


def noise(own_key, dims, width, reach, cuts=(), kind=jnp.bfloat16):
    factor_of = steps_of(own_key, dims, cuts, -0.22, 0.18) if cuts else 1.0
    drawn = jax.random.normal(own_key, dims, jnp.float32) * width * factor_of
    return jnp.minimum(jnp.maximum(drawn, -reach), reach).astype(kind)


def setup_inputs(seed: int = 0) -> dict:
    streams_of = jax.random.split(jax.random.key(seed), 15)
    return {
        "tokens": draw_tokens(jax.random.fold_in(streams_of[14], 71), 0),
        "positions": draw_positions(jax.random.fold_in(streams_of[14], 71), 0),
        "valid": draw_valid(jax.random.fold_in(streams_of[14], 71), 0),
        "piece_starts": draw_piece_starts(jax.random.fold_in(streams_of[14], 71), 0),
        "d_out": noise(streams_of[4], (SEQUENCES, LEN, D), 1.0, 6.0, ((0, 4), (1, 4))),
        "attn_gain": jnp.clip(1.0 + 0.1 * jax.random.normal(streams_of[5], (LAYERS, D), jnp.float32), 0.5, 1.5).astype(jnp.bfloat16),
        "w_query": noise(streams_of[6], (LAYERS, D, HEADS * HEAD_DIM), D ** -0.5, 0.15625, ((1, 4), (2, 2))),
        "w_key": noise(streams_of[7], (LAYERS, D, KV_HEADS * HEAD_DIM), D ** -0.5, 0.15625, ((1, 4), (2, 2))),
        "w_value": noise(streams_of[8], (LAYERS, D, KV_HEADS * HEAD_DIM), D ** -0.5, 0.15625, ((1, 4), (2, 2))),
        "w_out": noise(streams_of[9], (LAYERS, HEADS * HEAD_DIM, D), (D // 64) ** -0.5, 1.25, ((1, 2), (2, 4))),
        "mlp_gain": jnp.clip(1.0 + 0.1 * jax.random.normal(streams_of[10], (LAYERS, D), jnp.float32), 0.5, 1.5).astype(jnp.bfloat16),
        "w_gate": noise(streams_of[11], (LAYERS, D, FF), D ** -0.5, 0.15625, ((1, 4), (2, 2))),
        "w_up": noise(streams_of[12], (LAYERS, D, FF), D ** -0.5, 0.15625, ((1, 4), (2, 2))),
        "w_down": noise(streams_of[13], (LAYERS, FF, D), FF ** -0.5, 0.09375, ((1, 2), (2, 4))),
    }


epsilon = 1e-05
rope_base = 100000.0
neg_big = -1e+30
highest = lax.Precision.HIGHEST

@jax.custom_vjp
def low(v):
    return lax.optimization_barrier(v.astype(jnp.bfloat16)).astype(jnp.float32)

@jax.custom_vjp
def low_back(v):
    return v

def low_keep(v):
    return (low(v), None)

def low_pass(kept, grad):
    return (grad,)

def back_keep(v):
    return (v, None)

def back_low(kept, grad):
    return (low(grad),)
low.defvjp(low_keep, low_pass)
low_back.defvjp(back_keep, back_low)

def rope_tables(seq_pos):
    half_dim = HEAD_DIM // 2
    freqs = rope_base ** (-(jnp.arange(half_dim).astype(jnp.float32) * 2.0 / HEAD_DIM))
    angles = seq_pos.astype(jnp.float32)[:, None] * freqs[None, :]
    return (jnp.cos(angles)[:, None, :], jnp.sin(angles)[:, None, :])

def rotate(values, cosine, sine_t):
    half_dim = values.shape[-1] // 2
    lead_part = values[..., :half_dim]
    tail_part = values[..., half_dim:]
    return jnp.concatenate([lead_part * cosine - tail_part * sine_t, tail_part * cosine + lead_part * sine_t], axis=-1)

def normalize(stream, gain_vec):
    inv_rms = lax.rsqrt(lax.optimization_barrier(jnp.mean(stream * stream, axis=-1, keepdims=True)) + epsilon)
    return stream * inv_rms * gain_vec

def layer_forward(stream, weights, cosine, sine_t, allowed, valid_f):
    gain_a, w_q, w_k, w_v, w_o, gain_m, w_g, w_u, w_d = weights
    normed_a = low(normalize(stream, gain_a))
    query_heads = low_back(jnp.dot(normed_a, w_q, precision=highest)).reshape(LEN, HEADS, HEAD_DIM)
    query_heads = low(rotate(query_heads, cosine, sine_t))
    key_heads = low_back(jnp.dot(normed_a, w_k, precision=highest)).reshape(LEN, KV_HEADS, HEAD_DIM)
    key_heads = low(rotate(key_heads, cosine, sine_t))
    value_heads = low(low_back(jnp.dot(normed_a, w_v, precision=highest))).reshape(LEN, KV_HEADS, HEAD_DIM)
    key_heads = jnp.repeat(key_heads, HEADS // KV_HEADS, axis=1)
    value_heads = jnp.repeat(value_heads, HEADS // KV_HEADS, axis=1)
    raw_scores = low_back(jnp.einsum('qhd,khd->hqk', query_heads, key_heads, precision=highest) * HEAD_DIM ** (-0.5))
    raw_scores = jnp.where(allowed[None], raw_scores, neg_big)
    row_max = lax.optimization_barrier(jnp.max(raw_scores, axis=-1, keepdims=True))
    exp_scores = jnp.exp(raw_scores - row_max)
    softmax_p = exp_scores / lax.optimization_barrier(jnp.sum(exp_scores, axis=-1, keepdims=True))
    mixed_heads = jnp.einsum('hqk,khd->qhd', low(softmax_p), value_heads, precision=highest).reshape(LEN, HEADS * HEAD_DIM)
    mixed_heads = low(low_back(mixed_heads))
    attn_branch = low_back(jnp.dot(mixed_heads, w_o, precision=highest))
    middle = stream + attn_branch
    normed_m = low(normalize(middle, gain_m))
    gate_act = low_back(jnp.dot(normed_m, w_g, precision=highest))
    up_act = low_back(jnp.dot(normed_m, w_u, precision=highest))
    hidden = low(jax.nn.silu(gate_act) * up_act)
    mlp_branch = low_back(jnp.dot(hidden, w_d, precision=highest))
    squares = jnp.stack([jnp.sum(valid_f[:, None] * stream * stream), jnp.sum(valid_f[:, None] * attn_branch * attn_branch), jnp.sum(valid_f[:, None] * mlp_branch * mlp_branch)])
    return (middle + mlp_branch, squares)

def sequence_forward(seq_tokens, params, cosine, sine_t, allowed, valid_f):
    stream = seq_tokens
    stat_rows = []
    for layer_no in range(LAYERS):
        weights = tuple((p[layer_no] for p in params))
        stream, squares = layer_forward(stream, weights, cosine, sine_t, allowed, valid_f)
        stat_rows.append(squares)
    return (stream, jnp.stack(stat_rows))

def reference(tokens, positions, valid, piece_starts, d_out, attn_gain, w_query, w_key, w_value, w_out, mlp_gain, w_gate, w_up, w_down):
    params = tuple((w.astype(jnp.float32) for w in (attn_gain, w_query, w_key, w_value, w_out, mlp_gain, w_gate, w_up, w_down)))
    tok_index = jnp.arange(LEN, dtype=jnp.int32)

    def step(running, inputs):
        grad_sums, square_sums = running
        seq_tokens, seq_pos, seq_valid, seq_starts, seq_cot = inputs
        cosine, sine_t = rope_tables(seq_pos)
        inside = (tok_index[None, :] >= seq_starts[:, None]) & (tok_index[None, :] < seq_starts[:, None] + PIECE_LEN)
        same_piece = jnp.any(inside[:, :, None] & inside[:, None, :], axis=0)
        causal = tok_index[None, :] <= tok_index[:, None]
        diagonal = tok_index[None, :] == tok_index[:, None]
        allowed = (causal | same_piece) & ((seq_valid[None, :] > 0) | diagonal)
        valid_f = seq_valid.astype(jnp.float32)

        def forward_fn(stream_in, weight_set):
            return sequence_forward(stream_in, weight_set, cosine, sine_t, allowed, valid_f)
        seq_out, pull_back, seq_squares = jax.vjp(forward_fn, seq_tokens.astype(jnp.float32), params, has_aux=True)
        grad_in, grad_params = pull_back(seq_cot.astype(jnp.float32))
        grad_sums = tuple((a + b for a, b in zip(grad_sums, grad_params)))
        return ((grad_sums, square_sums + seq_squares), (seq_out.astype(jnp.bfloat16), grad_in))
    start_grads = tuple((jnp.zeros_like(p) for p in params))
    start_squares = jnp.zeros((LAYERS, 3), jnp.float32)
    (grad_sums, square_sums), (output, input_grad) = lax.scan(step, (start_grads, start_squares), (tokens, positions, valid, piece_starts, d_out))
    valid_count = jnp.sum(valid.astype(jnp.float32))
    rms_stats = jnp.sqrt(square_sums / (valid_count * D))
    return (output, input_grad, grad_sums[0], grad_sums[1], grad_sums[2], grad_sums[3], grad_sums[4], grad_sums[5], grad_sums[6], grad_sums[7], grad_sums[8], rms_stats)
```

```python
import functools

import jax
import jax.numpy as jnp
from jax import lax
from jax.experimental import pallas as pl
from jax.experimental.pallas import tpu as pltpu
from jax.sharding import PartitionSpec as P

MESH = pl.DeviceIdType.MESH

HEADS = 16
KV_HEADS = 8
HEAD_DIM = 96
PIECE_LEN = 256


epsilon = 1e-05
rope_base = 100000.0
neg_big = -1e30


def rope_tables(positions, head_dim):
    half_dim = head_dim // 2
    freqs = rope_base ** (-(jnp.arange(half_dim).astype(jnp.float32) * 2.0 / head_dim))
    angles = positions.astype(jnp.float32)[..., None] * freqs
    return (jnp.cos(angles)[:, :, None, :], jnp.sin(angles)[:, :, None, :])


def rotate(values, cosine, sine_t):
    half_dim = values.shape[-1] // 2
    lead_part = values[..., :half_dim]
    tail_part = values[..., half_dim:]
    return jnp.concatenate(
        [lead_part * cosine - tail_part * sine_t, tail_part * cosine + lead_part * sine_t], axis=-1
    )


def normalize(stream, gain_vec):
    inv_rms = lax.rsqrt(jnp.mean(stream * stream, axis=-1, keepdims=True) + epsilon)
    return stream * inv_rms * gain_vec.astype(jnp.float32)


def norm_back(stream, gain_vec, grad_out):
    inv_rms = lax.rsqrt(jnp.mean(stream * stream, axis=-1, keepdims=True) + epsilon)
    scaled_grad = gain_vec.astype(jnp.float32) * grad_out
    grad_in = inv_rms * scaled_grad - stream * inv_rms**3 * jnp.mean(
        scaled_grad * stream, axis=-1, keepdims=True
    )
    grad_gain = jnp.sum(grad_out * stream * inv_rms, axis=0)
    return (grad_in, grad_gain)


def score_block(query_b, key_heads, allowed, score_scale):
    raw_scores = (
        jnp.einsum("sckgd,snkd->skgcn", query_b, key_heads, preferred_element_type=jnp.float32)
        * score_scale
    )
    return jnp.where(allowed[:, None, None], raw_scores, neg_big)


def general(
    tokens,
    positions,
    valid,
    piece_starts,
    d_out,
    attn_gain,
    w_query,
    w_key,
    w_value,
    w_out,
    mlp_gain,
    w_gate,
    w_up,
    w_down,
):
    seq_count, shard_len, model_width = tokens.shape
    tok_rows = seq_count * shard_len
    tp_count = lax.axis_size("tp")
    local_heads = HEADS // tp_count
    local_kv = KV_HEADS // tp_count
    group_size = HEADS // KV_HEADS
    score_scale = HEAD_DIM ** (-0.5)
    seq_length = shard_len * lax.axis_size("ctx")
    start_tok = lax.axis_index("ctx") * shard_len
    query_index = start_tok + jnp.arange(shard_len, dtype=jnp.int32)
    key_index = jnp.arange(seq_length, dtype=jnp.int32)
    cosine, sine_t = rope_tables(positions, HEAD_DIM)
    valid_flat = valid.astype(jnp.float32).reshape(tok_rows)
    in_query = (query_index[None, None, :] >= piece_starts[:, :, None]) & (
        query_index[None, None, :] < piece_starts[:, :, None] + PIECE_LEN
    )
    in_key = (key_index[None, None, :] >= piece_starts[:, :, None]) & (
        key_index[None, None, :] < piece_starts[:, :, None] + PIECE_LEN
    )
    same_piece = jnp.any(in_query[:, :, :, None] & in_key[:, :, None, :], axis=1)
    causal = key_index[None, :] <= query_index[:, None]
    diagonal = key_index[None, :] == query_index[:, None]
    layer_count = attn_gain.shape[0]
    stream = tokens.astype(jnp.float32).reshape(tok_rows, model_width)
    saved = []
    stat_rows = []
    for layer_no in range(layer_count):
        weights = (
            lax.all_gather(attn_gain[layer_no], "fsdp", axis=0, tiled=True),
            lax.all_gather(w_query[layer_no], "fsdp", axis=0, tiled=True),
            lax.all_gather(w_key[layer_no], "fsdp", axis=0, tiled=True),
            lax.all_gather(w_value[layer_no], "fsdp", axis=0, tiled=True),
            lax.all_gather(w_out[layer_no], "fsdp", axis=1, tiled=True),
            lax.all_gather(mlp_gain[layer_no], "fsdp", axis=0, tiled=True),
            lax.all_gather(w_gate[layer_no], "fsdp", axis=0, tiled=True),
            lax.all_gather(w_up[layer_no], "fsdp", axis=0, tiled=True),
            lax.all_gather(w_down[layer_no], "fsdp", axis=1, tiled=True),
        )
        gain_a, w_q, w_k, w_v, w_o, gain_m, w_g, w_u, w_d = weights
        normed_a = normalize(stream, gain_a).astype(jnp.bfloat16)
        query_heads = jnp.dot(normed_a, w_q, preferred_element_type=jnp.float32).reshape(
            seq_count, shard_len, local_heads, HEAD_DIM
        )
        query_b = (
            rotate(query_heads, cosine, sine_t)
            .astype(jnp.bfloat16)
            .reshape(seq_count, shard_len, local_kv, group_size, HEAD_DIM)
        )
        key_local = jnp.dot(normed_a, w_k, preferred_element_type=jnp.float32).reshape(
            seq_count, shard_len, local_kv, HEAD_DIM
        )
        key_local = (
            rotate(key_local, cosine, sine_t)
            .astype(jnp.bfloat16)
            .reshape(seq_count, shard_len, local_kv * HEAD_DIM)
        )
        value_local = (
            jnp.dot(normed_a, w_v, preferred_element_type=jnp.float32)
            .astype(jnp.bfloat16)
            .reshape(seq_count, shard_len, local_kv * HEAD_DIM)
        )
        key_all, value_all, valid_all = (
            lax.all_gather(key_local, "ctx", axis=1, tiled=True),
            lax.all_gather(value_local, "ctx", axis=1, tiled=True),
            lax.all_gather(valid.astype(jnp.bfloat16), "ctx", axis=1, tiled=True),
        )
        allowed = (causal[None] | same_piece) & ((valid_all[:, None, :] > 0.5) | diagonal[None])
        key_heads = key_all.reshape(seq_count, seq_length, local_kv, HEAD_DIM)
        value_heads = value_all.reshape(seq_count, seq_length, local_kv, HEAD_DIM)
        raw_scores = score_block(query_b, key_heads, allowed, score_scale)
        row_max = jnp.max(raw_scores, axis=-1, keepdims=True)
        log_total = row_max + jnp.log(
            jnp.sum(jnp.exp(raw_scores - row_max), axis=-1, keepdims=True)
        )
        softmax_b = jnp.exp(raw_scores - log_total).astype(jnp.bfloat16)
        mixed_heads = jnp.einsum(
            "skgcn,snkd->sckgd", softmax_b, value_heads, preferred_element_type=jnp.float32
        )
        mixed_b = mixed_heads.astype(jnp.bfloat16).reshape(tok_rows, local_heads * HEAD_DIM)
        attn_branch = lax.psum(
            jnp.dot(mixed_b, w_o, preferred_element_type=jnp.float32).astype(jnp.bfloat16), "tp"
        ).astype(jnp.float32)
        middle = stream + attn_branch
        normed_m = normalize(middle, gain_m).astype(jnp.bfloat16)
        gate_act = jnp.dot(normed_m, w_g, preferred_element_type=jnp.float32)
        up_act = jnp.dot(normed_m, w_u, preferred_element_type=jnp.float32)
        hidden = (jax.nn.silu(gate_act) * up_act).astype(jnp.bfloat16)
        mlp_branch = lax.psum(
            jnp.dot(hidden, w_d, preferred_element_type=jnp.float32).astype(jnp.bfloat16), "tp"
        ).astype(jnp.float32)
        stat_rows.append(
            jnp.stack(
                [
                    jnp.sum(valid_flat[:, None] * stream * stream),
                    jnp.sum(valid_flat[:, None] * attn_branch * attn_branch),
                    jnp.sum(valid_flat[:, None] * mlp_branch * mlp_branch),
                ]
            )
        )
        kept_weights = None
        saved.append(
            (
                stream,
                normed_a,
                query_b,
                key_heads,
                value_heads,
                allowed,
                log_total,
                mixed_b,
                middle,
                normed_m,
                gate_act,
                up_act,
                hidden,
                kept_weights,
            )
        )
        stream = middle + mlp_branch
    output = stream.astype(jnp.bfloat16).reshape(seq_count, shard_len, model_width)
    total_squares, total_count = lax.psum(
        (jnp.stack(stat_rows), jnp.sum(valid_flat)), ("fsdp", "ctx")
    )
    rms_stats = jnp.sqrt(total_squares / (total_count * model_width))
    grad_stream = d_out.astype(jnp.float32).reshape(tok_rows, model_width)
    results = [None] * layer_count
    for layer_no in reversed(range(layer_count)):
        (
            stream_in,
            normed_a,
            query_b,
            key_heads,
            value_heads,
            allowed,
            log_total,
            mixed_b,
            middle,
            normed_m,
            gate_act,
            up_act,
            hidden,
            kept_weights,
        ) = saved[layer_no]
        weights = (
            lax.all_gather(attn_gain[layer_no], "fsdp", axis=0, tiled=True),
            lax.all_gather(w_query[layer_no], "fsdp", axis=0, tiled=True),
            lax.all_gather(w_key[layer_no], "fsdp", axis=0, tiled=True),
            lax.all_gather(w_value[layer_no], "fsdp", axis=0, tiled=True),
            lax.all_gather(w_out[layer_no], "fsdp", axis=1, tiled=True),
            lax.all_gather(mlp_gain[layer_no], "fsdp", axis=0, tiled=True),
            lax.all_gather(w_gate[layer_no], "fsdp", axis=0, tiled=True),
            lax.all_gather(w_up[layer_no], "fsdp", axis=0, tiled=True),
            lax.all_gather(w_down[layer_no], "fsdp", axis=1, tiled=True),
        )
        gain_a, w_q, w_k, w_v, w_o, gain_m, w_g, w_u, w_d = weights
        grad_mlp = grad_stream.astype(jnp.bfloat16)
        grad_hidden = jnp.einsum("rd,fd->rf", grad_mlp, w_d, preferred_element_type=jnp.float32)
        g_down = jnp.einsum("rf,rd->fd", hidden, grad_mlp, preferred_element_type=jnp.float32)
        sigmoid_g = jax.nn.sigmoid(gate_act)
        grad_gate = (
            grad_hidden * up_act * sigmoid_g * (1.0 + gate_act * (1.0 - sigmoid_g))
        ).astype(jnp.bfloat16)
        grad_up = (grad_hidden * gate_act * sigmoid_g).astype(jnp.bfloat16)
        grad_normed_m = lax.psum(
            (
                jnp.einsum("rf,df->rd", grad_gate, w_g, preferred_element_type=jnp.float32)
                + jnp.einsum("rf,df->rd", grad_up, w_u, preferred_element_type=jnp.float32)
            ).astype(jnp.bfloat16),
            "tp",
        ).astype(jnp.float32)
        g_gate = jnp.einsum("rd,rf->df", normed_m, grad_gate, preferred_element_type=jnp.float32)
        g_up = jnp.einsum("rd,rf->df", normed_m, grad_up, preferred_element_type=jnp.float32)
        grad_from_norm, g_gain_m = norm_back(middle, gain_m, grad_normed_m)
        grad_middle = grad_stream + grad_from_norm
        grad_attn = grad_middle.astype(jnp.bfloat16)
        grad_heads = jnp.einsum(
            "rd,hd->rh", grad_attn, w_o, preferred_element_type=jnp.float32
        ).astype(jnp.bfloat16)
        g_out = jnp.einsum("rh,rd->hd", mixed_b, grad_attn, preferred_element_type=jnp.float32)
        grad_heads = grad_heads.reshape(seq_count, shard_len, local_kv, group_size, HEAD_DIM)
        raw_scores = score_block(query_b, key_heads, allowed, score_scale)
        softmax_p = jnp.exp(raw_scores - log_total)
        grad_probs = jnp.einsum(
            "sckgd,snkd->skgcn", grad_heads, value_heads, preferred_element_type=jnp.float32
        )
        row_dots = jnp.sum(softmax_p * grad_probs, axis=-1, keepdims=True)
        grad_scores = (softmax_p * (grad_probs - row_dots)).astype(jnp.bfloat16)
        grad_query = (
            jnp.einsum(
                "skgcn,snkd->sckgd", grad_scores, key_heads, preferred_element_type=jnp.float32
            )
            * score_scale
        )
        grad_key_all = (
            jnp.einsum(
                "skgcn,sckgd->snkd", grad_scores, query_b, preferred_element_type=jnp.float32
            )
            * score_scale
        )
        grad_value_all = jnp.einsum(
            "skgcn,sckgd->snkd",
            softmax_p.astype(jnp.bfloat16),
            grad_heads,
            preferred_element_type=jnp.float32,
        )
        grad_key, grad_value = (
            lax.psum_scatter(
                grad_key_all.reshape(seq_count, seq_length, local_kv * HEAD_DIM).astype(
                    jnp.bfloat16
                ),
                "ctx",
                scatter_dimension=1,
                tiled=True,
            ).astype(jnp.float32),
            lax.psum_scatter(
                grad_value_all.reshape(seq_count, seq_length, local_kv * HEAD_DIM).astype(
                    jnp.bfloat16
                ),
                "ctx",
                scatter_dimension=1,
                tiled=True,
            ).astype(jnp.float32),
        )
        grad_query_b = rotate(
            grad_query.reshape(seq_count, shard_len, local_heads, HEAD_DIM), cosine, -sine_t
        )
        grad_query_b = grad_query_b.astype(jnp.bfloat16).reshape(tok_rows, local_heads * HEAD_DIM)
        grad_key_b = rotate(
            grad_key.reshape(seq_count, shard_len, local_kv, HEAD_DIM), cosine, -sine_t
        )
        grad_key_b = grad_key_b.astype(jnp.bfloat16).reshape(tok_rows, local_kv * HEAD_DIM)
        grad_value_b = grad_value.astype(jnp.bfloat16).reshape(tok_rows, local_kv * HEAD_DIM)
        grad_normed_a = lax.psum(
            (
                jnp.einsum("rh,dh->rd", grad_query_b, w_q, preferred_element_type=jnp.float32)
                + jnp.einsum("rh,dh->rd", grad_key_b, w_k, preferred_element_type=jnp.float32)
                + jnp.einsum("rh,dh->rd", grad_value_b, w_v, preferred_element_type=jnp.float32)
            ).astype(jnp.bfloat16),
            "tp",
        ).astype(jnp.float32)
        g_query = jnp.einsum(
            "rd,rh->dh", normed_a, grad_query_b, preferred_element_type=jnp.float32
        )
        g_key = jnp.einsum("rd,rh->dh", normed_a, grad_key_b, preferred_element_type=jnp.float32)
        g_value = jnp.einsum(
            "rd,rh->dh", normed_a, grad_value_b, preferred_element_type=jnp.float32
        )
        grad_from_attn_norm, g_gain_a = norm_back(stream_in, gain_a, grad_normed_a)
        grad_stream = grad_middle + grad_from_attn_norm
        grad_terms = (g_gain_a, g_query, g_key, g_value, g_out, g_gain_m, g_gate, g_up, g_down)
        shares = (
            lax.psum_scatter(grad_terms[0], ("fsdp", "ctx"), scatter_dimension=0, tiled=True),
            lax.psum_scatter(grad_terms[1], ("fsdp", "ctx"), scatter_dimension=0, tiled=True),
            lax.psum_scatter(grad_terms[2], ("fsdp", "ctx"), scatter_dimension=0, tiled=True),
            lax.psum_scatter(grad_terms[3], ("fsdp", "ctx"), scatter_dimension=0, tiled=True),
            lax.psum_scatter(grad_terms[4], ("fsdp", "ctx"), scatter_dimension=1, tiled=True),
            lax.psum_scatter(grad_terms[5], ("fsdp", "ctx"), scatter_dimension=0, tiled=True),
            lax.psum_scatter(grad_terms[6], ("fsdp", "ctx"), scatter_dimension=0, tiled=True),
            lax.psum_scatter(grad_terms[7], ("fsdp", "ctx"), scatter_dimension=0, tiled=True),
            lax.psum_scatter(grad_terms[8], ("fsdp", "ctx"), scatter_dimension=1, tiled=True),
        )
        results[layer_no] = (
            lax.all_gather(shares[0].astype(jnp.bfloat16), "ctx", axis=0, tiled=True).astype(
                jnp.float32
            ),
            lax.all_gather(shares[1].astype(jnp.bfloat16), "ctx", axis=0, tiled=True).astype(
                jnp.float32
            ),
            lax.all_gather(shares[2].astype(jnp.bfloat16), "ctx", axis=0, tiled=True).astype(
                jnp.float32
            ),
            lax.all_gather(shares[3].astype(jnp.bfloat16), "ctx", axis=0, tiled=True).astype(
                jnp.float32
            ),
            lax.all_gather(shares[4].astype(jnp.bfloat16), "ctx", axis=1, tiled=True).astype(
                jnp.float32
            ),
            lax.all_gather(shares[5].astype(jnp.bfloat16), "ctx", axis=0, tiled=True).astype(
                jnp.float32
            ),
            lax.all_gather(shares[6].astype(jnp.bfloat16), "ctx", axis=0, tiled=True).astype(
                jnp.float32
            ),
            lax.all_gather(shares[7].astype(jnp.bfloat16), "ctx", axis=0, tiled=True).astype(
                jnp.float32
            ),
            lax.all_gather(shares[8].astype(jnp.bfloat16), "ctx", axis=1, tiled=True).astype(
                jnp.float32
            ),
        )
    stacked = [
        jnp.stack([results[layer_no][member] for layer_no in range(layer_count)])
        for member in range(9)
    ]
    input_grad = grad_stream.reshape(seq_count, shard_len, model_width)
    return (
        output,
        input_grad,
        stacked[0],
        stacked[1],
        stacked[2],
        stacked[3],
        stacked[4],
        stacked[5],
        stacked[6],
        stacked[7],
        stacked[8],
        rms_stats,
    )


def partners():
    me = lax.axis_index("ctx")
    return me, me ^ 1, me ^ 2, me ^ 3


def greet(peers):
    barrier = pltpu.get_barrier_semaphore()
    for peer in peers:
        pl.semaphore_signal(barrier, inc=1, device_id={"ctx": peer}, device_id_type=MESH)
    pl.semaphore_wait(barrier, len(peers))


def send(src, dst, sems, slot, peer):
    copy = pltpu.make_async_remote_copy(
        src_ref=src,
        dst_ref=dst,
        send_sem=sems[0].at[slot],
        recv_sem=sems[1].at[slot],
        device_id={"ctx": peer},
        device_id_type=MESH,
    )
    copy.start()
    return copy


def gather_rows(full, sems, place):
    me, side_x, side_y, _ = place
    half = full.shape[1] // 2
    top, low = pl.ds(0, half), pl.ds(half, half)
    first = [
        send(full.at[me, top], full.at[me, top], sems, 0, side_x),
        send(full.at[me, low], full.at[me, low], sems, 1, side_y),
    ]
    rest = [
        send(full.at[me, top], full.at[me, top], sems, 2, side_y),
        send(full.at[me, low], full.at[me, low], sems, 3, side_x),
    ]
    first[0].wait_recv()
    rest.append(send(full.at[side_x, top], full.at[side_x, top], sems, 4, side_y))
    first[1].wait_recv()
    rest.append(send(full.at[side_y, low], full.at[side_y, low], sems, 5, side_x))
    for copy in rest:
        copy.wait()
    for copy in first:
        copy.wait_send()


def scatter_rows(part, from_x, from_y, passed, last, sems, place):
    me, side_x, side_y, across = place
    half = part.shape[1] // 2
    top, low = pl.ds(0, half), pl.ds(half, half)
    early = [
        send(part.at[across, top], from_x.at[1], sems, 0, side_x),
        send(part.at[across, low], from_y.at[1], sems, 1, side_y),
    ]
    rest = [
        send(part.at[side_x, top], from_x.at[0], sems, 2, side_x),
        send(part.at[side_y, low], from_y.at[0], sems, 3, side_y),
    ]
    step = 16

    def add_to(slot, owner, start, came):
        @pl.loop(0, half // step)
        def _(i):
            rows = pl.ds(pl.multiple_of(i * step, step), step)
            mine = part[owner, pl.ds(pl.multiple_of(start + i * step, step), step), :]
            total = mine.astype(jnp.float32) + came[1, rows, :].astype(jnp.float32)
            passed[slot, rows, :] = total.astype(passed.dtype)

    early[0].wait_recv()
    add_to(0, side_y, 0, from_x)
    rest.append(send(passed.at[0], last.at[0], sems, 4, side_y))
    early[1].wait_recv()
    add_to(1, side_x, half, from_y)
    rest.append(send(passed.at[1], last.at[1], sems, 5, side_x))
    for copy in rest:
        copy.wait()
    for copy in early:
        copy.wait_send()


def own_sum(part, from_x, from_y, last, me, side, rows, start, step):
    came = from_x if side == 0 else from_y
    total = part[me, pl.ds(pl.multiple_of(start, step), step), :].astype(jnp.float32)
    total += came[0, rows, :].astype(jnp.float32)
    return total + last[side, rows, :].astype(jnp.float32)


def gather_kernel(x_ref, full_ref, local_sem, send_sems, recv_sems):
    place = partners()
    greet(place[1:3])
    copy = pltpu.make_async_copy(x_ref, full_ref.at[place[0]], local_sem)
    copy.start()
    copy.wait()
    gather_rows(full_ref, (send_sems, recv_sems), place)


def forward_kernel(
    part, stream, gain, valid, middle, full, branch_sq,
    from_x, from_y, passed, last, send_a, recv_a, send_b, recv_b,
):
    place = partners()
    me = place[0]
    greet(place[1:3])
    scatter_rows(part, from_x, from_y, passed, last, (send_a, recv_a), place)
    half = part.shape[1] // 2
    step = 16
    for side in range(2):
        @pl.loop(0, half // step)
        def _(i):
            rows = pl.ds(pl.multiple_of(i * step, step), step)
            start = side * half + i * step
            whole_rows = pl.ds(pl.multiple_of(start, step), step)
            branch = own_sum(part, from_x, from_y, last, me, side, rows, start, step)
            total = stream[whole_rows, :] + branch
            middle[whole_rows, :] = total
            inv_rms = lax.rsqrt(jnp.mean(total * total, axis=-1, keepdims=True) + epsilon)
            full[me, whole_rows, :] = (total * inv_rms * gain[...]).astype(full.dtype)
            branch_sq[whole_rows, :] = valid[whole_rows, :] * jnp.sum(
                branch * branch, axis=-1, keepdims=True
            )
    gather_rows(full, (send_b, recv_b), place)


def backward_kernel(
    part, stream, gain, grad, grad_new, full, gain_rows,
    from_x, from_y, passed, last, send_a, recv_a, send_b, recv_b,
):
    place = partners()
    me = place[0]
    greet(place[1:3])
    scatter_rows(part, from_x, from_y, passed, last, (send_a, recv_a), place)
    half = part.shape[1] // 2
    step = 16
    gain_rows[...] = jnp.zeros_like(gain_rows)
    for side in range(2):
        @pl.loop(0, half // step)
        def _(i):
            rows = pl.ds(pl.multiple_of(i * step, step), step)
            start = side * half + i * step
            whole_rows = pl.ds(pl.multiple_of(start, step), step)
            came = own_sum(part, from_x, from_y, last, me, side, rows, start, step)
            x = stream[whole_rows, :]
            inv_rms = lax.rsqrt(jnp.mean(x * x, axis=-1, keepdims=True) + epsilon)
            scaled = gain[...] * came
            along = jnp.mean(scaled * x, axis=-1, keepdims=True)
            total = grad[whole_rows, :] + inv_rms * scaled - x * (inv_rms * inv_rms * inv_rms * along)
            grad_new[whole_rows, :] = total
            full[me, whole_rows, :] = total.astype(full.dtype)
            gain_rows[...] += came * x * inv_rms
    gather_rows(full, (send_b, recv_b), place)


def scatter_kernel(
    part, out, from_x, from_y, passed, last, send_a, recv_a,
):
    place = partners()
    me = place[0]
    greet(place[1:3])
    scatter_rows(part, from_x, from_y, passed, last, (send_a, recv_a), place)
    half = part.shape[1] // 2
    step = 16
    for side in range(2):
        @pl.loop(0, half // step)
        def _(i):
            rows = pl.ds(pl.multiple_of(i * step, step), step)
            start = side * half + i * step
            out[pl.ds(pl.multiple_of(start, step), step), :] = own_sum(
                part, from_x, from_y, last, me, side, rows, start, step
            )


def rs_scratch(rows, width):
    half = rows // 2
    return [
        pltpu.VMEM((2, half, width), jnp.bfloat16),
        pltpu.VMEM((2, half, width), jnp.bfloat16),
        pltpu.VMEM((2, half, width), jnp.bfloat16),
        pltpu.VMEM((2, half, width), jnp.bfloat16),
    ]


def dma_sems(count):
    return [pltpu.SemaphoreType.DMA((count,)), pltpu.SemaphoreType.DMA((count,))]


def linked_call(kernel, number, out_shape, scratch, micros, *args):
    vmem = pl.BlockSpec(memory_space=pltpu.VMEM)
    return pl.pallas_call(
        kernel,
        out_shape=out_shape,
        in_specs=[vmem] * len(args),
        out_specs=jax.tree.map(lambda _: vmem, out_shape),
        scratch_shapes=scratch,
        compiler_params=pltpu.CompilerParams(
            collective_id=number, has_side_effects=True, vmem_limit_bytes=48 << 20
        ),
        cost_estimate=pl.CostEstimate(
            flops=0, bytes_accessed=int(micros * 3.6e6), transcendentals=0
        ),
    )(*args)


def gather_ctx(x):
    rows, width = x.shape
    return linked_call(
        gather_kernel, 1, jax.ShapeDtypeStruct((4, rows, width), x.dtype),
        [pltpu.SemaphoreType.DMA] + dma_sems(6), 31, x,
    )


def forward_step(part, stream, gain, valid):
    rows, width = stream.shape
    return linked_call(
        forward_kernel, 2,
        (
            jax.ShapeDtypeStruct((rows, width), jnp.float32),
            jax.ShapeDtypeStruct((4, rows, width), jnp.bfloat16),
            jax.ShapeDtypeStruct((rows, 1), jnp.float32),
        ),
        rs_scratch(rows, width) + dma_sems(6) + dma_sems(6), 65,
        part, stream, gain, valid,
    )


def backward_step(part, stream, gain, grad):
    rows, width = stream.shape
    return linked_call(
        backward_kernel, 3,
        (
            jax.ShapeDtypeStruct((rows, width), jnp.float32),
            jax.ShapeDtypeStruct((4, rows, width), jnp.bfloat16),
            jax.ShapeDtypeStruct((16, width), jnp.float32),
        ),
        rs_scratch(rows, width) + dma_sems(6) + dma_sems(6), 65,
        part, stream, gain, grad,
    )


def scatter_ctx(part):
    _, rows, width = part.shape
    return linked_call(
        scatter_kernel, 4, jax.ShapeDtypeStruct((rows, width), jnp.float32),
        rs_scratch(rows, width) + dma_sems(6), 31, part,
    )


def dot32(a, b, dims):
    return lax.dot_general(a, b, (dims, ((), ())), preferred_element_type=jnp.float32)


def planned(
    tokens, positions, valid, piece_starts, d_out,
    attn_gain, w_query, w_key, w_value, w_out, mlp_gain, w_gate, w_up, w_down,
):
    seq_count, rows, width = tokens.shape
    layers = attn_gain.shape[0]
    ctx_count = lax.axis_size("ctx")
    tp_count = lax.axis_size("tp")
    me = lax.axis_index("ctx")
    side = lax.axis_index("tp")
    length = rows * ctx_count
    heads_q = HEADS // tp_count // ctx_count
    heads_k = KV_HEADS // tp_count // ctx_count
    group = HEADS // KV_HEADS
    cols_q = heads_q * HEAD_DIM
    cols_k = heads_k * HEAD_DIM
    units = w_gate.shape[2] // ctx_count
    score_scale = HEAD_DIM ** (-0.5)

    def own(a):
        return lax.dynamic_index_in_dim(a, side, 0, keepdims=False)

    def cut(w, axis, count):
        return lax.dynamic_slice_in_dim(w, me * count, count, axis)

    def whole(w):
        return lax.all_gather(w, ("tp", "fsdp"), axis=0, tiled=True).reshape(
            tp_count, width, w.shape[1]
        )

    attn_w, mlp_w = [], []
    for layer in range(layers):
        attn_w.append(whole(jnp.concatenate([
            cut(w_query[layer], 1, cols_q),
            cut(w_key[layer], 1, cols_k),
            cut(w_value[layer], 1, cols_k),
            cut(w_out[layer], 0, cols_q).T,
        ], axis=1)))
        mlp_w.append(whole(jnp.concatenate([
            cut(w_gate[layer], 1, units),
            cut(w_up[layer], 1, units),
            cut(w_down[layer], 0, units).T,
        ], axis=1)))
    gains = lax.all_gather(
        jnp.concatenate([attn_gain, mlp_gain], 0), "fsdp", axis=1, tiled=True
    ).astype(jnp.float32)
    gain_a = [gains[layer][None] for layer in range(layers)]
    gain_m = [gains[layers + layer][None] for layer in range(layers)]

    seq_pos, seq_valid = own(positions), own(valid)
    starts = own(piece_starts)
    both = lax.all_gather(jnp.stack([seq_pos, seq_valid]), "ctx", axis=1, tiled=True)
    pos_all, valid_all = both[0], both[1]
    half_dim = HEAD_DIM // 2
    freqs = rope_base ** (-(jnp.arange(half_dim).astype(jnp.float32) * 2.0 / HEAD_DIM))
    angles = pos_all.astype(jnp.float32)[:, None] * freqs
    cosine, sine_t = jnp.cos(angles)[None], jnp.sin(angles)[None]
    index = jnp.arange(length, dtype=jnp.int32)
    inside = (index[None, :] >= starts[:, None]) & (index[None, :] < starts[:, None] + PIECE_LEN)
    same_piece = jnp.any(inside[:, :, None] & inside[:, None, :], axis=0)
    causal = index[None, :] <= index[:, None]
    diagonal = index[None, :] == index[:, None]
    allowed = (causal | same_piece) & ((valid_all[None, :] > 0) | diagonal)

    valid_f = seq_valid.astype(jnp.float32)[:, None]
    stream = own(tokens).astype(jnp.float32)
    grad = own(d_out).astype(jnp.float32)
    down_grad = gather_ctx(own(d_out)).reshape(length, width)
    normed = gather_ctx(normalize(stream, gain_a[0]).astype(jnp.bfloat16))

    def heads_of(flat, count):
        return flat.reshape(length, count, HEAD_DIM).swapaxes(0, 1)

    def flat_of(heads):
        return heads.swapaxes(0, 1).reshape(length, -1)

    def attn_scores(query, key):
        raw = jnp.einsum(
            "kgqd,knd->kgqn", query, key, preferred_element_type=jnp.float32
        ) * score_scale
        return jnp.where(allowed, raw, neg_big)

    kv_total = heads_k * tp_count
    stat_rows = []
    saved = []
    branch_out = None
    for layer in range(layers):
        normed_a = normed.reshape(length, width)
        parts = [dot32(normed_a, attn_w[layer][t][:, : cols_q + 2 * cols_k], ((1,), (0,))) for t in range(tp_count)]
        query = jnp.concatenate([heads_of(p[:, :cols_q], heads_q) for p in parts])
        key = jnp.concatenate([heads_of(p[:, cols_q : cols_q + cols_k], heads_k) for p in parts])
        value = jnp.concatenate([heads_of(p[:, cols_q + cols_k :], heads_k) for p in parts])
        query = rotate(query, cosine, sine_t).astype(jnp.bfloat16).reshape(kv_total, group, length, HEAD_DIM)
        key = rotate(key, cosine, sine_t).astype(jnp.bfloat16)
        value = value.astype(jnp.bfloat16)
        raw = attn_scores(query, key)
        row_max = jnp.max(raw, axis=-1, keepdims=True)
        log_total = row_max + jnp.log(jnp.sum(jnp.exp(raw - row_max), axis=-1, keepdims=True))
        probs = jnp.exp(raw - log_total).astype(jnp.bfloat16)
        mixed = jnp.einsum("kgqn,knd->kgqd", probs, value, preferred_element_type=jnp.float32)
        mixed = mixed.astype(jnp.bfloat16).reshape(tp_count, heads_q, length, HEAD_DIM)
        mixed = [flat_of(mixed[t]) for t in range(tp_count)]
        part = sum(
            dot32(mixed[t], attn_w[layer][t][:, cols_q + 2 * cols_k :], ((1,), (1,))) for t in range(tp_count)
        )
        middle, normed_m, attn_sq = forward_step(
            part.astype(jnp.bfloat16).reshape(4, rows, width), stream, gain_m[layer], valid_f
        )
        normed_m = normed_m.reshape(length, width)
        gates = [dot32(normed_m, mlp_w[layer][t][:, :units], ((1,), (0,))) for t in range(tp_count)]
        ups = [dot32(normed_m, mlp_w[layer][t][:, units : 2 * units], ((1,), (0,))) for t in range(tp_count)]
        hidden = [(jax.nn.silu(g) * u).astype(jnp.bfloat16) for g, u in zip(gates, ups)]
        part = sum(dot32(hidden[t], mlp_w[layer][t][:, 2 * units :], ((1,), (1,))) for t in range(tp_count))
        part = part.astype(jnp.bfloat16).reshape(4, rows, width)
        saved.append((stream, normed_a, query, key, value, log_total, mixed, middle, normed_m, gates, ups, hidden))
        stat_rows.append(jnp.sum(valid_f * stream * stream))
        stat_rows.append(jnp.sum(attn_sq))
        if layer + 1 < layers:
            stream, normed, mlp_sq = forward_step(part, middle, gain_a[layer + 1], valid_f)
            stat_rows.append(jnp.sum(mlp_sq))
        else:
            branch_out = scatter_ctx(part)
            stat_rows.append(jnp.sum(valid_f * branch_out * branch_out))
            stream = middle + branch_out
    output = lax.all_gather(stream.astype(jnp.bfloat16), "tp", axis=0)
    sums = lax.psum(
        jnp.concatenate([jnp.stack(stat_rows), jnp.sum(valid_f)[None]]), ("fsdp", "ctx", "tp")
    )
    rms_stats = jnp.sqrt(sums[:-1] / (sums[-1] * width)).reshape(layers, 3)

    def reduced(g):
        return lax.psum_scatter(
            g.astype(jnp.bfloat16).reshape(tp_count * width, -1), ("tp", "fsdp"), scatter_dimension=0, tiled=True
        )

    results = [None] * layers
    input_grad = None
    for layer in reversed(range(layers)):
        stream_in, normed_a, query, key, value, log_total, mixed, middle, normed_m, gates, ups, hidden = saved[layer]
        grad_gate, grad_up, part = [], [], 0.0
        for t in range(tp_count):
            wt = mlp_w[layer][t]
            grad_hidden = dot32(down_grad, wt[:, 2 * units :], ((1,), (0,)))
            sig = jax.nn.sigmoid(gates[t])
            grad_gate.append((grad_hidden * ups[t] * sig * (1.0 + gates[t] * (1.0 - sig))).astype(jnp.bfloat16))
            grad_up.append((grad_hidden * gates[t] * sig).astype(jnp.bfloat16))
            part += dot32(grad_gate[t], wt[:, :units], ((1,), (1,)))
            part += dot32(grad_up[t], wt[:, units : 2 * units], ((1,), (1,)))
        g_down = jnp.stack([dot32(down_grad, hidden[t], ((0,), (0,))).astype(jnp.bfloat16) for t in range(tp_count)])
        g_gate = jnp.stack([dot32(normed_m, grad_gate[t], ((0,), (0,))).astype(jnp.bfloat16) for t in range(tp_count)])
        g_up = jnp.stack([dot32(normed_m, grad_up[t], ((0,), (0,))).astype(jnp.bfloat16) for t in range(tp_count)])
        share_mlp = jnp.concatenate([reduced(g_gate), reduced(g_up), reduced(g_down)], axis=1)
        grad_mid, attn_grad, gm_rows = backward_step(
            part.astype(jnp.bfloat16).reshape(4, rows, width), middle, gain_m[layer], grad
        )
        attn_grad = attn_grad.reshape(length, width)
        grad_heads = [dot32(attn_grad, attn_w[layer][t][:, cols_q + 2 * cols_k :], ((1,), (0,))).astype(jnp.bfloat16) for t in range(tp_count)]
        g_out = [dot32(attn_grad, mixed[t], ((0,), (0,))).astype(jnp.bfloat16) for t in range(tp_count)]
        gh = jnp.concatenate([heads_of(g, heads_q) for g in grad_heads]).reshape(kv_total, group, length, HEAD_DIM)
        probs = jnp.exp(attn_scores(query, key) - log_total)
        grad_probs = jnp.einsum("kgqd,knd->kgqn", gh, value, preferred_element_type=jnp.float32)
        row_dots = jnp.sum(probs * grad_probs, axis=-1, keepdims=True)
        grad_scores = (probs * (grad_probs - row_dots)).astype(jnp.bfloat16)
        gq = jnp.einsum("kgqn,knd->kgqd", grad_scores, key, preferred_element_type=jnp.float32) * score_scale
        gk = jnp.einsum("kgqn,kgqd->knd", grad_scores, query, preferred_element_type=jnp.float32) * score_scale
        gv = jnp.einsum("kgqn,kgqd->knd", probs.astype(jnp.bfloat16), gh, preferred_element_type=jnp.float32)
        gq = rotate(gq.reshape(kv_total * group, length, HEAD_DIM), cosine, -sine_t).astype(jnp.bfloat16)
        gk = rotate(gk, cosine, -sine_t).astype(jnp.bfloat16)
        gv = gv.astype(jnp.bfloat16)
        part = 0.0
        g_attn = []
        for t in range(tp_count):
            gqkv = jnp.concatenate([
                flat_of(gq[t * heads_q : (t + 1) * heads_q]),
                flat_of(gk[t * heads_k : (t + 1) * heads_k]),
                flat_of(gv[t * heads_k : (t + 1) * heads_k]),
            ], axis=1)
            part += dot32(gqkv, attn_w[layer][t][:, : cols_q + 2 * cols_k], ((1,), (1,)))
            g_attn.append(dot32(normed_a, gqkv, ((0,), (0,))).astype(jnp.bfloat16))
        grad, down_grad, ga_rows = backward_step(
            part.astype(jnp.bfloat16).reshape(4, rows, width), stream_in, gain_a[layer], grad_mid
        )
        down_grad = down_grad.reshape(length, width)
        gain_grads = jnp.stack([jnp.sum(ga_rows, 0), jnp.sum(gm_rows, 0)], axis=1).astype(jnp.bfloat16)
        g_attn = jnp.stack([jnp.concatenate([g_attn[t], g_out[t], gain_grads if t == 0 else jnp.zeros_like(gain_grads)], axis=1) for t in range(tp_count)])
        share_attn = reduced(g_attn)
        results[layer] = (share_attn, share_mlp)
    input_grad = lax.all_gather(grad, "tp", axis=0)

    outs = [[] for _ in range(9)]
    for layer in range(layers):
        share_attn, share_mlp = results[layer]
        ga = lax.all_gather(share_attn, "ctx", axis=0).astype(jnp.float32)
        gm = lax.all_gather(share_mlp, "ctx", axis=0).astype(jnp.float32)

        def columns(a):
            return a.swapaxes(0, 1).reshape(a.shape[1], -1)

        def turned(a):
            return a.swapaxes(1, 2).reshape(-1, a.shape[1])

        base = cols_q + 2 * cols_k
        gain_sum = lax.psum(jnp.sum(ga[:, :, base + cols_q :], 0), "tp")
        outs[0].append(gain_sum[:, 0])
        outs[1].append(columns(ga[:, :, :cols_q]))
        outs[2].append(columns(ga[:, :, cols_q : cols_q + cols_k]))
        outs[3].append(columns(ga[:, :, cols_q + cols_k : base]))
        outs[4].append(turned(ga[:, :, base : base + cols_q]))
        outs[5].append(gain_sum[:, 1])
        outs[6].append(columns(gm[:, :, :units]))
        outs[7].append(columns(gm[:, :, units : 2 * units]))
        outs[8].append(turned(gm[:, :, 2 * units :]))
    stacked = [jnp.stack(o) for o in outs]
    return (output, input_grad, *stacked, rms_stats)


def fits(mesh):
    tp_count, ctx_count = mesh.shape["tp"], mesh.shape["ctx"]
    return ctx_count == 4 and tp_count == 2


def solution(mesh):
    in_specs = (
        P("fsdp", "ctx", None),
        P("fsdp", "ctx"),
        P("fsdp", "ctx"),
        P("fsdp", None),
        P("fsdp", "ctx", None),
        P(None, "fsdp"),
        P(None, "fsdp", "tp"),
        P(None, "fsdp", "tp"),
        P(None, "fsdp", "tp"),
        P(None, "tp", "fsdp"),
        P(None, "fsdp"),
        P(None, "fsdp", "tp"),
        P(None, "fsdp", "tp"),
        P(None, "tp", "fsdp"),
    )
    out_specs = (
        P("fsdp", "ctx", None),
        P("fsdp", "ctx", None),
        P(None, "fsdp"),
        P(None, "fsdp", "tp"),
        P(None, "fsdp", "tp"),
        P(None, "fsdp", "tp"),
        P(None, "tp", "fsdp"),
        P(None, "fsdp"),
        P(None, "fsdp", "tp"),
        P(None, "fsdp", "tp"),
        P(None, "tp", "fsdp"),
        P(),
    )
    return jax.shard_map(planned if fits(mesh) else general, mesh=mesh, in_specs=in_specs, out_specs=out_specs, check_vma=False)
```

```python
import functools

import jax
import jax.numpy as jnp
from jax import lax
from jax.experimental import pallas as pl
from jax.experimental.pallas import tpu as pltpu
from jax.sharding import PartitionSpec as P

MESH = pl.DeviceIdType.MESH

HEADS = 16
KV_HEADS = 8
HEAD_DIM = 96
PIECE_LEN = 256


epsilon = 1e-05
rope_base = 100000.0
neg_big = -1e30


def rope_tables(positions, head_dim):
    half_dim = head_dim // 2
    freqs = rope_base ** (-(jnp.arange(half_dim).astype(jnp.float32) * 2.0 / head_dim))
    angles = positions.astype(jnp.float32)[..., None] * freqs
    return (jnp.cos(angles)[:, :, None, :], jnp.sin(angles)[:, :, None, :])


def rotate(values, cosine, sine_t):
    half_dim = values.shape[-1] // 2
    lead_part = values[..., :half_dim]
    tail_part = values[..., half_dim:]
    return jnp.concatenate(
        [lead_part * cosine - tail_part * sine_t, tail_part * cosine + lead_part * sine_t], axis=-1
    )


def normalize(stream, gain_vec):
    inv_rms = lax.rsqrt(jnp.mean(stream * stream, axis=-1, keepdims=True) + epsilon)
    return stream * inv_rms * gain_vec.astype(jnp.float32)


def norm_back(stream, gain_vec, grad_out):
    inv_rms = lax.rsqrt(jnp.mean(stream * stream, axis=-1, keepdims=True) + epsilon)
    scaled_grad = gain_vec.astype(jnp.float32) * grad_out
    grad_in = inv_rms * scaled_grad - stream * inv_rms**3 * jnp.mean(
        scaled_grad * stream, axis=-1, keepdims=True
    )
    grad_gain = jnp.sum(grad_out * stream * inv_rms, axis=0)
    return (grad_in, grad_gain)


def score_block(query_b, key_heads, allowed, score_scale):
    raw_scores = (
        jnp.einsum("sckgd,snkd->skgcn", query_b, key_heads, preferred_element_type=jnp.float32)
        * score_scale
    )
    return jnp.where(allowed[:, None, None], raw_scores, neg_big)


def general(
    tokens,
    positions,
    valid,
    piece_starts,
    d_out,
    attn_gain,
    w_query,
    w_key,
    w_value,
    w_out,
    mlp_gain,
    w_gate,
    w_up,
    w_down,
):
    seq_count, shard_len, model_width = tokens.shape
    tok_rows = seq_count * shard_len
    tp_count = lax.axis_size("tp")
    local_heads = HEADS // tp_count
    local_kv = KV_HEADS // tp_count
    group_size = HEADS // KV_HEADS
    score_scale = HEAD_DIM ** (-0.5)
    seq_length = shard_len * lax.axis_size("ctx")
    start_tok = lax.axis_index("ctx") * shard_len
    query_index = start_tok + jnp.arange(shard_len, dtype=jnp.int32)
    key_index = jnp.arange(seq_length, dtype=jnp.int32)
    cosine, sine_t = rope_tables(positions, HEAD_DIM)
    valid_flat = valid.astype(jnp.float32).reshape(tok_rows)
    in_query = (query_index[None, None, :] >= piece_starts[:, :, None]) & (
        query_index[None, None, :] < piece_starts[:, :, None] + PIECE_LEN
    )
    in_key = (key_index[None, None, :] >= piece_starts[:, :, None]) & (
        key_index[None, None, :] < piece_starts[:, :, None] + PIECE_LEN
    )
    same_piece = jnp.any(in_query[:, :, :, None] & in_key[:, :, None, :], axis=1)
    causal = key_index[None, :] <= query_index[:, None]
    diagonal = key_index[None, :] == query_index[:, None]
    layer_count = attn_gain.shape[0]
    stream = tokens.astype(jnp.float32).reshape(tok_rows, model_width)
    saved = []
    stat_rows = []
    for layer_no in range(layer_count):
        weights = (
            lax.all_gather(attn_gain[layer_no], "fsdp", axis=0, tiled=True),
            lax.all_gather(w_query[layer_no], "fsdp", axis=0, tiled=True),
            lax.all_gather(w_key[layer_no], "fsdp", axis=0, tiled=True),
            lax.all_gather(w_value[layer_no], "fsdp", axis=0, tiled=True),
            lax.all_gather(w_out[layer_no], "fsdp", axis=1, tiled=True),
            lax.all_gather(mlp_gain[layer_no], "fsdp", axis=0, tiled=True),
            lax.all_gather(w_gate[layer_no], "fsdp", axis=0, tiled=True),
            lax.all_gather(w_up[layer_no], "fsdp", axis=0, tiled=True),
            lax.all_gather(w_down[layer_no], "fsdp", axis=1, tiled=True),
        )
        gain_a, w_q, w_k, w_v, w_o, gain_m, w_g, w_u, w_d = weights
        normed_a = normalize(stream, gain_a).astype(jnp.bfloat16)
        query_heads = jnp.dot(normed_a, w_q, preferred_element_type=jnp.float32).reshape(
            seq_count, shard_len, local_heads, HEAD_DIM
        )
        query_b = (
            rotate(query_heads, cosine, sine_t)
            .astype(jnp.bfloat16)
            .reshape(seq_count, shard_len, local_kv, group_size, HEAD_DIM)
        )
        key_local = jnp.dot(normed_a, w_k, preferred_element_type=jnp.float32).reshape(
            seq_count, shard_len, local_kv, HEAD_DIM
        )
        key_local = (
            rotate(key_local, cosine, sine_t)
            .astype(jnp.bfloat16)
            .reshape(seq_count, shard_len, local_kv * HEAD_DIM)
        )
        value_local = (
            jnp.dot(normed_a, w_v, preferred_element_type=jnp.float32)
            .astype(jnp.bfloat16)
            .reshape(seq_count, shard_len, local_kv * HEAD_DIM)
        )
        key_all, value_all, valid_all = (
            lax.all_gather(key_local, "ctx", axis=1, tiled=True),
            lax.all_gather(value_local, "ctx", axis=1, tiled=True),
            lax.all_gather(valid.astype(jnp.bfloat16), "ctx", axis=1, tiled=True),
        )
        allowed = (causal[None] | same_piece) & ((valid_all[:, None, :] > 0.5) | diagonal[None])
        key_heads = key_all.reshape(seq_count, seq_length, local_kv, HEAD_DIM)
        value_heads = value_all.reshape(seq_count, seq_length, local_kv, HEAD_DIM)
        raw_scores = score_block(query_b, key_heads, allowed, score_scale)
        row_max = jnp.max(raw_scores, axis=-1, keepdims=True)
        log_total = row_max + jnp.log(
            jnp.sum(jnp.exp(raw_scores - row_max), axis=-1, keepdims=True)
        )
        softmax_b = jnp.exp(raw_scores - log_total).astype(jnp.bfloat16)
        mixed_heads = jnp.einsum(
            "skgcn,snkd->sckgd", softmax_b, value_heads, preferred_element_type=jnp.float32
        )
        mixed_b = mixed_heads.astype(jnp.bfloat16).reshape(tok_rows, local_heads * HEAD_DIM)
        attn_branch = lax.psum(
            jnp.dot(mixed_b, w_o, preferred_element_type=jnp.float32).astype(jnp.bfloat16), "tp"
        ).astype(jnp.float32)
        middle = stream + attn_branch
        normed_m = normalize(middle, gain_m).astype(jnp.bfloat16)
        gate_act = jnp.dot(normed_m, w_g, preferred_element_type=jnp.float32)
        up_act = jnp.dot(normed_m, w_u, preferred_element_type=jnp.float32)
        hidden = (jax.nn.silu(gate_act) * up_act).astype(jnp.bfloat16)
        mlp_branch = lax.psum(
            jnp.dot(hidden, w_d, preferred_element_type=jnp.float32).astype(jnp.bfloat16), "tp"
        ).astype(jnp.float32)
        stat_rows.append(
            jnp.stack(
                [
                    jnp.sum(valid_flat[:, None] * stream * stream),
                    jnp.sum(valid_flat[:, None] * attn_branch * attn_branch),
                    jnp.sum(valid_flat[:, None] * mlp_branch * mlp_branch),
                ]
            )
        )
        kept_weights = None
        saved.append(
            (
                stream,
                normed_a,
                query_b,
                key_heads,
                value_heads,
                allowed,
                log_total,
                mixed_b,
                middle,
                normed_m,
                gate_act,
                up_act,
                hidden,
                kept_weights,
            )
        )
        stream = middle + mlp_branch
    output = stream.astype(jnp.bfloat16).reshape(seq_count, shard_len, model_width)
    total_squares, total_count = lax.psum(
        (jnp.stack(stat_rows), jnp.sum(valid_flat)), ("fsdp", "ctx")
    )
    rms_stats = jnp.sqrt(total_squares / (total_count * model_width))
    grad_stream = d_out.astype(jnp.float32).reshape(tok_rows, model_width)
    results = [None] * layer_count
    for layer_no in reversed(range(layer_count)):
        (
            stream_in,
            normed_a,
            query_b,
            key_heads,
            value_heads,
            allowed,
            log_total,
            mixed_b,
            middle,
            normed_m,
            gate_act,
            up_act,
            hidden,
            kept_weights,
        ) = saved[layer_no]
        weights = (
            lax.all_gather(attn_gain[layer_no], "fsdp", axis=0, tiled=True),
            lax.all_gather(w_query[layer_no], "fsdp", axis=0, tiled=True),
            lax.all_gather(w_key[layer_no], "fsdp", axis=0, tiled=True),
            lax.all_gather(w_value[layer_no], "fsdp", axis=0, tiled=True),
            lax.all_gather(w_out[layer_no], "fsdp", axis=1, tiled=True),
            lax.all_gather(mlp_gain[layer_no], "fsdp", axis=0, tiled=True),
            lax.all_gather(w_gate[layer_no], "fsdp", axis=0, tiled=True),
            lax.all_gather(w_up[layer_no], "fsdp", axis=0, tiled=True),
            lax.all_gather(w_down[layer_no], "fsdp", axis=1, tiled=True),
        )
        gain_a, w_q, w_k, w_v, w_o, gain_m, w_g, w_u, w_d = weights
        grad_mlp = grad_stream.astype(jnp.bfloat16)
        grad_hidden = jnp.einsum("rd,fd->rf", grad_mlp, w_d, preferred_element_type=jnp.float32)
        g_down = jnp.einsum("rf,rd->fd", hidden, grad_mlp, preferred_element_type=jnp.float32)
        sigmoid_g = jax.nn.sigmoid(gate_act)
        grad_gate = (
            grad_hidden * up_act * sigmoid_g * (1.0 + gate_act * (1.0 - sigmoid_g))
        ).astype(jnp.bfloat16)
        grad_up = (grad_hidden * gate_act * sigmoid_g).astype(jnp.bfloat16)
        grad_normed_m = lax.psum(
            (
                jnp.einsum("rf,df->rd", grad_gate, w_g, preferred_element_type=jnp.float32)
                + jnp.einsum("rf,df->rd", grad_up, w_u, preferred_element_type=jnp.float32)
            ).astype(jnp.bfloat16),
            "tp",
        ).astype(jnp.float32)
        g_gate = jnp.einsum("rd,rf->df", normed_m, grad_gate, preferred_element_type=jnp.float32)
        g_up = jnp.einsum("rd,rf->df", normed_m, grad_up, preferred_element_type=jnp.float32)
        grad_from_norm, g_gain_m = norm_back(middle, gain_m, grad_normed_m)
        grad_middle = grad_stream + grad_from_norm
        grad_attn = grad_middle.astype(jnp.bfloat16)
        grad_heads = jnp.einsum(
            "rd,hd->rh", grad_attn, w_o, preferred_element_type=jnp.float32
        ).astype(jnp.bfloat16)
        g_out = jnp.einsum("rh,rd->hd", mixed_b, grad_attn, preferred_element_type=jnp.float32)
        grad_heads = grad_heads.reshape(seq_count, shard_len, local_kv, group_size, HEAD_DIM)
        raw_scores = score_block(query_b, key_heads, allowed, score_scale)
        softmax_p = jnp.exp(raw_scores - log_total)
        grad_probs = jnp.einsum(
            "sckgd,snkd->skgcn", grad_heads, value_heads, preferred_element_type=jnp.float32
        )
        row_dots = jnp.sum(softmax_p * grad_probs, axis=-1, keepdims=True)
        grad_scores = (softmax_p * (grad_probs - row_dots)).astype(jnp.bfloat16)
        grad_query = (
            jnp.einsum(
                "skgcn,snkd->sckgd", grad_scores, key_heads, preferred_element_type=jnp.float32
            )
            * score_scale
        )
        grad_key_all = (
            jnp.einsum(
                "skgcn,sckgd->snkd", grad_scores, query_b, preferred_element_type=jnp.float32
            )
            * score_scale
        )
        grad_value_all = jnp.einsum(
            "skgcn,sckgd->snkd",
            softmax_p.astype(jnp.bfloat16),
            grad_heads,
            preferred_element_type=jnp.float32,
        )
        grad_key, grad_value = (
            lax.psum_scatter(
                grad_key_all.reshape(seq_count, seq_length, local_kv * HEAD_DIM).astype(
                    jnp.bfloat16
                ),
                "ctx",
                scatter_dimension=1,
                tiled=True,
            ).astype(jnp.float32),
            lax.psum_scatter(
                grad_value_all.reshape(seq_count, seq_length, local_kv * HEAD_DIM).astype(
                    jnp.bfloat16
                ),
                "ctx",
                scatter_dimension=1,
                tiled=True,
            ).astype(jnp.float32),
        )
        grad_query_b = rotate(
            grad_query.reshape(seq_count, shard_len, local_heads, HEAD_DIM), cosine, -sine_t
        )
        grad_query_b = grad_query_b.astype(jnp.bfloat16).reshape(tok_rows, local_heads * HEAD_DIM)
        grad_key_b = rotate(
            grad_key.reshape(seq_count, shard_len, local_kv, HEAD_DIM), cosine, -sine_t
        )
        grad_key_b = grad_key_b.astype(jnp.bfloat16).reshape(tok_rows, local_kv * HEAD_DIM)
        grad_value_b = grad_value.astype(jnp.bfloat16).reshape(tok_rows, local_kv * HEAD_DIM)
        grad_normed_a = lax.psum(
            (
                jnp.einsum("rh,dh->rd", grad_query_b, w_q, preferred_element_type=jnp.float32)
                + jnp.einsum("rh,dh->rd", grad_key_b, w_k, preferred_element_type=jnp.float32)
                + jnp.einsum("rh,dh->rd", grad_value_b, w_v, preferred_element_type=jnp.float32)
            ).astype(jnp.bfloat16),
            "tp",
        ).astype(jnp.float32)
        g_query = jnp.einsum(
            "rd,rh->dh", normed_a, grad_query_b, preferred_element_type=jnp.float32
        )
        g_key = jnp.einsum("rd,rh->dh", normed_a, grad_key_b, preferred_element_type=jnp.float32)
        g_value = jnp.einsum(
            "rd,rh->dh", normed_a, grad_value_b, preferred_element_type=jnp.float32
        )
        grad_from_attn_norm, g_gain_a = norm_back(stream_in, gain_a, grad_normed_a)
        grad_stream = grad_middle + grad_from_attn_norm
        grad_terms = (g_gain_a, g_query, g_key, g_value, g_out, g_gain_m, g_gate, g_up, g_down)
        shares = (
            lax.psum_scatter(grad_terms[0], ("fsdp", "ctx"), scatter_dimension=0, tiled=True),
            lax.psum_scatter(grad_terms[1], ("fsdp", "ctx"), scatter_dimension=0, tiled=True),
            lax.psum_scatter(grad_terms[2], ("fsdp", "ctx"), scatter_dimension=0, tiled=True),
            lax.psum_scatter(grad_terms[3], ("fsdp", "ctx"), scatter_dimension=0, tiled=True),
            lax.psum_scatter(grad_terms[4], ("fsdp", "ctx"), scatter_dimension=1, tiled=True),
            lax.psum_scatter(grad_terms[5], ("fsdp", "ctx"), scatter_dimension=0, tiled=True),
            lax.psum_scatter(grad_terms[6], ("fsdp", "ctx"), scatter_dimension=0, tiled=True),
            lax.psum_scatter(grad_terms[7], ("fsdp", "ctx"), scatter_dimension=0, tiled=True),
            lax.psum_scatter(grad_terms[8], ("fsdp", "ctx"), scatter_dimension=1, tiled=True),
        )
        results[layer_no] = (
            lax.all_gather(shares[0].astype(jnp.bfloat16), "ctx", axis=0, tiled=True).astype(
                jnp.float32
            ),
            lax.all_gather(shares[1].astype(jnp.bfloat16), "ctx", axis=0, tiled=True).astype(
                jnp.float32
            ),
            lax.all_gather(shares[2].astype(jnp.bfloat16), "ctx", axis=0, tiled=True).astype(
                jnp.float32
            ),
            lax.all_gather(shares[3].astype(jnp.bfloat16), "ctx", axis=0, tiled=True).astype(
                jnp.float32
            ),
            lax.all_gather(shares[4].astype(jnp.bfloat16), "ctx", axis=1, tiled=True).astype(
                jnp.float32
            ),
            lax.all_gather(shares[5].astype(jnp.bfloat16), "ctx", axis=0, tiled=True).astype(
                jnp.float32
            ),
            lax.all_gather(shares[6].astype(jnp.bfloat16), "ctx", axis=0, tiled=True).astype(
                jnp.float32
            ),
            lax.all_gather(shares[7].astype(jnp.bfloat16), "ctx", axis=0, tiled=True).astype(
                jnp.float32
            ),
            lax.all_gather(shares[8].astype(jnp.bfloat16), "ctx", axis=1, tiled=True).astype(
                jnp.float32
            ),
        )
    stacked = [
        jnp.stack([results[layer_no][member] for layer_no in range(layer_count)])
        for member in range(9)
    ]
    input_grad = grad_stream.reshape(seq_count, shard_len, model_width)
    return (
        output,
        input_grad,
        stacked[0],
        stacked[1],
        stacked[2],
        stacked[3],
        stacked[4],
        stacked[5],
        stacked[6],
        stacked[7],
        stacked[8],
        rms_stats,
    )


def partners():
    me = lax.axis_index("ctx")
    return me, me ^ 1, me ^ 2, me ^ 3


def greet(*places):
    barrier = pltpu.get_barrier_semaphore()
    for place in places:
        pl.semaphore_signal(barrier, inc=1, device_id=place, device_id_type=MESH)
    pl.semaphore_wait(barrier, len(places))


def send(src, dst, sems, slot, place):
    copy = pltpu.make_async_remote_copy(
        src_ref=src,
        dst_ref=dst,
        send_sem=sems[0].at[slot],
        recv_sem=sems[1].at[slot],
        device_id=place,
        device_id_type=MESH,
    )
    copy.start()
    return copy


def nothing():
    pass


def gather_rows(full, sems, place, work=(nothing, nothing)):
    me, side_x, side_y, _ = place
    to_x, to_y = {"ctx": side_x}, {"ctx": side_y}
    half = full.shape[1] // 2
    top, low = pl.ds(0, half), pl.ds(half, half)
    first = [
        send(full.at[me, top], full.at[me, top], sems, 0, to_x),
        send(full.at[me, low], full.at[me, low], sems, 1, to_y),
    ]
    rest = [
        send(full.at[me, top], full.at[me, top], sems, 2, to_y),
        send(full.at[me, low], full.at[me, low], sems, 3, to_x),
    ]
    work[0]()
    first[0].wait_recv()
    rest.append(send(full.at[side_x, top], full.at[side_x, top], sems, 4, to_y))
    first[1].wait_recv()
    rest.append(send(full.at[side_y, low], full.at[side_y, low], sems, 5, to_x))
    work[1]()
    for copy in rest:
        copy.wait()
    for copy in first:
        copy.wait_send()


def scatter_rows(part, from_x, from_y, passed, last, sems, place, work=(nothing, nothing)):
    me, side_x, side_y, across = place
    to_x, to_y = {"ctx": side_x}, {"ctx": side_y}
    half = part.shape[1] // 2
    top, low = pl.ds(0, half), pl.ds(half, half)
    early = [
        send(part.at[across, top], from_x.at[1], sems, 0, to_x),
        send(part.at[across, low], from_y.at[1], sems, 1, to_y),
    ]
    rest = [
        send(part.at[side_x, top], from_x.at[0], sems, 2, to_x),
        send(part.at[side_y, low], from_y.at[0], sems, 3, to_y),
    ]
    step = 16

    def add_to(slot, owner, start, came):
        @pl.loop(0, half // step)
        def _(i):
            rows = pl.ds(pl.multiple_of(i * step, step), step)
            mine = part[owner, pl.ds(pl.multiple_of(start + i * step, step), step), :]
            total = mine.astype(jnp.float32) + came[1, rows, :].astype(jnp.float32)
            passed[slot, rows, :] = total.astype(passed.dtype)

    work[0]()
    early[0].wait_recv()
    add_to(0, side_y, 0, from_x)
    rest.append(send(passed.at[0], last.at[0], sems, 4, to_y))
    early[1].wait_recv()
    add_to(1, side_x, half, from_y)
    rest.append(send(passed.at[1], last.at[1], sems, 5, to_x))
    work[1]()
    for copy in rest:
        copy.wait()
    for copy in early:
        copy.wait_send()


def own_sum(part, from_x, from_y, last, me, side, rows, start, step):
    came = from_x if side == 0 else from_y
    total = part[me, pl.ds(pl.multiple_of(start, step), step), :].astype(jnp.float32)
    total += came[0, rows, :].astype(jnp.float32)
    return total + last[side, rows, :].astype(jnp.float32)


def gather_kernel(x_ref, full_ref, local_sem, send_sems, recv_sems):
    place = partners()
    greet({"ctx": place[1]}, {"ctx": place[2]})
    copy = pltpu.make_async_copy(x_ref, full_ref.at[place[0]], local_sem)
    copy.start()
    copy.wait()
    gather_rows(full_ref, (send_sems, recv_sems), place)


def forward_kernel(
    part, stream, gain, valid, middle, full, branch_sq,
    from_x, from_y, passed, last, send_a, recv_a, send_b, recv_b,
):
    place = partners()
    me = place[0]
    greet({"ctx": place[1]}, {"ctx": place[2]})
    scatter_rows(part, from_x, from_y, passed, last, (send_a, recv_a), place)
    half = part.shape[1] // 2
    step = 16
    for side in range(2):
        @pl.loop(0, half // step)
        def _(i):
            rows = pl.ds(pl.multiple_of(i * step, step), step)
            start = side * half + i * step
            whole_rows = pl.ds(pl.multiple_of(start, step), step)
            branch = own_sum(part, from_x, from_y, last, me, side, rows, start, step)
            total = stream[whole_rows, :] + branch
            middle[whole_rows, :] = total
            inv_rms = lax.rsqrt(jnp.mean(total * total, axis=-1, keepdims=True) + epsilon)
            full[me, whole_rows, :] = (total * inv_rms * gain[...]).astype(full.dtype)
            branch_sq[whole_rows, :] = valid[whole_rows, :] * jnp.sum(
                branch * branch, axis=-1, keepdims=True
            )
    gather_rows(full, (send_b, recv_b), place)


def backward_kernel(plan, *refs):
    refs = list(refs)

    def take(count):
        taken = refs[:count]
        del refs[:count]
        return taken

    count = len(plan.sizes)
    part, stream, gain, grad = take(4)
    other_rows = take(1)[0] if plan.attn else None
    left_in = take(2)
    right_in = [take(n) for n in plan.pieces]
    grad_new = take(1)[0]
    full = None if plan.last else take(1)[0]
    gain_rows = take(1)[0]
    summed = take(1)[0]
    from_x, from_y, passed, last = take(4)
    left = take(2)
    right, sent, came = take(count), take(count), take(count)
    gain_sent, gain_came = take(2) if plan.attn else (None, None)
    send_a, recv_a, send_b, recv_b, send_c, recv_c, local_sems = refs

    place = partners()
    me = place[0]
    side = lax.axis_index("tp")
    sibling = {"tp": 1 - side}
    greet({"ctx": place[1]}, {"ctx": place[2]}, sibling)
    loads = []
    for p in range(2):
        loads.append([pltpu.make_async_copy(left_in[p], left[p], local_sems.at[p])])
    for p in range(count):
        if plan.pieces[p] == 1:
            loads.append([pltpu.make_async_copy(right_in[p][0], right[p], local_sems.at[2 + 2 * p])])
            continue
        loads.append([
            pltpu.make_async_copy(right_in[p][t], right[p].at[t], local_sems.at[2 + 2 * p + t]) for t in range(2)
        ])
    for group in loads:
        for load in group:
            load.start()
    starts = [sum(plan.sizes[:p]) for p in range(count)]
    block = 256
    width = stream.shape[1]
    copies = []

    def product(p, t, dst, start):
        @pl.loop(0, width // block)
        def _(i):
            cols = pl.ds(pl.multiple_of(i * block, block), block)
            dst[cols, start : start + plan.sizes[p]] = dot32(
                left[plan.lefts[p]][:, cols], right[p][t], ((0,), (0,))
            ).astype(jnp.bfloat16)

    def theirs(p):
        product(p, 1 - side, sent[p], 0)
        copies.append(send(sent[p], came[p], (send_c, recv_c), p, sibling))

    def ours(p):
        product(p, side, summed, starts[p])

    def add_up():
        for p in range(count):
            copies[p].wait_recv()
            step = 64

            @pl.loop(0, width // step)
            def _(i):
                rows = pl.ds(pl.multiple_of(i * step, step), step)
                cols = slice(starts[p], starts[p] + plan.sizes[p])
                total = summed[rows, cols].astype(jnp.float32) + came[p][rows, :].astype(jnp.float32)
                summed[rows, cols] = total.astype(jnp.bfloat16)

    def work(slot):
        def run():
            if slot == 0:
                for group in loads:
                    for load in group:
                        load.wait()
            for whose, p in plan.slots[slot]:
                (theirs if whose else ours)(p)
        return run

    scatter_rows(part, from_x, from_y, passed, last, (send_a, recv_a), place, (work(0), work(1)))
    half = part.shape[1] // 2
    step = 16
    gain_rows[...] = jnp.zeros_like(gain_rows)
    for part_no in range(2):
        @pl.loop(0, half // step)
        def _(i):
            rows = pl.ds(pl.multiple_of(i * step, step), step)
            start = part_no * half + i * step
            whole_rows = pl.ds(pl.multiple_of(start, step), step)
            got = own_sum(part, from_x, from_y, last, me, part_no, rows, start, step)
            x = stream[whole_rows, :]
            inv_rms = lax.rsqrt(jnp.mean(x * x, axis=-1, keepdims=True) + epsilon)
            scaled = gain[...] * got
            along = jnp.mean(scaled * x, axis=-1, keepdims=True)
            total = grad[whole_rows, :] + inv_rms * scaled - x * (inv_rms * inv_rms * inv_rms * along)
            if plan.last:
                grad_new[side, whole_rows, :] = total
            else:
                grad_new[whole_rows, :] = total
                full[me, whole_rows, :] = total.astype(full.dtype)
            gain_rows[...] += got * x * inv_rms
    if plan.last:
        copies.append(send(grad_new.at[side], grad_new.at[side], (send_c, recv_c), count + 1, sibling))
    if plan.attn:
        gain_sent[...] = jnp.zeros_like(gain_sent)
        gain_sent[0:1, :] = jnp.sum(gain_rows[...], axis=0, keepdims=True)
        gain_sent[1:2, :] = jnp.sum(other_rows[...], axis=0, keepdims=True)
        copies.append(send(gain_sent, gain_came, (send_c, recv_c), count, sibling))
    if plan.last:
        work(2)()
        work(3)()
        add_up()
    else:
        def finish():
            work(3)()
            add_up()

        gather_rows(full, (send_b, recv_b), place, (work(2), finish))
    for copy in copies[count:]:
        copy.wait_recv()
    if plan.attn:
        both = gain_sent[...] + gain_came[...]
        spread = jnp.concatenate([both, jnp.zeros((120, width), jnp.float32)], axis=0).T
        total = sum(plan.sizes)
        summed[:, total : total + 64] = spread[:, :64].astype(jnp.bfloat16)
    for copy in copies:
        copy.wait_send()


class Stage:
    def __init__(self, sizes, pieces, lefts, slots, attn, last):
        self.sizes, self.pieces, self.lefts, self.slots = sizes, pieces, lefts, slots
        self.attn, self.last = attn, last


def start_kernel(gains, places, all_gains, all_places, local_sems, send_a, recv_a, send_b, recv_b):
    groups = (
        ("fsdp", gains, all_gains, (send_a, recv_a)),
        ("ctx", places, all_places, (send_b, recv_b)),
    )
    peers = []
    for axis, _, _, _ in groups:
        count = lax.axis_size(axis)
        peers.append([lax.rem(lax.axis_index(axis) + step, count) for step in range(1, count)])
    greet(*[{groups[n][0]: peer} for n in range(2) for peer in peers[n]])
    copies = []
    for n, (axis, src, dst, sems) in enumerate(groups):
        me = lax.axis_index(axis)
        for step, peer in enumerate(peers[n]):
            copies.append(send(src, dst.at[me], sems, step, {axis: peer}))
        mine = pltpu.make_async_copy(src, dst.at[me], local_sems.at[n])
        mine.start()
        mine.wait()
    for copy in copies:
        copy.wait()


def end_kernel(
    part, middle, valid, stats, out, all_stats,
    from_x, from_y, passed, last, sums, stat_sent, stat_came, z_came, send_a, recv_a, send_c, recv_c, send_d, recv_d,
):
    place = partners()
    me = place[0]
    side = lax.axis_index("tp")
    depth = lax.axis_size("fsdp")
    level = lax.axis_index("fsdp")
    sibling = {"tp": 1 - side}
    others = [{"fsdp": lax.rem(level + step, depth)} for step in range(1, depth)]
    greet({"ctx": place[1]}, {"ctx": place[2]}, sibling, *others)
    scatter_rows(part, from_x, from_y, passed, last, (send_a, recv_a), place)
    half = part.shape[1] // 2
    step = 16
    sums[...] = jnp.zeros_like(sums)
    for part_no in range(2):
        @pl.loop(0, half // step)
        def _(i):
            rows = pl.ds(pl.multiple_of(i * step, step), step)
            start = part_no * half + i * step
            whole_rows = pl.ds(pl.multiple_of(start, step), step)
            branch = own_sum(part, from_x, from_y, last, me, part_no, rows, start, step)
            out[side, whole_rows, :] = (middle[whole_rows, :] + branch).astype(out.dtype)
            sums[...] += valid[whole_rows, :] * jnp.sum(branch * branch, axis=-1, keepdims=True)
    handed = send(out.at[side], out.at[side], (send_c, recv_c), 0, sibling)
    total = jnp.sum(sums[...], axis=0, keepdims=True)
    lane = lax.broadcasted_iota(jnp.int32, (8, 128), 1)
    held = stats[...] + jnp.where(lane == 5, total, 0.0)
    for n, peer in enumerate((sibling, {"ctx": place[1]}, {"ctx": place[2]})):
        stat_sent[n] = held
        send(stat_sent.at[n], stat_came.at[n], (send_d, recv_d), n, peer).wait()
        held = held + stat_came[n]
    z_came[level] = held
    copies = [
        send(z_came.at[level], z_came.at[level], (send_d, recv_d), 3 + n, peer) for n, peer in enumerate(others)
    ]
    for copy in copies:
        copy.wait()
    held = z_came[0]
    for n in range(1, depth):
        held = held + z_came[n]
    all_stats[...] = held
    handed.wait()


def rs_scratch(rows, width):
    half = rows // 2
    return [
        pltpu.VMEM((2, half, width), jnp.bfloat16),
        pltpu.VMEM((2, half, width), jnp.bfloat16),
        pltpu.VMEM((2, half, width), jnp.bfloat16),
        pltpu.VMEM((2, half, width), jnp.bfloat16),
    ]


def dma_sems(count):
    return [pltpu.SemaphoreType.DMA((count,)), pltpu.SemaphoreType.DMA((count,))]


def linked_call(kernel, number, out_shape, scratch, micros, args, far=()):
    vmem = pl.BlockSpec(memory_space=pltpu.VMEM)
    hbm = pl.BlockSpec(memory_space=pl.ANY)
    return pl.pallas_call(
        kernel,
        out_shape=out_shape,
        in_specs=[vmem] * len(args) + [hbm] * len(far),
        out_specs=jax.tree.map(lambda _: vmem, out_shape),
        scratch_shapes=scratch,
        compiler_params=pltpu.CompilerParams(
            collective_id=number, has_side_effects=True, vmem_limit_bytes=60 << 20
        ),
        cost_estimate=pl.CostEstimate(
            flops=0, bytes_accessed=int(micros * 3.6e6), transcendentals=0
        ),
    )(*args, *far)


def gather_ctx(x):
    rows, width = x.shape
    return linked_call(
        gather_kernel, 1, jax.ShapeDtypeStruct((4, rows, width), x.dtype),
        [pltpu.SemaphoreType.DMA] + dma_sems(6), 31, [x],
    )


def forward_step(part, stream, gain, valid):
    rows, width = stream.shape
    return linked_call(
        forward_kernel, 2,
        (
            jax.ShapeDtypeStruct((rows, width), jnp.float32),
            jax.ShapeDtypeStruct((4, rows, width), jnp.bfloat16),
            jax.ShapeDtypeStruct((rows, 1), jnp.float32),
        ),
        rs_scratch(rows, width) + dma_sems(6) + dma_sems(6), 65,
        [part, stream, gain, valid],
    )


def backward_step(number, part, stream, gain, grad, lefts, rights, pairs, slots, other_rows=None, last=False):
    rows, width = stream.shape
    length = lefts[0].shape[0]
    sizes = [r[0].shape[-1] for r in rights]
    pieces = [len(r) for r in rights]
    attn = other_rows is not None
    total = sum(sizes) + (64 if attn else 0)
    bf16, f32 = jnp.bfloat16, jnp.float32
    outs = [jax.ShapeDtypeStruct(((2,) if last else ()) + (rows, width), f32)]
    if not last:
        outs.append(jax.ShapeDtypeStruct((4, rows, width), bf16))
    outs += [jax.ShapeDtypeStruct((16, width), f32), jax.ShapeDtypeStruct((width, total), bf16)]
    scratch = rs_scratch(rows, width)
    scratch += [pltpu.VMEM((length, width), bf16)] * 2
    scratch += [pltpu.VMEM((2, length, n), bf16) for n in sizes]
    scratch += [pltpu.VMEM((width, n), bf16) for n in sizes] * 2
    if attn:
        scratch += [pltpu.VMEM((8, width), f32)] * 2
    scratch += dma_sems(6) + dma_sems(6) + dma_sems(len(sizes) + 2)
    scratch += [pltpu.SemaphoreType.DMA((2 + 2 * len(sizes),))]
    return linked_call(
        functools.partial(backward_kernel, Stage(sizes, pieces, pairs, slots, attn, last)),
        number, outs, scratch, 35 if last else 65,
        [part, stream, gain, grad] + ([other_rows] if attn else []),
        list(lefts) + [half for r in rights for half in r],
    )


def end_step(part, middle, valid, stats):
    rows, width = middle.shape
    depth = lax.axis_size("fsdp")
    f32 = jnp.float32
    return linked_call(
        end_kernel, 4,
        (jax.ShapeDtypeStruct((2, rows, width), jnp.bfloat16), jax.ShapeDtypeStruct((8, 128), f32)),
        rs_scratch(rows, width)
        + [pltpu.VMEM((16, 1), f32), pltpu.VMEM((3, 8, 128), f32), pltpu.VMEM((3, 8, 128), f32)]
        + [pltpu.VMEM((depth, 8, 128), f32)]
        + dma_sems(6) + dma_sems(1) + dma_sems(3 + depth),
        31, [part, middle, valid, stats],
    )


def start_step(gains, places):
    depth, across = lax.axis_size("fsdp"), lax.axis_size("ctx")
    return linked_call(
        start_kernel, 8,
        (
            jax.ShapeDtypeStruct((depth, *gains.shape), gains.dtype),
            jax.ShapeDtypeStruct((across, *places.shape), places.dtype),
        ),
        [pltpu.SemaphoreType.DMA((2,))] + dma_sems(depth) + dma_sems(across),
        5, [gains, places],
    )


def dot32(a, b, dims):
    return lax.dot_general(a, b, (dims, ((), ())), preferred_element_type=jnp.float32)


QUERIES = 128
ROWS = 384
LOG2E = 1.4426950408889634


def turn(x, cos_row, sin_row):
    half_dim = HEAD_DIM // 2
    swapped = jnp.concatenate([x[:, half_dim:], x[:, :half_dim]], axis=1)
    return x * cos_row + swapped * sin_row


def block_groups(length):
    count = length // QUERIES
    per = 3 if count % 3 == 0 else 1
    groups = []
    for first in range(0, count, per):
        seen = min(length, (first + per) * QUERIES + PIECE_LEN)
        groups.append((first, per, seen))
    return groups


def attend_kernel(normed, weights, cos_ref, sin_ref, bias, part, query, key, value, lse, mixed):
    length = normed.shape[0]
    pairs = weights.shape[0]
    cols_q = 2 * HEAD_DIM
    base = 4 * HEAD_DIM
    blocks = ROWS // QUERIES

    @pl.loop(0, length // ROWS)
    def _(i):
        rows = pl.ds(pl.multiple_of(i * ROWS, ROWS), ROWS)
        cos_b, sin_b = cos_ref[rows, :], sin_ref[rows, :]
        for t in range(pairs):
            flat = dot32(normed[rows, :], weights[t, :, :base], ((1,), (0,)))
            for g in range(2):
                head = turn(flat[:, g * HEAD_DIM : (g + 1) * HEAD_DIM], cos_b, sin_b).astype(jnp.bfloat16)
                for n in range(blocks):
                    query[t, i * blocks + n, g * QUERIES : (g + 1) * QUERIES, :] = head[n * QUERIES : (n + 1) * QUERIES]
            key[t, rows, :] = turn(flat[:, cols_q : cols_q + HEAD_DIM], cos_b, sin_b).astype(jnp.bfloat16)
            value[t, rows, :] = flat[:, cols_q + HEAD_DIM : base].astype(jnp.bfloat16)

    factor = HEAD_DIM ** (-0.5) * LOG2E
    for first, count, seen in block_groups(length):
        @pl.loop(0, pairs * count)
        def _(n):
            t = n // count
            block = first + n % count
            rows = pl.ds(pl.multiple_of(block * QUERIES, QUERIES), QUERIES)
            raw = dot32(key[t, :seen, :], query[t, block], ((1,), (1,)))
            low = bias[:seen, rows].astype(jnp.float32)
            raw = raw * factor + jnp.concatenate([low, low], axis=1)
            top = jnp.max(raw, axis=0, keepdims=True)
            probs = jnp.exp2(raw - top)
            total = jnp.sum(probs, axis=0, keepdims=True)
            out = dot32(value[t, :seen, :], probs.astype(jnp.bfloat16), ((0,), (0,)))
            out = (out * (1.0 / total)).T.astype(jnp.bfloat16)
            lse[t, block] = top + jnp.log2(total)
            for g in range(2):
                mixed[t, rows, g * HEAD_DIM : (g + 1) * HEAD_DIM] = out[g * QUERIES : (g + 1) * QUERIES]

    @pl.loop(0, length // ROWS)
    def _(i):
        rows = pl.ds(pl.multiple_of(i * ROWS, ROWS), ROWS)
        total = dot32(mixed[0, rows, :], weights[0, :, base:], ((1,), (1,)))
        for t in range(1, pairs):
            total += dot32(mixed[t, rows, :], weights[t, :, base:], ((1,), (1,)))
        part[rows, :] = total.astype(jnp.bfloat16)


def attend_back_kernel(grad, weights, cos_ref, sin_ref, bias, query, key, value, lse, part, grad_qkv, heads, g_key, g_value):
    length = grad.shape[0]
    pairs = weights.shape[0]
    cols_q = 2 * HEAD_DIM
    base = 4 * HEAD_DIM
    blocks = ROWS // QUERIES
    scale = HEAD_DIM ** (-0.5)
    factor = scale * LOG2E

    @pl.loop(0, length // ROWS)
    def _(i):
        rows = pl.ds(pl.multiple_of(i * ROWS, ROWS), ROWS)
        for t in range(pairs):
            flat = dot32(grad[rows, :], weights[t, :, base:], ((1,), (0,))).astype(jnp.bfloat16)
            for g in range(2):
                for n in range(blocks):
                    heads[t, i * blocks + n, g * QUERIES : (g + 1) * QUERIES, :] = flat[
                        n * QUERIES : (n + 1) * QUERIES, g * HEAD_DIM : (g + 1) * HEAD_DIM
                    ]
    g_key[...] = jnp.zeros_like(g_key)
    g_value[...] = jnp.zeros_like(g_value)
    for first, count, seen in block_groups(length):
        @pl.loop(0, pairs * count)
        def _(n):
            t = n // count
            block = first + n % count
            rows = pl.ds(pl.multiple_of(block * QUERIES, QUERIES), QUERIES)
            low = bias[:seen, rows].astype(jnp.float32)
            raw = dot32(key[t, :seen, :], query[t, block], ((1,), (1,)))
            probs = jnp.exp2(raw * factor + jnp.concatenate([low, low], axis=1) - lse[t, block])
            g_probs = dot32(value[t, :seen, :], heads[t, block], ((1,), (1,)))
            weighed = probs * g_probs
            along = jnp.sum(weighed, axis=0, keepdims=True)
            g_scores = (weighed - probs * along).astype(jnp.bfloat16)
            g_value[t, :seen, :] += dot32(probs.astype(jnp.bfloat16), heads[t, block], ((1,), (0,)))
            g_key[t, :seen, :] += dot32(g_scores, query[t, block], ((1,), (0,)))
            g_query = dot32(key[t, :seen, :], g_scores, ((0,), (0,))).T * scale
            cos_b, sin_b = cos_ref[rows, :], sin_ref[rows, :]
            for g in range(2):
                grad_qkv[t, rows, g * HEAD_DIM : (g + 1) * HEAD_DIM] = turn(
                    g_query[g * QUERIES : (g + 1) * QUERIES], cos_b, -sin_b
                ).astype(jnp.bfloat16)

    @pl.loop(0, length // ROWS)
    def _(i):
        rows = pl.ds(pl.multiple_of(i * ROWS, ROWS), ROWS)
        cos_b, sin_b = cos_ref[rows, :], sin_ref[rows, :]
        total = 0.0
        for t in range(pairs):
            grad_qkv[t, rows, cols_q : cols_q + HEAD_DIM] = turn(g_key[t, rows, :] * scale, cos_b, -sin_b).astype(jnp.bfloat16)
            grad_qkv[t, rows, cols_q + HEAD_DIM : base] = g_value[t, rows, :].astype(jnp.bfloat16)
            total += dot32(grad_qkv[t, rows, :], weights[t, :, :base], ((1,), (1,)))
        part[rows, :] = total.astype(jnp.bfloat16)


def local_call(kernel, out_shape, scratch, micros, *args):
    vmem = pl.BlockSpec(memory_space=pltpu.VMEM)
    return pl.pallas_call(
        kernel,
        out_shape=out_shape,
        in_specs=[vmem] * len(args),
        out_specs=jax.tree.map(lambda _: vmem, out_shape),
        scratch_shapes=scratch,
        compiler_params=pltpu.CompilerParams(vmem_limit_bytes=60 << 20),
        cost_estimate=pl.CostEstimate(flops=0, bytes_accessed=int(micros * 3.6e6), transcendentals=0),
    )(*args)


def attend(normed, weights, cosine, sine_t, bias):
    length, width = normed.shape
    pairs = weights.shape[0]
    blocks = length // QUERIES
    bf16 = jnp.bfloat16
    shape = jax.ShapeDtypeStruct
    outs = [
        shape((length, width), bf16),
        shape((pairs, blocks, 2 * QUERIES, HEAD_DIM), bf16),
        shape((pairs, length, HEAD_DIM), bf16),
        shape((pairs, length, HEAD_DIM), bf16),
        shape((pairs, blocks, 1, 2 * QUERIES), jnp.float32),
        shape((pairs, length, 2 * HEAD_DIM), bf16),
    ]
    return local_call(attend_kernel, outs, [], 20, normed, weights, cosine, sine_t, bias)


def attend_back(grad, weights, cosine, sine_t, bias, query, key, value, lse):
    length, width = grad.shape
    pairs = weights.shape[0]
    bf16 = jnp.bfloat16
    shape = jax.ShapeDtypeStruct
    outs = [shape((length, width), bf16), shape((pairs, length, 4 * HEAD_DIM), bf16)]
    scratch = [
        pltpu.VMEM(query.shape, bf16),
        pltpu.VMEM(key.shape, jnp.float32),
        pltpu.VMEM(key.shape, jnp.float32),
    ]
    return local_call(
        attend_back_kernel, outs, scratch, 30, grad, weights, cosine, sine_t, bias, query, key, value, lse
    )


def planned(
    tokens, positions, valid, piece_starts, d_out,
    attn_gain, w_query, w_key, w_value, w_out, mlp_gain, w_gate, w_up, w_down,
):
    seq_count, rows, width = tokens.shape
    layers = attn_gain.shape[0]
    ctx_count = lax.axis_size("ctx")
    tp_count = lax.axis_size("tp")
    me = lax.axis_index("ctx")
    side = lax.axis_index("tp")
    length = rows * ctx_count
    heads_q = HEADS // tp_count // ctx_count
    heads_k = KV_HEADS // tp_count // ctx_count
    group = HEADS // KV_HEADS
    cols_q = heads_q * HEAD_DIM
    cols_k = heads_k * HEAD_DIM
    units = w_gate.shape[2] // ctx_count
    score_scale = HEAD_DIM ** (-0.5)

    def own(a):
        return lax.dynamic_index_in_dim(a, side, 0, keepdims=False)

    def cut(w, axis, count):
        return lax.dynamic_slice_in_dim(w, me * count, count, axis)

    def whole(w):
        return lax.all_gather(w, ("tp", "fsdp"), axis=0, tiled=True).reshape(
            tp_count, width, w.shape[1]
        )

    attn_w, mlp_w = [], []
    for layer in range(layers):
        attn_w.append(whole(jnp.concatenate([
            cut(w_query[layer], 1, cols_q),
            cut(w_key[layer], 1, cols_k),
            cut(w_value[layer], 1, cols_k),
            cut(w_out[layer], 0, cols_q).T,
        ], axis=1)))
        mlp_w.append(whole(jnp.concatenate([
            cut(w_gate[layer], 1, units),
            cut(w_up[layer], 1, units),
            cut(w_down[layer], 0, units).T,
        ], axis=1)))
    seq_pos, seq_valid = own(positions), own(valid)
    gains, places = start_step(
        jnp.pad(jnp.concatenate([attn_gain, mlp_gain], 0).astype(jnp.float32), ((0, 8 - 2 * layers), (0, 0))),
        jnp.pad(jnp.stack([seq_pos, seq_valid]), ((0, 6), (0, 0))),
    )
    gains = gains.swapaxes(0, 1).reshape(8, width)
    places = places.swapaxes(0, 1).reshape(8, length)
    gain_a = [gains[layer][None] for layer in range(layers)]
    gain_m = [gains[layers + layer][None] for layer in range(layers)]
    pos_all, valid_all = places[0], places[1]
    stream = own(tokens).astype(jnp.float32)
    grad = own(d_out).astype(jnp.float32)
    valid_f = seq_valid.astype(jnp.float32)[:, None]
    normed = gather_ctx(normalize(stream, gain_a[0]).astype(jnp.bfloat16))
    down_grad = lax.all_gather(own(d_out), "ctx", axis=0, tiled=True)

    half_dim = HEAD_DIM // 2
    freqs = rope_base ** (-(jnp.arange(half_dim).astype(jnp.float32) * 2.0 / HEAD_DIM))
    angles = pos_all.astype(jnp.float32)[:, None] * freqs
    cosine, sine_t = jnp.cos(angles), jnp.sin(angles)
    cosine = jnp.concatenate([cosine, cosine], axis=1)
    sine_t = jnp.concatenate([-sine_t, sine_t], axis=1)
    starts = own(piece_starts)
    index = jnp.arange(length, dtype=jnp.int32)
    inside = (index[None, :] >= starts[:, None]) & (index[None, :] < starts[:, None] + PIECE_LEN)
    same_piece = jnp.any(inside[:, :, None] & inside[:, None, :], axis=0)
    causal = index[:, None] <= index[None, :]
    diagonal = index[:, None] == index[None, :]
    allowed = (causal | same_piece) & ((valid_all[:, None] > 0) | diagonal)
    bias = jnp.where(allowed, 0.0, neg_big).astype(jnp.bfloat16)

    stat_rows = []
    saved = []
    for layer in range(layers):
        normed_a = normed.reshape(length, width)
        part, query, key, value, lse, mixed = attend(normed_a, attn_w[layer], cosine, sine_t, bias)
        middle, normed_m, attn_sq = forward_step(
            part.reshape(4, rows, width), stream, gain_m[layer], valid_f
        )
        normed_m = normed_m.reshape(length, width)
        gates = [dot32(normed_m, mlp_w[layer][t][:, :units], ((1,), (0,))) for t in range(tp_count)]
        ups = [dot32(normed_m, mlp_w[layer][t][:, units : 2 * units], ((1,), (0,))) for t in range(tp_count)]
        hidden = [(jax.nn.silu(g) * u).astype(jnp.bfloat16) for g, u in zip(gates, ups)]
        part = sum(dot32(hidden[t], mlp_w[layer][t][:, 2 * units :], ((1,), (1,))) for t in range(tp_count))
        part = part.astype(jnp.bfloat16).reshape(4, rows, width)
        saved.append((stream, normed_a, query, key, value, lse, mixed, middle, normed_m, gates, ups, hidden))
        stat_rows.append(jnp.sum(valid_f * stream * stream))
        stat_rows.append(jnp.sum(attn_sq))
        if layer + 1 < layers:
            stream, normed, mlp_sq = forward_step(part, middle, gain_a[layer + 1], valid_f)
            stat_rows.append(jnp.sum(mlp_sq))
        else:
            last_part, last_middle = part, middle
    stat_rows.append(0.0)
    stat_rows.append(jnp.sum(valid_f))
    stats = jnp.pad(jnp.stack(stat_rows)[None], ((0, 7), (0, 121)))

    def reduced(g):
        return lax.psum_scatter(g, "fsdp", scatter_dimension=0, tiled=True)

    base = cols_q + 2 * cols_k
    waiting = {}

    def after(x, names):
        names = [n for n in names if n in waiting]
        if not names:
            return x
        x, done = lax.optimization_barrier((x, [waiting[n] for n in names]))
        for n, value in zip(names, done):
            waiting[n] = value
        return x

    for layer in reversed(range(layers)):
        stream_in, normed_a, query, key, value, lse, mixed, middle, normed_m, gates, ups, hidden = saved[layer]
        up_one = layer + 1
        grad_gate, grad_up, part = [], [], 0.0
        for t in range(tp_count):
            wt = mlp_w[layer][t]
            grad_hidden = dot32(down_grad, wt[:, 2 * units :], ((1,), (0,)))
            sig = jax.nn.sigmoid(gates[t])
            grad_gate.append((grad_hidden * ups[t] * sig * (1.0 + gates[t] * (1.0 - sig))).astype(jnp.bfloat16))
            grad_up.append((grad_hidden * gates[t] * sig).astype(jnp.bfloat16))
            part += dot32(grad_gate[t], wt[:, :units], ((1,), (1,)))
            part += dot32(grad_up[t], wt[:, units : 2 * units], ((1,), (1,)))
        part = after(part.astype(jnp.bfloat16).reshape(4, rows, width), [(up_one, "mlp")])
        grad_mid, attn_grad, gm_rows, g_mlp = backward_step(
            5, part, middle, gain_m[layer], grad, [normed_m, down_grad], [grad_gate, grad_up, hidden], [0, 0, 1],
            [[(1, 0), (1, 1)], [(1, 2), (0, 0)], [(0, 1)], [(0, 2)]],
        )
        waiting[layer, "mlp"] = reduced(g_mlp)
        attn_grad = attn_grad.reshape(length, width)
        if (up_one, "mlp") in waiting:
            waiting[up_one, "mlp_all"] = lax.all_gather(waiting[up_one, "mlp"], "ctx", axis=0)
        part, gqkv = attend_back(attn_grad, attn_w[layer], cosine, sine_t, bias, query, key, value, lse)
        part = after(part.reshape(4, rows, width), [(up_one, "attn"), (up_one, "mlp_all")])
        came = backward_step(
            6 if layer else 7, part, stream_in, gain_a[layer], grad_mid, [normed_a, attn_grad], [[gqkv], [mixed]], [0, 1],
            [[(1, 0), (1, 1)], [(0, 0), (0, 1)], [], []], other_rows=gm_rows, last=layer == 0,
        )
        if layer:
            grad, down_grad, _, g_attn = came
            down_grad = down_grad.reshape(length, width)
        else:
            input_grad, _, g_attn = came
        if (up_one, "attn") in waiting:
            waiting[up_one, "attn_all"] = lax.all_gather(waiting[up_one, "attn"], "ctx", axis=0)
        waiting[layer, "attn"] = reduced(after(g_attn, [(up_one, "attn_all"), (layer, "mlp")] if layer == 0 else []))
    waiting[0, "mlp_all"] = lax.all_gather(waiting[0, "mlp"], "ctx", axis=0)
    output, stats = end_step(last_part, last_middle, valid_f, stats)
    rms_stats = jnp.sqrt(stats[0, : 3 * layers] / (stats[0, 3 * layers] * width)).reshape(layers, 3)
    waiting[0, "attn_all"] = lax.all_gather(waiting[0, "attn"], "ctx", axis=0)
    mlp_outs = place_outs(
        [waiting[layer, "mlp_all"] for layer in range(layers)],
        [(0, units, False), (units, units, False), (2 * units, units, True)],
    )
    attn_all = [waiting[layer, "attn_all"] for layer in range(layers)]
    attn_outs = place_outs(
        attn_all,
        [(0, cols_q, False), (cols_q, cols_k, False), (cols_q + cols_k, cols_k, False), (base, cols_q, True)],
    )
    gain_sum = jnp.stack([
        jnp.sum(a[:, :, base + cols_q : base + cols_q + 2].astype(jnp.float32), 0) for a in attn_all
    ])
    return (
        output, input_grad, gain_sum[:, :, 0], *attn_outs, gain_sum[:, :, 1], *mlp_outs, rms_stats,
    )


def place_kernel(pieces, ctx_count, *refs):
    ins, outs = refs[:-len(pieces)], refs[-len(pieces):]
    for layer, came in enumerate(ins):
        for (start, size, turn), out in zip(pieces, outs):
            for c in range(ctx_count):
                block = came[c, :, start : start + size].astype(jnp.float32)
                if turn:
                    out[layer, c * size : (c + 1) * size, :] = block.T
                else:
                    out[layer, :, c * size : (c + 1) * size] = block


def place_outs(came, pieces):
    ctx_count, depth, _ = came[0].shape
    layers = len(came)
    shapes = [
        jax.ShapeDtypeStruct(
            (layers, ctx_count * size, depth) if turn else (layers, depth, ctx_count * size), jnp.float32
        )
        for _, size, turn in pieces
    ]
    vmem = pl.BlockSpec(memory_space=pltpu.VMEM)
    return pl.pallas_call(
        functools.partial(place_kernel, pieces, ctx_count),
        out_shape=shapes,
        in_specs=[vmem] * layers,
        out_specs=[vmem] * len(shapes),
        compiler_params=pltpu.CompilerParams(vmem_limit_bytes=60 << 20),
    )(*came)


def fits(mesh):
    tp_count, ctx_count = mesh.shape["tp"], mesh.shape["ctx"]
    return ctx_count == 4 and tp_count == 2


def solution(mesh):
    in_specs = (
        P("fsdp", "ctx", None),
        P("fsdp", "ctx"),
        P("fsdp", "ctx"),
        P("fsdp", None),
        P("fsdp", "ctx", None),
        P(None, "fsdp"),
        P(None, "fsdp", "tp"),
        P(None, "fsdp", "tp"),
        P(None, "fsdp", "tp"),
        P(None, "tp", "fsdp"),
        P(None, "fsdp"),
        P(None, "fsdp", "tp"),
        P(None, "fsdp", "tp"),
        P(None, "tp", "fsdp"),
    )
    out_specs = (
        P("fsdp", "ctx", None),
        P("fsdp", "ctx", None),
        P(None, "fsdp"),
        P(None, "fsdp", "tp"),
        P(None, "fsdp", "tp"),
        P(None, "fsdp", "tp"),
        P(None, "tp", "fsdp"),
        P(None, "fsdp"),
        P(None, "fsdp", "tp"),
        P(None, "fsdp", "tp"),
        P(None, "tp", "fsdp"),
        P(),
    )
    return jax.shard_map(planned if fits(mesh) else general, mesh=mesh, in_specs=in_specs, out_specs=out_specs, check_vma=False)
```

```python
import functools

import jax
import jax.numpy as jnp
from jax import lax
from jax.experimental import pallas as pl
from jax.experimental.layout import Layout, with_layout_constraint
from jax.experimental.pallas import tpu as pltpu
from jax.sharding import PartitionSpec as P

MESH = pl.DeviceIdType.MESH

HEADS = 16
KV_HEADS = 8
HEAD_DIM = 96
PIECE_LEN = 256


epsilon = 1e-05
rope_base = 100000.0
neg_big = -1e30


def rope_tables(positions, head_dim):
    half_dim = head_dim // 2
    freqs = rope_base ** (-(jnp.arange(half_dim).astype(jnp.float32) * 2.0 / head_dim))
    angles = positions.astype(jnp.float32)[..., None] * freqs
    return (jnp.cos(angles)[:, :, None, :], jnp.sin(angles)[:, :, None, :])


def rotate(values, cosine, sine_t):
    half_dim = values.shape[-1] // 2
    lead_part = values[..., :half_dim]
    tail_part = values[..., half_dim:]
    return jnp.concatenate(
        [lead_part * cosine - tail_part * sine_t, tail_part * cosine + lead_part * sine_t], axis=-1
    )


def normalize(stream, gain_vec):
    inv_rms = lax.rsqrt(jnp.mean(stream * stream, axis=-1, keepdims=True) + epsilon)
    return stream * inv_rms * gain_vec.astype(jnp.float32)


def norm_back(stream, gain_vec, grad_out):
    inv_rms = lax.rsqrt(jnp.mean(stream * stream, axis=-1, keepdims=True) + epsilon)
    scaled_grad = gain_vec.astype(jnp.float32) * grad_out
    grad_in = inv_rms * scaled_grad - stream * inv_rms**3 * jnp.mean(
        scaled_grad * stream, axis=-1, keepdims=True
    )
    grad_gain = jnp.sum(grad_out * stream * inv_rms, axis=0)
    return (grad_in, grad_gain)


def score_block(query_b, key_heads, allowed, score_scale):
    raw_scores = (
        jnp.einsum("sckgd,snkd->skgcn", query_b, key_heads, preferred_element_type=jnp.float32)
        * score_scale
    )
    return jnp.where(allowed[:, None, None], raw_scores, neg_big)


def general(
    tokens,
    positions,
    valid,
    piece_starts,
    d_out,
    attn_gain,
    w_query,
    w_key,
    w_value,
    w_out,
    mlp_gain,
    w_gate,
    w_up,
    w_down,
):
    seq_count, shard_len, model_width = tokens.shape
    tok_rows = seq_count * shard_len
    tp_count = lax.axis_size("tp")
    local_heads = HEADS // tp_count
    local_kv = KV_HEADS // tp_count
    group_size = HEADS // KV_HEADS
    score_scale = HEAD_DIM ** (-0.5)
    seq_length = shard_len * lax.axis_size("ctx")
    start_tok = lax.axis_index("ctx") * shard_len
    query_index = start_tok + jnp.arange(shard_len, dtype=jnp.int32)
    key_index = jnp.arange(seq_length, dtype=jnp.int32)
    cosine, sine_t = rope_tables(positions, HEAD_DIM)
    valid_flat = valid.astype(jnp.float32).reshape(tok_rows)
    in_query = (query_index[None, None, :] >= piece_starts[:, :, None]) & (
        query_index[None, None, :] < piece_starts[:, :, None] + PIECE_LEN
    )
    in_key = (key_index[None, None, :] >= piece_starts[:, :, None]) & (
        key_index[None, None, :] < piece_starts[:, :, None] + PIECE_LEN
    )
    same_piece = jnp.any(in_query[:, :, :, None] & in_key[:, :, None, :], axis=1)
    causal = key_index[None, :] <= query_index[:, None]
    diagonal = key_index[None, :] == query_index[:, None]
    layer_count = attn_gain.shape[0]
    stream = tokens.astype(jnp.float32).reshape(tok_rows, model_width)
    saved = []
    stat_rows = []
    for layer_no in range(layer_count):
        weights = (
            lax.all_gather(attn_gain[layer_no], "fsdp", axis=0, tiled=True),
            lax.all_gather(w_query[layer_no], "fsdp", axis=0, tiled=True),
            lax.all_gather(w_key[layer_no], "fsdp", axis=0, tiled=True),
            lax.all_gather(w_value[layer_no], "fsdp", axis=0, tiled=True),
            lax.all_gather(w_out[layer_no], "fsdp", axis=1, tiled=True),
            lax.all_gather(mlp_gain[layer_no], "fsdp", axis=0, tiled=True),
            lax.all_gather(w_gate[layer_no], "fsdp", axis=0, tiled=True),
            lax.all_gather(w_up[layer_no], "fsdp", axis=0, tiled=True),
            lax.all_gather(w_down[layer_no], "fsdp", axis=1, tiled=True),
        )
        gain_a, w_q, w_k, w_v, w_o, gain_m, w_g, w_u, w_d = weights
        normed_a = normalize(stream, gain_a).astype(jnp.bfloat16)
        query_heads = jnp.dot(normed_a, w_q, preferred_element_type=jnp.float32).reshape(
            seq_count, shard_len, local_heads, HEAD_DIM
        )
        query_b = (
            rotate(query_heads, cosine, sine_t)
            .astype(jnp.bfloat16)
            .reshape(seq_count, shard_len, local_kv, group_size, HEAD_DIM)
        )
        key_local = jnp.dot(normed_a, w_k, preferred_element_type=jnp.float32).reshape(
            seq_count, shard_len, local_kv, HEAD_DIM
        )
        key_local = (
            rotate(key_local, cosine, sine_t)
            .astype(jnp.bfloat16)
            .reshape(seq_count, shard_len, local_kv * HEAD_DIM)
        )
        value_local = (
            jnp.dot(normed_a, w_v, preferred_element_type=jnp.float32)
            .astype(jnp.bfloat16)
            .reshape(seq_count, shard_len, local_kv * HEAD_DIM)
        )
        key_all, value_all, valid_all = (
            lax.all_gather(key_local, "ctx", axis=1, tiled=True),
            lax.all_gather(value_local, "ctx", axis=1, tiled=True),
            lax.all_gather(valid.astype(jnp.bfloat16), "ctx", axis=1, tiled=True),
        )
        allowed = (causal[None] | same_piece) & ((valid_all[:, None, :] > 0.5) | diagonal[None])
        key_heads = key_all.reshape(seq_count, seq_length, local_kv, HEAD_DIM)
        value_heads = value_all.reshape(seq_count, seq_length, local_kv, HEAD_DIM)
        raw_scores = score_block(query_b, key_heads, allowed, score_scale)
        row_max = jnp.max(raw_scores, axis=-1, keepdims=True)
        log_total = row_max + jnp.log(
            jnp.sum(jnp.exp(raw_scores - row_max), axis=-1, keepdims=True)
        )
        softmax_b = jnp.exp(raw_scores - log_total).astype(jnp.bfloat16)
        mixed_heads = jnp.einsum(
            "skgcn,snkd->sckgd", softmax_b, value_heads, preferred_element_type=jnp.float32
        )
        mixed_b = mixed_heads.astype(jnp.bfloat16).reshape(tok_rows, local_heads * HEAD_DIM)
        attn_branch = lax.psum(
            jnp.dot(mixed_b, w_o, preferred_element_type=jnp.float32).astype(jnp.bfloat16), "tp"
        ).astype(jnp.float32)
        middle = stream + attn_branch
        normed_m = normalize(middle, gain_m).astype(jnp.bfloat16)
        gate_act = jnp.dot(normed_m, w_g, preferred_element_type=jnp.float32)
        up_act = jnp.dot(normed_m, w_u, preferred_element_type=jnp.float32)
        hidden = (jax.nn.silu(gate_act) * up_act).astype(jnp.bfloat16)
        mlp_branch = lax.psum(
            jnp.dot(hidden, w_d, preferred_element_type=jnp.float32).astype(jnp.bfloat16), "tp"
        ).astype(jnp.float32)
        stat_rows.append(
            jnp.stack(
                [
                    jnp.sum(valid_flat[:, None] * stream * stream),
                    jnp.sum(valid_flat[:, None] * attn_branch * attn_branch),
                    jnp.sum(valid_flat[:, None] * mlp_branch * mlp_branch),
                ]
            )
        )
        kept_weights = None
        saved.append(
            (
                stream,
                normed_a,
                query_b,
                key_heads,
                value_heads,
                allowed,
                log_total,
                mixed_b,
                middle,
                normed_m,
                gate_act,
                up_act,
                hidden,
                kept_weights,
            )
        )
        stream = middle + mlp_branch
    output = stream.astype(jnp.bfloat16).reshape(seq_count, shard_len, model_width)
    total_squares, total_count = lax.psum(
        (jnp.stack(stat_rows), jnp.sum(valid_flat)), ("fsdp", "ctx")
    )
    rms_stats = jnp.sqrt(total_squares / (total_count * model_width))
    grad_stream = d_out.astype(jnp.float32).reshape(tok_rows, model_width)
    results = [None] * layer_count
    for layer_no in reversed(range(layer_count)):
        (
            stream_in,
            normed_a,
            query_b,
            key_heads,
            value_heads,
            allowed,
            log_total,
            mixed_b,
            middle,
            normed_m,
            gate_act,
            up_act,
            hidden,
            kept_weights,
        ) = saved[layer_no]
        weights = (
            lax.all_gather(attn_gain[layer_no], "fsdp", axis=0, tiled=True),
            lax.all_gather(w_query[layer_no], "fsdp", axis=0, tiled=True),
            lax.all_gather(w_key[layer_no], "fsdp", axis=0, tiled=True),
            lax.all_gather(w_value[layer_no], "fsdp", axis=0, tiled=True),
            lax.all_gather(w_out[layer_no], "fsdp", axis=1, tiled=True),
            lax.all_gather(mlp_gain[layer_no], "fsdp", axis=0, tiled=True),
            lax.all_gather(w_gate[layer_no], "fsdp", axis=0, tiled=True),
            lax.all_gather(w_up[layer_no], "fsdp", axis=0, tiled=True),
            lax.all_gather(w_down[layer_no], "fsdp", axis=1, tiled=True),
        )
        gain_a, w_q, w_k, w_v, w_o, gain_m, w_g, w_u, w_d = weights
        grad_mlp = grad_stream.astype(jnp.bfloat16)
        grad_hidden = jnp.einsum("rd,fd->rf", grad_mlp, w_d, preferred_element_type=jnp.float32)
        g_down = jnp.einsum("rf,rd->fd", hidden, grad_mlp, preferred_element_type=jnp.float32)
        sigmoid_g = jax.nn.sigmoid(gate_act)
        grad_gate = (
            grad_hidden * up_act * sigmoid_g * (1.0 + gate_act * (1.0 - sigmoid_g))
        ).astype(jnp.bfloat16)
        grad_up = (grad_hidden * gate_act * sigmoid_g).astype(jnp.bfloat16)
        grad_normed_m = lax.psum(
            (
                jnp.einsum("rf,df->rd", grad_gate, w_g, preferred_element_type=jnp.float32)
                + jnp.einsum("rf,df->rd", grad_up, w_u, preferred_element_type=jnp.float32)
            ).astype(jnp.bfloat16),
            "tp",
        ).astype(jnp.float32)
        g_gate = jnp.einsum("rd,rf->df", normed_m, grad_gate, preferred_element_type=jnp.float32)
        g_up = jnp.einsum("rd,rf->df", normed_m, grad_up, preferred_element_type=jnp.float32)
        grad_from_norm, g_gain_m = norm_back(middle, gain_m, grad_normed_m)
        grad_middle = grad_stream + grad_from_norm
        grad_attn = grad_middle.astype(jnp.bfloat16)
        grad_heads = jnp.einsum(
            "rd,hd->rh", grad_attn, w_o, preferred_element_type=jnp.float32
        ).astype(jnp.bfloat16)
        g_out = jnp.einsum("rh,rd->hd", mixed_b, grad_attn, preferred_element_type=jnp.float32)
        grad_heads = grad_heads.reshape(seq_count, shard_len, local_kv, group_size, HEAD_DIM)
        raw_scores = score_block(query_b, key_heads, allowed, score_scale)
        softmax_p = jnp.exp(raw_scores - log_total)
        grad_probs = jnp.einsum(
            "sckgd,snkd->skgcn", grad_heads, value_heads, preferred_element_type=jnp.float32
        )
        row_dots = jnp.sum(softmax_p * grad_probs, axis=-1, keepdims=True)
        grad_scores = (softmax_p * (grad_probs - row_dots)).astype(jnp.bfloat16)
        grad_query = (
            jnp.einsum(
                "skgcn,snkd->sckgd", grad_scores, key_heads, preferred_element_type=jnp.float32
            )
            * score_scale
        )
        grad_key_all = (
            jnp.einsum(
                "skgcn,sckgd->snkd", grad_scores, query_b, preferred_element_type=jnp.float32
            )
            * score_scale
        )
        grad_value_all = jnp.einsum(
            "skgcn,sckgd->snkd",
            softmax_p.astype(jnp.bfloat16),
            grad_heads,
            preferred_element_type=jnp.float32,
        )
        grad_key, grad_value = (
            lax.psum_scatter(
                grad_key_all.reshape(seq_count, seq_length, local_kv * HEAD_DIM).astype(
                    jnp.bfloat16
                ),
                "ctx",
                scatter_dimension=1,
                tiled=True,
            ).astype(jnp.float32),
            lax.psum_scatter(
                grad_value_all.reshape(seq_count, seq_length, local_kv * HEAD_DIM).astype(
                    jnp.bfloat16
                ),
                "ctx",
                scatter_dimension=1,
                tiled=True,
            ).astype(jnp.float32),
        )
        grad_query_b = rotate(
            grad_query.reshape(seq_count, shard_len, local_heads, HEAD_DIM), cosine, -sine_t
        )
        grad_query_b = grad_query_b.astype(jnp.bfloat16).reshape(tok_rows, local_heads * HEAD_DIM)
        grad_key_b = rotate(
            grad_key.reshape(seq_count, shard_len, local_kv, HEAD_DIM), cosine, -sine_t
        )
        grad_key_b = grad_key_b.astype(jnp.bfloat16).reshape(tok_rows, local_kv * HEAD_DIM)
        grad_value_b = grad_value.astype(jnp.bfloat16).reshape(tok_rows, local_kv * HEAD_DIM)
        grad_normed_a = lax.psum(
            (
                jnp.einsum("rh,dh->rd", grad_query_b, w_q, preferred_element_type=jnp.float32)
                + jnp.einsum("rh,dh->rd", grad_key_b, w_k, preferred_element_type=jnp.float32)
                + jnp.einsum("rh,dh->rd", grad_value_b, w_v, preferred_element_type=jnp.float32)
            ).astype(jnp.bfloat16),
            "tp",
        ).astype(jnp.float32)
        g_query = jnp.einsum(
            "rd,rh->dh", normed_a, grad_query_b, preferred_element_type=jnp.float32
        )
        g_key = jnp.einsum("rd,rh->dh", normed_a, grad_key_b, preferred_element_type=jnp.float32)
        g_value = jnp.einsum(
            "rd,rh->dh", normed_a, grad_value_b, preferred_element_type=jnp.float32
        )
        grad_from_attn_norm, g_gain_a = norm_back(stream_in, gain_a, grad_normed_a)
        grad_stream = grad_middle + grad_from_attn_norm
        grad_terms = (g_gain_a, g_query, g_key, g_value, g_out, g_gain_m, g_gate, g_up, g_down)
        shares = (
            lax.psum_scatter(grad_terms[0], ("fsdp", "ctx"), scatter_dimension=0, tiled=True),
            lax.psum_scatter(grad_terms[1], ("fsdp", "ctx"), scatter_dimension=0, tiled=True),
            lax.psum_scatter(grad_terms[2], ("fsdp", "ctx"), scatter_dimension=0, tiled=True),
            lax.psum_scatter(grad_terms[3], ("fsdp", "ctx"), scatter_dimension=0, tiled=True),
            lax.psum_scatter(grad_terms[4], ("fsdp", "ctx"), scatter_dimension=1, tiled=True),
            lax.psum_scatter(grad_terms[5], ("fsdp", "ctx"), scatter_dimension=0, tiled=True),
            lax.psum_scatter(grad_terms[6], ("fsdp", "ctx"), scatter_dimension=0, tiled=True),
            lax.psum_scatter(grad_terms[7], ("fsdp", "ctx"), scatter_dimension=0, tiled=True),
            lax.psum_scatter(grad_terms[8], ("fsdp", "ctx"), scatter_dimension=1, tiled=True),
        )
        results[layer_no] = (
            lax.all_gather(shares[0].astype(jnp.bfloat16), "ctx", axis=0, tiled=True).astype(
                jnp.float32
            ),
            lax.all_gather(shares[1].astype(jnp.bfloat16), "ctx", axis=0, tiled=True).astype(
                jnp.float32
            ),
            lax.all_gather(shares[2].astype(jnp.bfloat16), "ctx", axis=0, tiled=True).astype(
                jnp.float32
            ),
            lax.all_gather(shares[3].astype(jnp.bfloat16), "ctx", axis=0, tiled=True).astype(
                jnp.float32
            ),
            lax.all_gather(shares[4].astype(jnp.bfloat16), "ctx", axis=1, tiled=True).astype(
                jnp.float32
            ),
            lax.all_gather(shares[5].astype(jnp.bfloat16), "ctx", axis=0, tiled=True).astype(
                jnp.float32
            ),
            lax.all_gather(shares[6].astype(jnp.bfloat16), "ctx", axis=0, tiled=True).astype(
                jnp.float32
            ),
            lax.all_gather(shares[7].astype(jnp.bfloat16), "ctx", axis=0, tiled=True).astype(
                jnp.float32
            ),
            lax.all_gather(shares[8].astype(jnp.bfloat16), "ctx", axis=1, tiled=True).astype(
                jnp.float32
            ),
        )
    stacked = [
        jnp.stack([results[layer_no][member] for layer_no in range(layer_count)])
        for member in range(9)
    ]
    input_grad = grad_stream.reshape(seq_count, shard_len, model_width)
    return (
        output,
        input_grad,
        stacked[0],
        stacked[1],
        stacked[2],
        stacked[3],
        stacked[4],
        stacked[5],
        stacked[6],
        stacked[7],
        stacked[8],
        rms_stats,
    )


def partners():
    me = lax.axis_index("ctx")
    return me, me ^ 1, me ^ 2, me ^ 3


def greet(*places):
    barrier = pltpu.get_barrier_semaphore()
    for place in places:
        pl.semaphore_signal(barrier, inc=1, device_id=place, device_id_type=MESH)
    pl.semaphore_wait(barrier, len(places))


def send(src, dst, sems, slot, place):
    copy = pltpu.make_async_remote_copy(
        src_ref=src,
        dst_ref=dst,
        send_sem=sems[0].at[slot],
        recv_sem=sems[1].at[slot],
        device_id=place,
        device_id_type=MESH,
    )
    copy.start()
    return copy


def run(steps, work=()):
    for n, _ in enumerate(steps):
        if n < len(work):
            work[n]()


def gather_rows(full, sems, place):
    me, side_x, side_y, _ = place
    to_x, to_y = {"ctx": side_x}, {"ctx": side_y}
    half = full.shape[1] // 2
    top, low = pl.ds(0, half), pl.ds(half, half)
    first = [
        send(full.at[me, top], full.at[me, top], sems, 0, to_x),
        send(full.at[me, low], full.at[me, low], sems, 1, to_y),
    ]
    rest = [
        send(full.at[me, top], full.at[me, top], sems, 2, to_y),
        send(full.at[me, low], full.at[me, low], sems, 3, to_x),
    ]
    yield
    first[0].wait_recv()
    rest.append(send(full.at[side_x, top], full.at[side_x, top], sems, 4, to_y))
    first[1].wait_recv()
    rest.append(send(full.at[side_y, low], full.at[side_y, low], sems, 5, to_x))
    yield
    rest[0].wait_recv()
    rest[1].wait_recv()
    yield
    rest[2].wait_recv()
    rest[3].wait_recv()
    for copy in first + rest:
        copy.wait_send()


def scatter_rows(part, from_x, from_y, passed, last, sems, place):
    me, side_x, side_y, across = place
    to_x, to_y = {"ctx": side_x}, {"ctx": side_y}
    half = part.shape[1] // 2
    top, low = pl.ds(0, half), pl.ds(half, half)
    early = [
        send(part.at[across, top], from_x.at[1], sems, 0, to_x),
        send(part.at[across, low], from_y.at[1], sems, 1, to_y),
    ]
    rest = [
        send(part.at[side_x, top], from_x.at[0], sems, 2, to_x),
        send(part.at[side_y, low], from_y.at[0], sems, 3, to_y),
    ]
    step = 16

    def add_to(slot, owner, start, came):
        @pl.loop(0, half // step)
        def _(i):
            rows = pl.ds(pl.multiple_of(i * step, step), step)
            mine = part[owner, pl.ds(pl.multiple_of(start + i * step, step), step), :]
            total = mine.astype(jnp.float32) + came[1, rows, :].astype(jnp.float32)
            passed[slot, rows, :] = total.astype(passed.dtype)

    yield
    early[0].wait_recv()
    add_to(0, side_y, 0, from_x)
    rest.append(send(passed.at[0], last.at[0], sems, 4, to_y))
    early[1].wait_recv()
    add_to(1, side_x, half, from_y)
    rest.append(send(passed.at[1], last.at[1], sems, 5, to_x))
    yield
    for copy in rest:
        copy.wait()
    for copy in early:
        copy.wait_send()


def own_sum(part, from_x, from_y, last, me, side, rows, start, step):
    came = from_x if side == 0 else from_y
    total = part[me, pl.ds(pl.multiple_of(start, step), step), :].astype(jnp.float32)
    total += came[0, rows, :].astype(jnp.float32)
    return total + last[side, rows, :].astype(jnp.float32)


def norm_sum(part, stream, gain, valid, middle, full, branch_sq, from_x, from_y, last, me):
    half = part.shape[1] // 2
    step = 16
    for side in range(2):
        @pl.loop(0, half // step)
        def _(i):
            rows = pl.ds(pl.multiple_of(i * step, step), step)
            start = side * half + i * step
            whole_rows = pl.ds(pl.multiple_of(start, step), step)
            branch = own_sum(part, from_x, from_y, last, me, side, rows, start, step)
            total = stream[whole_rows, :] + branch
            middle[whole_rows, :] = total
            inv_rms = lax.rsqrt(jnp.mean(total * total, axis=-1, keepdims=True) + epsilon)
            full[me, whole_rows, :] = (total * inv_rms * gain[...]).astype(full.dtype)
            branch_sq[whole_rows, :] = valid[whole_rows, :] * jnp.sum(
                branch * branch, axis=-1, keepdims=True
            )


def forward_kernel(
    part, stream, gain, valid, middle, full, branch_sq,
    from_x, from_y, passed, last, send_a, recv_a, send_b, recv_b,
):
    place = partners()
    greet({"ctx": place[1]}, {"ctx": place[2]})
    run(scatter_rows(part, from_x, from_y, passed, last, (send_a, recv_a), place))
    norm_sum(part, stream, gain, valid, middle, full, branch_sq, from_x, from_y, last, place[0])
    run(gather_rows(full, (send_b, recv_b), place))


def rows_of(ref, lead, top_of, low_of):
    half = ref.shape[-2] // 2
    return jnp.concatenate([ref[(*lead, top_of, pl.ds(0, half))], ref[(*lead, low_of, pl.ds(half, half))]], axis=0)


def put_rows(ref, lead, top_of, low_of, value):
    half = ref.shape[-2] // 2
    ref[(*lead, top_of, pl.ds(0, half))] = value[:half].astype(ref.dtype)
    ref[(*lead, low_of, pl.ds(half, half))] = value[half:].astype(ref.dtype)


def mlp_rows(full, weights, top_of, low_of, hidden, part, gate=None, up=None, back=None):
    units = hidden.shape[-1]
    x = rows_of(full, (), top_of, low_of)
    total, g_total = 0.0, 0.0
    for t in range(weights.shape[0]):
        gate_act = dot32(x, weights[t, :, :units], ((1,), (0,)))
        up_act = dot32(x, weights[t, :, units : 2 * units], ((1,), (0,)))
        sig = jax.nn.sigmoid(gate_act)
        unit = (gate_act * sig * up_act).astype(jnp.bfloat16)
        put_rows(hidden, (t,), top_of, low_of, unit)
        total += dot32(unit, weights[t, :, 2 * units :], ((1,), (1,)))
        if back is None:
            put_rows(gate, (t,), top_of, low_of, gate_act)
            put_rows(up, (t,), top_of, low_of, up_act)
        else:
            g_total += mlp_back_rows(
                rows_of(back[0], (), top_of, low_of), weights, t, top_of, low_of, gate_act, up_act, sig, back[1], back[2]
            )
    put_rows(part, (), top_of, low_of, total)
    if back is not None:
        put_rows(back[3], (), top_of, low_of, g_total)


def mlp_back_rows(grad, weights, t, top_of, low_of, gate_act, up_act, sig, grad_gate, grad_up):
    units = grad_gate.shape[-1]
    g_hidden = dot32(grad, weights[t, :, 2 * units :], ((1,), (0,)))
    g_gate = (g_hidden * up_act * sig * (1.0 + gate_act * (1.0 - sig))).astype(jnp.bfloat16)
    g_up = (g_hidden * gate_act * sig).astype(jnp.bfloat16)
    put_rows(grad_gate, (t,), top_of, low_of, g_gate)
    put_rows(grad_up, (t,), top_of, low_of, g_up)
    total = dot32(g_gate, weights[t, :, :units], ((1,), (1,)))
    return total + dot32(g_up, weights[t, :, units : 2 * units], ((1,), (1,)))


def in_turn(steps, place, work):
    me, side_x, side_y, across = place
    next(steps)
    work(me, me)
    next(steps)
    work(side_x, side_y)
    next(steps)
    work(side_y, side_x)
    run(steps)
    work(across, across)


def forward_mlp_kernel(back, part, stream, gain, valid, *refs):
    refs = list(refs)
    weights_in, grad_in = refs.pop(0), refs.pop(0) if back else None
    middle, full, branch_sq, out = refs[:4]
    del refs[:4]
    hidden, one, two = refs[:3]
    del refs[:3]
    out_back = refs.pop(0) if back else None
    from_x, from_y, passed, last, weights = refs[:5]
    del refs[:5]
    grad = refs.pop(0) if back else None
    send_a, recv_a, send_b, recv_b, local_sems = refs
    place = partners()
    greet({"ctx": place[1]}, {"ctx": place[2]})
    loads = [pltpu.make_async_copy(weights_in, weights, local_sems.at[0])]
    if back:
        loads.append(pltpu.make_async_copy(grad_in, grad, local_sems.at[1]))
    for load in loads:
        load.start()
    run(scatter_rows(part, from_x, from_y, passed, last, (send_a, recv_a), place))
    norm_sum(part, stream, gain, valid, middle, full, branch_sq, from_x, from_y, last, place[0])
    for load in loads:
        load.wait()

    def work(top_of, low_of):
        if back:
            mlp_rows(full, weights, top_of, low_of, hidden, out, back=(grad, one, two, out_back))
        else:
            mlp_rows(full, weights, top_of, low_of, hidden, out, one, two)

    in_turn(gather_rows(full, (send_b, recv_b), place), place, work)


def backward_kernel(plan, *refs):
    refs = list(refs)

    def take(count):
        taken = refs[:count]
        del refs[:count]
        return taken

    count = len(plan.sizes)
    part, stream, gain, grad = take(4)
    other_rows = take(1)[0] if plan.attn else None
    share = take(1)[0] if plan.last else None
    gate, up, weights_in = take(3) if plan.mlp else (None, None, None)
    left_in = take(2)
    right_in = [take(n) for n in plan.pieces]
    grad_new = take(1)[0]
    full = None if plan.last else take(1)[0]
    gain_rows = take(1)[0]
    summed = take(1)[0]
    gathered = take(1)[0] if plan.last else None
    out, grad_gate, grad_up = take(3) if plan.mlp else (None, None, None)
    from_x, from_y, passed, last = take(4)
    left = take(2)
    right, sent, came = take(count), take(count), take(count)
    gain_sent, gain_came = take(2) if plan.attn else (None, None)
    weights = take(1)[0] if plan.mlp else None
    send_a, recv_a, send_b, recv_b, send_c, recv_c, local_sems = refs

    place = partners()
    me = place[0]
    side = lax.axis_index("tp")
    sibling = {"tp": 1 - side}
    greet({"ctx": place[1]}, {"ctx": place[2]}, sibling)
    loads = []
    for p in range(2):
        loads.append([pltpu.make_async_copy(left_in[p], left[p], local_sems.at[p])])
    for p in range(count):
        if plan.pieces[p] == 1:
            loads.append([pltpu.make_async_copy(right_in[p][0], right[p], local_sems.at[2 + 2 * p])])
            continue
        loads.append([
            pltpu.make_async_copy(right_in[p][t], right[p].at[t], local_sems.at[2 + 2 * p + t]) for t in range(2)
        ])
    for group in loads:
        for load in group:
            load.start()
    if plan.mlp:
        weights_load = pltpu.make_async_copy(weights_in, weights, local_sems.at[2 + 2 * count])
        weights_load.start()
    starts = [sum(plan.sizes[:p]) for p in range(count)]
    block = 256
    width = stream.shape[1]
    copies = []

    def product(p, t, dst, start):
        @pl.loop(0, width // block)
        def _(i):
            cols = pl.ds(pl.multiple_of(i * block, block), block)
            dst[cols, start : start + plan.sizes[p]] = dot32(
                left[plan.lefts[p]][:, cols], right[p][t], ((0,), (0,))
            ).astype(jnp.bfloat16)

    def theirs(p):
        product(p, 1 - side, sent[p], 0)
        copies.append(send(sent[p], came[p], (send_c, recv_c), p, sibling))

    def ours(p):
        product(p, side, summed, starts[p])

    def add_up():
        for p in range(count):
            copies[p].wait_recv()
            step = 64

            @pl.loop(0, width // step)
            def _(i):
                rows = pl.ds(pl.multiple_of(i * step, step), step)
                cols = slice(starts[p], starts[p] + plan.sizes[p])
                total = summed[rows, cols].astype(jnp.float32) + came[p][rows, :].astype(jnp.float32)
                summed[rows, cols] = total.astype(jnp.bfloat16)

    def work(slot):
        def run():
            if slot == 0:
                for group in loads:
                    for load in group:
                        load.wait()
            for whose, p in plan.slots[slot]:
                (theirs if whose else ours)(p)
        return run

    if plan.last:
        load = pltpu.make_async_copy(share, gathered.at[me], local_sems.at[2 + 2 * count])
        load.start()
        load.wait()
        round_it = gather_rows(gathered, (send_b, recv_b), place)

        def both(slot):
            def now():
                next(round_it)
                work(slot)()
            return now

        run(scatter_rows(part, from_x, from_y, passed, last, (send_a, recv_a), place), (both(0), both(1)))
    else:
        run(scatter_rows(part, from_x, from_y, passed, last, (send_a, recv_a), place), (work(0), work(1)))
    half = part.shape[1] // 2
    step = 16
    gain_rows[...] = jnp.zeros_like(gain_rows)
    for part_no in range(2):
        @pl.loop(0, half // step)
        def _(i):
            rows = pl.ds(pl.multiple_of(i * step, step), step)
            start = part_no * half + i * step
            whole_rows = pl.ds(pl.multiple_of(start, step), step)
            got = own_sum(part, from_x, from_y, last, me, part_no, rows, start, step)
            x = stream[whole_rows, :]
            inv_rms = lax.rsqrt(jnp.mean(x * x, axis=-1, keepdims=True) + epsilon)
            scaled = gain[...] * got
            along = jnp.mean(scaled * x, axis=-1, keepdims=True)
            total = grad[whole_rows, :] + inv_rms * scaled - x * (inv_rms * inv_rms * inv_rms * along)
            if plan.last:
                grad_new[side, whole_rows, :] = total
            else:
                grad_new[whole_rows, :] = total
                full[me, whole_rows, :] = total.astype(full.dtype)
            gain_rows[...] += got * x * inv_rms
    if plan.last:
        copies.append(send(grad_new.at[side], grad_new.at[side], (send_c, recv_c), count + 1, sibling))
    if plan.attn:
        gain_sent[...] = jnp.zeros_like(gain_sent)
        gain_sent[0:1, :] = jnp.sum(gain_rows[...], axis=0, keepdims=True)
        gain_sent[1:2, :] = jnp.sum(other_rows[...], axis=0, keepdims=True)
        copies.append(send(gain_sent, gain_came, (send_c, recv_c), count, sibling))
    if plan.last:
        work(2)()
        work(3)()
        add_up()
        run(round_it)
    elif plan.mlp:
        add_up()
        weights_load.wait()

        def back_rows(top_of, low_of):
            total = 0.0
            for t in range(weights.shape[0]):
                gate_act = rows_of(gate, (t,), top_of, low_of).astype(jnp.float32)
                total += mlp_back_rows(
                    rows_of(full, (), top_of, low_of), weights, t, top_of, low_of, gate_act,
                    rows_of(up, (t,), top_of, low_of).astype(jnp.float32), jax.nn.sigmoid(gate_act), grad_gate, grad_up,
                )
            put_rows(out, (), top_of, low_of, total)

        in_turn(gather_rows(full, (send_b, recv_b), place), place, back_rows)
    else:
        def finish():
            work(3)()
            add_up()

        run(gather_rows(full, (send_b, recv_b), place), (work(2), finish))
    for copy in copies[count:]:
        copy.wait_recv()
    if plan.attn:
        both = gain_sent[...] + gain_came[...]
        spread = jnp.concatenate([both, jnp.zeros((120, width), jnp.float32)], axis=0).T
        total = sum(plan.sizes)
        summed[:, total : total + 64] = spread[:, :64].astype(jnp.bfloat16)
    for copy in copies:
        copy.wait_send()


class Stage:
    def __init__(self, sizes, pieces, lefts, slots, attn, last, mlp):
        self.sizes, self.pieces, self.lefts, self.slots = sizes, pieces, lefts, slots
        self.attn, self.last, self.mlp = attn, last, mlp


def start_kernel(
    gains, places, starts, x, gate, up, down,
    all_gains, all_places, normed, bias, packed,
    full, turned, local_sems, send_a, recv_a, send_b, recv_b, send_c, recv_c,
):
    place = partners()
    me, side_x, side_y, across = place
    groups = (
        ("fsdp", gains, all_gains, (send_a, recv_a)),
        ("ctx", places, all_places, (send_b, recv_b)),
    )
    peers = []
    for axis, _, _, _ in groups:
        count = lax.axis_size(axis)
        peers.append([lax.rem(lax.axis_index(axis) + step, count) for step in range(1, count)])
    greet(*[{groups[n][0]: peer} for n in range(2) for peer in peers[n]])
    own = pltpu.make_async_copy(x, full.at[me], local_sems.at[0])
    own.start()
    copies = []
    for n, (axis, src, dst, sems) in enumerate(groups):
        mine = pltpu.make_async_copy(src, dst.at[lax.axis_index(axis)], local_sems.at[1 + n])
        mine.start()
        for step, peer in enumerate(peers[n]):
            copies.append(send(src, dst.at[lax.axis_index(axis)], sems, step, {axis: peer}))
        mine.wait()
    layers, depth, units = packed.shape[0], packed.shape[1], turned.shape[1]
    loads = []
    for layer in range(layers):
        cut = pl.ds(pl.multiple_of(me * units, units), units)
        for n, (src, dst) in enumerate((
            (gate.at[layer, :, cut], packed.at[layer, :, pl.ds(0, units)]),
            (up.at[layer, :, cut], packed.at[layer, :, pl.ds(units, units)]),
            (down.at[layer, cut], turned.at[layer]),
        )):
            loads.append(pltpu.make_async_copy(src, dst, local_sems.at[3 + 3 * layer + n]))
    for load in loads:
        load.start()
    own.wait()
    steps = gather_rows(full, (send_c, recv_c), place)
    next(steps)
    for copy in copies:
        copy.wait()
    gain = jnp.concatenate([all_gains[n, 0:1, :] for n in range(lax.axis_size("fsdp"))], axis=1)
    rows = full.shape[1]
    half = rows // 2
    step = 16

    def norm(top_of, low_of):
        for part_no, owner in enumerate((top_of, low_of)):
            @pl.loop(0, half // step)
            def _(i):
                here = pl.ds(pl.multiple_of(part_no * half + i * step, step), step)
                row = full[owner, here, :].astype(jnp.float32)
                inv_rms = lax.rsqrt(jnp.mean(row * row, axis=-1, keepdims=True) + epsilon)
                normed[owner, here, :] = (row * inv_rms * gain).astype(normed.dtype)

    def mask():
        length = bias.shape[0]
        block = 96
        query = lax.broadcasted_iota(jnp.int32, (1, length), 1)
        firsts = [starts[0:1, n : n + 1] for n in range(starts.shape[1])]
        in_query = [jnp.where((query >= f) & (query < f + PIECE_LEN), 1, 0) for f in firsts]
        for owner in range(all_places.shape[0]):
            @pl.loop(0, rows // block)
            def _(i):
                here = pl.ds(pl.multiple_of(i * block, block), block)
                key = owner * rows + i * block + lax.broadcasted_iota(jnp.int32, (block, 1), 0)
                valid = all_places[owner, here, 1:2]
                seen = 0
                for f, row in zip(firsts, in_query):
                    seen += jnp.where((key >= f) & (key < f + PIECE_LEN), 1, 0) * row
                seen = jnp.where(key <= query, 1, seen) * valid
                seen = jnp.where(key == query, 1, seen)
                bias[pl.ds(pl.multiple_of(owner * rows + i * block, block), block), :] = jnp.where(
                    seen > 0, 0.0, neg_big
                ).astype(bias.dtype)

    norm(me, me)
    mask()
    next(steps)
    norm(side_x, side_y)
    for load in loads:
        load.wait()
    for layer in range(layers):
        packed[layer, :, 2 * units :] = turned[layer].astype(jnp.float32).T.astype(packed.dtype)
    next(steps)
    norm(side_y, side_x)
    run(steps)
    norm(across, across)


def end_steps(part, middle, valid, out, branch_sq, from_x, from_y, passed, last, send_a, recv_a, send_c, recv_c):
    place = partners()
    me = place[0]
    side = lax.axis_index("tp")
    sibling = {"tp": 1 - side}
    greet({"ctx": place[1]}, {"ctx": place[2]}, sibling)
    yield from scatter_rows(part, from_x, from_y, passed, last, (send_a, recv_a), place)
    half = part.shape[1] // 2
    step = 16
    for part_no in range(2):
        @pl.loop(0, half // step)
        def _(i):
            rows = pl.ds(pl.multiple_of(i * step, step), step)
            start = part_no * half + i * step
            whole_rows = pl.ds(pl.multiple_of(start, step), step)
            branch = own_sum(part, from_x, from_y, last, me, part_no, rows, start, step)
            out[side, whole_rows, :] = (middle[whole_rows, :] + branch).astype(out.dtype)
            branch_sq[whole_rows, :] = valid[whole_rows, :] * jnp.sum(
                branch * branch, axis=-1, keepdims=True
            )
    send(out.at[side], out.at[side], (send_c, recv_c), 0, sibling).wait()


def stat_steps(stats, all_stats, stat_sent, stat_came, z_came, sems, place):
    depth = lax.axis_size("fsdp")
    level = lax.axis_index("fsdp")
    sibling = {"tp": 1 - lax.axis_index("tp")}
    others = [{"fsdp": lax.rem(level + step, depth)} for step in range(1, depth)]
    stat_sent[0] = stats[...]
    for n, peer in enumerate((sibling, {"ctx": place[1]}, {"ctx": place[2]})):
        copy = send(stat_sent.at[n], stat_came.at[n], sems, n, peer)
        yield
        copy.wait()
        stat_sent[n + 1] = stat_sent[n] + stat_came[n]
    z_came[level] = stat_sent[3]
    copies = [send(z_came.at[level], z_came.at[level], sems, 3 + n, peer) for n, peer in enumerate(others)]
    yield
    for copy in copies:
        copy.wait()
    held = z_came[0]
    for n in range(1, depth):
        held = held + z_came[n]
    all_stats[...] = held


def gather_steps(share, full, local_sem, send_sems, recv_sems):
    place = partners()
    greet({"ctx": place[1]}, {"ctx": place[2]})
    copy = pltpu.make_async_copy(share, full.at[place[0]], local_sem)
    copy.start()
    copy.wait()
    yield from gather_rows(full, (send_sems, recv_sems), place)


def tail_kernel(
    summed, share, stats, gathered, last_all, all_stats, z_came, stat_sent, stat_came, stat_z,
    local_sem, send_a, recv_a, send_b, recv_b, send_c, recv_c, send_d, recv_d,
):
    place = partners()
    me = place[0]
    depth = lax.axis_size("fsdp")
    level = lax.axis_index("fsdp")
    peers = [lax.rem(level + step, depth) for step in range(1, depth)]
    greet({"ctx": place[1]}, {"ctx": place[2]}, {"tp": 1 - lax.axis_index("tp")}, *[{"fsdp": peer} for peer in peers])
    rows = share.shape[0]
    counts = stat_steps(stats, all_stats, stat_sent, stat_came, stat_z, (send_c, recv_c), place)
    next(counts)
    copies = []
    for step, peer in enumerate(peers):
        block = summed.at[pl.ds(pl.multiple_of(peer * rows, rows), rows)]
        copies.append(send(block, z_came.at[level], (send_a, recv_a), step, {"fsdp": peer}))
    mine = pltpu.make_async_copy(share, gathered.at[me], local_sem)
    mine.start()
    mine.wait()
    first = gather_rows(gathered, (send_b, recv_b), place)
    next(first)
    next(counts)
    next(counts)
    next(first)
    next(counts)
    run(counts)
    for copy in copies:
        copy.wait_recv()
    step = 48

    @pl.loop(0, rows // step)
    def _(i):
        part_rows = pl.ds(pl.multiple_of(i * step, step), step)
        total = summed[pl.ds(pl.multiple_of(level * rows + i * step, step), step), :].astype(jnp.float32)
        for peer in peers:
            total += z_came[peer, part_rows, :].astype(jnp.float32)
        last_all[me, part_rows, :] = total.astype(last_all.dtype)

    run(gather_rows(last_all, (send_d, recv_d), place))
    run(first)
    for copy in copies:
        copy.wait_send()


def rs_scratch(rows, width):
    half = rows // 2
    return [
        pltpu.VMEM((2, half, width), jnp.bfloat16),
        pltpu.VMEM((2, half, width), jnp.bfloat16),
        pltpu.VMEM((2, half, width), jnp.bfloat16),
        pltpu.VMEM((2, half, width), jnp.bfloat16),
    ]


def dma_sems(count):
    return [pltpu.SemaphoreType.DMA((count,)), pltpu.SemaphoreType.DMA((count,))]


def linked_call(kernel, number, out_shape, scratch, micros, args, far=()):
    vmem = pl.BlockSpec(memory_space=pltpu.VMEM)
    hbm = pl.BlockSpec(memory_space=pl.ANY)
    return pl.pallas_call(
        kernel,
        out_shape=out_shape,
        in_specs=[vmem] * len(args) + [hbm] * len(far),
        out_specs=jax.tree.map(lambda _: vmem, out_shape),
        scratch_shapes=scratch,
        compiler_params=pltpu.CompilerParams(
            collective_id=number, has_side_effects=True, vmem_limit_bytes=60 << 20
        ),
        cost_estimate=pl.CostEstimate(
            flops=0, bytes_accessed=int(micros * 3.6e6), transcendentals=0
        ),
    )(*args, *far)


def forward_step(part, stream, gain, valid):
    rows, width = stream.shape
    return linked_call(
        forward_kernel, 2,
        (
            jax.ShapeDtypeStruct((rows, width), jnp.float32),
            jax.ShapeDtypeStruct((4, rows, width), jnp.bfloat16),
            jax.ShapeDtypeStruct((rows, 1), jnp.float32),
        ),
        rs_scratch(rows, width) + dma_sems(6) + dma_sems(6), 65,
        [part, stream, gain, valid],
    )


def forward_mlp_step(part, stream, gain, valid, weights, grad=None):
    rows, width = stream.shape
    pairs, units = weights.shape[0], weights.shape[2] // 3
    bf16, f32 = jnp.bfloat16, jnp.float32
    shape = jax.ShapeDtypeStruct
    whole = shape((4, rows, width), bf16)
    outs = [shape((rows, width), f32), whole, shape((rows, 1), f32), whole]
    outs += [shape((pairs, 4, rows, units), bf16)] * 3
    back = grad is not None
    scratch = rs_scratch(rows, width) + [pltpu.VMEM(weights.shape, bf16)]
    if back:
        outs.append(whole)
        scratch.append(pltpu.VMEM(whole.shape, bf16))
    scratch += dma_sems(6) + dma_sems(6) + [pltpu.SemaphoreType.DMA((2,))]
    return linked_call(
        functools.partial(forward_mlp_kernel, back), 13 if back else 12, outs, scratch, 75,
        [part, stream, gain, valid], [weights] + ([grad] if back else []),
    )


def backward_step(number, part, stream, gain, grad, lefts, rights, pairs, slots, other_rows=None, share=None, mlp=None):
    rows, width = stream.shape
    length = lefts[0].shape[0]
    sizes = [r[0].shape[-1] for r in rights]
    pieces = [len(r) for r in rights]
    attn = other_rows is not None
    last = share is not None
    total = sum(sizes) + (64 if attn else 0)
    bf16, f32 = jnp.bfloat16, jnp.float32
    outs = [jax.ShapeDtypeStruct(((2,) if last else ()) + (rows, width), f32)]
    if not last:
        outs.append(jax.ShapeDtypeStruct((4, rows, width), bf16))
    outs += [jax.ShapeDtypeStruct((16, width), f32), jax.ShapeDtypeStruct((width, total), bf16)]
    if last:
        outs.append(jax.ShapeDtypeStruct((4, *share.shape), bf16))
    if mlp is not None:
        outs += [jax.ShapeDtypeStruct((4, rows, width), bf16)] + [jax.ShapeDtypeStruct(mlp[0].shape, bf16)] * 2
    scratch = rs_scratch(rows, width)
    scratch += [pltpu.VMEM((length, width), bf16)] * 2
    scratch += [pltpu.VMEM((2, length, n), bf16) for n in sizes]
    scratch += [pltpu.VMEM((width, n), bf16) for n in sizes] * 2
    if attn:
        scratch += [pltpu.VMEM((8, width), f32)] * 2
    if mlp is not None:
        scratch.append(pltpu.VMEM(mlp[2].shape, bf16))
    scratch += dma_sems(6) + dma_sems(6) + dma_sems(len(sizes) + 2)
    scratch += [pltpu.SemaphoreType.DMA((3 + 2 * len(sizes),))]
    return linked_call(
        functools.partial(backward_kernel, Stage(sizes, pieces, pairs, slots, attn, last, mlp is not None)),
        number, outs, scratch, 35 if last else 65,
        [part, stream, gain, grad] + ([other_rows] if attn else []) + ([share] if last else [])
        + (list(mlp[:2]) if mlp is not None else []),
        (list(mlp[2:]) if mlp is not None else []) + list(lefts) + [half for r in rights for half in r],
    )


def tail_step(summed, share, stats):
    depth = lax.axis_size("fsdp")
    shape = jax.ShapeDtypeStruct
    bf16, f32 = jnp.bfloat16, jnp.float32
    last = (share.shape[0], summed.shape[1])
    outs = [shape((4, *share.shape), bf16), shape((4, *last), bf16), shape((8, 128), f32)]
    return linked_call(
        tail_kernel, 10, outs,
        [pltpu.VMEM((depth, *last), bf16), pltpu.VMEM((4, 8, 128), f32), pltpu.VMEM((3, 8, 128), f32)]
        + [pltpu.VMEM((depth, 8, 128), f32), pltpu.SemaphoreType.DMA]
        + dma_sems(depth) + dma_sems(6) + dma_sems(3 + depth) + dma_sems(6),
        60, [summed, share, stats],
    )


def start_step(gains, places, starts, x, gate, up, down):
    depth, across = lax.axis_size("fsdp"), lax.axis_size("ctx")
    layers, rows = gate.shape[:2]
    units = gate.shape[2] // across
    length = across * x.shape[0]
    bf16 = jnp.bfloat16
    shape = jax.ShapeDtypeStruct
    return linked_call(
        start_kernel, 8,
        (
            shape((depth, *gains.shape), gains.dtype),
            shape((across, *places.shape), places.dtype),
            shape((across, *x.shape), bf16),
            shape((length, length), bf16),
            shape((layers, rows, 3 * units), bf16),
        ),
        [
            pltpu.VMEM((across, *x.shape), bf16),
            pltpu.VMEM((layers, units, rows), bf16),
            pltpu.SemaphoreType.DMA((3 + 3 * layers,)),
        ] + dma_sems(depth) + dma_sems(across) + dma_sems(6),
        38, [gains, places, starts, x], [gate, up, down],
    )


def dot32(a, b, dims):
    return lax.dot_general(a, b, (dims, ((), ())), preferred_element_type=jnp.float32)


QUERIES = 128
ROWS = 384
LOG2E = 1.4426950408889634


def turn(x, cos_row, sin_row):
    half_dim = HEAD_DIM // 2
    swapped = jnp.concatenate([x[:, half_dim:], x[:, :half_dim]], axis=1)
    return x * cos_row + swapped * sin_row


def block_groups(length):
    count = length // QUERIES
    per = 3 if count % 3 == 0 else 1
    groups = []
    for first in range(0, count, per):
        seen = min(length, (first + per) * QUERIES + PIECE_LEN)
        groups.append((first, per, seen))
    return groups


def attend_kernel(
    normed, weights, cos_ref, sin_ref, bias, share, part, query, key, value, lse, mixed, gathered, *sems
):
    job = gather_steps(share, gathered, *sems)
    next(job)
    attend_rows(normed, weights, cos_ref, sin_ref, bias, part, query, key, value, lse, mixed, lambda: next(job))
    run(job)


def attend_rows(normed, weights, cos_ref, sin_ref, bias, part, query, key, value, lse, mixed, between=lambda: None):
    length = normed.shape[0]
    pairs = weights.shape[0]
    cols_q = 2 * HEAD_DIM
    base = 4 * HEAD_DIM
    blocks = ROWS // QUERIES

    @pl.loop(0, length // ROWS)
    def _(i):
        rows = pl.ds(pl.multiple_of(i * ROWS, ROWS), ROWS)
        cos_b, sin_b = cos_ref[rows, :], sin_ref[rows, :]
        for t in range(pairs):
            flat = dot32(normed[rows, :], weights[t, :, :base], ((1,), (0,)))
            for g in range(2):
                head = turn(flat[:, g * HEAD_DIM : (g + 1) * HEAD_DIM], cos_b, sin_b).astype(jnp.bfloat16)
                for n in range(blocks):
                    query[t, i * blocks + n, g * QUERIES : (g + 1) * QUERIES, :] = head[n * QUERIES : (n + 1) * QUERIES]
            key[t, rows, :] = turn(flat[:, cols_q : cols_q + HEAD_DIM], cos_b, sin_b).astype(jnp.bfloat16)
            value[t, rows, :] = flat[:, cols_q + HEAD_DIM : base].astype(jnp.bfloat16)

    factor = HEAD_DIM ** (-0.5) * LOG2E
    for first, count, seen in block_groups(length):
        @pl.loop(0, pairs * count)
        def _(n):
            t = n // count
            block = first + n % count
            rows = pl.ds(pl.multiple_of(block * QUERIES, QUERIES), QUERIES)
            raw = dot32(key[t, :seen, :], query[t, block], ((1,), (1,)))
            low = bias[:seen, rows].astype(jnp.float32)
            raw = raw * factor + jnp.concatenate([low, low], axis=1)
            top = jnp.max(raw, axis=0, keepdims=True)
            probs = jnp.exp2(raw - top)
            total = jnp.sum(probs, axis=0, keepdims=True)
            out = dot32(value[t, :seen, :], probs.astype(jnp.bfloat16), ((0,), (0,)))
            out = (out * (1.0 / total)).T.astype(jnp.bfloat16)
            lse[t, block] = top + jnp.log2(total)
            for g in range(2):
                mixed[t, rows, g * HEAD_DIM : (g + 1) * HEAD_DIM] = out[g * QUERIES : (g + 1) * QUERIES]
        if first == 0:
            between()

    @pl.loop(0, length // ROWS)
    def _(i):
        rows = pl.ds(pl.multiple_of(i * ROWS, ROWS), ROWS)
        total = dot32(mixed[0, rows, :], weights[0, :, base : base + cols_q], ((1,), (1,)))
        for t in range(1, pairs):
            total += dot32(mixed[t, rows, :], weights[t, :, base : base + cols_q], ((1,), (1,)))
        part[rows, :] = total.astype(jnp.bfloat16)


def attend_back_kernel(steps, counts, *refs):
    refs = list(refs)

    def take(count):
        taken = refs[:count]
        del refs[:count]
        return taken

    grad, weights, cos_ref, sin_ref, bias, query, key, value, lse = take(9)
    job_refs = take(counts[0])
    part, grad_qkv = take(2)
    job_refs += take(counts[1])
    heads, g_key, g_value = take(3)
    job = steps(*job_refs, *refs)
    next(job)
    length = grad.shape[0]
    pairs = weights.shape[0]
    cols_q = 2 * HEAD_DIM
    base = 4 * HEAD_DIM
    blocks = ROWS // QUERIES
    scale = HEAD_DIM ** (-0.5)
    factor = scale * LOG2E

    @pl.loop(0, length // ROWS)
    def _(i):
        rows = pl.ds(pl.multiple_of(i * ROWS, ROWS), ROWS)
        for t in range(pairs):
            flat = dot32(grad[rows, :], weights[t, :, base : base + cols_q], ((1,), (0,))).astype(jnp.bfloat16)
            for g in range(2):
                for n in range(blocks):
                    heads[t, i * blocks + n, g * QUERIES : (g + 1) * QUERIES, :] = flat[
                        n * QUERIES : (n + 1) * QUERIES, g * HEAD_DIM : (g + 1) * HEAD_DIM
                    ]
    g_key[...] = jnp.zeros_like(g_key)
    g_value[...] = jnp.zeros_like(g_value)
    for first, count, seen in block_groups(length):
        @pl.loop(0, pairs * count)
        def _(n):
            t = n // count
            block = first + n % count
            rows = pl.ds(pl.multiple_of(block * QUERIES, QUERIES), QUERIES)
            low = bias[:seen, rows].astype(jnp.float32)
            raw = dot32(key[t, :seen, :], query[t, block], ((1,), (1,)))
            probs = jnp.exp2(raw * factor + jnp.concatenate([low, low], axis=1) - lse[t, block])
            g_probs = dot32(value[t, :seen, :], heads[t, block], ((1,), (1,)))
            weighed = probs * g_probs
            along = jnp.sum(weighed, axis=0, keepdims=True)
            g_scores = (weighed - probs * along).astype(jnp.bfloat16)
            g_value[t, :seen, :] += dot32(probs.astype(jnp.bfloat16), heads[t, block], ((1,), (0,)))
            g_key[t, :seen, :] += dot32(g_scores, query[t, block], ((1,), (0,)))
            g_query = dot32(key[t, :seen, :], g_scores, ((0,), (0,))).T * scale
            cos_b, sin_b = cos_ref[rows, :], sin_ref[rows, :]
            for g in range(2):
                grad_qkv[t, rows, g * HEAD_DIM : (g + 1) * HEAD_DIM] = turn(
                    g_query[g * QUERIES : (g + 1) * QUERIES], cos_b, -sin_b
                ).astype(jnp.bfloat16)
        if first == 0:
            next(job)

    @pl.loop(0, length // ROWS)
    def _(i):
        rows = pl.ds(pl.multiple_of(i * ROWS, ROWS), ROWS)
        cos_b, sin_b = cos_ref[rows, :], sin_ref[rows, :]
        total = 0.0
        for t in range(pairs):
            grad_qkv[t, rows, cols_q : cols_q + HEAD_DIM] = turn(g_key[t, rows, :] * scale, cos_b, -sin_b).astype(jnp.bfloat16)
            grad_qkv[t, rows, cols_q + HEAD_DIM : base] = g_value[t, rows, :].astype(jnp.bfloat16)
            total += dot32(grad_qkv[t, rows, :], weights[t, :, :base], ((1,), (1,)))
        part[rows, :] = total.astype(jnp.bfloat16)
    run(job)


def local_call(kernel, out_shape, scratch, micros, *args):
    vmem = pl.BlockSpec(memory_space=pltpu.VMEM)
    return pl.pallas_call(
        kernel,
        out_shape=out_shape,
        in_specs=[vmem] * len(args),
        out_specs=jax.tree.map(lambda _: vmem, out_shape),
        scratch_shapes=scratch,
        compiler_params=pltpu.CompilerParams(vmem_limit_bytes=60 << 20),
        cost_estimate=pl.CostEstimate(flops=0, bytes_accessed=int(micros * 3.6e6), transcendentals=0),
    )(*args)


def attend(normed, weights, cosine, sine_t, bias, share=None):
    length, width = normed.shape
    pairs = weights.shape[0]
    blocks = length // QUERIES
    bf16 = jnp.bfloat16
    shape = jax.ShapeDtypeStruct
    outs = [
        shape((length, width), bf16),
        shape((pairs, blocks, 2 * QUERIES, HEAD_DIM), bf16),
        shape((pairs, length, HEAD_DIM), bf16),
        shape((pairs, length, HEAD_DIM), bf16),
        shape((pairs, blocks, 1, 2 * QUERIES), jnp.float32),
        shape((pairs, length, 2 * HEAD_DIM), bf16),
    ]
    if share is None:
        return local_call(attend_rows, outs, [], 30, normed, weights, cosine, sine_t, bias)
    return linked_call(
        attend_kernel, 11, outs + [shape((4, *share.shape), bf16)], [pltpu.SemaphoreType.DMA] + dma_sems(6), 35,
        [normed, weights, cosine, sine_t, bias, share],
    )


def attend_back(grad, weights, cosine, sine_t, bias, query, key, value, lse, share=None, end=None):
    length, width = grad.shape
    pairs = weights.shape[0]
    bf16, f32 = jnp.bfloat16, jnp.float32
    shape = jax.ShapeDtypeStruct
    outs = [shape((length, width), bf16), shape((pairs, length, 4 * HEAD_DIM), bf16)]
    scratch = [pltpu.VMEM(query.shape, bf16), pltpu.VMEM(key.shape, f32), pltpu.VMEM(key.shape, f32)]
    if end is None:
        steps, number, more = gather_steps, 9, [share]
        more_outs = [shape((4, *share.shape), bf16)]
        scratch += [pltpu.SemaphoreType.DMA] + dma_sems(6)
    else:
        steps, number, more = end_steps, 4, end
        rows = end[1].shape[0]
        more_outs = [shape((2, rows, width), bf16), shape((rows, 1), f32)]
        scratch += rs_scratch(rows, width) + dma_sems(6) + dma_sems(1)
    return linked_call(
        functools.partial(attend_back_kernel, steps, (len(more), len(more_outs))),
        number, outs + more_outs, scratch, 40,
        [grad, weights, cosine, sine_t, bias, query, key, value, lse, *more],
    )


def planned(
    tokens, positions, valid, piece_starts, d_out,
    attn_gain, w_query, w_key, w_value, w_out, mlp_gain, w_gate, w_up, w_down,
):
    seq_count, rows, width = tokens.shape
    layers = attn_gain.shape[0]
    ctx_count = lax.axis_size("ctx")
    tp_count = lax.axis_size("tp")
    me = lax.axis_index("ctx")
    side = lax.axis_index("tp")
    length = rows * ctx_count
    heads_q = HEADS // tp_count // ctx_count
    heads_k = KV_HEADS // tp_count // ctx_count
    cols_q = heads_q * HEAD_DIM
    cols_k = heads_k * HEAD_DIM
    units = w_gate.shape[2] // ctx_count

    def own(a):
        return lax.dynamic_index_in_dim(a, side, 0, keepdims=False)

    def cut(w, axis, count):
        return lax.dynamic_slice_in_dim(w, me * count, count, axis)

    def whole(w):
        return lax.all_gather(w, ("tp", "fsdp"), axis=0, tiled=True).reshape(
            tp_count, width, w.shape[1]
        )

    def pack(*pieces):
        return with_layout_constraint(jnp.concatenate(pieces, axis=1), Layout(major_to_minor=(0, 1)))

    def pack_attn(layer):
        return pack(
            cut(w_query[layer], 1, cols_q),
            cut(w_key[layer], 1, cols_k),
            cut(w_value[layer], 1, cols_k),
            cut(w_out[layer], 0, cols_q).T,
            jnp.zeros((w_query.shape[1], 64), w_query.dtype),
        )

    attn_w = [whole(pack_attn(0))]
    packed_attn = [None] + [pack_attn(layer) for layer in range(1, layers)]
    mlp_w = []
    seq_pos, seq_valid = own(positions), own(valid)
    starts = own(piece_starts)
    gains, places, normed, bias, packed = start_step(
        jnp.pad(jnp.concatenate([attn_gain, mlp_gain], 0).astype(jnp.float32), ((0, 8 - 2 * layers), (0, 0))),
        jnp.pad(jnp.stack([seq_pos, seq_valid], axis=1), ((0, 0), (0, 6))),
        starts[None], own(tokens), w_gate, w_up, w_down,
    )
    packed_mlp = [packed[layer] for layer in range(layers)]
    gains = gains.swapaxes(0, 1).reshape(8, width)
    gain_a = [gains[layer][None] for layer in range(layers)]
    gain_m = [gains[layers + layer][None] for layer in range(layers)]
    pos_all = places[:, :, 0].reshape(length)
    stream = own(tokens).astype(jnp.float32)
    grad = own(d_out).astype(jnp.float32)
    valid_f = seq_valid.astype(jnp.float32)[:, None]
    mlp_w.append(whole(packed_mlp[0]))
    half_dim = HEAD_DIM // 2
    freqs = rope_base ** (-(jnp.arange(half_dim).astype(jnp.float32) * 2.0 / HEAD_DIM))
    angles = pos_all.astype(jnp.float32)[:, None] * freqs
    cosine, sine_t = jnp.cos(angles), jnp.sin(angles)
    cosine = jnp.concatenate([cosine, cosine], axis=1)
    sine_t = jnp.concatenate([-sine_t, sine_t], axis=1)
    stat_rows = []
    saved = []
    for layer in range(layers):
        normed_a = normed.reshape(length, width)
        if layer:
            part, query, key, value, lse, mixed = attend(normed_a, attn_w[layer], cosine, sine_t, bias)
        else:
            part, query, key, value, lse, mixed, down_grad = attend(
                normed_a, attn_w[layer], cosine, sine_t, bias, own(d_out)
            )
        came = forward_mlp_step(
            part.reshape(4, rows, width), stream, gain_m[layer], valid_f, mlp_w[layer],
            down_grad if layer + 1 == layers else None,
        )
        middle, normed_m, attn_sq, mlp_part = came[:4]
        if layer + 1 < layers:
            normed_m, packed_attn[layer + 1], packed_mlp[layer + 1] = lax.optimization_barrier(
                (normed_m, packed_attn[layer + 1], packed_mlp[layer + 1])
            )
            attn_w.append(whole(packed_attn[layer + 1]))
            mlp_w.append(whole(packed_mlp[layer + 1]))
        normed_m = normed_m.reshape(length, width)
        saved.append((stream, normed_a, query, key, value, lse, mixed, middle, normed_m, came[4:]))
        stat_rows.append(jnp.sum(valid_f * stream * stream))
        stat_rows.append(jnp.sum(attn_sq))
        if layer + 1 < layers:
            stream, normed, mlp_sq = forward_step(mlp_part, middle, gain_a[layer + 1], valid_f)
            stat_rows.append(jnp.sum(mlp_sq))
    last_part, last_middle = mlp_part, middle

    def reduced(g):
        return lax.psum_scatter(g, "fsdp", scatter_dimension=0, tiled=True)

    base = cols_q + 2 * cols_k
    waiting = {}
    mlp_all, attn_all = [None] * layers, [None] * layers

    def after(x, names):
        names = [n for n in names if n in waiting]
        if not names:
            return x
        x, done = lax.optimization_barrier((x, [waiting[n] for n in names]))
        for n, value in zip(names, done):
            waiting[n] = value
        return x

    for layer in reversed(range(layers)):
        stream_in, normed_a, query, key, value, lse, mixed, middle, normed_m, units_kept = saved[layer]
        up_one = layer + 1
        hidden = units_kept[0].reshape(tp_count, length, units)
        if up_one == layers:
            grad_gate, grad_up, part = units_kept[1:]
        grad_gate = grad_gate.reshape(tp_count, length, units)
        grad_up = grad_up.reshape(tp_count, length, units)
        part = after(part, [(up_one, "mlp")])
        grad_mid, attn_grad, gm_rows, g_mlp = backward_step(
            5, part, middle, gain_m[layer], grad, [normed_m, down_grad.reshape(length, width)],
            [[grad_gate], [grad_up], [hidden]], [0, 0, 1],
            [[(1, 0), (1, 1)], [(1, 2), (0, 0)], [(0, 1)], [(0, 2)]],
        )
        waiting[layer, "mlp"] = reduced(g_mlp)
        attn_grad = attn_grad.reshape(length, width)
        if layer + 1 == layers:
            part, gqkv, output, mlp_sq = attend_back(
                attn_grad, attn_w[layer], cosine, sine_t, bias, query, key, value, lse,
                end=[last_part, last_middle, valid_f],
            )
            stat_rows += [jnp.sum(mlp_sq), jnp.sum(valid_f)]
        else:
            part, gqkv, mlp_all[up_one] = attend_back(
                attn_grad, attn_w[layer], cosine, sine_t, bias, query, key, value, lse,
                share=waiting[up_one, "mlp"],
            )
        part = after(part.reshape(4, rows, width), [(up_one, "attn")])
        came = backward_step(
            6 if layer else 7, part, stream_in, gain_a[layer], grad_mid, [normed_a, attn_grad], [[gqkv], [mixed]], [0, 1],
            [[(1, 0), (1, 1)], [(0, 0), (0, 1)], [], []], other_rows=gm_rows, share=None if layer else waiting[1, "attn"],
            mlp=[*saved[layer - 1][-1][1:], mlp_w[layer - 1]] if layer else None,
        )
        if layer:
            grad, down_grad, _, g_attn, part, grad_gate, grad_up = came
        else:
            input_grad, _, g_attn, attn_all[1] = came
        if layer:
            waiting[layer, "attn"] = reduced(g_attn)
    stats = jnp.pad(jnp.stack(stat_rows)[None], ((0, 7), (0, 121)))
    mlp_all[0], attn_all[0], stats = tail_step(g_attn, waiting[0, "mlp"], stats)
    rms_stats = jnp.sqrt(stats[0, : 3 * layers] / (stats[0, 3 * layers] * width)).reshape(layers, 3)
    placed = place_outs(
        attn_all, mlp_all,
        [(0, cols_q, False), (cols_q, cols_k, False), (cols_q + cols_k, cols_k, False), (base, cols_q, True)],
        [(0, units, False), (units, units, False), (2 * units, units, True)],
    )
    gain_sum = jnp.stack([
        jnp.sum(a[:, :, base + cols_q : base + cols_q + 2].astype(jnp.float32), 0) for a in attn_all
    ])
    return (
        output, input_grad, gain_sum[:, :, 0], *placed[:4], gain_sum[:, :, 1], *placed[4:], rms_stats,
    )


def place_kernel(moves, count, *refs):
    refs = list(refs)
    outs_count = 1 + max(out for pieces in moves for _, _, _, out, _ in pieces)
    ins, outs = refs[:count], refs[count : count + outs_count]
    held = refs[count + outs_count : 2 * count + outs_count]
    laid = refs[2 * count + outs_count : -2]
    in_sems, out_sems = refs[-2:]
    loads = [pltpu.make_async_copy(ins[n], held[n], in_sems.at[n]) for n in range(count)]
    for load in loads:
        load.start()
    stores = []
    for n, pieces in enumerate(moves):
        loads[n].wait()
        for start, size, flip, out, layer in pieces:
            for c in range(held[n].shape[0]):
                block = held[n][c, :, start : start + size].astype(jnp.float32)
                if flip:
                    laid[out][layer, c * size : (c + 1) * size, :] = block.T
                else:
                    laid[out][layer, :, c * size : (c + 1) * size] = block
            store = pltpu.make_async_copy(laid[out].at[layer], outs[out].at[layer], out_sems.at[len(stores)])
            store.start()
            stores.append(store)
    for store in stores:
        store.wait()


def place_outs(attn_all, mlp_all, attn_pieces, mlp_pieces):
    layers = len(attn_all)
    shapes = []
    for came, pieces in ((attn_all, attn_pieces), (mlp_all, mlp_pieces)):
        ctx_count, depth, _ = came[0].shape
        for _, size, flip in pieces:
            wide = ctx_count * size
            shapes.append((layers, wide, depth) if flip else (layers, depth, wide))
    ins, moves = [], []
    for layer in reversed(range(layers)):
        for came, pieces, base in ((mlp_all, mlp_pieces, len(attn_pieces)), (attn_all, attn_pieces, 0)):
            ins.append(came[layer])
            moves.append([(*piece, base + n, layer) for n, piece in enumerate(pieces)])
    hbm = pl.BlockSpec(memory_space=pl.ANY)
    return pl.pallas_call(
        functools.partial(place_kernel, moves, len(ins)),
        out_shape=[jax.ShapeDtypeStruct(s, jnp.float32) for s in shapes],
        in_specs=[hbm] * len(ins),
        out_specs=[hbm] * len(shapes),
        scratch_shapes=[pltpu.VMEM(a.shape, a.dtype) for a in ins]
        + [pltpu.VMEM(s, jnp.float32) for s in shapes]
        + [pltpu.SemaphoreType.DMA((len(ins),)), pltpu.SemaphoreType.DMA((sum(len(m) for m in moves),))],
        compiler_params=pltpu.CompilerParams(vmem_limit_bytes=60 << 20),
    )(*ins)


def fits(mesh):
    tp_count, ctx_count = mesh.shape["tp"], mesh.shape["ctx"]
    return ctx_count == 4 and tp_count == 2


def solution(mesh):
    in_specs = (
        P("fsdp", "ctx", None),
        P("fsdp", "ctx"),
        P("fsdp", "ctx"),
        P("fsdp", None),
        P("fsdp", "ctx", None),
        P(None, "fsdp"),
        P(None, "fsdp", "tp"),
        P(None, "fsdp", "tp"),
        P(None, "fsdp", "tp"),
        P(None, "tp", "fsdp"),
        P(None, "fsdp"),
        P(None, "fsdp", "tp"),
        P(None, "fsdp", "tp"),
        P(None, "tp", "fsdp"),
    )
    out_specs = (
        P("fsdp", "ctx", None),
        P("fsdp", "ctx", None),
        P(None, "fsdp"),
        P(None, "fsdp", "tp"),
        P(None, "fsdp", "tp"),
        P(None, "fsdp", "tp"),
        P(None, "tp", "fsdp"),
        P(None, "fsdp"),
        P(None, "fsdp", "tp"),
        P(None, "fsdp", "tp"),
        P(None, "tp", "fsdp"),
        P(),
    )
    return jax.shard_map(planned if fits(mesh) else general, mesh=mesh, in_specs=in_specs, out_specs=out_specs, check_vma=False)
```

```python
import functools

import jax
import jax.numpy as jnp
from jax import lax
from jax.experimental import pallas as pl
from jax.experimental.layout import Layout, with_layout_constraint
from jax.experimental.pallas import tpu as pltpu
from jax.sharding import PartitionSpec as P

MESH = pl.DeviceIdType.MESH
FSDP, CTX, TP = "fsdp", "ctx", "tp"

HEADS = 16
KV_HEADS = 8
HEAD_DIM = 96
PIECE_LEN = 256


epsilon = 1e-05
rope_base = 100000.0
neg_big = -1e30


def rope_tables(positions, head_dim):
    half_dim = head_dim // 2
    freqs = rope_base ** (-(jnp.arange(half_dim).astype(jnp.float32) * 2.0 / head_dim))
    angles = positions.astype(jnp.float32)[..., None] * freqs
    return (jnp.cos(angles)[:, :, None, :], jnp.sin(angles)[:, :, None, :])


def rotate(values, cosine, sine_t):
    half_dim = values.shape[-1] // 2
    lead_part = values[..., :half_dim]
    tail_part = values[..., half_dim:]
    return jnp.concatenate(
        [lead_part * cosine - tail_part * sine_t, tail_part * cosine + lead_part * sine_t], axis=-1
    )


def normalize(stream, gain_vec):
    inv_rms = lax.rsqrt(jnp.mean(stream * stream, axis=-1, keepdims=True) + epsilon)
    return stream * inv_rms * gain_vec.astype(jnp.float32)


def norm_back(stream, gain_vec, grad_out):
    inv_rms = lax.rsqrt(jnp.mean(stream * stream, axis=-1, keepdims=True) + epsilon)
    scaled_grad = gain_vec.astype(jnp.float32) * grad_out
    grad_in = inv_rms * scaled_grad - stream * inv_rms**3 * jnp.mean(
        scaled_grad * stream, axis=-1, keepdims=True
    )
    grad_gain = jnp.sum(grad_out * stream * inv_rms, axis=0)
    return (grad_in, grad_gain)


def score_block(query_b, key_heads, allowed, score_scale):
    raw_scores = (
        jnp.einsum("sckgd,snkd->skgcn", query_b, key_heads, preferred_element_type=jnp.float32)
        * score_scale
    )
    return jnp.where(allowed[:, None, None], raw_scores, neg_big)


def general(
    tokens,
    positions,
    valid,
    piece_starts,
    d_out,
    attn_gain,
    w_query,
    w_key,
    w_value,
    w_out,
    mlp_gain,
    w_gate,
    w_up,
    w_down,
):
    seq_count, shard_len, model_width = tokens.shape
    tok_rows = seq_count * shard_len
    tp_count = lax.axis_size(TP)
    local_heads = HEADS // tp_count
    local_kv = KV_HEADS // tp_count
    group_size = HEADS // KV_HEADS
    score_scale = HEAD_DIM ** (-0.5)
    seq_length = shard_len * lax.axis_size(CTX)
    start_tok = lax.axis_index(CTX) * shard_len
    query_index = start_tok + jnp.arange(shard_len, dtype=jnp.int32)
    key_index = jnp.arange(seq_length, dtype=jnp.int32)
    cosine, sine_t = rope_tables(positions, HEAD_DIM)
    valid_flat = valid.astype(jnp.float32).reshape(tok_rows)
    in_query = (query_index[None, None, :] >= piece_starts[:, :, None]) & (
        query_index[None, None, :] < piece_starts[:, :, None] + PIECE_LEN
    )
    in_key = (key_index[None, None, :] >= piece_starts[:, :, None]) & (
        key_index[None, None, :] < piece_starts[:, :, None] + PIECE_LEN
    )
    same_piece = jnp.any(in_query[:, :, :, None] & in_key[:, :, None, :], axis=1)
    causal = key_index[None, :] <= query_index[:, None]
    diagonal = key_index[None, :] == query_index[:, None]
    layer_count = attn_gain.shape[0]
    stream = tokens.astype(jnp.float32).reshape(tok_rows, model_width)
    saved = []
    stat_rows = []
    for layer_no in range(layer_count):
        weights = (
            lax.all_gather(attn_gain[layer_no], FSDP, axis=0, tiled=True),
            lax.all_gather(w_query[layer_no], FSDP, axis=0, tiled=True),
            lax.all_gather(w_key[layer_no], FSDP, axis=0, tiled=True),
            lax.all_gather(w_value[layer_no], FSDP, axis=0, tiled=True),
            lax.all_gather(w_out[layer_no], FSDP, axis=1, tiled=True),
            lax.all_gather(mlp_gain[layer_no], FSDP, axis=0, tiled=True),
            lax.all_gather(w_gate[layer_no], FSDP, axis=0, tiled=True),
            lax.all_gather(w_up[layer_no], FSDP, axis=0, tiled=True),
            lax.all_gather(w_down[layer_no], FSDP, axis=1, tiled=True),
        )
        gain_a, w_q, w_k, w_v, w_o, gain_m, w_g, w_u, w_d = weights
        normed_a = normalize(stream, gain_a).astype(jnp.bfloat16)
        query_heads = jnp.dot(normed_a, w_q, preferred_element_type=jnp.float32).reshape(
            seq_count, shard_len, local_heads, HEAD_DIM
        )
        query_b = (
            rotate(query_heads, cosine, sine_t)
            .astype(jnp.bfloat16)
            .reshape(seq_count, shard_len, local_kv, group_size, HEAD_DIM)
        )
        key_local = jnp.dot(normed_a, w_k, preferred_element_type=jnp.float32).reshape(
            seq_count, shard_len, local_kv, HEAD_DIM
        )
        key_local = (
            rotate(key_local, cosine, sine_t)
            .astype(jnp.bfloat16)
            .reshape(seq_count, shard_len, local_kv * HEAD_DIM)
        )
        value_local = (
            jnp.dot(normed_a, w_v, preferred_element_type=jnp.float32)
            .astype(jnp.bfloat16)
            .reshape(seq_count, shard_len, local_kv * HEAD_DIM)
        )
        key_all, value_all, valid_all = (
            lax.all_gather(key_local, CTX, axis=1, tiled=True),
            lax.all_gather(value_local, CTX, axis=1, tiled=True),
            lax.all_gather(valid.astype(jnp.bfloat16), CTX, axis=1, tiled=True),
        )
        allowed = (causal[None] | same_piece) & ((valid_all[:, None, :] > 0.5) | diagonal[None])
        key_heads = key_all.reshape(seq_count, seq_length, local_kv, HEAD_DIM)
        value_heads = value_all.reshape(seq_count, seq_length, local_kv, HEAD_DIM)
        raw_scores = score_block(query_b, key_heads, allowed, score_scale)
        row_max = jnp.max(raw_scores, axis=-1, keepdims=True)
        log_total = row_max + jnp.log(
            jnp.sum(jnp.exp(raw_scores - row_max), axis=-1, keepdims=True)
        )
        softmax_b = jnp.exp(raw_scores - log_total).astype(jnp.bfloat16)
        mixed_heads = jnp.einsum(
            "skgcn,snkd->sckgd", softmax_b, value_heads, preferred_element_type=jnp.float32
        )
        mixed_b = mixed_heads.astype(jnp.bfloat16).reshape(tok_rows, local_heads * HEAD_DIM)
        attn_branch = lax.psum(
            jnp.dot(mixed_b, w_o, preferred_element_type=jnp.float32).astype(jnp.bfloat16), TP
        ).astype(jnp.float32)
        middle = stream + attn_branch
        normed_m = normalize(middle, gain_m).astype(jnp.bfloat16)
        gate_act = jnp.dot(normed_m, w_g, preferred_element_type=jnp.float32)
        up_act = jnp.dot(normed_m, w_u, preferred_element_type=jnp.float32)
        hidden = (jax.nn.silu(gate_act) * up_act).astype(jnp.bfloat16)
        mlp_branch = lax.psum(
            jnp.dot(hidden, w_d, preferred_element_type=jnp.float32).astype(jnp.bfloat16), TP
        ).astype(jnp.float32)
        stat_rows.append(
            jnp.stack(
                [
                    jnp.sum(valid_flat[:, None] * stream * stream),
                    jnp.sum(valid_flat[:, None] * attn_branch * attn_branch),
                    jnp.sum(valid_flat[:, None] * mlp_branch * mlp_branch),
                ]
            )
        )
        kept_weights = None
        saved.append(
            (
                stream,
                normed_a,
                query_b,
                key_heads,
                value_heads,
                allowed,
                log_total,
                mixed_b,
                middle,
                normed_m,
                gate_act,
                up_act,
                hidden,
                kept_weights,
            )
        )
        stream = middle + mlp_branch
    output = stream.astype(jnp.bfloat16).reshape(seq_count, shard_len, model_width)
    total_squares, total_count = lax.psum(
        (jnp.stack(stat_rows), jnp.sum(valid_flat)), (FSDP, CTX)
    )
    rms_stats = jnp.sqrt(total_squares / (total_count * model_width))
    grad_stream = d_out.astype(jnp.float32).reshape(tok_rows, model_width)
    results = [None] * layer_count
    for layer_no in reversed(range(layer_count)):
        (
            stream_in,
            normed_a,
            query_b,
            key_heads,
            value_heads,
            allowed,
            log_total,
            mixed_b,
            middle,
            normed_m,
            gate_act,
            up_act,
            hidden,
            kept_weights,
        ) = saved[layer_no]
        weights = (
            lax.all_gather(attn_gain[layer_no], FSDP, axis=0, tiled=True),
            lax.all_gather(w_query[layer_no], FSDP, axis=0, tiled=True),
            lax.all_gather(w_key[layer_no], FSDP, axis=0, tiled=True),
            lax.all_gather(w_value[layer_no], FSDP, axis=0, tiled=True),
            lax.all_gather(w_out[layer_no], FSDP, axis=1, tiled=True),
            lax.all_gather(mlp_gain[layer_no], FSDP, axis=0, tiled=True),
            lax.all_gather(w_gate[layer_no], FSDP, axis=0, tiled=True),
            lax.all_gather(w_up[layer_no], FSDP, axis=0, tiled=True),
            lax.all_gather(w_down[layer_no], FSDP, axis=1, tiled=True),
        )
        gain_a, w_q, w_k, w_v, w_o, gain_m, w_g, w_u, w_d = weights
        grad_mlp = grad_stream.astype(jnp.bfloat16)
        grad_hidden = jnp.einsum("rd,fd->rf", grad_mlp, w_d, preferred_element_type=jnp.float32)
        g_down = jnp.einsum("rf,rd->fd", hidden, grad_mlp, preferred_element_type=jnp.float32)
        sigmoid_g = jax.nn.sigmoid(gate_act)
        grad_gate = (
            grad_hidden * up_act * sigmoid_g * (1.0 + gate_act * (1.0 - sigmoid_g))
        ).astype(jnp.bfloat16)
        grad_up = (grad_hidden * gate_act * sigmoid_g).astype(jnp.bfloat16)
        grad_normed_m = lax.psum(
            (
                jnp.einsum("rf,df->rd", grad_gate, w_g, preferred_element_type=jnp.float32)
                + jnp.einsum("rf,df->rd", grad_up, w_u, preferred_element_type=jnp.float32)
            ).astype(jnp.bfloat16),
            TP,
        ).astype(jnp.float32)
        g_gate = jnp.einsum("rd,rf->df", normed_m, grad_gate, preferred_element_type=jnp.float32)
        g_up = jnp.einsum("rd,rf->df", normed_m, grad_up, preferred_element_type=jnp.float32)
        grad_from_norm, g_gain_m = norm_back(middle, gain_m, grad_normed_m)
        grad_middle = grad_stream + grad_from_norm
        grad_attn = grad_middle.astype(jnp.bfloat16)
        grad_heads = jnp.einsum(
            "rd,hd->rh", grad_attn, w_o, preferred_element_type=jnp.float32
        ).astype(jnp.bfloat16)
        g_out = jnp.einsum("rh,rd->hd", mixed_b, grad_attn, preferred_element_type=jnp.float32)
        grad_heads = grad_heads.reshape(seq_count, shard_len, local_kv, group_size, HEAD_DIM)
        raw_scores = score_block(query_b, key_heads, allowed, score_scale)
        softmax_p = jnp.exp(raw_scores - log_total)
        grad_probs = jnp.einsum(
            "sckgd,snkd->skgcn", grad_heads, value_heads, preferred_element_type=jnp.float32
        )
        row_dots = jnp.sum(softmax_p * grad_probs, axis=-1, keepdims=True)
        grad_scores = (softmax_p * (grad_probs - row_dots)).astype(jnp.bfloat16)
        grad_query = (
            jnp.einsum(
                "skgcn,snkd->sckgd", grad_scores, key_heads, preferred_element_type=jnp.float32
            )
            * score_scale
        )
        grad_key_all = (
            jnp.einsum(
                "skgcn,sckgd->snkd", grad_scores, query_b, preferred_element_type=jnp.float32
            )
            * score_scale
        )
        grad_value_all = jnp.einsum(
            "skgcn,sckgd->snkd",
            softmax_p.astype(jnp.bfloat16),
            grad_heads,
            preferred_element_type=jnp.float32,
        )
        grad_key, grad_value = (
            lax.psum_scatter(
                grad_key_all.reshape(seq_count, seq_length, local_kv * HEAD_DIM).astype(
                    jnp.bfloat16
                ),
                CTX,
                scatter_dimension=1,
                tiled=True,
            ).astype(jnp.float32),
            lax.psum_scatter(
                grad_value_all.reshape(seq_count, seq_length, local_kv * HEAD_DIM).astype(
                    jnp.bfloat16
                ),
                CTX,
                scatter_dimension=1,
                tiled=True,
            ).astype(jnp.float32),
        )
        grad_query_b = rotate(
            grad_query.reshape(seq_count, shard_len, local_heads, HEAD_DIM), cosine, -sine_t
        )
        grad_query_b = grad_query_b.astype(jnp.bfloat16).reshape(tok_rows, local_heads * HEAD_DIM)
        grad_key_b = rotate(
            grad_key.reshape(seq_count, shard_len, local_kv, HEAD_DIM), cosine, -sine_t
        )
        grad_key_b = grad_key_b.astype(jnp.bfloat16).reshape(tok_rows, local_kv * HEAD_DIM)
        grad_value_b = grad_value.astype(jnp.bfloat16).reshape(tok_rows, local_kv * HEAD_DIM)
        grad_normed_a = lax.psum(
            (
                jnp.einsum("rh,dh->rd", grad_query_b, w_q, preferred_element_type=jnp.float32)
                + jnp.einsum("rh,dh->rd", grad_key_b, w_k, preferred_element_type=jnp.float32)
                + jnp.einsum("rh,dh->rd", grad_value_b, w_v, preferred_element_type=jnp.float32)
            ).astype(jnp.bfloat16),
            TP,
        ).astype(jnp.float32)
        g_query = jnp.einsum(
            "rd,rh->dh", normed_a, grad_query_b, preferred_element_type=jnp.float32
        )
        g_key = jnp.einsum("rd,rh->dh", normed_a, grad_key_b, preferred_element_type=jnp.float32)
        g_value = jnp.einsum(
            "rd,rh->dh", normed_a, grad_value_b, preferred_element_type=jnp.float32
        )
        grad_from_attn_norm, g_gain_a = norm_back(stream_in, gain_a, grad_normed_a)
        grad_stream = grad_middle + grad_from_attn_norm
        grad_terms = (g_gain_a, g_query, g_key, g_value, g_out, g_gain_m, g_gate, g_up, g_down)
        shares = (
            lax.psum_scatter(grad_terms[0], (FSDP, CTX), scatter_dimension=0, tiled=True),
            lax.psum_scatter(grad_terms[1], (FSDP, CTX), scatter_dimension=0, tiled=True),
            lax.psum_scatter(grad_terms[2], (FSDP, CTX), scatter_dimension=0, tiled=True),
            lax.psum_scatter(grad_terms[3], (FSDP, CTX), scatter_dimension=0, tiled=True),
            lax.psum_scatter(grad_terms[4], (FSDP, CTX), scatter_dimension=1, tiled=True),
            lax.psum_scatter(grad_terms[5], (FSDP, CTX), scatter_dimension=0, tiled=True),
            lax.psum_scatter(grad_terms[6], (FSDP, CTX), scatter_dimension=0, tiled=True),
            lax.psum_scatter(grad_terms[7], (FSDP, CTX), scatter_dimension=0, tiled=True),
            lax.psum_scatter(grad_terms[8], (FSDP, CTX), scatter_dimension=1, tiled=True),
        )
        results[layer_no] = (
            lax.all_gather(shares[0].astype(jnp.bfloat16), CTX, axis=0, tiled=True).astype(
                jnp.float32
            ),
            lax.all_gather(shares[1].astype(jnp.bfloat16), CTX, axis=0, tiled=True).astype(
                jnp.float32
            ),
            lax.all_gather(shares[2].astype(jnp.bfloat16), CTX, axis=0, tiled=True).astype(
                jnp.float32
            ),
            lax.all_gather(shares[3].astype(jnp.bfloat16), CTX, axis=0, tiled=True).astype(
                jnp.float32
            ),
            lax.all_gather(shares[4].astype(jnp.bfloat16), CTX, axis=1, tiled=True).astype(
                jnp.float32
            ),
            lax.all_gather(shares[5].astype(jnp.bfloat16), CTX, axis=0, tiled=True).astype(
                jnp.float32
            ),
            lax.all_gather(shares[6].astype(jnp.bfloat16), CTX, axis=0, tiled=True).astype(
                jnp.float32
            ),
            lax.all_gather(shares[7].astype(jnp.bfloat16), CTX, axis=0, tiled=True).astype(
                jnp.float32
            ),
            lax.all_gather(shares[8].astype(jnp.bfloat16), CTX, axis=1, tiled=True).astype(
                jnp.float32
            ),
        )
    stacked = [
        jnp.stack([results[layer_no][member] for layer_no in range(layer_count)])
        for member in range(9)
    ]
    input_grad = grad_stream.reshape(seq_count, shard_len, model_width)
    return (
        output,
        input_grad,
        stacked[0],
        stacked[1],
        stacked[2],
        stacked[3],
        stacked[4],
        stacked[5],
        stacked[6],
        stacked[7],
        stacked[8],
        rms_stats,
    )


def partners():
    me = lax.axis_index(CTX)
    return me, me ^ 1, me ^ 2, me ^ 3


def greet(*places):
    barrier = pltpu.get_barrier_semaphore()
    for place in places:
        pl.semaphore_signal(barrier, inc=1, device_id=place, device_id_type=MESH)
    pl.semaphore_wait(barrier, len(places))


def send(src, dst, sems, slot, place):
    copy = pltpu.make_async_remote_copy(
        src_ref=src,
        dst_ref=dst,
        send_sem=sems[0].at[slot],
        recv_sem=sems[1].at[slot],
        device_id=place,
        device_id_type=MESH,
    )
    copy.start()
    return copy


def run(steps, work=()):
    for n, _ in enumerate(steps):
        if n < len(work):
            work[n]()


def gather_rows(full, sems, place, own):
    me, side_x, side_y, _ = place
    to_x, to_y = {CTX: side_x}, {CTX: side_y}
    half = full.shape[1] // 2
    top, low = pl.ds(0, half), pl.ds(half, half)
    first = [
        send(own.at[top], full.at[me, top], sems, 0, to_x),
        send(own.at[low], full.at[me, low], sems, 1, to_y),
    ]
    rest = [
        send(own.at[top], full.at[me, top], sems, 2, to_y),
        send(own.at[low], full.at[me, low], sems, 3, to_x),
    ]
    yield
    first[0].wait_recv()
    rest.append(send(full.at[side_x, top], full.at[side_x, top], sems, 4, to_y))
    first[1].wait_recv()
    rest.append(send(full.at[side_y, low], full.at[side_y, low], sems, 5, to_x))
    yield
    rest[0].wait_recv()
    rest[1].wait_recv()
    yield
    rest[2].wait_recv()
    rest[3].wait_recv()
    for copy in first + rest:
        copy.wait_send()


def dot32(a, b, dims):
    return lax.dot_general(a, b, (dims, ((), ())), preferred_element_type=jnp.float32)


def start_kernel(r):
    place = partners()
    me, side_x, side_y, across = place
    groups = (
        (FSDP, r.gains, r.all_gains, (r.gain_send, r.gain_recv)),
        (CTX, r.places, r.all_places, (r.place_send, r.place_recv)),
    )
    peers = []
    for axis, _, _, _ in groups:
        count = lax.axis_size(axis)
        peers.append([lax.rem(lax.axis_index(axis) + step, count) for step in range(1, count)])
    full = r.full
    own = pltpu.make_async_copy(r.x.at[lax.axis_index(TP)], full.at[me], r.load.at[0])
    own.start()
    greet(*[{groups[n][0]: peer} for n in range(2) for peer in peers[n]])
    copies = []
    for n, (axis, src, dst, sems) in enumerate(groups):
        mine = pltpu.make_async_copy(src, dst.at[lax.axis_index(axis)], r.load.at[1 + n])
        mine.start()
        for step, peer in enumerate(peers[n]):
            copies.append(send(src, dst.at[lax.axis_index(axis)], sems, step, {axis: peer}))
        mine.wait()
    packed = [getattr(r, f"packed_{layer}") for layer in range(r.gate.shape[0])]
    layers, units = len(packed), r.turned.shape[1]
    loads = []
    for layer in range(layers):
        cut = pl.ds(pl.multiple_of(me * units, units), units)
        for n, (src, dst) in enumerate((
            (r.gate.at[layer, :, cut], packed[layer].at[:, pl.ds(0, units)]),
            (r.up.at[layer, :, cut], packed[layer].at[:, pl.ds(units, units)]),
            (r.down.at[layer, cut], r.turned.at[layer]),
        )):
            loads.append(pltpu.make_async_copy(src, dst, r.load.at[3 + 3 * layer + n]))
    for load in loads:
        load.start()
    steps = gather_rows(full, (r.ag_send, r.ag_recv), place, r.x.at[lax.axis_index(TP)])
    next(steps)
    own.wait()
    for copy in copies:
        copy.wait()
    gain = jnp.concatenate([r.all_gains[n, 0:1, :] for n in range(lax.axis_size(FSDP))], axis=1)
    rows = full.shape[1]
    half = rows // 2
    step = 16

    def norm(top_of, low_of):
        for part_no, owner in enumerate((top_of, low_of)):
            @pl.loop(0, half // step)
            def _(i):
                here = pl.ds(pl.multiple_of(part_no * half + i * step, step), step)
                row = full[owner, here, :].astype(jnp.float32)
                inv_rms = lax.rsqrt(jnp.mean(row * row, axis=-1, keepdims=True) + epsilon)
                r.normed[owner, here, :] = (row * inv_rms * gain).astype(jnp.bfloat16)

    def mask():
        length = r.bias.shape[1]
        block = 96
        query = lax.broadcasted_iota(jnp.int32, (1, length), 1)
        firsts = [r.starts[0:1, n : n + 1] for n in range(r.starts.shape[1])]
        in_query = [jnp.where((query >= f) & (query < f + PIECE_LEN), 1, 0) for f in firsts]
        for owner in range(r.all_places.shape[0]):
            @pl.loop(0, rows // block)
            def _(i):
                here = pl.ds(pl.multiple_of(i * block, block), block)
                key = owner * rows + i * block + lax.broadcasted_iota(jnp.int32, (block, 1), 0)
                valid = r.all_places[owner, here, 1:2]
                seen = 0
                for f, row in zip(firsts, in_query):
                    seen += jnp.where((key >= f) & (key < f + PIECE_LEN), 1, 0) * row
                seen = jnp.where(key <= query, 1, seen) * valid
                seen = jnp.where(key == query, 1, seen)
                added = jnp.where(seen > 0, 0.0, neg_big).astype(jnp.bfloat16)
                keys = pl.ds(pl.multiple_of(owner * rows + i * block, block), block)
                for n in range(r.all_places.shape[0]):
                    one = added[:, n * rows : (n + 1) * rows]
                    r.bias[n, keys, :] = jnp.concatenate([one, one], axis=1)

    norm(me, me)
    mask()
    r.keep("bias")
    next(steps)
    norm(side_x, side_y)
    for load in loads:
        load.wait()
    for layer in range(layers):
        packed[layer][:, 2 * units :] = r.turned[layer].astype(jnp.float32).T.astype(jnp.bfloat16)
        r.keep(f"packed_{layer}")
    next(steps)
    norm(side_y, side_x)
    run(steps)
    norm(across, across)


def stat_steps(r, place):
    depth = lax.axis_size(FSDP)
    level = lax.axis_index(FSDP)
    others = [{FSDP: lax.rem(level + step, depth)} for step in range(1, depth)]
    here = (r.stat_send, r.stat_recv)
    layers = len(r.attn_stats)
    lane = lax.broadcasted_iota(jnp.int32, (8, 128), 1)
    tile = jnp.zeros((8, 128), jnp.float32)
    wanted = [(3 * layers, r.attn_stats[0], 2)]
    for layer in range(layers):
        wanted += [(3 * layer, r.attn_stats[layer], 1), (3 * layer + 1, r.attn_stats[layer], 0)]
        wanted.append((3 * layer + 2, r.mlp_stats[layer], 0))
    for to, ref, at in wanted:
        row = jnp.sum(ref[...], axis=0, keepdims=True)
        value = jnp.sum(jnp.where(lane[0:1] == at, row, 0.0), axis=1, keepdims=True)
        tile += jnp.where(lane == to, value, 0.0)
    width = r.width
    r.stat_sent[0, :, pl.ds(width, 128)] = tile
    r.stat_sent[0, :, pl.ds(0, width)] = jnp.zeros((8, width), jnp.float32)
    for n, ref in enumerate(r.gain_rows):
        r.stat_sent[0, n : n + 1, pl.ds(0, width)] = jnp.sum(ref[...], axis=0, keepdims=True)
    for n, peer in enumerate((sibling(), {CTX: place[1]}, {CTX: place[2]})):
        copy = send(r.stat_sent.at[n], r.stat_came.at[n], here, n, peer)
        yield
        copy.wait()
        r.stat_sent[n + 1] = r.stat_sent[n] + r.stat_came[n]
    r.stat_z[level] = r.stat_sent[3]
    copies = [send(r.stat_z.at[level], r.stat_z.at[level], here, 3 + n, peer) for n, peer in enumerate(others)]
    yield
    for copy in copies:
        copy.wait()
    part = width // depth
    here = pl.ds(pl.multiple_of(level * part, 128), part)
    gains, held = r.stat_z[0, :, here], r.stat_z[0, :, pl.ds(width, 128)]
    for n in range(1, depth):
        gains += r.stat_z[n, :, here]
        held += r.stat_z[n, :, pl.ds(width, 128)]
    r.gains[...] = gains
    count = jnp.sum(jnp.where(lane[0:1] == 3 * layers, held[0:1], 0.0), axis=1, keepdims=True)
    r.all_stats[...] = jnp.sqrt(held / (count * r.width))


def tail_kernel(width, r):
    r.width = width
    place = partners()
    me = place[0]
    depth = lax.axis_size(FSDP)
    level = lax.axis_index(FSDP)
    peers = [lax.rem(level + step, depth) for step in range(1, depth)]
    mine = pltpu.make_async_copy(r.share, r.gathered.at[me], r.load.at[0])
    mine.start()
    greet_near(place, sibling(), *[{FSDP: peer} for peer in peers])
    rows = r.share.shape[0]
    half = rows // 2
    r.gain_rows = [r.gain_rows_0, r.gain_rows_1, r.gain_rows_2, r.gain_rows_3]
    r.attn_stats = [r.attn_stats_0, r.attn_stats_1]
    r.mlp_stats = [r.mlp_stats_0, r.mlp_stats_1]
    counts = stat_steps(r, place)
    copies = []
    for part_no in range(2):
        copies.append([])
        for step, peer in enumerate(peers):
            block = r.summed.at[pl.ds(pl.multiple_of(peer * rows + part_no * half, half), half)]
            copies[part_no].append(
                send(block, r.z_came.at[part_no, level], (r.z_send, r.z_recv), part_no * depth + step, {FSDP: peer})
            )
    first = gather_rows(r.gathered, (r.ag_send, r.ag_recv), place, r.share)
    next(first)
    next(counts)
    next(first)
    next(counts)
    next(counts)
    next(counts)
    run(counts)
    step = 48
    lasts = (r.last_0, r.last_1)
    steps = []
    for part_no in range(2):
        for copy in copies[part_no]:
            copy.wait_recv()

        @pl.loop(0, half // step)
        def _(i):
            here = pl.ds(pl.multiple_of(i * step, step), step)
            start = pl.multiple_of(level * rows + part_no * half + i * step, step)
            total = r.summed[pl.ds(start, step), :].astype(jnp.float32)
            for peer in peers:
                total += r.z_came[part_no, peer, here, :].astype(jnp.float32)
            lasts[part_no][me, here, :] = total.astype(jnp.bfloat16)

        steps.append(gather_rows(lasts[part_no], ((r.l0_send, r.l0_recv), (r.l1_send, r.l1_recv))[part_no], place, lasts[part_no].at[me]))
        next(steps[part_no])
        if part_no == 0:
            next(steps[0])
    run(first)
    mine.wait()
    r.keep("gathered")
    run(steps[0])
    run(steps[1])
    for copy in copies[0] + copies[1]:
        copy.wait_send()


class Scatter:
    def __init__(self, part, buffers, sems, place):
        self.part, self.sems, self.place = part, sems, place
        self.from_x, self.from_y, self.passed, self.last = buffers
        self.half = part.shape[1] // 2
        self.copies = {}

    def send(self, slot, src, dst, axis_peer):
        self.copies[slot] = send(src, dst, self.sems, slot, {CTX: axis_peer})

    def across(self):
        _, side_x, side_y, far = self.place
        self.send(0, self.part.at[far, pl.ds(0, self.half)], self.from_x.at[1], side_x)
        self.send(1, self.part.at[far, pl.ds(self.half, self.half)], self.from_y.at[1], side_y)

    def x_out(self, some=None):
        side_x = self.place[1]
        slot, rows = self.cut(some)
        self.send(slot, self.part.at[side_x, rows], self.from_x.at[0, rows], side_x)

    def y_out(self, some=None):
        side_y = self.place[2]
        slot, rows = self.cut(some)
        below = pl.ds(self.half + rows.start, rows.size)
        self.send(slot + 1, self.part.at[side_y, below], self.from_y.at[0, rows], side_y)

    def cut(self, some):
        if some is None:
            return 2, pl.ds(0, self.half)
        first = self.half // 48 * 16
        return (2, pl.ds(0, first)) if some == 0 else (6, pl.ds(first, self.half - first))

    def add_to(self, slot, owner, start, came):
        step = 16

        @pl.loop(0, self.half // step)
        def _(i):
            rows = pl.ds(pl.multiple_of(i * step, step), step)
            mine = self.part[owner, pl.ds(pl.multiple_of(start + i * step, step), step), :]
            total = mine.astype(jnp.float32) + came[1, rows, :].astype(jnp.float32)
            self.passed[slot, rows, :] = total.astype(self.passed.dtype)

    def forward(self):
        _, side_x, side_y, _ = self.place
        self.copies[0].wait_recv()
        self.add_to(0, side_y, 0, self.from_x)
        self.send(4, self.passed.at[0], self.last.at[0], side_y)
        self.copies[1].wait_recv()
        self.add_to(1, side_x, self.half, self.from_y)
        self.send(5, self.passed.at[1], self.last.at[1], side_x)

    def finish(self):
        for slot in self.copies:
            if slot > 1:
                self.copies[slot].wait_recv()
        for slot in self.copies:
            self.copies[slot].wait_send()

    def each_row(self, work, step=16):
        me = self.place[0]
        for side in range(2):
            came = self.from_x if side == 0 else self.from_y

            @pl.loop(0, self.half // step)
            def _(i):
                rows = pl.ds(pl.multiple_of(i * step, step), step)
                whole = pl.ds(pl.multiple_of(side * self.half + i * step, step), step)
                total = self.part[me, whole, :].astype(jnp.float32)
                total += came[0, rows, :].astype(jnp.float32)
                work(whole, total + self.last[side, rows, :].astype(jnp.float32))


def scatter_steps(scatter):
    scatter.across()
    scatter.x_out()
    scatter.y_out()
    yield
    scatter.forward()
    yield
    scatter.finish()


class WeightGrads:
    def __init__(self, lefts, rights, sent, came, summed, sems):
        self.lefts, self.rights, self.sent, self.came, self.summed, self.sems = lefts, rights, sent, came, summed, sems
        self.sizes = [r.shape[-1] for r in rights]
        self.side = lax.axis_index(TP)
        self.copies = []

    def product(self, p, t, put):
        block = 256
        left, right = self.lefts[p], self.rights[p]
        width = left.shape[-1]

        @pl.loop(0, width // block)
        def _(i):
            cols = pl.ds(pl.multiple_of(i * block, block), block)
            one = left[:, :, cols].reshape(-1, block)
            put(cols, dot32(one, right[t].reshape(one.shape[0], -1), ((0,), (0,))).astype(jnp.bfloat16))

    def theirs(self, p):
        def put(rows, value):
            self.sent[p][rows, : self.sizes[p]] = value

        self.product(p, 1 - self.side, put)
        self.copies.append(send(self.sent[p], self.came[p], self.sems, p, {TP: 1 - self.side}))

    def cols(self, p):
        start = sum(self.sizes[:p])
        return slice(start, start + self.sizes[p])

    def ours(self, p):
        def put(rows, value):
            self.summed[rows, self.cols(p)] = value

        self.product(p, self.side, put)

    def add_up(self):
        step = 64
        for p, copy in enumerate(self.copies):
            copy.wait_recv()

            @pl.loop(0, self.summed.shape[0] // step)
            def _(i):
                rows = pl.ds(pl.multiple_of(i * step, step), step)
                total = self.summed[rows, self.cols(p)].astype(jnp.float32) + self.came[p][rows, : self.sizes[p]].astype(jnp.float32)
                self.summed[rows, self.cols(p)] = total.astype(jnp.bfloat16)

    def close(self):
        for copy in self.copies:
            copy.wait_send()


def add_stats(stats, valid, *values):
    lane = lax.broadcasted_iota(jnp.int32, stats.shape, 1)
    total = stats[...] + jnp.where(lane == 2, valid, 0.0)
    for n, value in enumerate(values):
        total += jnp.where(lane == n, valid * jnp.sum(value * value, axis=-1, keepdims=True), 0.0)
    stats[...] = total


def norm_sum(scatter, stream, gain, valid, middle, normed, stats):
    stats[...] = jnp.zeros_like(stats)

    def work(rows, branch):
        before = stream[rows, :].astype(jnp.float32)
        total = before + branch
        middle[rows, :] = total
        inv_rms = lax.rsqrt(jnp.mean(total * total, axis=-1, keepdims=True) + epsilon)
        normed[rows, :] = (total * inv_rms * gain[...]).astype(normed.dtype)
        add_stats(stats, valid[rows, :], branch, before)

    scatter.each_row(work)


def norm_sum_back(scatter, stream, gain, grad, gain_rows, put):
    gain_rows[...] = jnp.zeros_like(gain_rows)

    def work(rows, got):
        x = stream[rows, :].astype(jnp.float32)
        inv_rms = lax.rsqrt(jnp.mean(x * x, axis=-1, keepdims=True) + epsilon)
        scaled = gain[...] * got
        along = jnp.mean(scaled * x, axis=-1, keepdims=True)
        put(rows, grad[rows, :].astype(jnp.float32) + inv_rms * scaled - x * (inv_rms * inv_rms * inv_rms * along))
        gain_rows[...] += got * x * inv_rms

    scatter.each_row(work)


def rows_of(ref, lead, top_of, low_of):
    half = ref.shape[-2] // 2
    return jnp.concatenate([ref[(*lead, top_of, pl.ds(0, half))], ref[(*lead, low_of, pl.ds(half, half))]], axis=0)


def put_rows(ref, lead, top_of, low_of, value):
    half = ref.shape[-2] // 2
    ref[(*lead, top_of, pl.ds(0, half))] = value[:half].astype(ref.dtype)
    ref[(*lead, low_of, pl.ds(half, half))] = value[half:].astype(ref.dtype)


def greet_near(place, *more):
    greet({CTX: place[1]}, {CTX: place[2]}, *more)


def sibling():
    return {TP: 1 - lax.axis_index(TP)}


def mlp_rows(r, top_of, low_of, back):
    units = r.hidden.shape[-1]
    x = rows_of(r.full, (), top_of, low_of)
    total, g_total = 0.0, 0.0
    for t in range(r.weights.shape[0]):
        gate_act = dot32(x, r.weights[t, :, :units], ((1,), (0,)))
        up_act = dot32(x, r.weights[t, :, units : 2 * units], ((1,), (0,)))
        sig = jax.nn.sigmoid(gate_act)
        unit = (gate_act * sig * up_act).astype(jnp.bfloat16)
        put_rows(r.hidden, (t,), top_of, low_of, unit)
        total += dot32(unit, r.weights[t, :, 2 * units :], ((1,), (1,)))
        if back:
            g_total += mlp_back_rows(r, rows_of(r.grad_all, (), top_of, low_of), t, top_of, low_of, gate_act, up_act, sig)
        else:
            put_rows(r.gate, (t,), top_of, low_of, gate_act)
            put_rows(r.up, (t,), top_of, low_of, up_act)
    put_rows(r.part_out if back else r.part, (), top_of, low_of, total)
    if back:
        put_rows(r.part, (), top_of, low_of, g_total)


def mlp_back_rows(r, grad, t, top_of, low_of, gate_act, up_act, sig):
    units = r.grad_gate.shape[-1]
    g_hidden = dot32(grad, r.weights[t, :, 2 * units :], ((1,), (0,)))
    g_gate = (g_hidden * up_act * sig * (1.0 + gate_act * (1.0 - sig))).astype(jnp.bfloat16)
    g_up = (g_hidden * gate_act * sig).astype(jnp.bfloat16)
    put_rows(r.grad_gate, (t,), top_of, low_of, g_gate)
    put_rows(r.grad_up, (t,), top_of, low_of, g_up)
    total = dot32(g_gate, r.weights[t, :, :units], ((1,), (1,)))
    return total + dot32(g_up, r.weights[t, :, units : 2 * units], ((1,), (1,)))


def gathered_work(r, place, scatter, work, rows_own, own, cut=True):
    me, side_x, side_y, across = place
    steps = gather_rows(r.full, (r.ag_send, r.ag_recv), place, rows_own)
    next(steps)
    own.wait()
    work(me, me)
    next(steps)
    work(side_x, side_y)
    next(steps)
    work(side_y, side_x)
    scatter.x_out(0 if cut else None)
    scatter.y_out(0 if cut else None)
    run(steps)
    work(across, across)
    scatter.across()
    if cut:
        scatter.x_out(1)
        scatter.y_out(1)


def mlp_kernel(r):
    place = partners()
    me = place[0]
    own = pltpu.make_async_copy(r.normed, r.full.at[me], r.load.at[0])
    own.start()
    greet_near(place)
    scatter = Scatter(r.part, (r.from_x, r.from_y, r.passed, r.last), (r.rs_send, r.rs_recv), place)

    def work(top_of, low_of):
        r.need("weights")
        mlp_rows(r, top_of, low_of, False)

    gathered_work(r, place, scatter, work, r.normed, own)
    r.keep("full", "hidden", "gate", "up")
    scatter.forward()
    scatter.finish()
    r.need("middle")
    norm_sum(scatter, r.middle, r.gain, r.valid, r.stream, r.normed_next, r.stats)


def mlp_back_kernel(both, r):
    place = partners()
    me = place[0]
    own = pltpu.make_async_copy(r.rows_own, r.full.at[me], r.load.at[0])
    own.start()
    greet_near(place, sibling())
    scatter = Scatter(r.part, (r.from_x, r.from_y, r.passed, r.last), (r.rs_send, r.rs_recv), place)

    def both_rows(top_of, low_of):
        r.need("weights", "grad_all")
        mlp_rows(r, top_of, low_of, True)

    def back_rows(top_of, low_of):
        r.need("weights", "grad_gate", "grad_up")
        total = 0.0
        grad = rows_of(r.full, (), top_of, low_of)
        for t in range(r.weights.shape[0]):
            gate_act = rows_of(r.grad_gate, (t,), top_of, low_of).astype(jnp.float32)
            up_act = rows_of(r.grad_up, (t,), top_of, low_of).astype(jnp.float32)
            total += mlp_back_rows(r, grad, t, top_of, low_of, gate_act, up_act, jax.nn.sigmoid(gate_act))
        put_rows(r.part, (), top_of, low_of, total)

    gathered_work(r, place, scatter, both_rows if both else back_rows, r.rows_own, own, not both)
    if both:
        r.keep("part_out")
        job = None
    else:
        job = gather_part(r.share, 0, r.gathered, r.load.at[1], r.ja_send, r.ja_recv, place)
        next(job)
    normed, grad = (r.full, r.grad_all) if both else (r.normed, r.full)
    r.need("normed", "hidden")
    units = r.hidden.shape[-1]
    sent = [r.weights.at[0, :, pl.ds(p * units, units)] for p in range(3)]
    sums = WeightGrads(
        [normed, normed, grad], [r.grad_gate, r.grad_up, r.hidden], sent, [r.came_0, r.came_1, r.came_2],
        r.summed, (r.tp_send, r.tp_recv),
    )
    sums.theirs(0)
    sums.theirs(1)
    scatter.forward()
    sums.theirs(2)
    sums.ours(0)
    if job:
        next(job)
    sums.ours(1)
    sums.ours(2)
    sums.add_up()
    r.keep("summed")
    scatter.finish()
    r.need("middle", "grad")

    def put(rows, total):
        r.grad_new[rows, :] = total
        r.grad_rows[rows, :] = total.astype(r.grad_rows.dtype)

    norm_sum_back(scatter, r.middle, r.gain, r.grad, r.gain_rows, put)
    if job:
        run(job)
        r.keep("gathered")
    sums.close()


LOG2E = 1.4426950408889634


def turn(x, cos_row, sin_row):
    half_dim = HEAD_DIM // 2
    swapped = jnp.concatenate([x[:, half_dim:], x[:, :half_dim]], axis=1)
    return x * cos_row + swapped * sin_row


def project_rows(r, full, top_of, low_of):
    cols_q, base = 2 * HEAD_DIM, 4 * HEAD_DIM
    x = rows_of(full, (), top_of, low_of)
    cos_b, sin_b = rows_of(r.cosine, (), top_of, low_of), rows_of(r.sine, (), top_of, low_of)
    for t in range(r.weights.shape[0]):
        flat = dot32(x, r.weights[t, :, :base], ((1,), (0,)))
        for g in range(2):
            put_rows(r.query, (t, g), top_of, low_of, turn(flat[:, g * HEAD_DIM : (g + 1) * HEAD_DIM], cos_b, sin_b))
        put_rows(r.key, (t,), top_of, low_of, turn(flat[:, cols_q : cols_q + HEAD_DIM], cos_b, sin_b))
        put_rows(r.value, (t,), top_of, low_of, flat[:, cols_q + HEAD_DIM : base])


def attend_rows(r, owner):
    base = 4 * HEAD_DIM
    pairs, _, rows, _ = r.key.shape
    factor = HEAD_DIM ** (-0.5) * LOG2E

    for t in range(pairs):
        key = r.key[t].reshape(-1, HEAD_DIM)
        value = r.value[t].reshape(-1, HEAD_DIM)
        query = jnp.concatenate([r.query[t, 0, owner], r.query[t, 1, owner]], axis=0)
        raw = dot32(key, query, ((1,), (1,)))
        raw = raw * factor + r.bias[owner].astype(jnp.float32)
        top = jnp.max(raw, axis=0, keepdims=True)
        probs = jnp.exp2(raw - top)
        total = jnp.sum(probs, axis=0, keepdims=True)
        out = dot32(value, probs.astype(jnp.bfloat16), ((0,), (0,))) * (1.0 / total)
        fill = -out.shape[1] % 128
        out = jnp.concatenate([out, jnp.zeros((HEAD_DIM, fill), jnp.float32)], axis=1).T.astype(jnp.bfloat16)
        r.lse[t, owner] = top + jnp.log2(total)
        for g in range(2):
            r.mixed[t, owner, :, g * HEAD_DIM : (g + 1) * HEAD_DIM] = out[g * rows : (g + 1) * rows]

    total = 0.0
    for t in range(pairs):
        total += dot32(r.mixed[t, owner], r.weights[t, :, base : base + 2 * HEAD_DIM], ((1,), (1,)))
    r.part[owner] = total.astype(r.part.dtype)


def attend_kernel(first, r):
    place = partners()
    me, side_x, side_y, across = place
    rows_own = r.share.at[lax.axis_index(TP)] if first else r.normed
    own = pltpu.make_async_copy(rows_own, r.full.at[me], r.load.at[0])
    own.start()
    greet_near(place)
    steps = gather_rows(r.full, (r.ag_send, r.ag_recv), place, rows_own)
    next(steps)
    own.wait()
    rows = r.normed if first else r.full
    r.need("weights", "cosine", "sine", "normed")
    if first:
        for owner in range(4):
            project_rows(r, rows, owner, owner)
    else:
        project_rows(r, rows, me, me)
        next(steps)
        project_rows(r, rows, side_x, side_y)
        next(steps)
        project_rows(r, rows, side_y, side_x)
        run(steps)
        project_rows(r, rows, across, across)
        r.keep("full")
    r.keep("query", "key", "value")
    scatter = Scatter(r.part, (r.from_x, r.from_y, r.passed, r.last), (r.rs_send, r.rs_recv), place)
    r.need("bias")
    attend_rows(r, across)
    scatter.across()
    if first:
        next(steps)
    attend_rows(r, side_x)
    scatter.x_out()
    attend_rows(r, side_y)
    scatter.y_out()
    scatter.forward()
    attend_rows(r, me)
    r.keep("lse", "mixed")
    if first:
        run(steps)
        r.keep("full")
    scatter.finish()
    r.need("stream")
    norm_sum(scatter, r.stream, r.gain, r.valid, r.middle, r.normed_next, r.stats)


def attend_back_kernel(last, r):
    place = partners()
    me, side_x, side_y, across = place
    own = pltpu.make_async_copy(r.rows_own, r.full.at[me], r.load.at[0])
    own.start()
    greet_near(place, sibling())
    cols_q, base = 2 * HEAD_DIM, 4 * HEAD_DIM
    pairs = r.weights.shape[0]
    rows = r.full.shape[1]
    scale = HEAD_DIM ** (-0.5)
    factor = scale * LOG2E
    order = (me, side_x, side_y, across)
    masks = [pltpu.make_async_copy(r.bias_in.at[owner], r.bias.at[n % 2], r.bias_load.at[n]) for n, owner in enumerate(order)]
    masks[0].start()
    masks[1].start()
    r.g_key[...] = jnp.zeros_like(r.g_key)
    r.g_value[...] = jnp.zeros_like(r.g_value)

    def project(top_of, low_of):
        r.need("weights")
        x = rows_of(r.full, (), top_of, low_of)
        for t in range(pairs):
            flat = dot32(x, r.weights[t, :, base : base + cols_q], ((1,), (0,)))
            for g in range(2):
                put_rows(r.heads, (t, g), top_of, low_of, flat[:, g * HEAD_DIM : (g + 1) * HEAD_DIM])

    def two(ref, t, owner):
        return jnp.concatenate([ref[t, 0, owner], ref[t, 1, owner]], axis=0)

    def queries_back(n):
        owner = order[n]
        masks[n].wait()
        for t in range(pairs):
            query, heads = two(r.query, t, owner), two(r.heads, t, owner)
            mixed = r.mixed[t, owner].astype(jnp.float32)
            mixed = jnp.concatenate([mixed[:, :HEAD_DIM], mixed[:, HEAD_DIM:]], axis=0)
            along = lax.dot_general(
                jnp.ones((8, HEAD_DIM), jnp.float32), heads.astype(jnp.float32) * mixed, (((1,), (1,)), ((), ())),
                precision=lax.Precision.HIGHEST, preferred_element_type=jnp.float32,
            )[0:1]
            lse = r.lse[t, owner]
            r.g_query[...] = jnp.zeros_like(r.g_query)

            @pl.loop(0, jnp.minimum(owner + 2, 4))
            def _(kept):
                here = pl.ds(pl.multiple_of(kept * rows, 16), rows)
                key, value = r.key[t, kept], r.value[t, kept]
                raw = dot32(key, query, ((1,), (1,)))
                probs = jnp.exp2(raw * factor + r.bias[n % 2, here, :].astype(jnp.float32) - lse)
                g_probs = dot32(value, heads, ((1,), (1,)))
                g_scores = (probs * (g_probs - along)).astype(jnp.bfloat16)
                r.g_value[t, kept] += dot32(probs.astype(jnp.bfloat16), heads, ((1,), (0,)))
                r.g_key[t, kept] += dot32(g_scores, query, ((1,), (0,)))
                r.g_query[...] += dot32(key, g_scores, ((0,), (0,)))

            fill = jnp.zeros((HEAD_DIM, -2 * rows % 128), jnp.float32)
            g_query = jnp.concatenate([r.g_query[...], fill], axis=1).T * scale
            for g in range(2):
                r.grad_qkv[t, owner, :, g * HEAD_DIM : (g + 1) * HEAD_DIM] = turn(
                    g_query[g * rows : (g + 1) * rows], r.cosine[owner], -r.sine[owner]
                ).astype(jnp.bfloat16)
        if n + 2 < 4:
            masks[n + 2].start()

    steps = gather_rows(r.full, (r.ag_send, r.ag_recv), place, r.rows_own)
    next(steps)
    own.wait()
    project(me, me)
    r.need("key", "value", "query", "lse", "mixed", "cosine", "sine")
    queries_back(0)
    next(steps)
    jobs = [
        gather_part(r.share_a, 1, r.gathered_a, r.load.at[1], r.ja_send, r.ja_recv, place),
        gather_part(r.share_b, None, r.gathered_b, r.load.at[2], r.jb_send, r.jb_recv, place),
    ] if last else [end_steps(r, place)]
    for job in jobs:
        next(job)
    project(side_x, side_y)
    next(steps)
    project(side_y, side_x)
    queries_back(1)
    queries_back(2)
    run(steps)
    project(across, across)
    queries_back(3)

    @pl.loop(0, 4)
    def _(owner):
        for t in range(pairs):
            r.grad_qkv[t, owner, :, cols_q : cols_q + HEAD_DIM] = turn(
                r.g_key[t, owner] * scale, r.cosine[owner], -r.sine[owner]
            ).astype(jnp.bfloat16)
            r.grad_qkv[t, owner, :, cols_q + HEAD_DIM :] = r.g_value[t, owner].astype(jnp.bfloat16)

    def branch(owner):
        total = 0.0
        for t in range(pairs):
            total += dot32(r.grad_qkv[t, owner], r.weights[t, :, :base], ((1,), (1,)))
        r.part[owner] = total.astype(r.part.dtype)

    scatter = Scatter(r.part, (r.from_x, r.from_y, r.passed, r.last), (r.rs_send, r.rs_recv), place)
    branch(across)
    scatter.across()
    branch(side_x)
    scatter.x_out()
    branch(side_y)
    scatter.y_out()
    branch(me)
    r.need("normed")
    sums = WeightGrads(
        [r.normed, r.full], [r.grad_qkv, r.mixed],
        [r.weights.at[0, :, pl.ds(0, base)], r.weights.at[1, :, pl.ds(0, r.came_1.shape[1])]], [r.came_0, r.came_1],
        r.summed, (r.tp_send, r.tp_recv),
    )
    sums.theirs(0)
    for job in jobs:
        next(job)
    scatter.forward()
    sums.theirs(1)
    sums.ours(0)
    sums.ours(1)
    r.summed[:, base + cols_q :] = jnp.zeros((r.summed.shape[0], r.summed.shape[1] - base - cols_q), jnp.bfloat16)
    sums.add_up()
    r.keep("summed")
    scatter.finish()
    r.need("stream", "grad")
    side = lax.axis_index(TP)

    def put(here, total):
        if last:
            r.grad_new[side, here, :] = total
        else:
            r.grad_new[here, :] = total
            r.grad_rows[here, :] = total.astype(r.grad_rows.dtype)

    norm_sum_back(scatter, r.stream, r.gain, r.grad, r.gain_rows, put)
    handed = []
    if last:
        handed.append(send(r.grad_new.at[side], r.grad_new.at[side], (r.tp_send, r.tp_recv), 2, sibling()))
    for job in jobs:
        run(job)
    if last:
        r.keep("gathered_a", "gathered_b")
    else:
        r.keep("out")
    for copy in handed:
        copy.wait()
    sums.close()


def end_steps(r, place):
    side = lax.axis_index(TP)
    r.need("end_part")
    scatter = Scatter(
        r.end_part, (r.end_from_x, r.end_from_y, r.end_passed, r.end_last), (r.end_send, r.end_recv), place
    )
    yield from scatter_steps(scatter)

    r.stats[...] = jnp.zeros_like(r.stats)

    def work(rows, branch):
        r.out[side, rows, :] = (r.end_middle[rows, :] + branch).astype(r.out.dtype)
        add_stats(r.stats, r.valid[rows, :], branch)

    r.need("end_middle")
    scatter.each_row(work)
    send(r.out.at[side], r.out.at[side], (r.out_send, r.out_recv), 0, sibling()).wait()


def gather_part(share, part_no, full, local_sem, send_sems, recv_sems, place):
    rows = full.shape[1]
    src = share if part_no is None else share.at[pl.ds(part_no * rows, rows)]
    copy = pltpu.make_async_copy(src, full.at[place[0]], local_sem)
    copy.start()
    yield from gather_rows(full, (send_sems, recv_sems), place, src)
    copy.wait()


class Refs:
    def need(self, *names):
        for name in names:
            if name in self.loads:
                self.loads.pop(name).wait()

    def keep(self, *names):
        for name in names:
            src, dst, sem = self.late[name]
            store = pltpu.make_async_copy(src, dst, sem)
            store.start()
            self.stores.append(store)


def linked(kernel, number, micros, near, far, lazy, outs, late, scratch):
    names = [*near, *far, *lazy, *outs, *late, *scratch]
    halves = [name for name, value in lazy.items() if isinstance(value, tuple)]
    lazy = {name: value[0] if name in halves else value for name, value in lazy.items()}
    lazy_rooms = [pltpu.VMEM(v.shape[1:] if name in halves else v.shape, v.dtype) for name, v in lazy.items()]
    lazy_names, late_names = list(lazy), list(late)

    def body(*refs):
        r = Refs()
        count = len(names)
        rest = list(refs[count:])
        by_name = dict(zip(names, refs))
        r.loads, r.late, r.stores = {}, {}, []
        held = rest[: len(lazy) + len(late)]
        for n, name in enumerate(lazy_names):
            src = by_name[name].at[lax.axis_index(TP)] if name in halves else by_name[name]
            r.loads[name] = pltpu.make_async_copy(src, held[n], rest[-2].at[n])
            by_name[name] = held[n]
        for n, name in enumerate(late_names):
            r.late[name] = (held[len(lazy) + n], by_name[name], rest[-1].at[n])
            by_name[name] = held[len(lazy) + n]
        for name, ref in by_name.items():
            setattr(r, name, ref)
        for load in r.loads.values():
            load.start()
        kernel(r)
        r.need(*lazy_names)
        for store in r.stores:
            store.wait()

    vmem = pl.BlockSpec(memory_space=pltpu.VMEM)
    hbm = pl.BlockSpec(memory_space=pl.ANY)
    came = pl.pallas_call(
        body,
        out_shape=[*outs.values(), *late.values()],
        in_specs=[vmem] * len(near) + [hbm] * (len(far) + len(lazy)),
        out_specs=[vmem] * len(outs) + [hbm] * len(late),
        scratch_shapes=[
            *scratch.values(), *lazy_rooms, *map(room, late.values()),
            pltpu.SemaphoreType.DMA((max(1, len(lazy)),)), pltpu.SemaphoreType.DMA((max(1, len(late)),)),
        ],
        compiler_params=pltpu.CompilerParams(
            collective_id=number, has_side_effects=True, vmem_limit_bytes=61 << 20
        ),
        cost_estimate=pl.CostEstimate(flops=0, bytes_accessed=int(micros * 3.6e6), transcendentals=0),
    )(*near.values(), *far.values(), *lazy.values())
    result = Refs()
    for name, value in zip([*outs, *late], came):
        setattr(result, name, value)
    return result


def sems(name, count):
    return {f"{name}_send": pltpu.SemaphoreType.DMA((count,)), f"{name}_recv": pltpu.SemaphoreType.DMA((count,))}


def sum_room(rows, width, prefix=""):
    names = ("from_x", "from_y", "passed", "last")
    return {prefix + name: pltpu.VMEM((2, rows // 2, width), jnp.bfloat16) for name in names}


def shape16(*dims):
    return jax.ShapeDtypeStruct(dims, jnp.bfloat16)


def shape32(*dims):
    return jax.ShapeDtypeStruct(dims, jnp.float32)


def room(like):
    return pltpu.VMEM(like.shape, like.dtype)


def mlp_step(normed, middle, gain, valid, weights):
    rows, width = middle.shape
    pairs, units = weights.shape[0], weights.shape[2] // 3
    kept = shape16(pairs, 4, rows, units)
    return linked(
        mlp_kernel, 12, 75,
        dict(gain=gain, valid=valid), dict(normed=normed), dict(weights=weights, middle=middle),
        dict(stream=shape32(rows, width), normed_next=shape16(rows, width), stats=shape32(16, 128)),
        dict(full=shape16(4, rows, width), hidden=kept, gate=kept, up=kept),
        dict(
            part=pltpu.VMEM((4, rows, width), jnp.bfloat16), load=pltpu.SemaphoreType.DMA((1,)),
            **sum_room(rows, width), **sems("ag", 6), **sems("rs", 8),
        ),
    )


def mlp_back_step(rows_own, middle, gain, grad, weights, grad_all=None, kept=None, share=None):
    rows, width = middle.shape
    pairs, units = weights.shape[0], weights.shape[2] // 3
    both = grad_all is not None
    whole, unit = shape16(4, rows, width), shape16(pairs, 4, rows, units)
    far = dict(rows_own=rows_own)
    lazy = dict(weights=weights)
    late = dict(summed=shape16(width, 3 * units))
    scratch = dict(
        full=room(whole), part=room(whole), load=pltpu.SemaphoreType.DMA((2,)),
        **{f"came_{p}": pltpu.VMEM((width, units), jnp.bfloat16) for p in range(3)},
        **sum_room(rows, width), **sems("ag", 6), **sems("rs", 8), **sems(TP, 3),
    )
    if both:
        lazy["grad_all"] = grad_all
        late["part_out"] = whole
        scratch.update(grad_gate=room(unit), grad_up=room(unit), hidden=room(unit))
    else:
        far["share"] = share
        lazy.update(grad_gate=kept.gate, grad_up=kept.up, hidden=kept.hidden, normed=kept.full)
        late["gathered"] = shape16(4, share.shape[0] // 2, share.shape[1])
        scratch.update(**sems("ja", 6))
    lazy.update(middle=middle, grad=grad)
    return linked(
        functools.partial(mlp_back_kernel, both), 13 if both else 5, 85,
        dict(gain=gain), far, lazy,
        dict(grad_new=shape32(rows, width), grad_rows=shape16(rows, width), gain_rows=shape32(16, width)),
        late, scratch,
    )


def attend_step(normed, stream, gain, valid, weights, cosine, sine, bias, share=None):
    first = share is not None
    rows, width = stream[0].shape[1:] if first else stream.shape
    pairs = weights.shape[0]
    far, lazy = {}, dict(weights=weights, cosine=cosine, sine=sine)
    if first:
        far["share"] = share
        lazy["normed"] = normed
    else:
        far["normed"] = normed
    lazy.update(bias=bias, stream=stream)
    return linked(
        functools.partial(attend_kernel, first), 11 if first else 9, 75,
        dict(gain=gain, valid=valid), far, lazy,
        dict(middle=shape32(rows, width), normed_next=shape16(rows, width), stats=shape32(16, 128)),
        dict(
            full=shape16(4, rows, width), query=shape16(pairs, 2, 4, rows, HEAD_DIM),
            key=shape16(pairs, 4, rows, HEAD_DIM), value=shape16(pairs, 4, rows, HEAD_DIM),
            lse=shape32(pairs, 4, 1, 2 * rows), mixed=shape16(pairs, 4, rows, 2 * HEAD_DIM),
        ),
        dict(
            part=pltpu.VMEM((4, rows, width), jnp.bfloat16), load=pltpu.SemaphoreType.DMA((1,)),
            **sum_room(rows, width), **sems("ag", 6), **sems("rs", 8),
        ),
    )


def attend_back_step(
    rows_own, stream, gain, grad, weights, cosine, sine, bias, kept, normed, shares=None, end=None
):
    rows, width = rows_own.shape
    pairs = weights.shape[0]
    length = 4 * rows
    last = shares is not None
    whole = shape16(4, rows, width)
    near = dict(gain=gain)
    far = dict(rows_own=rows_own, bias_in=bias)
    lazy = dict(
        weights=weights, key=kept.key, value=kept.value, query=kept.query, lse=kept.lse, mixed=kept.mixed,
        cosine=cosine, sine=sine, normed=normed, stream=stream, grad=grad,
    )
    sizes = (4 * HEAD_DIM, 2 * HEAD_DIM)
    total = sum(sizes) + 64
    outs = dict(gain_rows=shape32(16, width))
    late = dict(summed=shape16(width, total))
    scratch = dict(
        full=room(whole), part=room(whole),
        heads=room(kept.query), g_key=pltpu.VMEM(kept.key.shape, jnp.float32),
        g_value=pltpu.VMEM(kept.key.shape, jnp.float32), g_query=pltpu.VMEM((HEAD_DIM, 2 * rows), jnp.float32),
        grad_qkv=pltpu.VMEM((pairs, 4, rows, sizes[0]), jnp.bfloat16),
        bias=pltpu.VMEM((2, length, 2 * rows), jnp.bfloat16), bias_load=pltpu.SemaphoreType.DMA((4,)),
        came_0=pltpu.VMEM((width, sizes[0]), jnp.bfloat16), came_1=pltpu.VMEM((width, 256), jnp.bfloat16),
        load=pltpu.SemaphoreType.DMA((3,)),
        **sum_room(rows, width), **sems("ag", 6), **sems("rs", 8), **sems(TP, 4),
    )
    if last:
        far.update(share_a=shares[0], share_b=shares[1])
        outs.update(grad_new=shape32(2, rows, width))
        late.update(
            gathered_a=shape16(4, shares[0].shape[0] // 2, shares[0].shape[1]),
            gathered_b=shape16(4, *shares[1].shape),
        )
        scratch.update(**sems("ja", 6), **sems("jb", 6))
    else:
        lazy = dict(end_part=end[0], **lazy, end_middle=end[1])
        near["valid"] = end[2]
        outs.update(grad_new=shape32(rows, width), grad_rows=shape16(rows, width), stats=shape32(16, 128))
        late["out"] = shape16(2, rows, width)
        scratch.update(**sum_room(rows, width, "end_"), **sems("end", 6), **sems("out", 1))
    return linked(
        functools.partial(attend_back_kernel, last), 7 if last else 6, 100, near, far, lazy, outs, late, scratch,
    )


def tail_step(summed, share, attn_stats, mlp_stats, gain_rows):
    depth = lax.axis_size(FSDP)
    half, cols = share.shape[0] // 2, summed.shape[1]
    last = shape16(4, half, cols)
    wide = summed.shape[0] + 128
    return linked(
        functools.partial(tail_kernel, summed.shape[0]), 10, 60,
        dict(
            summed=summed,
            **{f"attn_stats_{layer}": a for layer, a in enumerate(attn_stats)},
            **{f"mlp_stats_{layer}": a for layer, a in enumerate(mlp_stats)},
            **{f"gain_rows_{n}": a for n, a in enumerate(gain_rows)},
        ),
        dict(share=share), {},
        dict(last_0=last, last_1=last, all_stats=shape32(8, 128), gains=shape32(8, summed.shape[0] // depth)), dict(gathered=shape16(4, *share.shape)),
        dict(
            z_came=pltpu.VMEM((2, depth, half, cols), jnp.bfloat16), stat_sent=pltpu.VMEM((4, 8, wide), jnp.float32),
            stat_came=pltpu.VMEM((3, 8, wide), jnp.float32), stat_z=pltpu.VMEM((depth, 8, wide), jnp.float32),
            load=pltpu.SemaphoreType.DMA((1,)), **sems("z", 2 * depth), **sems("ag", 6), **sems("stat", 3 + depth),
            **sems("l0", 6), **sems("l1", 6),
        ),
    )


def start_step(gains, places, starts, x, gate, up, down):
    depth, across = lax.axis_size(FSDP), lax.axis_size(CTX)
    layers, rows = gate.shape[:2]
    units = gate.shape[2] // across
    own = x.shape[1:]
    length = across * own[0]
    return linked(
        start_kernel, 8, 38,
        dict(gains=gains, places=places, starts=starts), dict(x=x, gate=gate, up=up, down=down), {},
        dict(
            all_gains=jax.ShapeDtypeStruct((depth, *gains.shape), gains.dtype),
            all_places=jax.ShapeDtypeStruct((across, *places.shape), places.dtype),
            normed=shape16(across, *own),
        ),
        dict(
            bias=shape16(across, length, 2 * own[0]),
            **{f"packed_{layer}": shape16(rows, 3 * units) for layer in range(layers)},
        ),
        dict(
            full=pltpu.VMEM((across, *own), jnp.bfloat16), turned=pltpu.VMEM((layers, units, rows), jnp.bfloat16),
            load=pltpu.SemaphoreType.DMA((3 + 3 * layers,)), **sems("gain", depth), **sems("place", across),
            **sems("ag", 6),
        ),
    )


def planned(
    tokens, positions, valid, piece_starts, d_out,
    attn_gain, w_query, w_key, w_value, w_out, mlp_gain, w_gate, w_up, w_down,
):
    seq_count, rows, width = tokens.shape
    layers = attn_gain.shape[0]
    ctx_count = lax.axis_size(CTX)
    tp_count = lax.axis_size(TP)
    me = lax.axis_index(CTX)
    side = lax.axis_index(TP)
    length = rows * ctx_count
    heads_q = HEADS // tp_count // ctx_count
    heads_k = KV_HEADS // tp_count // ctx_count
    cols_q = heads_q * HEAD_DIM
    cols_k = heads_k * HEAD_DIM
    units = w_gate.shape[2] // ctx_count

    def own(a):
        return lax.dynamic_index_in_dim(a, side, 0, keepdims=False)

    def cut(w, axis, count):
        return lax.dynamic_slice_in_dim(w, me * count, count, axis)

    def whole(w):
        return lax.all_gather(w, (TP, FSDP), axis=0, tiled=True).reshape(
            tp_count, width, w.shape[1]
        )

    def pack(*pieces):
        return with_layout_constraint(jnp.concatenate(pieces, axis=1), Layout(major_to_minor=(0, 1)))

    def pack_attn(layer):
        return pack(
            cut(w_query[layer], 1, cols_q),
            cut(w_key[layer], 1, cols_k),
            cut(w_value[layer], 1, cols_k),
            cut(w_out[layer], 0, cols_q).T,
            jnp.zeros((w_query.shape[1], 64), w_query.dtype),
        )

    attn_w = [whole(pack_attn(0))]
    packed_attn = [None] + [pack_attn(layer) for layer in range(1, layers)]
    mlp_w = []
    seq_pos, seq_valid = own(positions), own(valid)
    starts = own(piece_starts)
    begun = start_step(
        jnp.pad(jnp.concatenate([attn_gain, mlp_gain], 0).astype(jnp.float32), ((0, 8 - 2 * layers), (0, 0))),
        jnp.pad(jnp.stack([seq_pos, seq_valid], axis=1), ((0, 0), (0, 6))),
        starts[None], tokens, w_gate, w_up, w_down,
    )
    normed, bias = begun.normed, begun.bias
    packed_mlp = [getattr(begun, f"packed_{layer}") for layer in range(layers)]
    gains = begun.all_gains.swapaxes(0, 1).reshape(8, width)
    places = begun.all_places
    gain_a = [gains[layer][None] for layer in range(layers)]
    gain_m = [gains[layers + layer][None] for layer in range(layers)]
    pos_all = places[:, :, 0].reshape(length)
    valid_f = seq_valid.astype(jnp.float32)[:, None]
    grad = (d_out,)
    mlp_w.append(whole(packed_mlp[0]))
    half_dim = HEAD_DIM // 2
    freqs = rope_base ** (-(jnp.arange(half_dim).astype(jnp.float32) * 2.0 / HEAD_DIM))
    angles = pos_all.astype(jnp.float32)[:, None] * freqs
    cosine, sine_t = jnp.cos(angles), jnp.sin(angles)
    cosine = jnp.concatenate([cosine, cosine], axis=1)
    sine_t = jnp.concatenate([-sine_t, sine_t], axis=1)
    cosine, sine_t = lax.optimization_barrier(
        (cosine.reshape(ctx_count, rows, HEAD_DIM), sine_t.reshape(ctx_count, rows, HEAD_DIM))
    )

    streams, attends, mlps = [(tokens,)], [], []
    for layer in range(layers):
        kept = attend_step(
            normed, streams[layer], gain_m[layer], valid_f, attn_w[layer], cosine, sine_t, bias,
            None if layer else d_out,
        )
        if layer == 0:
            grad_all, kept.full = kept.full, normed
        attends.append(kept)
        if layer + 1 < layers:
            normed_m, packed_attn[layer + 1], packed_mlp[layer + 1] = lax.optimization_barrier(
                (kept.normed_next, packed_attn[layer + 1], packed_mlp[layer + 1])
            )
            attn_w.append(whole(packed_attn[layer + 1]))
            mlp_w.append(whole(packed_mlp[layer + 1]))
            mlps.append(mlp_step(normed_m, kept.middle, gain_a[layer + 1], valid_f, mlp_w[layer]))
            streams.append(mlps[layer].stream)
            normed = mlps[layer].normed_next

    def reduced(g):
        return lax.psum_scatter(g, FSDP, scatter_dimension=0, tiled=True)

    down_rows = None
    attn_gains, mlp_gains = [], []
    for layer in reversed(range(layers)):
        kept = attends[layer]
        if layer + 1 == layers:
            came = mlp_back_step(kept.normed_next, kept.middle, gain_m[layer], grad, mlp_w[layer], grad_all=grad_all)
            end = [came.part_out, kept.middle, valid_f]
        else:
            came = mlp_back_step(
                down_rows, kept.middle, gain_m[layer], grad, mlp_w[layer], kept=mlps[layer], share=shares[0]
            )
        mlp_share = reduced(came.summed)
        mlp_gains.insert(0, came.gain_rows)
        back = attend_back_step(
            came.grad_rows, streams[layer], gain_a[layer], came.grad_new, attn_w[layer], cosine, sine_t, bias,
            kept, kept.full, None if layer else shares, end if layer else None,
        )
        attn_gains.insert(0, back.gain_rows)
        if layer:
            grad, output = back.grad_new, back.out
            down_rows, mlp_share, summed = lax.optimization_barrier((back.grad_rows, mlp_share, back.summed))
            shares = [mlp_share, reduced(summed)]
            last_stats = back.stats
    ended = tail_step(
        back.summed, mlp_share, [kept.stats for kept in attends], [kept.stats for kept in mlps] + [last_stats],
        attn_gains + mlp_gains,
    )
    input_grad = back.grad_new
    mlp_all = [[ended.gathered], [came.gathered, back.gathered_a]]
    attn_all = [[ended.last_0, ended.last_1], [back.gathered_b]]
    rms_stats = ended.all_stats[0, : 3 * layers].reshape(layers, 3)
    base = cols_q + 2 * cols_k
    placed = place_outs(
        attn_all, mlp_all,
        [(0, cols_q, False), (cols_q, cols_k, False), (cols_q + cols_k, cols_k, False), (base, cols_q, True)],
        [(0, units, False), (units, units, False), (2 * units, units, True)],
    )
    gains = ended.gains
    return (
        output, input_grad, gains[:layers], *placed[:4], gains[layers : 2 * layers], *placed[4:], rms_stats,
    )


def place_kernel(moves, count, *refs):
    refs = list(refs)
    outs_count = 1 + max(out for _, _, pieces in moves for _, _, _, out in pieces)
    ins, outs = refs[:count], refs[count : count + outs_count]
    del refs[: count + outs_count]
    held, laid = refs[:count], refs[count:-2]
    in_sems, out_sems = refs[-2:]
    loads = [pltpu.make_async_copy(ins[n], held[n], in_sems.at[n]) for n in range(count)]
    for load in loads:
        load.start()
    stores = []
    for n, (layer, first, pieces) in enumerate(moves):
        loads[n].wait()
        rows = held[n].shape[1]
        for start, size, flip, out in pieces:
            for c in range(held[n].shape[0]):
                block = held[n][c, :, start : start + size].astype(jnp.float32)
                if flip:
                    laid[out][layer, c * size : (c + 1) * size, first : first + rows] = block.T
                else:
                    laid[out][layer, first : first + rows, c * size : (c + 1) * size] = block
            if any(layer == l and out == o for l, _, more in moves[n + 1 :] for _, _, _, o in more):
                continue
            store = pltpu.make_async_copy(laid[out].at[layer], outs[out].at[layer], out_sems.at[len(stores)])
            store.start()
            stores.append(store)
    for store in stores:
        store.wait()


def place_outs(attn_all, mlp_all, attn_pieces, mlp_pieces):
    layers = len(attn_all)
    shapes = []
    for came, pieces in ((attn_all, attn_pieces), (mlp_all, mlp_pieces)):
        ctx_count = came[0][0].shape[0]
        depth = sum(a.shape[1] for a in came[0])
        for _, size, flip in pieces:
            wide = ctx_count * size
            shapes.append((layers, wide, depth) if flip else (layers, depth, wide))
    ins, moves = [], []
    for layer in reversed(range(layers)):
        for came, pieces, base in ((mlp_all, mlp_pieces, len(attn_pieces)), (attn_all, attn_pieces, 0)):
            first = 0
            for a in came[layer]:
                ins.append(a)
                moves.append((layer, first, [(*piece, base + n) for n, piece in enumerate(pieces)]))
                first += a.shape[1]
    hbm = pl.BlockSpec(memory_space=pl.ANY)
    return pl.pallas_call(
        functools.partial(place_kernel, moves, len(ins)),
        out_shape=[jax.ShapeDtypeStruct(s, jnp.float32) for s in shapes],
        in_specs=[hbm] * len(ins),
        out_specs=[hbm] * len(shapes),
        scratch_shapes=[pltpu.VMEM(a.shape, a.dtype) for a in ins]
        + [pltpu.VMEM(s, jnp.float32) for s in shapes]
        + [pltpu.SemaphoreType.DMA((len(ins),)), pltpu.SemaphoreType.DMA((layers * len(shapes),))],
        compiler_params=pltpu.CompilerParams(vmem_limit_bytes=60 << 20),
    )(*ins)


def fits(mesh):
    tp_count, ctx_count = mesh.shape[TP], mesh.shape[CTX]
    return ctx_count == 4 and tp_count == 2


def solution(mesh):
    in_specs = (
        P(FSDP, CTX, None),
        P(FSDP, CTX),
        P(FSDP, CTX),
        P(FSDP, None),
        P(FSDP, CTX, None),
        P(None, FSDP),
        P(None, FSDP, TP),
        P(None, FSDP, TP),
        P(None, FSDP, TP),
        P(None, TP, FSDP),
        P(None, FSDP),
        P(None, FSDP, TP),
        P(None, FSDP, TP),
        P(None, TP, FSDP),
    )
    out_specs = (
        P(FSDP, CTX, None),
        P(FSDP, CTX, None),
        P(None, FSDP),
        P(None, FSDP, TP),
        P(None, FSDP, TP),
        P(None, FSDP, TP),
        P(None, TP, FSDP),
        P(None, FSDP),
        P(None, FSDP, TP),
        P(None, FSDP, TP),
        P(None, TP, FSDP),
        P(),
    )
    return jax.shard_map(planned if fits(mesh) else general, mesh=mesh, in_specs=in_specs, out_specs=out_specs, check_vma=False)
```

```python
import functools

import jax
import jax.numpy as jnp
from jax import lax
from jax.experimental import pallas as pl
from jax.experimental.layout import Layout, with_layout_constraint
from jax.experimental.pallas import tpu as pltpu
from jax.sharding import PartitionSpec as P

MESH = pl.DeviceIdType.MESH
FSDP, CTX, TP = "fsdp", "ctx", "tp"

HEADS = 16
KV_HEADS = 8
HEAD_DIM = 96
PIECE_LEN = 256


epsilon = 1e-05
rope_base = 100000.0
neg_big = -1e30


def rope_tables(positions, head_dim):
    half_dim = head_dim // 2
    freqs = rope_base ** (-(jnp.arange(half_dim).astype(jnp.float32) * 2.0 / head_dim))
    angles = positions.astype(jnp.float32)[..., None] * freqs
    return (jnp.cos(angles)[:, :, None, :], jnp.sin(angles)[:, :, None, :])


def rotate(values, cosine, sine_t):
    half_dim = values.shape[-1] // 2
    lead_part = values[..., :half_dim]
    tail_part = values[..., half_dim:]
    return jnp.concatenate(
        [lead_part * cosine - tail_part * sine_t, tail_part * cosine + lead_part * sine_t], axis=-1
    )


def normalize(stream, gain_vec):
    inv_rms = lax.rsqrt(jnp.mean(stream * stream, axis=-1, keepdims=True) + epsilon)
    return stream * inv_rms * gain_vec.astype(jnp.float32)


def norm_back(stream, gain_vec, grad_out):
    inv_rms = lax.rsqrt(jnp.mean(stream * stream, axis=-1, keepdims=True) + epsilon)
    scaled_grad = gain_vec.astype(jnp.float32) * grad_out
    grad_in = inv_rms * scaled_grad - stream * inv_rms**3 * jnp.mean(
        scaled_grad * stream, axis=-1, keepdims=True
    )
    grad_gain = jnp.sum(grad_out * stream * inv_rms, axis=0)
    return (grad_in, grad_gain)


def score_block(query_b, key_heads, allowed, score_scale):
    raw_scores = (
        jnp.einsum("sckgd,snkd->skgcn", query_b, key_heads, preferred_element_type=jnp.float32)
        * score_scale
    )
    return jnp.where(allowed[:, None, None], raw_scores, neg_big)


def general(
    tokens,
    positions,
    valid,
    piece_starts,
    d_out,
    attn_gain,
    w_query,
    w_key,
    w_value,
    w_out,
    mlp_gain,
    w_gate,
    w_up,
    w_down,
):
    seq_count, shard_len, model_width = tokens.shape
    tok_rows = seq_count * shard_len
    tp_count = lax.axis_size(TP)
    local_heads = HEADS // tp_count
    local_kv = KV_HEADS // tp_count
    group_size = HEADS // KV_HEADS
    score_scale = HEAD_DIM ** (-0.5)
    seq_length = shard_len * lax.axis_size(CTX)
    start_tok = lax.axis_index(CTX) * shard_len
    query_index = start_tok + jnp.arange(shard_len, dtype=jnp.int32)
    key_index = jnp.arange(seq_length, dtype=jnp.int32)
    cosine, sine_t = rope_tables(positions, HEAD_DIM)
    valid_flat = valid.astype(jnp.float32).reshape(tok_rows)
    in_query = (query_index[None, None, :] >= piece_starts[:, :, None]) & (
        query_index[None, None, :] < piece_starts[:, :, None] + PIECE_LEN
    )
    in_key = (key_index[None, None, :] >= piece_starts[:, :, None]) & (
        key_index[None, None, :] < piece_starts[:, :, None] + PIECE_LEN
    )
    same_piece = jnp.any(in_query[:, :, :, None] & in_key[:, :, None, :], axis=1)
    causal = key_index[None, :] <= query_index[:, None]
    diagonal = key_index[None, :] == query_index[:, None]
    layer_count = attn_gain.shape[0]
    stream = tokens.astype(jnp.float32).reshape(tok_rows, model_width)
    saved = []
    stat_rows = []
    for layer_no in range(layer_count):
        weights = (
            lax.all_gather(attn_gain[layer_no], FSDP, axis=0, tiled=True),
            lax.all_gather(w_query[layer_no], FSDP, axis=0, tiled=True),
            lax.all_gather(w_key[layer_no], FSDP, axis=0, tiled=True),
            lax.all_gather(w_value[layer_no], FSDP, axis=0, tiled=True),
            lax.all_gather(w_out[layer_no], FSDP, axis=1, tiled=True),
            lax.all_gather(mlp_gain[layer_no], FSDP, axis=0, tiled=True),
            lax.all_gather(w_gate[layer_no], FSDP, axis=0, tiled=True),
            lax.all_gather(w_up[layer_no], FSDP, axis=0, tiled=True),
            lax.all_gather(w_down[layer_no], FSDP, axis=1, tiled=True),
        )
        gain_a, w_q, w_k, w_v, w_o, gain_m, w_g, w_u, w_d = weights
        normed_a = normalize(stream, gain_a).astype(jnp.bfloat16)
        query_heads = jnp.dot(normed_a, w_q, preferred_element_type=jnp.float32).reshape(
            seq_count, shard_len, local_heads, HEAD_DIM
        )
        query_b = (
            rotate(query_heads, cosine, sine_t)
            .astype(jnp.bfloat16)
            .reshape(seq_count, shard_len, local_kv, group_size, HEAD_DIM)
        )
        key_local = jnp.dot(normed_a, w_k, preferred_element_type=jnp.float32).reshape(
            seq_count, shard_len, local_kv, HEAD_DIM
        )
        key_local = (
            rotate(key_local, cosine, sine_t)
            .astype(jnp.bfloat16)
            .reshape(seq_count, shard_len, local_kv * HEAD_DIM)
        )
        value_local = (
            jnp.dot(normed_a, w_v, preferred_element_type=jnp.float32)
            .astype(jnp.bfloat16)
            .reshape(seq_count, shard_len, local_kv * HEAD_DIM)
        )
        key_all, value_all, valid_all = (
            lax.all_gather(key_local, CTX, axis=1, tiled=True),
            lax.all_gather(value_local, CTX, axis=1, tiled=True),
            lax.all_gather(valid.astype(jnp.bfloat16), CTX, axis=1, tiled=True),
        )
        allowed = (causal[None] | same_piece) & ((valid_all[:, None, :] > 0.5) | diagonal[None])
        key_heads = key_all.reshape(seq_count, seq_length, local_kv, HEAD_DIM)
        value_heads = value_all.reshape(seq_count, seq_length, local_kv, HEAD_DIM)
        raw_scores = score_block(query_b, key_heads, allowed, score_scale)
        row_max = jnp.max(raw_scores, axis=-1, keepdims=True)
        log_total = row_max + jnp.log(
            jnp.sum(jnp.exp(raw_scores - row_max), axis=-1, keepdims=True)
        )
        softmax_b = jnp.exp(raw_scores - log_total).astype(jnp.bfloat16)
        mixed_heads = jnp.einsum(
            "skgcn,snkd->sckgd", softmax_b, value_heads, preferred_element_type=jnp.float32
        )
        mixed_b = mixed_heads.astype(jnp.bfloat16).reshape(tok_rows, local_heads * HEAD_DIM)
        attn_branch = lax.psum(
            jnp.dot(mixed_b, w_o, preferred_element_type=jnp.float32).astype(jnp.bfloat16), TP
        ).astype(jnp.float32)
        middle = stream + attn_branch
        normed_m = normalize(middle, gain_m).astype(jnp.bfloat16)
        gate_act = jnp.dot(normed_m, w_g, preferred_element_type=jnp.float32)
        up_act = jnp.dot(normed_m, w_u, preferred_element_type=jnp.float32)
        hidden = (jax.nn.silu(gate_act) * up_act).astype(jnp.bfloat16)
        mlp_branch = lax.psum(
            jnp.dot(hidden, w_d, preferred_element_type=jnp.float32).astype(jnp.bfloat16), TP
        ).astype(jnp.float32)
        stat_rows.append(
            jnp.stack(
                [
                    jnp.sum(valid_flat[:, None] * stream * stream),
                    jnp.sum(valid_flat[:, None] * attn_branch * attn_branch),
                    jnp.sum(valid_flat[:, None] * mlp_branch * mlp_branch),
                ]
            )
        )
        kept_weights = None
        saved.append(
            (
                stream,
                normed_a,
                query_b,
                key_heads,
                value_heads,
                allowed,
                log_total,
                mixed_b,
                middle,
                normed_m,
                gate_act,
                up_act,
                hidden,
                kept_weights,
            )
        )
        stream = middle + mlp_branch
    output = stream.astype(jnp.bfloat16).reshape(seq_count, shard_len, model_width)
    total_squares, total_count = lax.psum(
        (jnp.stack(stat_rows), jnp.sum(valid_flat)), (FSDP, CTX)
    )
    rms_stats = jnp.sqrt(total_squares / (total_count * model_width))
    grad_stream = d_out.astype(jnp.float32).reshape(tok_rows, model_width)
    results = [None] * layer_count
    for layer_no in reversed(range(layer_count)):
        (
            stream_in,
            normed_a,
            query_b,
            key_heads,
            value_heads,
            allowed,
            log_total,
            mixed_b,
            middle,
            normed_m,
            gate_act,
            up_act,
            hidden,
            kept_weights,
        ) = saved[layer_no]
        weights = (
            lax.all_gather(attn_gain[layer_no], FSDP, axis=0, tiled=True),
            lax.all_gather(w_query[layer_no], FSDP, axis=0, tiled=True),
            lax.all_gather(w_key[layer_no], FSDP, axis=0, tiled=True),
            lax.all_gather(w_value[layer_no], FSDP, axis=0, tiled=True),
            lax.all_gather(w_out[layer_no], FSDP, axis=1, tiled=True),
            lax.all_gather(mlp_gain[layer_no], FSDP, axis=0, tiled=True),
            lax.all_gather(w_gate[layer_no], FSDP, axis=0, tiled=True),
            lax.all_gather(w_up[layer_no], FSDP, axis=0, tiled=True),
            lax.all_gather(w_down[layer_no], FSDP, axis=1, tiled=True),
        )
        gain_a, w_q, w_k, w_v, w_o, gain_m, w_g, w_u, w_d = weights
        grad_mlp = grad_stream.astype(jnp.bfloat16)
        grad_hidden = jnp.einsum("rd,fd->rf", grad_mlp, w_d, preferred_element_type=jnp.float32)
        g_down = jnp.einsum("rf,rd->fd", hidden, grad_mlp, preferred_element_type=jnp.float32)
        sigmoid_g = jax.nn.sigmoid(gate_act)
        grad_gate = (
            grad_hidden * up_act * sigmoid_g * (1.0 + gate_act * (1.0 - sigmoid_g))
        ).astype(jnp.bfloat16)
        grad_up = (grad_hidden * gate_act * sigmoid_g).astype(jnp.bfloat16)
        grad_normed_m = lax.psum(
            (
                jnp.einsum("rf,df->rd", grad_gate, w_g, preferred_element_type=jnp.float32)
                + jnp.einsum("rf,df->rd", grad_up, w_u, preferred_element_type=jnp.float32)
            ).astype(jnp.bfloat16),
            TP,
        ).astype(jnp.float32)
        g_gate = jnp.einsum("rd,rf->df", normed_m, grad_gate, preferred_element_type=jnp.float32)
        g_up = jnp.einsum("rd,rf->df", normed_m, grad_up, preferred_element_type=jnp.float32)
        grad_from_norm, g_gain_m = norm_back(middle, gain_m, grad_normed_m)
        grad_middle = grad_stream + grad_from_norm
        grad_attn = grad_middle.astype(jnp.bfloat16)
        grad_heads = jnp.einsum(
            "rd,hd->rh", grad_attn, w_o, preferred_element_type=jnp.float32
        ).astype(jnp.bfloat16)
        g_out = jnp.einsum("rh,rd->hd", mixed_b, grad_attn, preferred_element_type=jnp.float32)
        grad_heads = grad_heads.reshape(seq_count, shard_len, local_kv, group_size, HEAD_DIM)
        raw_scores = score_block(query_b, key_heads, allowed, score_scale)
        softmax_p = jnp.exp(raw_scores - log_total)
        grad_probs = jnp.einsum(
            "sckgd,snkd->skgcn", grad_heads, value_heads, preferred_element_type=jnp.float32
        )
        row_dots = jnp.sum(softmax_p * grad_probs, axis=-1, keepdims=True)
        grad_scores = (softmax_p * (grad_probs - row_dots)).astype(jnp.bfloat16)
        grad_query = (
            jnp.einsum(
                "skgcn,snkd->sckgd", grad_scores, key_heads, preferred_element_type=jnp.float32
            )
            * score_scale
        )
        grad_key_all = (
            jnp.einsum(
                "skgcn,sckgd->snkd", grad_scores, query_b, preferred_element_type=jnp.float32
            )
            * score_scale
        )
        grad_value_all = jnp.einsum(
            "skgcn,sckgd->snkd",
            softmax_p.astype(jnp.bfloat16),
            grad_heads,
            preferred_element_type=jnp.float32,
        )
        grad_key, grad_value = (
            lax.psum_scatter(
                grad_key_all.reshape(seq_count, seq_length, local_kv * HEAD_DIM).astype(
                    jnp.bfloat16
                ),
                CTX,
                scatter_dimension=1,
                tiled=True,
            ).astype(jnp.float32),
            lax.psum_scatter(
                grad_value_all.reshape(seq_count, seq_length, local_kv * HEAD_DIM).astype(
                    jnp.bfloat16
                ),
                CTX,
                scatter_dimension=1,
                tiled=True,
            ).astype(jnp.float32),
        )
        grad_query_b = rotate(
            grad_query.reshape(seq_count, shard_len, local_heads, HEAD_DIM), cosine, -sine_t
        )
        grad_query_b = grad_query_b.astype(jnp.bfloat16).reshape(tok_rows, local_heads * HEAD_DIM)
        grad_key_b = rotate(
            grad_key.reshape(seq_count, shard_len, local_kv, HEAD_DIM), cosine, -sine_t
        )
        grad_key_b = grad_key_b.astype(jnp.bfloat16).reshape(tok_rows, local_kv * HEAD_DIM)
        grad_value_b = grad_value.astype(jnp.bfloat16).reshape(tok_rows, local_kv * HEAD_DIM)
        grad_normed_a = lax.psum(
            (
                jnp.einsum("rh,dh->rd", grad_query_b, w_q, preferred_element_type=jnp.float32)
                + jnp.einsum("rh,dh->rd", grad_key_b, w_k, preferred_element_type=jnp.float32)
                + jnp.einsum("rh,dh->rd", grad_value_b, w_v, preferred_element_type=jnp.float32)
            ).astype(jnp.bfloat16),
            TP,
        ).astype(jnp.float32)
        g_query = jnp.einsum(
            "rd,rh->dh", normed_a, grad_query_b, preferred_element_type=jnp.float32
        )
        g_key = jnp.einsum("rd,rh->dh", normed_a, grad_key_b, preferred_element_type=jnp.float32)
        g_value = jnp.einsum(
            "rd,rh->dh", normed_a, grad_value_b, preferred_element_type=jnp.float32
        )
        grad_from_attn_norm, g_gain_a = norm_back(stream_in, gain_a, grad_normed_a)
        grad_stream = grad_middle + grad_from_attn_norm
        grad_terms = (g_gain_a, g_query, g_key, g_value, g_out, g_gain_m, g_gate, g_up, g_down)
        shares = (
            lax.psum_scatter(grad_terms[0], (FSDP, CTX), scatter_dimension=0, tiled=True),
            lax.psum_scatter(grad_terms[1], (FSDP, CTX), scatter_dimension=0, tiled=True),
            lax.psum_scatter(grad_terms[2], (FSDP, CTX), scatter_dimension=0, tiled=True),
            lax.psum_scatter(grad_terms[3], (FSDP, CTX), scatter_dimension=0, tiled=True),
            lax.psum_scatter(grad_terms[4], (FSDP, CTX), scatter_dimension=1, tiled=True),
            lax.psum_scatter(grad_terms[5], (FSDP, CTX), scatter_dimension=0, tiled=True),
            lax.psum_scatter(grad_terms[6], (FSDP, CTX), scatter_dimension=0, tiled=True),
            lax.psum_scatter(grad_terms[7], (FSDP, CTX), scatter_dimension=0, tiled=True),
            lax.psum_scatter(grad_terms[8], (FSDP, CTX), scatter_dimension=1, tiled=True),
        )
        results[layer_no] = (
            lax.all_gather(shares[0].astype(jnp.bfloat16), CTX, axis=0, tiled=True).astype(
                jnp.float32
            ),
            lax.all_gather(shares[1].astype(jnp.bfloat16), CTX, axis=0, tiled=True).astype(
                jnp.float32
            ),
            lax.all_gather(shares[2].astype(jnp.bfloat16), CTX, axis=0, tiled=True).astype(
                jnp.float32
            ),
            lax.all_gather(shares[3].astype(jnp.bfloat16), CTX, axis=0, tiled=True).astype(
                jnp.float32
            ),
            lax.all_gather(shares[4].astype(jnp.bfloat16), CTX, axis=1, tiled=True).astype(
                jnp.float32
            ),
            lax.all_gather(shares[5].astype(jnp.bfloat16), CTX, axis=0, tiled=True).astype(
                jnp.float32
            ),
            lax.all_gather(shares[6].astype(jnp.bfloat16), CTX, axis=0, tiled=True).astype(
                jnp.float32
            ),
            lax.all_gather(shares[7].astype(jnp.bfloat16), CTX, axis=0, tiled=True).astype(
                jnp.float32
            ),
            lax.all_gather(shares[8].astype(jnp.bfloat16), CTX, axis=1, tiled=True).astype(
                jnp.float32
            ),
        )
    stacked = [
        jnp.stack([results[layer_no][member] for layer_no in range(layer_count)])
        for member in range(9)
    ]
    input_grad = grad_stream.reshape(seq_count, shard_len, model_width)
    return (
        output,
        input_grad,
        stacked[0],
        stacked[1],
        stacked[2],
        stacked[3],
        stacked[4],
        stacked[5],
        stacked[6],
        stacked[7],
        stacked[8],
        rms_stats,
    )


def partners():
    me = lax.axis_index(CTX)
    return me, me ^ 1, me ^ 2, me ^ 3


def greet(*places):
    barrier = pltpu.get_barrier_semaphore()
    for place in places:
        pl.semaphore_signal(barrier, inc=1, device_id=place, device_id_type=MESH)
    pl.semaphore_wait(barrier, len(places))


def send(src, dst, sems, slot, place):
    copy = pltpu.make_async_remote_copy(
        src_ref=src,
        dst_ref=dst,
        send_sem=sems[0].at[slot],
        recv_sem=sems[1].at[slot],
        device_id=place,
        device_id_type=MESH,
    )
    copy.start()
    return copy


def run(steps, work=()):
    for n, _ in enumerate(steps):
        if n < len(work):
            work[n]()


def gather_rows(full, sems, place, own):
    me, side_x, side_y, _ = place
    to_x, to_y = {CTX: side_x}, {CTX: side_y}
    half = full.shape[1] // 2
    top, low = pl.ds(0, half), pl.ds(half, half)
    first = [
        send(own.at[top], full.at[me, top], sems, 0, to_x),
        send(own.at[low], full.at[me, low], sems, 1, to_y),
    ]
    rest = [
        send(own.at[top], full.at[me, top], sems, 2, to_y),
        send(own.at[low], full.at[me, low], sems, 3, to_x),
    ]
    yield
    first[0].wait_recv()
    rest.append(send(full.at[side_x, top], full.at[side_x, top], sems, 4, to_y))
    first[1].wait_recv()
    rest.append(send(full.at[side_y, low], full.at[side_y, low], sems, 5, to_x))
    yield
    rest[0].wait_recv()
    rest[1].wait_recv()
    yield
    rest[2].wait_recv()
    rest[3].wait_recv()
    for copy in first + rest:
        copy.wait_send()


def dot32(a, b, dims):
    return lax.dot_general(a, b, (dims, ((), ())), preferred_element_type=jnp.float32)


def start_kernel(r):
    place = partners()
    me, side_x, side_y, across = place
    groups = (
        (FSDP, r.gains, r.all_gains, (r.gain_send, r.gain_recv)),
        (CTX, r.places, r.all_places, (r.place_send, r.place_recv)),
    )
    peers = []
    for axis, _, _, _ in groups:
        count = lax.axis_size(axis)
        peers.append([lax.rem(lax.axis_index(axis) + step, count) for step in range(1, count)])
    full = r.full
    own = pltpu.make_async_copy(r.x.at[lax.axis_index(TP)], full.at[me], r.load.at[0])
    own.start()
    greet(*[{groups[n][0]: peer} for n in range(2) for peer in peers[n]])
    copies = []
    for n, (axis, src, dst, sems) in enumerate(groups):
        mine = pltpu.make_async_copy(src, dst.at[lax.axis_index(axis)], r.load.at[1 + n])
        mine.start()
        for step, peer in enumerate(peers[n]):
            copies.append(send(src, dst.at[lax.axis_index(axis)], sems, step, {axis: peer}))
        copies.append(mine)
    steps = gather_rows(full, (r.ag_send, r.ag_recv), place, r.x.at[lax.axis_index(TP)])
    next(steps)
    packed = [getattr(r, f"packed_{layer}") for layer in range(r.gate.shape[0])]
    layers, units = len(packed), r.turned.shape[1]
    loads = []
    for layer in range(layers):
        cut = pl.ds(pl.multiple_of(me * units, units), units)
        for n, (src, dst) in enumerate((
            (r.gate.at[layer, :, cut], packed[layer].at[:, pl.ds(0, units)]),
            (r.up.at[layer, :, cut], packed[layer].at[:, pl.ds(units, units)]),
            (r.down.at[layer, cut], r.turned.at[layer]),
        )):
            loads.append(pltpu.make_async_copy(src, dst, r.load.at[3 + 3 * layer + n]))
    for load in loads:
        load.start()
    own.wait()
    for copy in copies:
        copy.wait()
    gain = jnp.concatenate([r.all_gains[n, 0:1, :] for n in range(lax.axis_size(FSDP))], axis=1)
    rows = full.shape[1]
    half = rows // 2
    step = 16

    def norm(top_of, low_of):
        for part_no, owner in enumerate((top_of, low_of)):
            @pl.loop(0, half // step)
            def _(i):
                here = pl.ds(pl.multiple_of(part_no * half + i * step, step), step)
                row = full[owner, here, :].astype(jnp.float32)
                inv_rms = lax.rsqrt(jnp.mean(row * row, axis=-1, keepdims=True) + epsilon)
                r.normed[owner, here, :] = (row * inv_rms * gain).astype(jnp.bfloat16)

    def mask():
        length = r.bias.shape[1]
        block = 96
        query = lax.broadcasted_iota(jnp.int32, (1, length), 1)
        firsts = [r.starts[0:1, n : n + 1] for n in range(r.starts.shape[1])]
        in_query = [jnp.where((query >= f) & (query < f + PIECE_LEN), 1.0, 0.0) for f in firsts]
        for owner in range(r.all_places.shape[0]):
            @pl.loop(0, rows // block)
            def _(i):
                here = pl.ds(pl.multiple_of(i * block, block), block)
                key = owner * rows + i * block + lax.broadcasted_iota(jnp.int32, (block, 1), 0)
                valid = r.all_places[owner, here, HEAD_DIM : HEAD_DIM + 1]
                seen = 0
                for f, row in zip(firsts, in_query):
                    seen += jnp.where((key >= f) & (key < f + PIECE_LEN), 1.0, 0.0) * row
                seen = jnp.where(key <= query, 1.0, seen) * valid
                seen = jnp.where(key == query, 1.0, seen)
                added = jnp.where(seen > 0, 0.0, neg_big).astype(jnp.bfloat16)
                keys = pl.ds(pl.multiple_of(owner * rows + i * block, block), block)
                for n in range(r.all_places.shape[0]):
                    one = added[:, n * rows : (n + 1) * rows]
                    r.bias[n, keys, :] = jnp.concatenate([one, one], axis=1)

    norm(me, me)
    mask()
    r.keep("bias")
    half_dim = HEAD_DIM // 2
    for owner in range(r.all_places.shape[0]):
        table = r.all_places[owner]
        cos_b, sin_b = table[:, :half_dim], table[:, half_dim:HEAD_DIM]
        r.cosine[owner] = jnp.concatenate([cos_b, cos_b], axis=1)
        r.sine[owner] = jnp.concatenate([-sin_b, sin_b], axis=1)
    r.keep("cosine", "sine")
    next(steps)
    norm(side_x, side_y)
    for load in loads:
        load.wait()
    for layer in range(layers):
        packed[layer][:, 2 * units :] = r.turned[layer].astype(jnp.float32).T.astype(jnp.bfloat16)
        r.keep(f"packed_{layer}")
    next(steps)
    norm(side_y, side_x)
    run(steps)
    norm(across, across)


def stat_steps(r, place):
    depth = lax.axis_size(FSDP)
    level = lax.axis_index(FSDP)
    others = [{FSDP: lax.rem(level + step, depth)} for step in range(1, depth)]
    here = (r.stat_send, r.stat_recv)
    layers = len(r.attn_stats)
    lane = lax.broadcasted_iota(jnp.int32, (8, 128), 1)
    tile = jnp.zeros((8, 128), jnp.float32)
    wanted = [(3 * layers, r.attn_stats[0], 2)]
    for layer in range(layers):
        wanted += [(3 * layer, r.attn_stats[layer], 1), (3 * layer + 1, r.attn_stats[layer], 0)]
        wanted.append((3 * layer + 2, r.mlp_stats[layer], 0))
    for to, ref, at in wanted:
        row = jnp.sum(ref[...], axis=0, keepdims=True)
        value = jnp.sum(jnp.where(lane[0:1] == at, row, 0.0), axis=1, keepdims=True)
        tile += jnp.where(lane == to, value, 0.0)
    width = r.width
    r.stat_sent[0, :, pl.ds(width, 128)] = tile
    r.stat_sent[0, :, pl.ds(0, width)] = jnp.zeros((8, width), jnp.float32)
    for n, ref in enumerate(r.gain_rows):
        r.stat_sent[0, n : n + 1, pl.ds(0, width)] = jnp.sum(ref[...], axis=0, keepdims=True)
    for n, peer in enumerate((sibling(), {CTX: place[1]}, {CTX: place[2]})):
        copy = send(r.stat_sent.at[n], r.stat_came.at[n], here, n, peer)
        yield
        copy.wait()
        r.stat_sent[n + 1] = r.stat_sent[n] + r.stat_came[n]
    r.stat_z[level] = r.stat_sent[3]
    copies = [send(r.stat_z.at[level], r.stat_z.at[level], here, 3 + n, peer) for n, peer in enumerate(others)]
    yield
    for copy in copies:
        copy.wait()
    part = width // depth
    here = pl.ds(pl.multiple_of(level * part, 128), part)
    gains, held = r.stat_z[0, :, here], r.stat_z[0, :, pl.ds(width, 128)]
    for n in range(1, depth):
        gains += r.stat_z[n, :, here]
        held += r.stat_z[n, :, pl.ds(width, 128)]
    r.gains[...] = gains
    count = jnp.sum(jnp.where(lane[0:1] == 3 * layers, held[0:1], 0.0), axis=1, keepdims=True)
    r.all_stats[...] = jnp.sqrt(held / (count * r.width))


def tail_kernel(width, r):
    r.width = width
    place = partners()
    me = place[0]
    depth = lax.axis_size(FSDP)
    level = lax.axis_index(FSDP)
    peers = [lax.rem(level + step, depth) for step in range(1, depth)]
    mine = pltpu.make_async_copy(r.share, r.gathered.at[me], r.load.at[0])
    mine.start()
    greet_near(place, sibling(), *[{FSDP: peer} for peer in peers])
    rows = r.share.shape[0]
    half = rows // 2
    r.gain_rows = [r.gain_rows_0, r.gain_rows_1, r.gain_rows_2, r.gain_rows_3]
    r.attn_stats = [r.attn_stats_0, r.attn_stats_1]
    r.mlp_stats = [r.mlp_stats_0, r.mlp_stats_1]
    counts = stat_steps(r, place)
    next(counts)
    copies = []
    for part_no in range(2):
        copies.append([])
        for step, peer in enumerate(peers):
            block = r.summed.at[pl.ds(pl.multiple_of(peer * rows + part_no * half, half), half)]
            copies[part_no].append(
                send(block, r.z_came.at[part_no, level], (r.z_send, r.z_recv), part_no * depth + step, {FSDP: peer})
            )
    first = gather_rows(r.gathered, (r.ag_send, r.ag_recv), place, r.share)
    next(first)
    next(counts)
    next(first)
    step = 48
    lasts = (r.last_0, r.last_1)
    steps = []
    for part_no in range(2):
        for copy in copies[part_no]:
            copy.wait_recv()

        @pl.loop(0, half // step)
        def _(i):
            here = pl.ds(pl.multiple_of(i * step, step), step)
            start = pl.multiple_of(level * rows + part_no * half + i * step, step)
            total = r.summed[pl.ds(start, step), :].astype(jnp.float32)
            for peer in peers:
                total += r.z_came[part_no, peer, here, :].astype(jnp.float32)
            lasts[part_no][me, here, :] = total.astype(jnp.bfloat16)

        steps.append(gather_rows(lasts[part_no], ((r.l0_send, r.l0_recv), (r.l1_send, r.l1_recv))[part_no], place, lasts[part_no].at[me]))
        next(steps[part_no])
        if part_no == 0:
            next(counts)
    next(steps[0])
    next(counts)
    next(steps[1])
    run(first)
    mine.wait()
    r.keep("gathered")
    run(steps[0])
    run(steps[1])
    run(counts)
    for copy in copies[0] + copies[1]:
        copy.wait_send()


class Scatter:
    def __init__(self, part, buffers, sems, place):
        self.part, self.sems, self.place = part, sems, place
        self.from_x, self.from_y, self.passed, self.last = buffers
        self.half = part.shape[1] // 2
        self.copies = {}

    def send(self, slot, src, dst, axis_peer):
        self.copies[slot] = send(src, dst, self.sems, slot, {CTX: axis_peer})

    def across(self):
        _, side_x, side_y, far = self.place
        self.send(0, self.part.at[far, pl.ds(0, self.half)], self.from_x.at[1], side_x)
        self.send(1, self.part.at[far, pl.ds(self.half, self.half)], self.from_y.at[1], side_y)

    def x_out(self, some=None):
        side_x = self.place[1]
        slot, rows = self.cut(some)
        self.send(slot, self.part.at[side_x, rows], self.from_x.at[0, rows], side_x)

    def y_out(self, some=None):
        side_y = self.place[2]
        slot, rows = self.cut(some)
        below = pl.ds(self.half + rows.start, rows.size)
        self.send(slot + 1, self.part.at[side_y, below], self.from_y.at[0, rows], side_y)

    def cut(self, some):
        if some is None:
            return 2, pl.ds(0, self.half)
        first = self.half // 48 * 16
        return (2, pl.ds(0, first)) if some == 0 else (6, pl.ds(first, self.half - first))

    def add_to(self, slot, owner, start, came):
        step = 16

        @pl.loop(0, self.half // step)
        def _(i):
            rows = pl.ds(pl.multiple_of(i * step, step), step)
            mine = self.part[owner, pl.ds(pl.multiple_of(start + i * step, step), step), :]
            total = mine.astype(jnp.float32) + came[1, rows, :].astype(jnp.float32)
            self.passed[slot, rows, :] = total.astype(self.passed.dtype)

    def forward(self):
        _, side_x, side_y, _ = self.place
        self.copies[0].wait_recv()
        self.add_to(0, side_y, 0, self.from_x)
        self.send(4, self.passed.at[0], self.last.at[0], side_y)
        self.copies[1].wait_recv()
        self.add_to(1, side_x, self.half, self.from_y)
        self.send(5, self.passed.at[1], self.last.at[1], side_x)

    def finish(self):
        for slot in self.copies:
            if slot > 1:
                self.copies[slot].wait_recv()
        for slot in self.copies:
            self.copies[slot].wait_send()

    def each_row(self, work, step=16):
        me = self.place[0]
        for side in range(2):
            came = self.from_x if side == 0 else self.from_y

            @pl.loop(0, self.half // step)
            def _(i):
                rows = pl.ds(pl.multiple_of(i * step, step), step)
                whole = pl.ds(pl.multiple_of(side * self.half + i * step, step), step)
                total = self.part[me, whole, :].astype(jnp.float32)
                total += came[0, rows, :].astype(jnp.float32)
                work(whole, total + self.last[side, rows, :].astype(jnp.float32))


def scatter_steps(scatter):
    scatter.across()
    scatter.x_out()
    scatter.y_out()
    yield
    scatter.forward()
    yield
    scatter.finish()


class WeightGrads:
    def __init__(self, lefts, rights, sent, came, summed, sems):
        self.lefts, self.rights, self.sent, self.came, self.summed, self.sems = lefts, rights, sent, came, summed, sems
        self.sizes = [r.shape[-1] for r in rights]
        self.side = lax.axis_index(TP)
        self.copies = []

    def product(self, p, t, put):
        block = 256
        left, right = self.lefts[p], self.rights[p]
        width = left.shape[-1]

        @pl.loop(0, width // block)
        def _(i):
            cols = pl.ds(pl.multiple_of(i * block, block), block)
            one = left[:, :, cols].reshape(-1, block)
            put(cols, dot32(one, right[t].reshape(one.shape[0], -1), ((0,), (0,))).astype(jnp.bfloat16))

    def theirs(self, p):
        def put(rows, value):
            self.sent[p][rows, : self.sizes[p]] = value

        self.product(p, 1 - self.side, put)
        self.copies.append(send(self.sent[p], self.came[p], self.sems, p, {TP: 1 - self.side}))

    def cols(self, p):
        start = sum(self.sizes[:p])
        return slice(start, start + self.sizes[p])

    def ours(self, p):
        def put(rows, value):
            self.summed[rows, self.cols(p)] = value

        self.product(p, self.side, put)

    def add_up(self):
        step = 64
        for p, copy in enumerate(self.copies):
            copy.wait_recv()

            @pl.loop(0, self.summed.shape[0] // step)
            def _(i):
                rows = pl.ds(pl.multiple_of(i * step, step), step)
                total = self.summed[rows, self.cols(p)].astype(jnp.float32) + self.came[p][rows, : self.sizes[p]].astype(jnp.float32)
                self.summed[rows, self.cols(p)] = total.astype(jnp.bfloat16)

    def close(self):
        for copy in self.copies:
            copy.wait_send()


def add_stats(stats, valid, *values):
    lane = lax.broadcasted_iota(jnp.int32, stats.shape, 1)
    total = stats[...] + jnp.where(lane == 2, valid, 0.0)
    for n, value in enumerate(values):
        total += jnp.where(lane == n, valid * jnp.sum(value * value, axis=-1, keepdims=True), 0.0)
    stats[...] = total


def norm_sum(scatter, stream, gain, valid, middle, normed, stats):
    stats[...] = jnp.zeros_like(stats)

    def work(rows, branch):
        before = stream[rows, :].astype(jnp.float32)
        total = before + branch
        middle[rows, :] = total
        inv_rms = lax.rsqrt(jnp.mean(total * total, axis=-1, keepdims=True) + epsilon)
        normed[rows, :] = (total * inv_rms * gain[...]).astype(normed.dtype)
        add_stats(stats, valid[rows, :], branch, before)

    scatter.each_row(work)


def norm_sum_back(scatter, stream, gain, grad, gain_rows, put):
    gain_rows[...] = jnp.zeros_like(gain_rows)

    def work(rows, got):
        x = stream[rows, :].astype(jnp.float32)
        inv_rms = lax.rsqrt(jnp.mean(x * x, axis=-1, keepdims=True) + epsilon)
        scaled = gain[...] * got
        along = jnp.mean(scaled * x, axis=-1, keepdims=True)
        put(rows, grad[rows, :].astype(jnp.float32) + inv_rms * scaled - x * (inv_rms * inv_rms * inv_rms * along))
        gain_rows[...] += got * x * inv_rms

    scatter.each_row(work)


def rows_of(ref, lead, top_of, low_of):
    half = ref.shape[-2] // 2
    return jnp.concatenate([ref[(*lead, top_of, pl.ds(0, half))], ref[(*lead, low_of, pl.ds(half, half))]], axis=0)


def put_rows(ref, lead, top_of, low_of, value):
    half = ref.shape[-2] // 2
    ref[(*lead, top_of, pl.ds(0, half))] = value[:half].astype(ref.dtype)
    ref[(*lead, low_of, pl.ds(half, half))] = value[half:].astype(ref.dtype)


def greet_near(place, *more):
    greet({CTX: place[1]}, {CTX: place[2]}, *more)


def sibling():
    return {TP: 1 - lax.axis_index(TP)}


def mlp_rows(r, top_of, low_of, back):
    units = r.hidden.shape[-1]
    x = rows_of(r.full, (), top_of, low_of)
    total, g_total = 0.0, 0.0
    for t in range(r.weights.shape[0]):
        gate_act = dot32(x, r.weights[t, :, :units], ((1,), (0,)))
        up_act = dot32(x, r.weights[t, :, units : 2 * units], ((1,), (0,)))
        sig = jax.nn.sigmoid(gate_act)
        unit = (gate_act * sig * up_act).astype(jnp.bfloat16)
        put_rows(r.hidden, (t,), top_of, low_of, unit)
        total += dot32(unit, r.weights[t, :, 2 * units :], ((1,), (1,)))
        if back:
            g_total += mlp_back_rows(r, rows_of(r.grad_all, (), top_of, low_of), t, top_of, low_of, gate_act, up_act, sig)
        else:
            put_rows(r.gate, (t,), top_of, low_of, gate_act)
            put_rows(r.up, (t,), top_of, low_of, up_act)
    put_rows(r.part_out if back else r.part, (), top_of, low_of, total)
    if back:
        put_rows(r.part, (), top_of, low_of, g_total)


def mlp_back_rows(r, grad, t, top_of, low_of, gate_act, up_act, sig):
    units = r.grad_gate.shape[-1]
    g_hidden = dot32(grad, r.weights[t, :, 2 * units :], ((1,), (0,)))
    g_gate = (g_hidden * up_act * sig * (1.0 + gate_act * (1.0 - sig))).astype(jnp.bfloat16)
    g_up = (g_hidden * gate_act * sig).astype(jnp.bfloat16)
    put_rows(r.grad_gate, (t,), top_of, low_of, g_gate)
    put_rows(r.grad_up, (t,), top_of, low_of, g_up)
    total = dot32(g_gate, r.weights[t, :, :units], ((1,), (1,)))
    return total + dot32(g_up, r.weights[t, :, units : 2 * units], ((1,), (1,)))


def gathered_work(r, place, scatter, work, rows_own, own, cut=True):
    me, side_x, side_y, across = place
    steps = gather_rows(r.full, (r.ag_send, r.ag_recv), place, rows_own)
    next(steps)
    own.wait()
    work(me, me)
    next(steps)
    work(side_x, side_y)
    next(steps)
    work(side_y, side_x)
    scatter.x_out(0 if cut else None)
    scatter.y_out(0 if cut else None)
    run(steps)
    work(across, across)
    scatter.across()
    if cut:
        scatter.x_out(1)
        scatter.y_out(1)


def mlp_kernel(r):
    place = partners()
    me = place[0]
    own = pltpu.make_async_copy(r.normed, r.full.at[me], r.load.at[0])
    own.start()
    greet_near(place)
    scatter = Scatter(r.part, (r.from_x, r.from_y, r.passed, r.last), (r.rs_send, r.rs_recv), place)

    def work(top_of, low_of):
        r.need("weights")
        mlp_rows(r, top_of, low_of, False)

    gathered_work(r, place, scatter, work, r.normed, own)
    r.keep("full", "hidden", "gate", "up")
    scatter.forward()
    scatter.finish()
    r.need("middle")
    norm_sum(scatter, r.middle, r.gain, r.valid, r.stream, r.normed_next, r.stats)


def mlp_back_kernel(both, r):
    place = partners()
    me = place[0]
    own = pltpu.make_async_copy(r.rows_own, r.full.at[me], r.load.at[0])
    own.start()
    greet_near(place, sibling())
    scatter = Scatter(r.part, (r.from_x, r.from_y, r.passed, r.last), (r.rs_send, r.rs_recv), place)

    def both_rows(top_of, low_of):
        r.need("weights", "grad_all")
        mlp_rows(r, top_of, low_of, True)

    def back_rows(top_of, low_of):
        r.need("weights", "grad_gate", "grad_up")
        total = 0.0
        grad = rows_of(r.full, (), top_of, low_of)
        for t in range(r.weights.shape[0]):
            gate_act = rows_of(r.grad_gate, (t,), top_of, low_of).astype(jnp.float32)
            up_act = rows_of(r.grad_up, (t,), top_of, low_of).astype(jnp.float32)
            total += mlp_back_rows(r, grad, t, top_of, low_of, gate_act, up_act, jax.nn.sigmoid(gate_act))
        put_rows(r.part, (), top_of, low_of, total)

    gathered_work(r, place, scatter, both_rows if both else back_rows, r.rows_own, own, not both)
    if both:
        r.keep("part_out")
    normed, grad = (r.full, r.grad_all) if both else (r.normed, r.full)
    r.need("normed", "hidden")
    units = r.hidden.shape[-1]
    sent = [r.weights.at[0, :, pl.ds(p * units, units)] for p in range(3)]
    sums = WeightGrads(
        [normed, normed, grad], [r.grad_gate, r.grad_up, r.hidden], sent, [r.came_0, r.came_1, r.came_2],
        r.summed, (r.tp_send, r.tp_recv),
    )
    sums.theirs(0)
    sums.theirs(1)
    scatter.forward()
    job = None if both else gather_part(r.share, 0, r.gathered, r.load.at[1], r.ja_send, r.ja_recv, place)
    if job:
        next(job)
    sums.theirs(2)
    sums.ours(0)
    sums.ours(1)
    sums.ours(2)
    sums.add_up()
    r.keep("summed")
    scatter.finish()
    r.need("middle", "grad")

    def put(rows, total):
        r.grad_new[rows, :] = total
        r.grad_rows[rows, :] = total.astype(r.grad_rows.dtype)

    if job:
        next(job)
    norm_sum_back(scatter, r.middle, r.gain, r.grad, r.gain_rows, put)
    if job:
        run(job)
        r.keep("gathered")
    sums.close()


LOG2E = 1.4426950408889634


def turn(x, cos_row, sin_row):
    half_dim = HEAD_DIM // 2
    swapped = jnp.concatenate([x[:, half_dim:], x[:, :half_dim]], axis=1)
    return x * cos_row + swapped * sin_row


def project_rows(r, full, top_of, low_of):
    cols_q, base = 2 * HEAD_DIM, 4 * HEAD_DIM
    x = rows_of(full, (), top_of, low_of)
    cos_b, sin_b = rows_of(r.cosine, (), top_of, low_of), rows_of(r.sine, (), top_of, low_of)
    for t in range(r.weights.shape[0]):
        flat = dot32(x, r.weights[t, :, :base], ((1,), (0,)))
        for g in range(2):
            put_rows(r.query, (t, g), top_of, low_of, turn(flat[:, g * HEAD_DIM : (g + 1) * HEAD_DIM], cos_b, sin_b))
        put_rows(r.key, (t,), top_of, low_of, turn(flat[:, cols_q : cols_q + HEAD_DIM], cos_b, sin_b))
        put_rows(r.value, (t,), top_of, low_of, flat[:, cols_q + HEAD_DIM : base])


def attend_rows(r, owner):
    base = 4 * HEAD_DIM
    pairs, _, rows, _ = r.key.shape
    factor = HEAD_DIM ** (-0.5) * LOG2E

    for t in range(pairs):
        key = r.key[t].reshape(-1, HEAD_DIM)
        value = r.value[t].reshape(-1, HEAD_DIM)
        query = jnp.concatenate([r.query[t, 0, owner], r.query[t, 1, owner]], axis=0)
        raw = dot32(key, query, ((1,), (1,)))
        raw = raw * factor + r.bias[owner].astype(jnp.float32)
        top = jnp.max(raw, axis=0, keepdims=True)
        probs = jnp.exp2(raw - top)
        total = jnp.sum(probs, axis=0, keepdims=True)
        out = dot32(value, probs.astype(jnp.bfloat16), ((0,), (0,))) * (1.0 / total)
        fill = -out.shape[1] % 128
        out = jnp.concatenate([out, jnp.zeros((HEAD_DIM, fill), jnp.float32)], axis=1).T.astype(jnp.bfloat16)
        r.lse[t, owner] = top + jnp.log2(total)
        for g in range(2):
            r.mixed[t, owner, :, g * HEAD_DIM : (g + 1) * HEAD_DIM] = out[g * rows : (g + 1) * rows]

    total = 0.0
    for t in range(pairs):
        total += dot32(r.mixed[t, owner], r.weights[t, :, base : base + 2 * HEAD_DIM], ((1,), (1,)))
    r.part[owner] = total.astype(r.part.dtype)


def attend_kernel(first, r):
    place = partners()
    me, side_x, side_y, across = place
    rows_own = r.share.at[lax.axis_index(TP)] if first else r.normed
    own = pltpu.make_async_copy(rows_own, r.full.at[me], r.load.at[0])
    own.start()
    greet_near(place)
    steps = gather_rows(r.full, (r.ag_send, r.ag_recv), place, rows_own)
    next(steps)
    own.wait()
    rows = r.normed if first else r.full
    r.need("weights", "cosine", "sine", "normed")
    if first:
        for owner in range(4):
            project_rows(r, rows, owner, owner)
    else:
        project_rows(r, rows, me, me)
        next(steps)
        project_rows(r, rows, side_x, side_y)
        next(steps)
        project_rows(r, rows, side_y, side_x)
        run(steps)
        project_rows(r, rows, across, across)
        r.keep("full")
    r.keep("query", "key", "value")
    scatter = Scatter(r.part, (r.from_x, r.from_y, r.passed, r.last), (r.rs_send, r.rs_recv), place)
    r.need("bias")
    attend_rows(r, across)
    scatter.across()
    if first:
        next(steps)
    attend_rows(r, side_x)
    scatter.x_out()
    attend_rows(r, side_y)
    scatter.y_out()
    scatter.forward()
    attend_rows(r, me)
    r.keep("lse", "mixed")
    if first:
        run(steps)
        r.keep("full")
    scatter.finish()
    r.need("stream")
    norm_sum(scatter, r.stream, r.gain, r.valid, r.middle, r.normed_next, r.stats)


def attend_back_kernel(last, r):
    place = partners()
    me, side_x, side_y, across = place
    own = pltpu.make_async_copy(r.rows_own, r.full.at[me], r.load.at[0])
    own.start()
    greet_near(place, sibling())
    cols_q, base = 2 * HEAD_DIM, 4 * HEAD_DIM
    pairs = r.weights.shape[0]
    rows = r.full.shape[1]
    scale = HEAD_DIM ** (-0.5)
    factor = scale * LOG2E
    order = (me, side_x, side_y, across)
    masks = [pltpu.make_async_copy(r.bias_in.at[owner], r.bias.at[n % 2], r.bias_load.at[n]) for n, owner in enumerate(order)]
    masks[0].start()
    masks[1].start()
    r.g_key[...] = jnp.zeros_like(r.g_key)
    r.g_value[...] = jnp.zeros_like(r.g_value)

    def project(top_of, low_of):
        r.need("weights")
        x = rows_of(r.full, (), top_of, low_of)
        for t in range(pairs):
            flat = dot32(x, r.weights[t, :, base : base + cols_q], ((1,), (0,)))
            for g in range(2):
                put_rows(r.heads, (t, g), top_of, low_of, flat[:, g * HEAD_DIM : (g + 1) * HEAD_DIM])

    def two(ref, t, owner):
        return jnp.concatenate([ref[t, 0, owner], ref[t, 1, owner]], axis=0)

    def queries_back(n):
        owner = order[n]
        masks[n].wait()
        for t in range(pairs):
            query, heads = two(r.query, t, owner), two(r.heads, t, owner)
            mixed = r.mixed[t, owner].astype(jnp.float32)
            mixed = jnp.concatenate([mixed[:, :HEAD_DIM], mixed[:, HEAD_DIM:]], axis=0)
            along = lax.dot_general(
                jnp.ones((8, HEAD_DIM), jnp.float32), heads.astype(jnp.float32) * mixed, (((1,), (1,)), ((), ())),
                precision=lax.Precision.HIGHEST, preferred_element_type=jnp.float32,
            )[0:1]
            lse = r.lse[t, owner]
            r.g_query[...] = jnp.zeros_like(r.g_query)

            @pl.loop(0, jnp.minimum(owner + 2, 4))
            def _(kept):
                here = pl.ds(pl.multiple_of(kept * rows, 16), rows)
                key, value = r.key[t, kept], r.value[t, kept]
                raw = dot32(key, query, ((1,), (1,)))
                probs = jnp.exp2(raw * factor + r.bias[n % 2, here, :].astype(jnp.float32) - lse)
                g_probs = dot32(value, heads, ((1,), (1,)))
                g_scores = (probs * (g_probs - along)).astype(jnp.bfloat16)
                r.g_value[t, kept] += dot32(probs.astype(jnp.bfloat16), heads, ((1,), (0,)))
                r.g_key[t, kept] += dot32(g_scores, query, ((1,), (0,)))
                r.g_query[...] += dot32(key, g_scores, ((0,), (0,)))

            fill = jnp.zeros((HEAD_DIM, -2 * rows % 128), jnp.float32)
            g_query = jnp.concatenate([r.g_query[...], fill], axis=1).T * scale
            for g in range(2):
                r.grad_qkv[t, owner, :, g * HEAD_DIM : (g + 1) * HEAD_DIM] = turn(
                    g_query[g * rows : (g + 1) * rows], r.cosine[owner], -r.sine[owner]
                ).astype(jnp.bfloat16)
        if n + 2 < 4:
            masks[n + 2].start()

    steps = gather_rows(r.full, (r.ag_send, r.ag_recv), place, r.rows_own)
    next(steps)
    own.wait()
    project(me, me)
    r.need("key", "value", "query", "lse", "mixed", "cosine", "sine")
    queries_back(0)
    next(steps)
    jobs = [
        gather_part(r.share_a, 1, r.gathered_a, r.load.at[1], r.ja_send, r.ja_recv, place),
        gather_part(r.share_b, None, r.gathered_b, r.load.at[2], r.jb_send, r.jb_recv, place),
    ] if last else [end_steps(r, place)]
    for job in jobs:
        next(job)
    project(side_x, side_y)
    next(steps)
    project(side_y, side_x)
    queries_back(1)
    queries_back(2)
    run(steps)
    project(across, across)
    queries_back(3)

    @pl.loop(0, 4)
    def _(owner):
        for t in range(pairs):
            r.grad_qkv[t, owner, :, cols_q : cols_q + HEAD_DIM] = turn(
                r.g_key[t, owner] * scale, r.cosine[owner], -r.sine[owner]
            ).astype(jnp.bfloat16)
            r.grad_qkv[t, owner, :, cols_q + HEAD_DIM :] = r.g_value[t, owner].astype(jnp.bfloat16)

    def branch(owner):
        total = 0.0
        for t in range(pairs):
            total += dot32(r.grad_qkv[t, owner], r.weights[t, :, :base], ((1,), (1,)))
        r.part[owner] = total.astype(r.part.dtype)

    scatter = Scatter(r.part, (r.from_x, r.from_y, r.passed, r.last), (r.rs_send, r.rs_recv), place)
    if not last:
        for job in jobs:
            next(job)
    branch(across)
    scatter.across()
    branch(side_x)
    scatter.x_out()
    branch(side_y)
    scatter.y_out()
    branch(me)
    r.need("normed")
    sums = WeightGrads(
        [r.normed, r.full], [r.grad_qkv, r.mixed],
        [r.weights.at[0, :, pl.ds(0, base)], r.weights.at[1, :, pl.ds(0, r.came_1.shape[1])]], [r.came_0, r.came_1],
        r.summed, (r.tp_send, r.tp_recv),
    )
    sums.theirs(0)
    scatter.forward()
    if last:
        for job in jobs:
            next(job)
    sums.theirs(1)
    sums.ours(0)
    sums.ours(1)
    r.summed[:, base + cols_q :] = jnp.zeros((r.summed.shape[0], r.summed.shape[1] - base - cols_q), jnp.bfloat16)
    sums.add_up()
    r.keep("summed")
    if not last:
        for job in jobs:
            run(job)
        r.keep("out")
    scatter.finish()
    r.need("stream", "grad")
    side = lax.axis_index(TP)

    def put(here, total):
        if last:
            r.grad_new[side, here, :] = total
        else:
            r.grad_new[here, :] = total
            r.grad_rows[here, :] = total.astype(r.grad_rows.dtype)

    norm_sum_back(scatter, r.stream, r.gain, r.grad, r.gain_rows, put)
    handed = []
    if last:
        handed.append(send(r.grad_new.at[side], r.grad_new.at[side], (r.tp_send, r.tp_recv), 2, sibling()))
    if last:
        for job in jobs:
            run(job)
        r.keep("gathered_a", "gathered_b")
    for copy in handed:
        copy.wait()
    sums.close()


def end_steps(r, place):
    side = lax.axis_index(TP)
    r.need("end_part")
    scatter = Scatter(
        r.end_part, (r.end_from_x, r.end_from_y, r.end_passed, r.end_last), (r.end_send, r.end_recv), place
    )
    yield from scatter_steps(scatter)

    r.stats[...] = jnp.zeros_like(r.stats)

    def work(rows, branch):
        r.out[side, rows, :] = (r.end_middle[rows, :] + branch).astype(r.out.dtype)
        add_stats(r.stats, r.valid[rows, :], branch)

    r.need("end_middle")
    scatter.each_row(work)
    send(r.out.at[side], r.out.at[side], (r.out_send, r.out_recv), 0, sibling()).wait()


def gather_part(share, part_no, full, local_sem, send_sems, recv_sems, place):
    rows = full.shape[1]
    src = share if part_no is None else share.at[pl.ds(part_no * rows, rows)]
    copy = pltpu.make_async_copy(src, full.at[place[0]], local_sem)
    copy.start()
    yield from gather_rows(full, (send_sems, recv_sems), place, src)
    copy.wait()


class Refs:
    def need(self, *names):
        for name in names:
            if name in self.loads:
                self.loads.pop(name).wait()

    def keep(self, *names):
        for name in names:
            src, dst, sem = self.late[name]
            store = pltpu.make_async_copy(src, dst, sem)
            store.start()
            self.stores.append(store)


def linked(kernel, number, micros, near, far, lazy, outs, late, scratch):
    names = [*near, *far, *lazy, *outs, *late, *scratch]
    halves = [name for name, value in lazy.items() if isinstance(value, tuple)]
    lazy = {name: value[0] if name in halves else value for name, value in lazy.items()}
    lazy_rooms = [pltpu.VMEM(v.shape[1:] if name in halves else v.shape, v.dtype) for name, v in lazy.items()]
    lazy_names, late_names = list(lazy), list(late)

    def body(*refs):
        r = Refs()
        count = len(names)
        rest = list(refs[count:])
        by_name = dict(zip(names, refs))
        r.loads, r.late, r.stores = {}, {}, []
        held = rest[: len(lazy) + len(late)]
        for n, name in enumerate(lazy_names):
            src = by_name[name].at[lax.axis_index(TP)] if name in halves else by_name[name]
            r.loads[name] = pltpu.make_async_copy(src, held[n], rest[-2].at[n])
            by_name[name] = held[n]
        for n, name in enumerate(late_names):
            r.late[name] = (held[len(lazy) + n], by_name[name], rest[-1].at[n])
            by_name[name] = held[len(lazy) + n]
        for name, ref in by_name.items():
            setattr(r, name, ref)
        for load in r.loads.values():
            load.start()
        kernel(r)
        r.need(*lazy_names)
        for store in r.stores:
            store.wait()

    vmem = pl.BlockSpec(memory_space=pltpu.VMEM)
    hbm = pl.BlockSpec(memory_space=pl.ANY)
    came = pl.pallas_call(
        body,
        out_shape=[*outs.values(), *late.values()],
        in_specs=[vmem] * len(near) + [hbm] * (len(far) + len(lazy)),
        out_specs=[vmem] * len(outs) + [hbm] * len(late),
        scratch_shapes=[
            *scratch.values(), *lazy_rooms, *map(room, late.values()),
            pltpu.SemaphoreType.DMA((max(1, len(lazy)),)), pltpu.SemaphoreType.DMA((max(1, len(late)),)),
        ],
        compiler_params=pltpu.CompilerParams(
            collective_id=number, has_side_effects=True, vmem_limit_bytes=61 << 20
        ),
        cost_estimate=pl.CostEstimate(flops=0, bytes_accessed=int(micros * 3.6e6), transcendentals=0),
    )(*near.values(), *far.values(), *lazy.values())
    result = Refs()
    for name, value in zip([*outs, *late], came):
        setattr(result, name, value)
    return result


def sems(name, count):
    return {f"{name}_send": pltpu.SemaphoreType.DMA((count,)), f"{name}_recv": pltpu.SemaphoreType.DMA((count,))}


def sum_room(rows, width, prefix=""):
    names = ("from_x", "from_y", "passed", "last")
    return {prefix + name: pltpu.VMEM((2, rows // 2, width), jnp.bfloat16) for name in names}


def shape16(*dims):
    return jax.ShapeDtypeStruct(dims, jnp.bfloat16)


def shape32(*dims):
    return jax.ShapeDtypeStruct(dims, jnp.float32)


def room(like):
    return pltpu.VMEM(like.shape, like.dtype)


def mlp_step(normed, middle, gain, valid, weights):
    rows, width = middle.shape
    pairs, units = weights.shape[0], weights.shape[2] // 3
    kept = shape16(pairs, 4, rows, units)
    return linked(
        mlp_kernel, 12, 75,
        dict(gain=gain, valid=valid), dict(normed=normed), dict(weights=weights, middle=middle),
        dict(stream=shape32(rows, width), normed_next=shape16(rows, width), stats=shape32(16, 128)),
        dict(full=shape16(4, rows, width), hidden=kept, gate=kept, up=kept),
        dict(
            part=pltpu.VMEM((4, rows, width), jnp.bfloat16), load=pltpu.SemaphoreType.DMA((1,)),
            **sum_room(rows, width), **sems("ag", 6), **sems("rs", 8),
        ),
    )


def mlp_back_step(rows_own, middle, gain, grad, weights, grad_all=None, kept=None, share=None):
    rows, width = middle.shape
    pairs, units = weights.shape[0], weights.shape[2] // 3
    both = grad_all is not None
    whole, unit = shape16(4, rows, width), shape16(pairs, 4, rows, units)
    far = dict(rows_own=rows_own)
    lazy = dict(weights=weights)
    late = dict(summed=shape16(width, 3 * units))
    scratch = dict(
        full=room(whole), part=room(whole), load=pltpu.SemaphoreType.DMA((2,)),
        **{f"came_{p}": pltpu.VMEM((width, units), jnp.bfloat16) for p in range(3)},
        **sum_room(rows, width), **sems("ag", 6), **sems("rs", 8), **sems(TP, 3),
    )
    if both:
        lazy["grad_all"] = grad_all
        late["part_out"] = whole
        scratch.update(grad_gate=room(unit), grad_up=room(unit), hidden=room(unit))
    else:
        far["share"] = share
        lazy.update(grad_gate=kept.gate, grad_up=kept.up, hidden=kept.hidden, normed=kept.full)
        late["gathered"] = shape16(4, share.shape[0] // 2, share.shape[1])
        scratch.update(**sems("ja", 6))
    lazy.update(middle=middle, grad=grad)
    return linked(
        functools.partial(mlp_back_kernel, both), 13 if both else 5, 85,
        dict(gain=gain), far, lazy,
        dict(grad_new=shape32(rows, width), grad_rows=shape16(rows, width), gain_rows=shape32(16, width)),
        late, scratch,
    )


def attend_step(normed, stream, gain, valid, weights, cosine, sine, bias, share=None):
    first = share is not None
    rows, width = stream[0].shape[1:] if first else stream.shape
    pairs = weights.shape[0]
    far, lazy = {}, dict(weights=weights, cosine=cosine, sine=sine)
    if first:
        far["share"] = share
        lazy["normed"] = normed
    else:
        far["normed"] = normed
    lazy.update(bias=bias, stream=stream)
    return linked(
        functools.partial(attend_kernel, first), 11 if first else 9, 75,
        dict(gain=gain, valid=valid), far, lazy,
        dict(middle=shape32(rows, width), normed_next=shape16(rows, width), stats=shape32(16, 128)),
        dict(
            full=shape16(4, rows, width), query=shape16(pairs, 2, 4, rows, HEAD_DIM),
            key=shape16(pairs, 4, rows, HEAD_DIM), value=shape16(pairs, 4, rows, HEAD_DIM),
            lse=shape32(pairs, 4, 1, 2 * rows), mixed=shape16(pairs, 4, rows, 2 * HEAD_DIM),
        ),
        dict(
            part=pltpu.VMEM((4, rows, width), jnp.bfloat16), load=pltpu.SemaphoreType.DMA((1,)),
            **sum_room(rows, width), **sems("ag", 6), **sems("rs", 8),
        ),
    )


def attend_back_step(
    rows_own, stream, gain, grad, weights, cosine, sine, bias, kept, normed, shares=None, end=None
):
    rows, width = rows_own.shape
    pairs = weights.shape[0]
    length = 4 * rows
    last = shares is not None
    whole = shape16(4, rows, width)
    near = dict(gain=gain)
    far = dict(rows_own=rows_own, bias_in=bias)
    lazy = dict(
        weights=weights, key=kept.key, value=kept.value, query=kept.query, lse=kept.lse, mixed=kept.mixed,
        cosine=cosine, sine=sine, normed=normed, stream=stream, grad=grad,
    )
    sizes = (4 * HEAD_DIM, 2 * HEAD_DIM)
    total = sum(sizes) + 64
    outs = dict(gain_rows=shape32(16, width))
    late = dict(summed=shape16(width, total))
    scratch = dict(
        full=room(whole), part=room(whole),
        heads=room(kept.query), g_key=pltpu.VMEM(kept.key.shape, jnp.float32),
        g_value=pltpu.VMEM(kept.key.shape, jnp.float32), g_query=pltpu.VMEM((HEAD_DIM, 2 * rows), jnp.float32),
        grad_qkv=pltpu.VMEM((pairs, 4, rows, sizes[0]), jnp.bfloat16),
        bias=pltpu.VMEM((2, length, 2 * rows), jnp.bfloat16), bias_load=pltpu.SemaphoreType.DMA((4,)),
        came_0=pltpu.VMEM((width, sizes[0]), jnp.bfloat16), came_1=pltpu.VMEM((width, 256), jnp.bfloat16),
        load=pltpu.SemaphoreType.DMA((3,)),
        **sum_room(rows, width), **sems("ag", 6), **sems("rs", 8), **sems(TP, 4),
    )
    if last:
        far.update(share_a=shares[0], share_b=shares[1])
        outs.update(grad_new=shape32(2, rows, width))
        late.update(
            gathered_a=shape16(4, shares[0].shape[0] // 2, shares[0].shape[1]),
            gathered_b=shape16(4, *shares[1].shape),
        )
        scratch.update(**sems("ja", 6), **sems("jb", 6))
    else:
        lazy = dict(end_part=end[0], **lazy, end_middle=end[1])
        near["valid"] = end[2]
        outs.update(grad_new=shape32(rows, width), grad_rows=shape16(rows, width), stats=shape32(16, 128))
        late["out"] = shape16(2, rows, width)
        scratch.update(**sum_room(rows, width, "end_"), **sems("end", 6), **sems("out", 1))
    return linked(
        functools.partial(attend_back_kernel, last), 7 if last else 6, 100, near, far, lazy, outs, late, scratch,
    )


def tail_step(summed, share, attn_stats, mlp_stats, gain_rows):
    depth = lax.axis_size(FSDP)
    half, cols = share.shape[0] // 2, summed.shape[1]
    last = shape16(4, half, cols)
    wide = summed.shape[0] + 128
    return linked(
        functools.partial(tail_kernel, summed.shape[0]), 10, 60,
        dict(
            summed=summed,
            **{f"attn_stats_{layer}": a for layer, a in enumerate(attn_stats)},
            **{f"mlp_stats_{layer}": a for layer, a in enumerate(mlp_stats)},
            **{f"gain_rows_{n}": a for n, a in enumerate(gain_rows)},
        ),
        dict(share=share), {},
        dict(last_0=last, last_1=last, all_stats=shape32(8, 128), gains=shape32(8, summed.shape[0] // depth)), dict(gathered=shape16(4, *share.shape)),
        dict(
            z_came=pltpu.VMEM((2, depth, half, cols), jnp.bfloat16), stat_sent=pltpu.VMEM((4, 8, wide), jnp.float32),
            stat_came=pltpu.VMEM((3, 8, wide), jnp.float32), stat_z=pltpu.VMEM((depth, 8, wide), jnp.float32),
            load=pltpu.SemaphoreType.DMA((1,)), **sems("z", 2 * depth), **sems("ag", 6), **sems("stat", 3 + depth),
            **sems("l0", 6), **sems("l1", 6),
        ),
    )


def start_step(gains, places, starts, x, gate, up, down):
    depth, across = lax.axis_size(FSDP), lax.axis_size(CTX)
    layers, rows = gate.shape[:2]
    units = gate.shape[2] // across
    own = x.shape[1:]
    length = across * own[0]
    return linked(
        start_kernel, 8, 38,
        dict(gains=gains, places=places, starts=starts), dict(x=x, gate=gate, up=up, down=down), {},
        dict(
            all_gains=jax.ShapeDtypeStruct((depth, *gains.shape), gains.dtype),
            normed=shape16(across, *own),
        ),
        dict(
            bias=shape16(across, length, 2 * own[0]), cosine=shape32(across, own[0], HEAD_DIM),
            sine=shape32(across, own[0], HEAD_DIM),
            **{f"packed_{layer}": shape16(rows, 3 * units) for layer in range(layers)},
        ),
        dict(
            all_places=pltpu.VMEM((across, *places.shape), places.dtype),
            full=pltpu.VMEM((across, *own), jnp.bfloat16), turned=pltpu.VMEM((layers, units, rows), jnp.bfloat16),
            load=pltpu.SemaphoreType.DMA((3 + 3 * layers,)), **sems("gain", depth), **sems("place", across),
            **sems("ag", 6),
        ),
    )


def planned(
    tokens, positions, valid, piece_starts, d_out,
    attn_gain, w_query, w_key, w_value, w_out, mlp_gain, w_gate, w_up, w_down,
):
    seq_count, rows, width = tokens.shape
    layers = attn_gain.shape[0]
    ctx_count = lax.axis_size(CTX)
    tp_count = lax.axis_size(TP)
    me = lax.axis_index(CTX)
    side = lax.axis_index(TP)
    length = rows * ctx_count
    heads_q = HEADS // tp_count // ctx_count
    heads_k = KV_HEADS // tp_count // ctx_count
    cols_q = heads_q * HEAD_DIM
    cols_k = heads_k * HEAD_DIM
    units = w_gate.shape[2] // ctx_count

    def own(a):
        return lax.dynamic_index_in_dim(a, side, 0, keepdims=False)

    def cut(w, axis, count):
        return lax.dynamic_slice_in_dim(w, me * count, count, axis)

    def whole(w):
        return lax.all_gather(w, (TP, FSDP), axis=0, tiled=True).reshape(
            tp_count, width, w.shape[1]
        )

    def pack(*pieces):
        return with_layout_constraint(jnp.concatenate(pieces, axis=1), Layout(major_to_minor=(0, 1)))

    def pack_attn(layer, w_query, w_key, w_value, w_out):
        return pack(
            cut(w_query[layer], 1, cols_q),
            cut(w_key[layer], 1, cols_k),
            cut(w_value[layer], 1, cols_k),
            cut(w_out[layer], 0, cols_q).T,
            jnp.zeros((w_query.shape[1], 64), w_query.dtype),
        )

    attn_w = [whole(pack_attn(0, w_query, w_key, w_value, w_out))]
    seq_pos, valid_f = own(positions), own(valid).astype(jnp.float32)[:, None]
    half_dim = HEAD_DIM // 2
    freqs = rope_base ** (-(jnp.arange(half_dim).astype(jnp.float32) * 2.0 / HEAD_DIM))
    angles = seq_pos.astype(jnp.float32)[:, None] * freqs
    begun = start_step(
        jnp.pad(jnp.concatenate([attn_gain, mlp_gain], 0).astype(jnp.float32), ((0, 8 - 2 * layers), (0, 0))),
        jnp.concatenate([jnp.cos(angles), jnp.sin(angles), valid_f, jnp.zeros((rows, 127 - HEAD_DIM), jnp.float32)], axis=1),
        own(piece_starts)[None], tokens, w_gate, w_up, w_down,
    )
    normed, bias = begun.normed, begun.bias
    packed_mlp = [getattr(begun, f"packed_{layer}") for layer in range(layers)]
    gains = begun.all_gains.swapaxes(0, 1).reshape(8, width)
    cosine, sine_t = begun.cosine, begun.sine
    gain_a = [gains[layer][None] for layer in range(layers)]
    gain_m = [gains[layers + layer][None] for layer in range(layers)]
    grad = (d_out,)
    mlp_w = [whole(packed_mlp[0])]

    streams, attends, mlps = [(tokens,)], [], []
    for layer in range(layers):
        kept = attend_step(
            normed, streams[layer], gain_m[layer], valid_f, attn_w[layer], cosine, sine_t, bias,
            None if layer else d_out,
        )
        if layer == 0:
            grad_all, kept.full = kept.full, normed
        attends.append(kept)
        if layer + 1 < layers:
            normed_m, w_query, w_key, w_value, w_out, packed_mlp[layer + 1] = lax.optimization_barrier(
                (kept.normed_next, w_query, w_key, w_value, w_out, packed_mlp[layer + 1])
            )
            attn_w.append(whole(pack_attn(layer + 1, w_query, w_key, w_value, w_out)))
            mlp_w.append(whole(packed_mlp[layer + 1]))
            mlps.append(mlp_step(normed_m, kept.middle, gain_a[layer + 1], valid_f, mlp_w[layer]))
            streams.append(mlps[layer].stream)
            normed = mlps[layer].normed_next

    def reduced(g):
        return lax.psum_scatter(g, FSDP, scatter_dimension=0, tiled=True)

    down_rows = None
    attn_gains, mlp_gains = [], []
    for layer in reversed(range(layers)):
        kept = attends[layer]
        if layer + 1 == layers:
            came = mlp_back_step(kept.normed_next, kept.middle, gain_m[layer], grad, mlp_w[layer], grad_all=grad_all)
            end = [came.part_out, kept.middle, valid_f]
        else:
            came = mlp_back_step(
                down_rows, kept.middle, gain_m[layer], grad, mlp_w[layer], kept=mlps[layer], share=shares[0]
            )
        mlp_share = reduced(came.summed)
        mlp_gains.insert(0, came.gain_rows)
        back = attend_back_step(
            came.grad_rows, streams[layer], gain_a[layer], came.grad_new, attn_w[layer], cosine, sine_t, bias,
            kept, kept.full, None if layer else shares, end if layer else None,
        )
        attn_gains.insert(0, back.gain_rows)
        if layer:
            grad, output = back.grad_new, back.out
            down_rows, mlp_share, summed = lax.optimization_barrier((back.grad_rows, mlp_share, back.summed))
            shares = [mlp_share, reduced(summed)]
            last_stats = back.stats
    ended = tail_step(
        back.summed, mlp_share, [kept.stats for kept in attends], [kept.stats for kept in mlps] + [last_stats],
        attn_gains + mlp_gains,
    )
    input_grad = back.grad_new
    mlp_all = [[ended.gathered], [came.gathered, back.gathered_a]]
    attn_all = [[ended.last_0, ended.last_1], [back.gathered_b]]
    rms_stats = ended.all_stats[0, : 3 * layers].reshape(layers, 3)
    base = cols_q + 2 * cols_k
    placed = place_outs(
        attn_all, mlp_all,
        [(0, cols_q, False), (cols_q, cols_k, False), (cols_q + cols_k, cols_k, False), (base, cols_q, True)],
        [(0, units, False), (units, units, False), (2 * units, units, True)],
        [output, input_grad],
    )
    gains = ended.gains
    return (
        *placed[7:], gains[:layers], *placed[:4], gains[layers : 2 * layers], *placed[4:7], rms_stats,
    )


def place_kernel(moves, count, more, *refs):
    refs = list(refs)
    outs_count = 1 + max(out for _, _, pieces in moves for _, _, _, out in pieces)
    ins, outs = refs[: count + more], refs[count + more : count + outs_count + 2 * more]
    del refs[: count + outs_count + 2 * more]
    held, laid = refs[: count + more], refs[count + more : -2]
    in_sems, out_sems = refs[-2:]
    loads = [pltpu.make_async_copy(ins[n], held[n], in_sems.at[n]) for n in range(count + more)]
    for load in loads:
        load.start()
    stores = []
    for n in range(more):
        loads[count + n].wait()
        store = pltpu.make_async_copy(held[count + n], outs[outs_count + n], out_sems.at[len(stores)])
        store.start()
        stores.append(store)
    for n, (layer, first, pieces) in enumerate(moves):
        loads[n].wait()
        rows = held[n].shape[1]
        for start, size, flip, out in pieces:
            for c in range(held[n].shape[0]):
                block = held[n][c, :, start : start + size].astype(jnp.float32)
                if flip:
                    laid[out][layer, c * size : (c + 1) * size, first : first + rows] = block.T
                else:
                    laid[out][layer, first : first + rows, c * size : (c + 1) * size] = block
            if any(layer == l and out == o for l, _, more in moves[n + 1 :] for _, _, _, o in more):
                continue
            store = pltpu.make_async_copy(laid[out].at[layer], outs[out].at[layer], out_sems.at[len(stores)])
            store.start()
            stores.append(store)
    for store in stores:
        store.wait()


def place_outs(attn_all, mlp_all, attn_pieces, mlp_pieces, handed):
    layers = len(attn_all)
    shapes = []
    for came, pieces in ((attn_all, attn_pieces), (mlp_all, mlp_pieces)):
        ctx_count = came[0][0].shape[0]
        depth = sum(a.shape[1] for a in came[0])
        for _, size, flip in pieces:
            wide = ctx_count * size
            shapes.append((layers, wide, depth) if flip else (layers, depth, wide))
    ins, moves = [], []
    for layer in reversed(range(layers)):
        for came, pieces, base in ((mlp_all, mlp_pieces, len(attn_pieces)), (attn_all, attn_pieces, 0)):
            first = 0
            for a in came[layer]:
                ins.append(a)
                moves.append((layer, first, [(*piece, base + n) for n, piece in enumerate(pieces)]))
                first += a.shape[1]
    hbm = pl.BlockSpec(memory_space=pl.ANY)
    return pl.pallas_call(
        functools.partial(place_kernel, moves, len(ins), len(handed)),
        out_shape=[jax.ShapeDtypeStruct(s, jnp.float32) for s in shapes]
        + [jax.ShapeDtypeStruct(a.shape, a.dtype) for a in handed],
        in_specs=[hbm] * (len(ins) + len(handed)),
        out_specs=[hbm] * (len(shapes) + len(handed)),
        scratch_shapes=[pltpu.VMEM(a.shape, a.dtype) for a in ins + handed]
        + [pltpu.VMEM(s, jnp.float32) for s in shapes]
        + [pltpu.SemaphoreType.DMA((len(ins) + len(handed),)),
           pltpu.SemaphoreType.DMA((layers * len(shapes) + len(handed),))],
        compiler_params=pltpu.CompilerParams(vmem_limit_bytes=60 << 20),
    )(*ins, *handed)


def fits(mesh):
    tp_count, ctx_count = mesh.shape[TP], mesh.shape[CTX]
    return ctx_count == 4 and tp_count == 2


def solution(mesh):
    in_specs = (
        P(FSDP, CTX, None),
        P(FSDP, CTX),
        P(FSDP, CTX),
        P(FSDP, None),
        P(FSDP, CTX, None),
        P(None, FSDP),
        P(None, FSDP, TP),
        P(None, FSDP, TP),
        P(None, FSDP, TP),
        P(None, TP, FSDP),
        P(None, FSDP),
        P(None, FSDP, TP),
        P(None, FSDP, TP),
        P(None, TP, FSDP),
    )
    out_specs = (
        P(FSDP, CTX, None),
        P(FSDP, CTX, None),
        P(None, FSDP),
        P(None, FSDP, TP),
        P(None, FSDP, TP),
        P(None, FSDP, TP),
        P(None, TP, FSDP),
        P(None, FSDP),
        P(None, FSDP, TP),
        P(None, FSDP, TP),
        P(None, TP, FSDP),
        P(),
    )
    return jax.shard_map(planned if fits(mesh) else general, mesh=mesh, in_specs=in_specs, out_specs=out_specs, check_vma=False)
```

```python
import functools

import jax
import jax.numpy as jnp
from jax import lax
from jax.experimental import pallas as pl
from jax.experimental.layout import Layout, with_layout_constraint
from jax.experimental.pallas import tpu as pltpu
from jax.sharding import PartitionSpec as P

MESH = pl.DeviceIdType.MESH
FSDP, CTX, TP = "fsdp", "ctx", "tp"

HEADS = 16
KV_HEADS = 8
HEAD_DIM = 96
PIECE_LEN = 256


epsilon = 1e-05
rope_base = 100000.0
neg_big = -1e30


def rope_tables(positions, head_dim):
    half_dim = head_dim // 2
    freqs = rope_base ** (-(jnp.arange(half_dim).astype(jnp.float32) * 2.0 / head_dim))
    angles = positions.astype(jnp.float32)[..., None] * freqs
    return (jnp.cos(angles)[:, :, None, :], jnp.sin(angles)[:, :, None, :])


def rotate(values, cosine, sine_t):
    half_dim = values.shape[-1] // 2
    lead_part = values[..., :half_dim]
    tail_part = values[..., half_dim:]
    return jnp.concatenate(
        [lead_part * cosine - tail_part * sine_t, tail_part * cosine + lead_part * sine_t], axis=-1
    )


def normalize(stream, gain_vec):
    inv_rms = lax.rsqrt(jnp.mean(stream * stream, axis=-1, keepdims=True) + epsilon)
    return stream * inv_rms * gain_vec.astype(jnp.float32)


def norm_back(stream, gain_vec, grad_out):
    inv_rms = lax.rsqrt(jnp.mean(stream * stream, axis=-1, keepdims=True) + epsilon)
    scaled_grad = gain_vec.astype(jnp.float32) * grad_out
    grad_in = inv_rms * scaled_grad - stream * inv_rms**3 * jnp.mean(
        scaled_grad * stream, axis=-1, keepdims=True
    )
    grad_gain = jnp.sum(grad_out * stream * inv_rms, axis=0)
    return (grad_in, grad_gain)


def score_block(query_b, key_heads, allowed, score_scale):
    raw_scores = (
        jnp.einsum("sckgd,snkd->skgcn", query_b, key_heads, preferred_element_type=jnp.float32)
        * score_scale
    )
    return jnp.where(allowed[:, None, None], raw_scores, neg_big)


def general(
    tokens,
    positions,
    valid,
    piece_starts,
    d_out,
    attn_gain,
    w_query,
    w_key,
    w_value,
    w_out,
    mlp_gain,
    w_gate,
    w_up,
    w_down,
):
    seq_count, shard_len, model_width = tokens.shape
    tok_rows = seq_count * shard_len
    tp_count = lax.axis_size(TP)
    local_heads = HEADS // tp_count
    local_kv = KV_HEADS // tp_count
    group_size = HEADS // KV_HEADS
    score_scale = HEAD_DIM ** (-0.5)
    seq_length = shard_len * lax.axis_size(CTX)
    start_tok = lax.axis_index(CTX) * shard_len
    query_index = start_tok + jnp.arange(shard_len, dtype=jnp.int32)
    key_index = jnp.arange(seq_length, dtype=jnp.int32)
    cosine, sine_t = rope_tables(positions, HEAD_DIM)
    valid_flat = valid.astype(jnp.float32).reshape(tok_rows)
    in_query = (query_index[None, None, :] >= piece_starts[:, :, None]) & (
        query_index[None, None, :] < piece_starts[:, :, None] + PIECE_LEN
    )
    in_key = (key_index[None, None, :] >= piece_starts[:, :, None]) & (
        key_index[None, None, :] < piece_starts[:, :, None] + PIECE_LEN
    )
    same_piece = jnp.any(in_query[:, :, :, None] & in_key[:, :, None, :], axis=1)
    causal = key_index[None, :] <= query_index[:, None]
    diagonal = key_index[None, :] == query_index[:, None]
    layer_count = attn_gain.shape[0]
    stream = tokens.astype(jnp.float32).reshape(tok_rows, model_width)
    saved = []
    stat_rows = []
    for layer_no in range(layer_count):
        weights = (
            lax.all_gather(attn_gain[layer_no], FSDP, axis=0, tiled=True),
            lax.all_gather(w_query[layer_no], FSDP, axis=0, tiled=True),
            lax.all_gather(w_key[layer_no], FSDP, axis=0, tiled=True),
            lax.all_gather(w_value[layer_no], FSDP, axis=0, tiled=True),
            lax.all_gather(w_out[layer_no], FSDP, axis=1, tiled=True),
            lax.all_gather(mlp_gain[layer_no], FSDP, axis=0, tiled=True),
            lax.all_gather(w_gate[layer_no], FSDP, axis=0, tiled=True),
            lax.all_gather(w_up[layer_no], FSDP, axis=0, tiled=True),
            lax.all_gather(w_down[layer_no], FSDP, axis=1, tiled=True),
        )
        gain_a, w_q, w_k, w_v, w_o, gain_m, w_g, w_u, w_d = weights
        normed_a = normalize(stream, gain_a).astype(jnp.bfloat16)
        query_heads = jnp.dot(normed_a, w_q, preferred_element_type=jnp.float32).reshape(
            seq_count, shard_len, local_heads, HEAD_DIM
        )
        query_b = (
            rotate(query_heads, cosine, sine_t)
            .astype(jnp.bfloat16)
            .reshape(seq_count, shard_len, local_kv, group_size, HEAD_DIM)
        )
        key_local = jnp.dot(normed_a, w_k, preferred_element_type=jnp.float32).reshape(
            seq_count, shard_len, local_kv, HEAD_DIM
        )
        key_local = (
            rotate(key_local, cosine, sine_t)
            .astype(jnp.bfloat16)
            .reshape(seq_count, shard_len, local_kv * HEAD_DIM)
        )
        value_local = (
            jnp.dot(normed_a, w_v, preferred_element_type=jnp.float32)
            .astype(jnp.bfloat16)
            .reshape(seq_count, shard_len, local_kv * HEAD_DIM)
        )
        key_all, value_all, valid_all = (
            lax.all_gather(key_local, CTX, axis=1, tiled=True),
            lax.all_gather(value_local, CTX, axis=1, tiled=True),
            lax.all_gather(valid.astype(jnp.bfloat16), CTX, axis=1, tiled=True),
        )
        allowed = (causal[None] | same_piece) & ((valid_all[:, None, :] > 0.5) | diagonal[None])
        key_heads = key_all.reshape(seq_count, seq_length, local_kv, HEAD_DIM)
        value_heads = value_all.reshape(seq_count, seq_length, local_kv, HEAD_DIM)
        raw_scores = score_block(query_b, key_heads, allowed, score_scale)
        row_max = jnp.max(raw_scores, axis=-1, keepdims=True)
        log_total = row_max + jnp.log(
            jnp.sum(jnp.exp(raw_scores - row_max), axis=-1, keepdims=True)
        )
        softmax_b = jnp.exp(raw_scores - log_total).astype(jnp.bfloat16)
        mixed_heads = jnp.einsum(
            "skgcn,snkd->sckgd", softmax_b, value_heads, preferred_element_type=jnp.float32
        )
        mixed_b = mixed_heads.astype(jnp.bfloat16).reshape(tok_rows, local_heads * HEAD_DIM)
        attn_branch = lax.psum(
            jnp.dot(mixed_b, w_o, preferred_element_type=jnp.float32).astype(jnp.bfloat16), TP
        ).astype(jnp.float32)
        middle = stream + attn_branch
        normed_m = normalize(middle, gain_m).astype(jnp.bfloat16)
        gate_act = jnp.dot(normed_m, w_g, preferred_element_type=jnp.float32)
        up_act = jnp.dot(normed_m, w_u, preferred_element_type=jnp.float32)
        hidden = (jax.nn.silu(gate_act) * up_act).astype(jnp.bfloat16)
        mlp_branch = lax.psum(
            jnp.dot(hidden, w_d, preferred_element_type=jnp.float32).astype(jnp.bfloat16), TP
        ).astype(jnp.float32)
        stat_rows.append(
            jnp.stack(
                [
                    jnp.sum(valid_flat[:, None] * stream * stream),
                    jnp.sum(valid_flat[:, None] * attn_branch * attn_branch),
                    jnp.sum(valid_flat[:, None] * mlp_branch * mlp_branch),
                ]
            )
        )
        kept_weights = None
        saved.append(
            (
                stream,
                normed_a,
                query_b,
                key_heads,
                value_heads,
                allowed,
                log_total,
                mixed_b,
                middle,
                normed_m,
                gate_act,
                up_act,
                hidden,
                kept_weights,
            )
        )
        stream = middle + mlp_branch
    output = stream.astype(jnp.bfloat16).reshape(seq_count, shard_len, model_width)
    total_squares, total_count = lax.psum(
        (jnp.stack(stat_rows), jnp.sum(valid_flat)), (FSDP, CTX)
    )
    rms_stats = jnp.sqrt(total_squares / (total_count * model_width))
    grad_stream = d_out.astype(jnp.float32).reshape(tok_rows, model_width)
    results = [None] * layer_count
    for layer_no in reversed(range(layer_count)):
        (
            stream_in,
            normed_a,
            query_b,
            key_heads,
            value_heads,
            allowed,
            log_total,
            mixed_b,
            middle,
            normed_m,
            gate_act,
            up_act,
            hidden,
            kept_weights,
        ) = saved[layer_no]
        weights = (
            lax.all_gather(attn_gain[layer_no], FSDP, axis=0, tiled=True),
            lax.all_gather(w_query[layer_no], FSDP, axis=0, tiled=True),
            lax.all_gather(w_key[layer_no], FSDP, axis=0, tiled=True),
            lax.all_gather(w_value[layer_no], FSDP, axis=0, tiled=True),
            lax.all_gather(w_out[layer_no], FSDP, axis=1, tiled=True),
            lax.all_gather(mlp_gain[layer_no], FSDP, axis=0, tiled=True),
            lax.all_gather(w_gate[layer_no], FSDP, axis=0, tiled=True),
            lax.all_gather(w_up[layer_no], FSDP, axis=0, tiled=True),
            lax.all_gather(w_down[layer_no], FSDP, axis=1, tiled=True),
        )
        gain_a, w_q, w_k, w_v, w_o, gain_m, w_g, w_u, w_d = weights
        grad_mlp = grad_stream.astype(jnp.bfloat16)
        grad_hidden = jnp.einsum("rd,fd->rf", grad_mlp, w_d, preferred_element_type=jnp.float32)
        g_down = jnp.einsum("rf,rd->fd", hidden, grad_mlp, preferred_element_type=jnp.float32)
        sigmoid_g = jax.nn.sigmoid(gate_act)
        grad_gate = (
            grad_hidden * up_act * sigmoid_g * (1.0 + gate_act * (1.0 - sigmoid_g))
        ).astype(jnp.bfloat16)
        grad_up = (grad_hidden * gate_act * sigmoid_g).astype(jnp.bfloat16)
        grad_normed_m = lax.psum(
            (
                jnp.einsum("rf,df->rd", grad_gate, w_g, preferred_element_type=jnp.float32)
                + jnp.einsum("rf,df->rd", grad_up, w_u, preferred_element_type=jnp.float32)
            ).astype(jnp.bfloat16),
            TP,
        ).astype(jnp.float32)
        g_gate = jnp.einsum("rd,rf->df", normed_m, grad_gate, preferred_element_type=jnp.float32)
        g_up = jnp.einsum("rd,rf->df", normed_m, grad_up, preferred_element_type=jnp.float32)
        grad_from_norm, g_gain_m = norm_back(middle, gain_m, grad_normed_m)
        grad_middle = grad_stream + grad_from_norm
        grad_attn = grad_middle.astype(jnp.bfloat16)
        grad_heads = jnp.einsum(
            "rd,hd->rh", grad_attn, w_o, preferred_element_type=jnp.float32
        ).astype(jnp.bfloat16)
        g_out = jnp.einsum("rh,rd->hd", mixed_b, grad_attn, preferred_element_type=jnp.float32)
        grad_heads = grad_heads.reshape(seq_count, shard_len, local_kv, group_size, HEAD_DIM)
        raw_scores = score_block(query_b, key_heads, allowed, score_scale)
        softmax_p = jnp.exp(raw_scores - log_total)
        grad_probs = jnp.einsum(
            "sckgd,snkd->skgcn", grad_heads, value_heads, preferred_element_type=jnp.float32
        )
        row_dots = jnp.sum(softmax_p * grad_probs, axis=-1, keepdims=True)
        grad_scores = (softmax_p * (grad_probs - row_dots)).astype(jnp.bfloat16)
        grad_query = (
            jnp.einsum(
                "skgcn,snkd->sckgd", grad_scores, key_heads, preferred_element_type=jnp.float32
            )
            * score_scale
        )
        grad_key_all = (
            jnp.einsum(
                "skgcn,sckgd->snkd", grad_scores, query_b, preferred_element_type=jnp.float32
            )
            * score_scale
        )
        grad_value_all = jnp.einsum(
            "skgcn,sckgd->snkd",
            softmax_p.astype(jnp.bfloat16),
            grad_heads,
            preferred_element_type=jnp.float32,
        )
        grad_key, grad_value = (
            lax.psum_scatter(
                grad_key_all.reshape(seq_count, seq_length, local_kv * HEAD_DIM).astype(
                    jnp.bfloat16
                ),
                CTX,
                scatter_dimension=1,
                tiled=True,
            ).astype(jnp.float32),
            lax.psum_scatter(
                grad_value_all.reshape(seq_count, seq_length, local_kv * HEAD_DIM).astype(
                    jnp.bfloat16
                ),
                CTX,
                scatter_dimension=1,
                tiled=True,
            ).astype(jnp.float32),
        )
        grad_query_b = rotate(
            grad_query.reshape(seq_count, shard_len, local_heads, HEAD_DIM), cosine, -sine_t
        )
        grad_query_b = grad_query_b.astype(jnp.bfloat16).reshape(tok_rows, local_heads * HEAD_DIM)
        grad_key_b = rotate(
            grad_key.reshape(seq_count, shard_len, local_kv, HEAD_DIM), cosine, -sine_t
        )
        grad_key_b = grad_key_b.astype(jnp.bfloat16).reshape(tok_rows, local_kv * HEAD_DIM)
        grad_value_b = grad_value.astype(jnp.bfloat16).reshape(tok_rows, local_kv * HEAD_DIM)
        grad_normed_a = lax.psum(
            (
                jnp.einsum("rh,dh->rd", grad_query_b, w_q, preferred_element_type=jnp.float32)
                + jnp.einsum("rh,dh->rd", grad_key_b, w_k, preferred_element_type=jnp.float32)
                + jnp.einsum("rh,dh->rd", grad_value_b, w_v, preferred_element_type=jnp.float32)
            ).astype(jnp.bfloat16),
            TP,
        ).astype(jnp.float32)
        g_query = jnp.einsum(
            "rd,rh->dh", normed_a, grad_query_b, preferred_element_type=jnp.float32
        )
        g_key = jnp.einsum("rd,rh->dh", normed_a, grad_key_b, preferred_element_type=jnp.float32)
        g_value = jnp.einsum(
            "rd,rh->dh", normed_a, grad_value_b, preferred_element_type=jnp.float32
        )
        grad_from_attn_norm, g_gain_a = norm_back(stream_in, gain_a, grad_normed_a)
        grad_stream = grad_middle + grad_from_attn_norm
        grad_terms = (g_gain_a, g_query, g_key, g_value, g_out, g_gain_m, g_gate, g_up, g_down)
        shares = (
            lax.psum_scatter(grad_terms[0], (FSDP, CTX), scatter_dimension=0, tiled=True),
            lax.psum_scatter(grad_terms[1], (FSDP, CTX), scatter_dimension=0, tiled=True),
            lax.psum_scatter(grad_terms[2], (FSDP, CTX), scatter_dimension=0, tiled=True),
            lax.psum_scatter(grad_terms[3], (FSDP, CTX), scatter_dimension=0, tiled=True),
            lax.psum_scatter(grad_terms[4], (FSDP, CTX), scatter_dimension=1, tiled=True),
            lax.psum_scatter(grad_terms[5], (FSDP, CTX), scatter_dimension=0, tiled=True),
            lax.psum_scatter(grad_terms[6], (FSDP, CTX), scatter_dimension=0, tiled=True),
            lax.psum_scatter(grad_terms[7], (FSDP, CTX), scatter_dimension=0, tiled=True),
            lax.psum_scatter(grad_terms[8], (FSDP, CTX), scatter_dimension=1, tiled=True),
        )
        results[layer_no] = (
            lax.all_gather(shares[0].astype(jnp.bfloat16), CTX, axis=0, tiled=True).astype(
                jnp.float32
            ),
            lax.all_gather(shares[1].astype(jnp.bfloat16), CTX, axis=0, tiled=True).astype(
                jnp.float32
            ),
            lax.all_gather(shares[2].astype(jnp.bfloat16), CTX, axis=0, tiled=True).astype(
                jnp.float32
            ),
            lax.all_gather(shares[3].astype(jnp.bfloat16), CTX, axis=0, tiled=True).astype(
                jnp.float32
            ),
            lax.all_gather(shares[4].astype(jnp.bfloat16), CTX, axis=1, tiled=True).astype(
                jnp.float32
            ),
            lax.all_gather(shares[5].astype(jnp.bfloat16), CTX, axis=0, tiled=True).astype(
                jnp.float32
            ),
            lax.all_gather(shares[6].astype(jnp.bfloat16), CTX, axis=0, tiled=True).astype(
                jnp.float32
            ),
            lax.all_gather(shares[7].astype(jnp.bfloat16), CTX, axis=0, tiled=True).astype(
                jnp.float32
            ),
            lax.all_gather(shares[8].astype(jnp.bfloat16), CTX, axis=1, tiled=True).astype(
                jnp.float32
            ),
        )
    stacked = [
        jnp.stack([results[layer_no][member] for layer_no in range(layer_count)])
        for member in range(9)
    ]
    input_grad = grad_stream.reshape(seq_count, shard_len, model_width)
    return (
        output,
        input_grad,
        stacked[0],
        stacked[1],
        stacked[2],
        stacked[3],
        stacked[4],
        stacked[5],
        stacked[6],
        stacked[7],
        stacked[8],
        rms_stats,
    )


def partners():
    me = lax.axis_index(CTX)
    return me, me ^ 1, me ^ 2, me ^ 3


def greet(*places):
    barrier = pltpu.get_barrier_semaphore()
    for place in places:
        pl.semaphore_signal(barrier, inc=1, device_id=place, device_id_type=MESH)
    pl.semaphore_wait(barrier, len(places))


def send(src, dst, sems, slot, place):
    copy = pltpu.make_async_remote_copy(
        src_ref=src,
        dst_ref=dst,
        send_sem=sems[0].at[slot],
        recv_sem=sems[1].at[slot],
        device_id=place,
        device_id_type=MESH,
    )
    copy.start()
    return copy


def run(steps, work=()):
    for n, _ in enumerate(steps):
        if n < len(work):
            work[n]()


def gather_rows(full, sems, place, own):
    me, side_x, side_y, _ = place
    to_x, to_y = {CTX: side_x}, {CTX: side_y}
    half = full.shape[1] // 2
    top, low = pl.ds(0, half), pl.ds(half, half)
    first = [
        send(own.at[top], full.at[me, top], sems, 0, to_x),
        send(own.at[low], full.at[me, low], sems, 1, to_y),
    ]
    rest = [
        send(own.at[top], full.at[me, top], sems, 2, to_y),
        send(own.at[low], full.at[me, low], sems, 3, to_x),
    ]
    yield
    first[0].wait_recv()
    rest.append(send(full.at[side_x, top], full.at[side_x, top], sems, 4, to_y))
    first[1].wait_recv()
    rest.append(send(full.at[side_y, low], full.at[side_y, low], sems, 5, to_x))
    yield
    rest[0].wait_recv()
    rest[1].wait_recv()
    yield
    rest[2].wait_recv()
    rest[3].wait_recv()
    for copy in first + rest:
        copy.wait_send()


def dot32(a, b, dims):
    return lax.dot_general(a, b, (dims, ((), ())), preferred_element_type=jnp.float32)


def start_kernel(r):
    place = partners()
    me, side_x, side_y, across = place
    groups = (
        (FSDP, r.gains, r.all_gains, (r.gain_send, r.gain_recv)),
        (CTX, r.places, r.all_places, (r.place_send, r.place_recv)),
    )
    peers = []
    for axis, _, _, _ in groups:
        count = lax.axis_size(axis)
        peers.append([lax.rem(lax.axis_index(axis) + step, count) for step in range(1, count)])
    layers = r.attn_gain.shape[0]
    r.gains[...] = jnp.zeros_like(r.gains)
    r.gains[0:layers, :] = r.attn_gain[...].astype(jnp.float32)
    r.gains[layers : 2 * layers, :] = r.mlp_gain[...].astype(jnp.float32)
    full = r.full
    own = pltpu.make_async_copy(r.x.at[lax.axis_index(TP)], full.at[me], r.load.at[0])
    own.start()
    greet(*[{groups[n][0]: peer} for n in range(2) for peer in peers[n]])
    copies = []
    for n, (axis, src, dst, sems) in enumerate(groups):
        mine = pltpu.make_async_copy(src, dst.at[lax.axis_index(axis)], r.load.at[1 + n])
        mine.start()
        for step, peer in enumerate(peers[n]):
            copies.append(send(src, dst.at[lax.axis_index(axis)], sems, step, {axis: peer}))
        copies.append(mine)
    steps = gather_rows(full, (r.ag_send, r.ag_recv), place, r.x.at[lax.axis_index(TP)])
    next(steps)
    packed = [getattr(r, f"packed_{layer}") for layer in range(r.gate.shape[0])]
    layers, units = len(packed), r.turned.shape[1]
    loads = []
    for layer in range(layers):
        cut = pl.ds(pl.multiple_of(me * units, units), units)
        for n, (src, dst) in enumerate((
            (r.gate.at[layer, :, cut], packed[layer].at[:, pl.ds(0, units)]),
            (r.up.at[layer, :, cut], packed[layer].at[:, pl.ds(units, units)]),
            (r.down.at[layer, cut], r.turned.at[layer]),
        )):
            loads.append(pltpu.make_async_copy(src, dst, r.load.at[3 + 3 * layer + n]))
    for load in loads:
        load.start()
    own.wait()
    for copy in copies:
        copy.wait()
    gain = jnp.concatenate([r.all_gains[n, 0:1, :] for n in range(lax.axis_size(FSDP))], axis=1)
    rows = full.shape[1]
    half = rows // 2
    step = 16

    def norm(top_of, low_of):
        for part_no, owner in enumerate((top_of, low_of)):
            @pl.loop(0, half // step)
            def _(i):
                here = pl.ds(pl.multiple_of(part_no * half + i * step, step), step)
                row = full[owner, here, :].astype(jnp.float32)
                inv_rms = lax.rsqrt(jnp.mean(row * row, axis=-1, keepdims=True) + epsilon)
                r.normed[owner, here, :] = (row * inv_rms * gain).astype(jnp.bfloat16)

    def mask():
        length = r.bias.shape[1]
        block = 96
        query = lax.broadcasted_iota(jnp.int32, (1, length), 1)
        here = r.starts[pl.ds(lax.axis_index(TP), 1), :]
        firsts = [here[:, n : n + 1] for n in range(r.starts.shape[1])]
        in_query = [jnp.where((query >= f) & (query < f + PIECE_LEN), 1.0, 0.0) for f in firsts]
        for owner in range(r.all_places.shape[0]):
            @pl.loop(0, rows // block)
            def _(i):
                here = pl.ds(pl.multiple_of(i * block, block), block)
                key = owner * rows + i * block + lax.broadcasted_iota(jnp.int32, (block, 1), 0)
                valid = r.all_places[owner, here, HEAD_DIM : HEAD_DIM + 1]
                seen = 0
                for f, row in zip(firsts, in_query):
                    seen += jnp.where((key >= f) & (key < f + PIECE_LEN), 1.0, 0.0) * row
                seen = jnp.where(key <= query, 1.0, seen) * valid
                seen = jnp.where(key == query, 1.0, seen)
                added = jnp.where(seen > 0, 0.0, neg_big).astype(jnp.bfloat16)
                keys = pl.ds(pl.multiple_of(owner * rows + i * block, block), block)
                for n in range(r.all_places.shape[0]):
                    one = added[:, n * rows : (n + 1) * rows]
                    r.bias[n, keys, :] = jnp.concatenate([one, one], axis=1)

    norm(me, me)
    mask()
    r.keep("bias")
    half_dim = HEAD_DIM // 2
    for owner in range(r.all_places.shape[0]):
        table = r.all_places[owner]
        cos_b, sin_b = table[:, :half_dim], table[:, half_dim:HEAD_DIM]
        r.cosine[owner] = jnp.concatenate([cos_b, cos_b], axis=1)
        r.sine[owner] = jnp.concatenate([-sin_b, sin_b], axis=1)
    r.keep("cosine", "sine")
    next(steps)
    norm(side_x, side_y)
    for load in loads:
        load.wait()
    for layer in range(layers):
        packed[layer][:, 2 * units :] = r.turned[layer].astype(jnp.float32).T.astype(jnp.bfloat16)
        r.keep(f"packed_{layer}")
    next(steps)
    norm(side_y, side_x)
    run(steps)
    norm(across, across)


def stat_steps(r, place):
    depth = lax.axis_size(FSDP)
    level = lax.axis_index(FSDP)
    others = [{FSDP: lax.rem(level + step, depth)} for step in range(1, depth)]
    here = (r.stat_send, r.stat_recv)
    layers = len(r.attn_stats)
    lane = lax.broadcasted_iota(jnp.int32, (8, 128), 1)
    tile = jnp.zeros((8, 128), jnp.float32)
    wanted = [(3 * layers, r.attn_stats[0], 2)]
    for layer in range(layers):
        wanted += [(3 * layer, r.attn_stats[layer], 1), (3 * layer + 1, r.attn_stats[layer], 0)]
        wanted.append((3 * layer + 2, r.mlp_stats[layer], 0))
    for to, ref, at in wanted:
        row = jnp.sum(ref[...], axis=0, keepdims=True)
        value = jnp.sum(jnp.where(lane[0:1] == at, row, 0.0), axis=1, keepdims=True)
        tile += jnp.where(lane == to, value, 0.0)
    width = r.width
    r.stat_sent[0, :, pl.ds(width, 128)] = tile
    r.stat_sent[0, :, pl.ds(0, width)] = jnp.zeros((8, width), jnp.float32)
    for n, ref in enumerate(r.gain_rows):
        r.stat_sent[0, n : n + 1, pl.ds(0, width)] = jnp.sum(ref[...], axis=0, keepdims=True)
    for n, peer in enumerate((sibling(), {CTX: place[1]}, {CTX: place[2]})):
        copy = send(r.stat_sent.at[n], r.stat_came.at[n], here, n, peer)
        yield
        copy.wait()
        r.stat_sent[n + 1] = r.stat_sent[n] + r.stat_came[n]
    r.stat_z[level] = r.stat_sent[3]
    copies = [send(r.stat_z.at[level], r.stat_z.at[level], here, 3 + n, peer) for n, peer in enumerate(others)]
    yield
    for copy in copies:
        copy.wait()
    part = width // depth
    here = pl.ds(pl.multiple_of(level * part, 128), part)
    gains, held = r.stat_z[0, :, here], r.stat_z[0, :, pl.ds(width, 128)]
    for n in range(1, depth):
        gains += r.stat_z[n, :, here]
        held += r.stat_z[n, :, pl.ds(width, 128)]
    r.gains[...] = gains
    count = jnp.sum(jnp.where(lane[0:1] == 3 * layers, held[0:1], 0.0), axis=1, keepdims=True)
    r.all_stats[...] = jnp.sqrt(held / (count * r.width))


def tail_kernel(width, r):
    r.width = width
    place = partners()
    me = place[0]
    depth = lax.axis_size(FSDP)
    level = lax.axis_index(FSDP)
    peers = [lax.rem(level + step, depth) for step in range(1, depth)]
    mine = pltpu.make_async_copy(r.share, r.gathered.at[me], r.load.at[0])
    mine.start()
    greet_near(place, sibling(), *[{FSDP: peer} for peer in peers])
    rows = r.share.shape[0]
    half = rows // 2
    r.gain_rows = [r.gain_rows_0, r.gain_rows_1, r.gain_rows_2, r.gain_rows_3]
    r.attn_stats = [r.attn_stats_0, r.attn_stats_1]
    r.mlp_stats = [r.mlp_stats_0, r.mlp_stats_1]
    counts = stat_steps(r, place)
    next(counts)
    copies = []
    for part_no in range(2):
        copies.append([])
        for step, peer in enumerate(peers):
            block = r.summed.at[pl.ds(pl.multiple_of(peer * rows + part_no * half, half), half)]
            copies[part_no].append(
                send(block, r.z_came.at[part_no, level], (r.z_send, r.z_recv), part_no * depth + step, {FSDP: peer})
            )
    first = gather_rows(r.gathered, (r.ag_send, r.ag_recv), place, r.share)
    next(first)
    next(counts)
    next(first)
    step = 48
    lasts = (r.last_0, r.last_1)
    steps = []
    for part_no in range(2):
        for copy in copies[part_no]:
            copy.wait_recv()

        @pl.loop(0, half // step)
        def _(i):
            here = pl.ds(pl.multiple_of(i * step, step), step)
            start = pl.multiple_of(level * rows + part_no * half + i * step, step)
            total = r.summed[pl.ds(start, step), :].astype(jnp.float32)
            for peer in peers:
                total += r.z_came[part_no, peer, here, :].astype(jnp.float32)
            lasts[part_no][me, here, :] = total.astype(jnp.bfloat16)

        steps.append(gather_rows(lasts[part_no], ((r.l0_send, r.l0_recv), (r.l1_send, r.l1_recv))[part_no], place, lasts[part_no].at[me]))
        next(steps[part_no])
        if part_no == 0:
            next(counts)
    next(steps[0])
    next(counts)
    next(steps[1])
    run(first)
    mine.wait()
    r.keep("gathered")
    run(steps[0])
    run(steps[1])
    run(counts)
    for copy in copies[0] + copies[1]:
        copy.wait_send()


class Scatter:
    def __init__(self, part, buffers, sems, place):
        self.part, self.sems, self.place = part, sems, place
        self.from_x, self.from_y, self.passed, self.last = buffers
        self.half = part.shape[1] // 2
        self.copies = {}

    def send(self, slot, src, dst, axis_peer):
        self.copies[slot] = send(src, dst, self.sems, slot, {CTX: axis_peer})

    def across(self):
        _, side_x, side_y, far = self.place
        self.send(0, self.part.at[far, pl.ds(0, self.half)], self.from_x.at[1], side_x)
        self.send(1, self.part.at[far, pl.ds(self.half, self.half)], self.from_y.at[1], side_y)

    def x_out(self, some=None):
        side_x = self.place[1]
        slot, rows = self.cut(some)
        self.send(slot, self.part.at[side_x, rows], self.from_x.at[0, rows], side_x)

    def y_out(self, some=None):
        side_y = self.place[2]
        slot, rows = self.cut(some)
        below = pl.ds(self.half + rows.start, rows.size)
        self.send(slot + 1, self.part.at[side_y, below], self.from_y.at[0, rows], side_y)

    def cut(self, some):
        if some is None:
            return 2, pl.ds(0, self.half)
        first = self.half // 48 * 16
        return (2, pl.ds(0, first)) if some == 0 else (6, pl.ds(first, self.half - first))

    def pieces(self):
        first = self.half // 32 * 16
        return (0, first), (first, self.half - first)

    def pass_on(self, side, owner, came, axis_peer):
        self.copies[side].wait_recv()
        step = 16
        for n, (first, count) in enumerate(self.pieces()):
            @pl.loop(0, count // step)
            def _(i):
                rows = pl.ds(pl.multiple_of(first + i * step, step), step)
                mine = self.part[owner, pl.ds(pl.multiple_of(side * self.half + first + i * step, step), step), :]
                total = mine.astype(jnp.float32) + came[1, rows, :].astype(jnp.float32)
                self.passed[side, rows, :] = total.astype(self.passed.dtype)

            piece = pl.ds(first, count)
            self.send(4 + side + 4 * n, self.passed.at[side, piece], self.last.at[side, piece], axis_peer)

    def forward(self):
        _, side_x, side_y, _ = self.place
        self.pass_on(0, side_y, self.from_x, side_y)
        self.pass_on(1, side_x, self.from_y, side_x)

    def finish(self):
        for slot in self.copies:
            if 1 < slot < 8:
                self.copies[slot].wait_recv()

    def each_row(self, work, step=16):
        me = self.place[0]
        for n, (first, count) in enumerate(self.pieces()):
            for side in range(2):
                if n == 1:
                    self.copies[8 + side].wait_recv()
                came = self.from_x if side == 0 else self.from_y

                @pl.loop(0, count // step)
                def _(i):
                    rows = pl.ds(pl.multiple_of(first + i * step, step), step)
                    whole = pl.ds(pl.multiple_of(side * self.half + first + i * step, step), step)
                    total = self.part[me, whole, :].astype(jnp.float32)
                    total += came[0, rows, :].astype(jnp.float32)
                    work(whole, total + self.last[side, rows, :].astype(jnp.float32))
        for copy in self.copies.values():
            copy.wait_send()


def scatter_steps(scatter):
    scatter.across()
    scatter.x_out()
    scatter.y_out()
    yield
    scatter.forward()
    yield
    scatter.finish()


class WeightGrads:
    def __init__(self, lefts, rights, sent, came, summed, sems):
        self.lefts, self.rights, self.sent, self.came, self.summed, self.sems = lefts, rights, sent, came, summed, sems
        self.sizes = [r.shape[-1] for r in rights]
        self.side = lax.axis_index(TP)
        self.copies = []

    def product(self, p, t, put):
        block = 768
        left, right = self.lefts[p], self.rights[p]
        width = left.shape[-1]

        @pl.loop(0, width // block)
        def _(i):
            cols = pl.ds(pl.multiple_of(i * block, block), block)
            one = left[:, :, cols].reshape(-1, block)
            put(cols, dot32(one, right[t].reshape(one.shape[0], -1), ((0,), (0,))).astype(jnp.bfloat16))

    def theirs(self, p):
        def put(rows, value):
            self.sent[p][rows, : self.sizes[p]] = value

        self.product(p, 1 - self.side, put)
        self.copies.append(send(self.sent[p], self.came[p], self.sems, p, {TP: 1 - self.side}))

    def cols(self, p):
        start = sum(self.sizes[:p])
        return slice(start, start + self.sizes[p])

    def ours(self, p):
        def put(rows, value):
            self.summed[rows, self.cols(p)] = value

        self.product(p, self.side, put)

    def add_up(self):
        step = 64
        for p, copy in enumerate(self.copies):
            copy.wait_recv()

            @pl.loop(0, self.summed.shape[0] // step)
            def _(i):
                rows = pl.ds(pl.multiple_of(i * step, step), step)
                total = self.summed[rows, self.cols(p)].astype(jnp.float32) + self.came[p][rows, : self.sizes[p]].astype(jnp.float32)
                self.summed[rows, self.cols(p)] = total.astype(jnp.bfloat16)

    def close(self):
        for copy in self.copies:
            copy.wait_send()


def add_stats(stats, valid, *values):
    lane = lax.broadcasted_iota(jnp.int32, stats.shape, 1)
    total = stats[...] + jnp.where(lane == 2, valid, 0.0)
    for n, value in enumerate(values):
        total += jnp.where(lane == n, valid * jnp.sum(value * value, axis=-1, keepdims=True), 0.0)
    stats[...] = total


def norm_sum(scatter, stream, gain, valid, middle, normed, stats):
    stats[...] = jnp.zeros_like(stats)

    def work(rows, branch):
        before = stream[rows, :].astype(jnp.float32)
        total = before + branch
        middle[rows, :] = total
        inv_rms = lax.rsqrt(jnp.mean(total * total, axis=-1, keepdims=True) + epsilon)
        normed[rows, :] = (total * inv_rms * gain[...]).astype(normed.dtype)
        add_stats(stats, valid[rows, :], branch, before)

    scatter.each_row(work)


def norm_sum_back(scatter, stream, gain, grad, gain_rows, put):
    gain_rows[...] = jnp.zeros_like(gain_rows)

    def work(rows, got):
        x = stream[rows, :].astype(jnp.float32)
        inv_rms = lax.rsqrt(jnp.mean(x * x, axis=-1, keepdims=True) + epsilon)
        scaled = gain[...] * got
        along = jnp.mean(scaled * x, axis=-1, keepdims=True)
        put(rows, grad[rows, :].astype(jnp.float32) + inv_rms * scaled - x * (inv_rms * inv_rms * inv_rms * along))
        gain_rows[...] += got * x * inv_rms

    scatter.each_row(work)


def rows_of(ref, lead, top_of, low_of):
    half = ref.shape[-2] // 2
    return jnp.concatenate([ref[(*lead, top_of, pl.ds(0, half))], ref[(*lead, low_of, pl.ds(half, half))]], axis=0)


def put_rows(ref, lead, top_of, low_of, value):
    half = ref.shape[-2] // 2
    ref[(*lead, top_of, pl.ds(0, half))] = value[:half].astype(ref.dtype)
    ref[(*lead, low_of, pl.ds(half, half))] = value[half:].astype(ref.dtype)


def greet_near(place, *more):
    greet({CTX: place[1]}, {CTX: place[2]}, *more)


def sibling():
    return {TP: 1 - lax.axis_index(TP)}


def mlp_rows(r, top_of, low_of, back):
    units = r.hidden.shape[-1]
    x = rows_of(r.full, (), top_of, low_of)
    total, g_total = 0.0, 0.0
    for t in range(r.weights.shape[0]):
        gate_act = dot32(x, r.weights[t, :, :units], ((1,), (0,)))
        up_act = dot32(x, r.weights[t, :, units : 2 * units], ((1,), (0,)))
        sig = jax.nn.sigmoid(gate_act)
        unit = (gate_act * sig * up_act).astype(jnp.bfloat16)
        put_rows(r.hidden, (t,), top_of, low_of, unit)
        total += dot32(unit, r.weights[t, :, 2 * units :], ((1,), (1,)))
        if back:
            g_total += mlp_back_rows(r, rows_of(r.grad_all, (), top_of, low_of), t, top_of, low_of, gate_act, up_act, sig)
        else:
            put_rows(r.gate, (t,), top_of, low_of, gate_act)
            put_rows(r.up, (t,), top_of, low_of, up_act)
    put_rows(r.part_out if back else r.part, (), top_of, low_of, total)
    if back:
        put_rows(r.part, (), top_of, low_of, g_total)


def mlp_back_rows(r, grad, t, top_of, low_of, gate_act, up_act, sig):
    units = r.grad_gate.shape[-1]
    g_hidden = dot32(grad, r.weights[t, :, 2 * units :], ((1,), (0,)))
    g_gate = (g_hidden * up_act * sig * (1.0 + gate_act * (1.0 - sig))).astype(jnp.bfloat16)
    g_up = (g_hidden * gate_act * sig).astype(jnp.bfloat16)
    put_rows(r.grad_gate, (t,), top_of, low_of, g_gate)
    put_rows(r.grad_up, (t,), top_of, low_of, g_up)
    total = dot32(g_gate, r.weights[t, :, :units], ((1,), (1,)))
    return total + dot32(g_up, r.weights[t, :, units : 2 * units], ((1,), (1,)))


def gathered_work(r, place, scatter, work, rows_own, own, cut=True):
    me, side_x, side_y, across = place
    steps = gather_rows(r.full, (r.ag_send, r.ag_recv), place, rows_own)
    next(steps)
    own.wait()
    work(me, me)
    next(steps)
    work(side_x, side_y)
    next(steps)
    work(side_y, side_x)
    scatter.x_out(0 if cut else None)
    scatter.y_out(0 if cut else None)
    run(steps)
    work(across, across)
    scatter.across()
    if cut:
        scatter.x_out(1)
        scatter.y_out(1)


def mlp_kernel(r):
    place = partners()
    me = place[0]
    own = pltpu.make_async_copy(r.normed, r.full.at[me], r.load.at[0])
    own.start()
    greet_near(place)
    scatter = Scatter(r.part, (r.from_x, r.from_y, r.passed, r.last), (r.rs_send, r.rs_recv), place)

    def work(top_of, low_of):
        r.need("weights")
        mlp_rows(r, top_of, low_of, False)

    gathered_work(r, place, scatter, work, r.normed, own)
    r.keep("full", "hidden", "gate", "up")
    scatter.forward()
    scatter.finish()
    r.need("middle")
    norm_sum(scatter, r.middle, r.gain, r.valid, r.stream, r.normed_next, r.stats)


def mlp_back_kernel(both, r):
    place = partners()
    me = place[0]
    own = pltpu.make_async_copy(r.rows_own, r.full.at[me], r.load.at[0])
    own.start()
    greet_near(place, sibling())
    scatter = Scatter(r.part, (r.from_x, r.from_y, r.passed, r.last), (r.rs_send, r.rs_recv), place)

    def both_rows(top_of, low_of):
        r.need("weights", "grad_all")
        mlp_rows(r, top_of, low_of, True)

    def back_rows(top_of, low_of):
        r.need("weights", "grad_gate", "grad_up")
        total = 0.0
        grad = rows_of(r.full, (), top_of, low_of)
        for t in range(r.weights.shape[0]):
            gate_act = rows_of(r.grad_gate, (t,), top_of, low_of).astype(jnp.float32)
            up_act = rows_of(r.grad_up, (t,), top_of, low_of).astype(jnp.float32)
            total += mlp_back_rows(r, grad, t, top_of, low_of, gate_act, up_act, jax.nn.sigmoid(gate_act))
        put_rows(r.part, (), top_of, low_of, total)

    gathered_work(r, place, scatter, both_rows if both else back_rows, r.rows_own, own, not both)
    if both:
        r.keep("part_out")
    normed, grad = (r.full, r.grad_all) if both else (r.normed, r.full)
    r.need("normed", "hidden")
    units = r.hidden.shape[-1]
    sent = [r.weights.at[0, :, pl.ds(p * units, units)] for p in range(3)]
    sums = WeightGrads(
        [normed, normed, grad], [r.grad_gate, r.grad_up, r.hidden], sent, [r.came_0, r.came_1, r.came_2],
        r.summed, (r.tp_send, r.tp_recv),
    )
    sums.theirs(0)
    sums.theirs(1)
    scatter.forward()
    job = None if both else gather_part(r.share, 0, r.gathered, r.load.at[1], r.ja_send, r.ja_recv, place)
    if job:
        next(job)
    sums.theirs(2)
    sums.ours(0)
    sums.ours(1)
    sums.ours(2)
    sums.add_up()
    r.keep("summed")
    scatter.finish()
    r.need("middle", "grad")

    def put(rows, total):
        r.grad_new[rows, :] = total
        r.grad_rows[rows, :] = total.astype(r.grad_rows.dtype)

    if job:
        next(job)
    norm_sum_back(scatter, r.middle, r.gain, r.grad, r.gain_rows, put)
    if job:
        run(job)
        r.keep("gathered")
    sums.close()


LOG2E = 1.4426950408889634


def turn(x, cos_row, sin_row):
    half_dim = HEAD_DIM // 2
    swapped = jnp.concatenate([x[:, half_dim:], x[:, :half_dim]], axis=1)
    return x * cos_row + swapped * sin_row


def project_rows(r, full, top_of, low_of):
    cols_q, base = 2 * HEAD_DIM, 4 * HEAD_DIM
    x = rows_of(full, (), top_of, low_of)
    cos_b, sin_b = rows_of(r.cosine, (), top_of, low_of), rows_of(r.sine, (), top_of, low_of)
    for t in range(r.weights.shape[0]):
        flat = dot32(x, r.weights[t, :, :base], ((1,), (0,)))
        for g in range(2):
            put_rows(r.query, (t, g), top_of, low_of, turn(flat[:, g * HEAD_DIM : (g + 1) * HEAD_DIM], cos_b, sin_b))
        put_rows(r.key, (t,), top_of, low_of, turn(flat[:, cols_q : cols_q + HEAD_DIM], cos_b, sin_b))
        put_rows(r.value, (t,), top_of, low_of, flat[:, cols_q + HEAD_DIM : base])


def attend_rows(r, owner):
    base = 4 * HEAD_DIM
    pairs, _, rows, _ = r.key.shape
    factor = HEAD_DIM ** (-0.5) * LOG2E

    for t in range(pairs):
        key = r.key[t].reshape(-1, HEAD_DIM)
        value = r.value[t].reshape(-1, HEAD_DIM)
        query = jnp.concatenate([r.query[t, 0, owner], r.query[t, 1, owner]], axis=0)
        raw = dot32(key, query, ((1,), (1,)))
        raw = raw * factor + r.bias[owner].astype(jnp.float32)
        top = jnp.max(raw, axis=0, keepdims=True)
        probs = jnp.exp2(raw - top)
        total = jnp.sum(probs, axis=0, keepdims=True)
        out = dot32(value, probs.astype(jnp.bfloat16), ((0,), (0,))) * (1.0 / total)
        fill = -out.shape[1] % 128
        out = jnp.concatenate([out, jnp.zeros((HEAD_DIM, fill), jnp.float32)], axis=1).T.astype(jnp.bfloat16)
        r.lse[t, owner] = top + jnp.log2(total)
        for g in range(2):
            r.mixed[t, owner, :, g * HEAD_DIM : (g + 1) * HEAD_DIM] = out[g * rows : (g + 1) * rows]

    total = 0.0
    for t in range(pairs):
        total += dot32(r.mixed[t, owner], r.weights[t, :, base : base + 2 * HEAD_DIM], ((1,), (1,)))
    r.part[owner] = total.astype(r.part.dtype)


def attend_kernel(first, r):
    place = partners()
    me, side_x, side_y, across = place
    rows_own = r.share.at[lax.axis_index(TP)] if first else r.normed
    own = pltpu.make_async_copy(rows_own, r.full.at[me], r.load.at[0])
    own.start()
    greet_near(place)
    steps = gather_rows(r.full, (r.ag_send, r.ag_recv), place, rows_own)
    next(steps)
    own.wait()
    rows = r.normed if first else r.full
    r.need("weights", "cosine", "sine", "normed")
    if first:
        for owner in range(4):
            project_rows(r, rows, owner, owner)
    else:
        project_rows(r, rows, me, me)
        next(steps)
        project_rows(r, rows, side_x, side_y)
        next(steps)
        project_rows(r, rows, side_y, side_x)
        run(steps)
        project_rows(r, rows, across, across)
        r.keep("full")
    r.keep("query", "key", "value")
    scatter = Scatter(r.part, (r.from_x, r.from_y, r.passed, r.last), (r.rs_send, r.rs_recv), place)
    r.need("bias")
    attend_rows(r, across)
    scatter.across()
    if first:
        next(steps)
    attend_rows(r, side_x)
    scatter.x_out()
    attend_rows(r, side_y)
    scatter.y_out()
    scatter.forward()
    attend_rows(r, me)
    r.keep("lse", "mixed")
    if first:
        run(steps)
        r.keep("full")
    scatter.finish()
    r.need("stream")
    norm_sum(scatter, r.stream, r.gain, r.valid, r.middle, r.normed_next, r.stats)


def attend_back_kernel(last, r):
    place = partners()
    me, side_x, side_y, across = place
    own = pltpu.make_async_copy(r.rows_own, r.full.at[me], r.load.at[0])
    own.start()
    greet_near(place, sibling())
    cols_q, base = 2 * HEAD_DIM, 4 * HEAD_DIM
    pairs = r.weights.shape[0]
    rows = r.full.shape[1]
    scale = HEAD_DIM ** (-0.5)
    factor = scale * LOG2E
    order = (me, side_x, side_y, across)
    masks = [pltpu.make_async_copy(r.bias_in.at[owner], r.bias.at[n % 2], r.bias_load.at[n]) for n, owner in enumerate(order)]
    masks[0].start()
    masks[1].start()
    r.g_key[...] = jnp.zeros_like(r.g_key)
    r.g_value[...] = jnp.zeros_like(r.g_value)

    def project(top_of, low_of):
        r.need("weights")
        x = rows_of(r.full, (), top_of, low_of)
        for t in range(pairs):
            flat = dot32(x, r.weights[t, :, base : base + cols_q], ((1,), (0,)))
            for g in range(2):
                put_rows(r.heads, (t, g), top_of, low_of, flat[:, g * HEAD_DIM : (g + 1) * HEAD_DIM])

    def two(ref, t, owner):
        return jnp.concatenate([ref[t, 0, owner], ref[t, 1, owner]], axis=0)

    def queries_back(n):
        owner = order[n]
        masks[n].wait()
        for t in range(pairs):
            query, heads = two(r.query, t, owner), two(r.heads, t, owner)
            mixed = r.mixed[t, owner].astype(jnp.float32)
            mixed = jnp.concatenate([mixed[:, :HEAD_DIM], mixed[:, HEAD_DIM:]], axis=0)
            along = lax.dot_general(
                jnp.ones((8, HEAD_DIM), jnp.float32), heads.astype(jnp.float32) * mixed, (((1,), (1,)), ((), ())),
                precision=lax.Precision.HIGHEST, preferred_element_type=jnp.float32,
            )[0:1]
            lse = r.lse[t, owner]
            r.g_query[...] = jnp.zeros_like(r.g_query)

            @pl.loop(0, jnp.minimum(owner + 2, 4))
            def _(kept):
                here = pl.ds(pl.multiple_of(kept * rows, 16), rows)
                key, value = r.key[t, kept], r.value[t, kept]
                raw = dot32(key, query, ((1,), (1,)))
                probs = jnp.exp2(raw * factor + r.bias[n % 2, here, :].astype(jnp.float32) - lse)
                g_probs = dot32(value, heads, ((1,), (1,)))
                g_scores = (probs * (g_probs - along)).astype(jnp.bfloat16)
                r.g_value[t, kept] += dot32(probs.astype(jnp.bfloat16), heads, ((1,), (0,)))
                r.g_key[t, kept] += dot32(g_scores, query, ((1,), (0,)))
                r.g_query[...] += dot32(key, g_scores, ((0,), (0,)))

            fill = jnp.zeros((HEAD_DIM, -2 * rows % 128), jnp.float32)
            g_query = jnp.concatenate([r.g_query[...], fill], axis=1).T * scale
            for g in range(2):
                r.grad_qkv[t, owner, :, g * HEAD_DIM : (g + 1) * HEAD_DIM] = turn(
                    g_query[g * rows : (g + 1) * rows], r.cosine[owner], -r.sine[owner]
                ).astype(jnp.bfloat16)
        if n + 2 < 4:
            masks[n + 2].start()

    steps = gather_rows(r.full, (r.ag_send, r.ag_recv), place, r.rows_own)
    next(steps)
    own.wait()
    project(me, me)
    r.need("key", "value", "query", "lse", "mixed", "cosine", "sine")
    queries_back(0)
    next(steps)
    jobs = [
        gather_part(r.share_a, 1, r.gathered_a, r.load.at[1], r.ja_send, r.ja_recv, place),
        gather_part(r.share_b, None, r.gathered_b, r.load.at[2], r.jb_send, r.jb_recv, place),
    ] if last else [end_steps(r, place)]
    for job in jobs:
        next(job)
    project(side_x, side_y)
    next(steps)
    project(side_y, side_x)
    queries_back(1)
    queries_back(2)
    run(steps)
    project(across, across)
    queries_back(3)

    @pl.loop(0, 4)
    def _(owner):
        for t in range(pairs):
            r.grad_qkv[t, owner, :, cols_q : cols_q + HEAD_DIM] = turn(
                r.g_key[t, owner] * scale, r.cosine[owner], -r.sine[owner]
            ).astype(jnp.bfloat16)
            r.grad_qkv[t, owner, :, cols_q + HEAD_DIM :] = r.g_value[t, owner].astype(jnp.bfloat16)

    def branch(owner):
        total = 0.0
        for t in range(pairs):
            total += dot32(r.grad_qkv[t, owner], r.weights[t, :, :base], ((1,), (1,)))
        r.part[owner] = total.astype(r.part.dtype)

    scatter = Scatter(r.part, (r.from_x, r.from_y, r.passed, r.last), (r.rs_send, r.rs_recv), place)
    if not last:
        for job in jobs:
            next(job)
    branch(across)
    scatter.across()
    branch(side_x)
    scatter.x_out()
    branch(side_y)
    scatter.y_out()
    branch(me)
    r.need("normed")
    sums = WeightGrads(
        [r.normed, r.full], [r.grad_qkv, r.mixed],
        [r.weights.at[0, :, pl.ds(0, base)], r.weights.at[1, :, pl.ds(0, r.came_1.shape[1])]], [r.came_0, r.came_1],
        r.summed, (r.tp_send, r.tp_recv),
    )
    sums.theirs(0)
    scatter.forward()
    if last:
        for job in jobs:
            next(job)
    sums.theirs(1)
    sums.ours(0)
    sums.ours(1)
    r.summed[:, base + cols_q :] = jnp.zeros((r.summed.shape[0], r.summed.shape[1] - base - cols_q), jnp.bfloat16)
    sums.add_up()
    r.keep("summed")
    if not last:
        for job in jobs:
            run(job)
        r.keep("out")
    scatter.finish()
    r.need("stream", "grad")
    side = lax.axis_index(TP)

    def put(here, total):
        if last:
            r.grad_new[side, here, :] = total
        else:
            r.grad_new[here, :] = total
            r.grad_rows[here, :] = total.astype(r.grad_rows.dtype)

    norm_sum_back(scatter, r.stream, r.gain, r.grad, r.gain_rows, put)
    handed = []
    if last:
        handed.append(send(r.grad_new.at[side], r.grad_new.at[side], (r.tp_send, r.tp_recv), 2, sibling()))
    if last:
        for job in jobs:
            run(job)
        r.keep("gathered_a", "gathered_b")
    for copy in handed:
        copy.wait()
    sums.close()


def end_steps(r, place):
    side = lax.axis_index(TP)
    r.need("end_part")
    scatter = Scatter(
        r.end_part, (r.end_from_x, r.end_from_y, r.end_passed, r.end_last), (r.end_send, r.end_recv), place
    )
    yield from scatter_steps(scatter)

    r.stats[...] = jnp.zeros_like(r.stats)

    def work(rows, branch):
        r.out[side, rows, :] = (r.end_middle[rows, :] + branch).astype(r.out.dtype)
        add_stats(r.stats, r.valid[rows, :], branch)

    r.need("end_middle")
    scatter.each_row(work)
    send(r.out.at[side], r.out.at[side], (r.out_send, r.out_recv), 0, sibling()).wait()


def gather_part(share, part_no, full, local_sem, send_sems, recv_sems, place):
    rows = full.shape[1]
    src = share if part_no is None else share.at[pl.ds(part_no * rows, rows)]
    copy = pltpu.make_async_copy(src, full.at[place[0]], local_sem)
    copy.start()
    yield from gather_rows(full, (send_sems, recv_sems), place, src)
    copy.wait()


class Refs:
    def need(self, *names):
        for name in names:
            if name in self.loads:
                self.loads.pop(name).wait()

    def keep(self, *names):
        for name in names:
            src, dst, sem = self.late[name]
            store = pltpu.make_async_copy(src, dst, sem)
            store.start()
            self.stores.append(store)


def linked(kernel, number, micros, near, far, lazy, outs, late, scratch):
    names = [*near, *far, *lazy, *outs, *late, *scratch]
    halves = [name for name, value in lazy.items() if isinstance(value, tuple)]
    lazy = {name: value[0] if name in halves else value for name, value in lazy.items()}
    lazy_rooms = [pltpu.VMEM(v.shape[1:] if name in halves else v.shape, v.dtype) for name, v in lazy.items()]
    lazy_names, late_names = list(lazy), list(late)

    def body(*refs):
        r = Refs()
        count = len(names)
        rest = list(refs[count:])
        by_name = dict(zip(names, refs))
        r.loads, r.late, r.stores = {}, {}, []
        held = rest[: len(lazy) + len(late)]
        for n, name in enumerate(lazy_names):
            src = by_name[name].at[lax.axis_index(TP)] if name in halves else by_name[name]
            r.loads[name] = pltpu.make_async_copy(src, held[n], rest[-2].at[n])
            by_name[name] = held[n]
        for n, name in enumerate(late_names):
            r.late[name] = (held[len(lazy) + n], by_name[name], rest[-1].at[n])
            by_name[name] = held[len(lazy) + n]
        for name, ref in by_name.items():
            setattr(r, name, ref)
        for load in r.loads.values():
            load.start()
        kernel(r)
        r.need(*lazy_names)
        for store in r.stores:
            store.wait()

    vmem = pl.BlockSpec(memory_space=pltpu.VMEM)
    hbm = pl.BlockSpec(memory_space=pl.ANY)
    came = pl.pallas_call(
        body,
        out_shape=[*outs.values(), *late.values()],
        in_specs=[vmem] * len(near) + [hbm] * (len(far) + len(lazy)),
        out_specs=[vmem] * len(outs) + [hbm] * len(late),
        scratch_shapes=[
            *scratch.values(), *lazy_rooms, *map(room, late.values()),
            pltpu.SemaphoreType.DMA((max(1, len(lazy)),)), pltpu.SemaphoreType.DMA((max(1, len(late)),)),
        ],
        compiler_params=pltpu.CompilerParams(
            collective_id=number, has_side_effects=True, vmem_limit_bytes=61 << 20
        ),
        cost_estimate=pl.CostEstimate(flops=0, bytes_accessed=int(micros * 3.6e6), transcendentals=0),
    )(*near.values(), *far.values(), *lazy.values())
    result = Refs()
    for name, value in zip([*outs, *late], came):
        setattr(result, name, value)
    return result


def sems(name, count):
    return {f"{name}_send": pltpu.SemaphoreType.DMA((count,)), f"{name}_recv": pltpu.SemaphoreType.DMA((count,))}


def sum_room(rows, width, prefix=""):
    names = ("from_x", "from_y", "passed", "last")
    return {prefix + name: pltpu.VMEM((2, rows // 2, width), jnp.bfloat16) for name in names}


def shape16(*dims):
    return jax.ShapeDtypeStruct(dims, jnp.bfloat16)


def shape32(*dims):
    return jax.ShapeDtypeStruct(dims, jnp.float32)


def room(like):
    return pltpu.VMEM(like.shape, like.dtype)


def mlp_step(normed, middle, gain, valid, weights):
    rows, width = middle.shape
    pairs, units = weights.shape[0], weights.shape[2] // 3
    kept = shape16(pairs, 4, rows, units)
    return linked(
        mlp_kernel, 12, 75,
        dict(gain=gain, valid=valid), dict(normed=normed), dict(weights=weights, middle=middle),
        dict(stream=shape32(rows, width), normed_next=shape16(rows, width), stats=shape32(16, 128)),
        dict(full=shape16(4, rows, width), hidden=kept, gate=kept, up=kept),
        dict(
            part=pltpu.VMEM((4, rows, width), jnp.bfloat16), load=pltpu.SemaphoreType.DMA((1,)),
            **sum_room(rows, width), **sems("ag", 6), **sems("rs", 10),
        ),
    )


def mlp_back_step(rows_own, middle, gain, grad, weights, grad_all=None, kept=None, share=None):
    rows, width = middle.shape
    pairs, units = weights.shape[0], weights.shape[2] // 3
    both = grad_all is not None
    whole, unit = shape16(4, rows, width), shape16(pairs, 4, rows, units)
    far = dict(rows_own=rows_own)
    lazy = dict(weights=weights)
    late = dict(summed=shape16(width, 3 * units))
    scratch = dict(
        full=room(whole), part=room(whole), load=pltpu.SemaphoreType.DMA((2,)),
        **{f"came_{p}": pltpu.VMEM((width, units), jnp.bfloat16) for p in range(3)},
        **sum_room(rows, width), **sems("ag", 6), **sems("rs", 10), **sems(TP, 3),
    )
    if both:
        lazy["grad_all"] = grad_all
        late["part_out"] = whole
        scratch.update(grad_gate=room(unit), grad_up=room(unit), hidden=room(unit))
    else:
        far["share"] = share
        lazy.update(grad_gate=kept.gate, grad_up=kept.up, hidden=kept.hidden, normed=kept.full)
        late["gathered"] = shape16(4, share.shape[0] // 2, share.shape[1])
        scratch.update(**sems("ja", 6))
    lazy.update(middle=middle, grad=grad)
    return linked(
        functools.partial(mlp_back_kernel, both), 13 if both else 5, 85,
        dict(gain=gain), far, lazy,
        dict(grad_new=shape32(rows, width), grad_rows=shape16(rows, width), gain_rows=shape32(16, width)),
        late, scratch,
    )


def attend_step(normed, stream, gain, valid, weights, cosine, sine, bias, share=None):
    first = share is not None
    rows, width = stream[0].shape[1:] if first else stream.shape
    pairs = weights.shape[0]
    far, lazy = {}, dict(weights=weights, cosine=cosine, sine=sine)
    if first:
        far["share"] = share
        lazy["normed"] = normed
    else:
        far["normed"] = normed
    lazy.update(bias=bias, stream=stream)
    return linked(
        functools.partial(attend_kernel, first), 11 if first else 9, 75,
        dict(gain=gain, valid=valid), far, lazy,
        dict(middle=shape32(rows, width), normed_next=shape16(rows, width), stats=shape32(16, 128)),
        dict(
            full=shape16(4, rows, width), query=shape16(pairs, 2, 4, rows, HEAD_DIM),
            key=shape16(pairs, 4, rows, HEAD_DIM), value=shape16(pairs, 4, rows, HEAD_DIM),
            lse=shape32(pairs, 4, 1, 2 * rows), mixed=shape16(pairs, 4, rows, 2 * HEAD_DIM),
        ),
        dict(
            part=pltpu.VMEM((4, rows, width), jnp.bfloat16), load=pltpu.SemaphoreType.DMA((1,)),
            **sum_room(rows, width), **sems("ag", 6), **sems("rs", 10),
        ),
    )


def attend_back_step(
    rows_own, stream, gain, grad, weights, cosine, sine, bias, kept, normed, shares=None, end=None
):
    rows, width = rows_own.shape
    pairs = weights.shape[0]
    length = 4 * rows
    last = shares is not None
    whole = shape16(4, rows, width)
    near = dict(gain=gain)
    far = dict(rows_own=rows_own, bias_in=bias)
    lazy = dict(
        weights=weights, key=kept.key, value=kept.value, query=kept.query, lse=kept.lse, mixed=kept.mixed,
        cosine=cosine, sine=sine, normed=normed, stream=stream, grad=grad,
    )
    sizes = (4 * HEAD_DIM, 2 * HEAD_DIM)
    total = sum(sizes) + 64
    outs = dict(gain_rows=shape32(16, width))
    late = dict(summed=shape16(width, total))
    scratch = dict(
        full=room(whole), part=room(whole),
        heads=room(kept.query), g_key=pltpu.VMEM(kept.key.shape, jnp.float32),
        g_value=pltpu.VMEM(kept.key.shape, jnp.float32), g_query=pltpu.VMEM((HEAD_DIM, 2 * rows), jnp.float32),
        grad_qkv=pltpu.VMEM((pairs, 4, rows, sizes[0]), jnp.bfloat16),
        bias=pltpu.VMEM((2, length, 2 * rows), jnp.bfloat16), bias_load=pltpu.SemaphoreType.DMA((4,)),
        came_0=pltpu.VMEM((width, sizes[0]), jnp.bfloat16), came_1=pltpu.VMEM((width, 256), jnp.bfloat16),
        load=pltpu.SemaphoreType.DMA((3,)),
        **sum_room(rows, width), **sems("ag", 6), **sems("rs", 10), **sems(TP, 4),
    )
    if last:
        far.update(share_a=shares[0], share_b=shares[1])
        outs.update(grad_new=shape32(2, rows, width))
        late.update(
            gathered_a=shape16(4, shares[0].shape[0] // 2, shares[0].shape[1]),
            gathered_b=shape16(4, *shares[1].shape),
        )
        scratch.update(**sems("ja", 6), **sems("jb", 6))
    else:
        lazy = dict(end_part=end[0], **lazy, end_middle=end[1])
        near["valid"] = end[2]
        outs.update(grad_new=shape32(rows, width), grad_rows=shape16(rows, width), stats=shape32(16, 128))
        late["out"] = shape16(2, rows, width)
        scratch.update(**sum_room(rows, width, "end_"), **sems("end", 10), **sems("out", 1))
    return linked(
        functools.partial(attend_back_kernel, last), 7 if last else 6, 100, near, far, lazy, outs, late, scratch,
    )


def tail_step(summed, share, attn_stats, mlp_stats, gain_rows):
    depth = lax.axis_size(FSDP)
    half, cols = share.shape[0] // 2, summed.shape[1]
    last = shape16(4, half, cols)
    wide = summed.shape[0] + 128
    return linked(
        functools.partial(tail_kernel, summed.shape[0]), 10, 60,
        dict(
            summed=summed,
            **{f"attn_stats_{layer}": a for layer, a in enumerate(attn_stats)},
            **{f"mlp_stats_{layer}": a for layer, a in enumerate(mlp_stats)},
            **{f"gain_rows_{n}": a for n, a in enumerate(gain_rows)},
        ),
        dict(share=share), {},
        dict(last_0=last, last_1=last, all_stats=shape32(8, 128), gains=shape32(8, summed.shape[0] // depth)), dict(gathered=shape16(4, *share.shape)),
        dict(
            z_came=pltpu.VMEM((2, depth, half, cols), jnp.bfloat16), stat_sent=pltpu.VMEM((4, 8, wide), jnp.float32),
            stat_came=pltpu.VMEM((3, 8, wide), jnp.float32), stat_z=pltpu.VMEM((depth, 8, wide), jnp.float32),
            load=pltpu.SemaphoreType.DMA((1,)), **sems("z", 2 * depth), **sems("ag", 6), **sems("stat", 3 + depth),
            **sems("l0", 6), **sems("l1", 6),
        ),
    )


def start_step(attn_gain, mlp_gain, places, starts, x, gate, up, down):
    depth, across = lax.axis_size(FSDP), lax.axis_size(CTX)
    layers, rows = gate.shape[:2]
    units = gate.shape[2] // across
    own = x.shape[1:]
    length = across * own[0]
    return linked(
        start_kernel, 8, 38,
        dict(attn_gain=attn_gain, mlp_gain=mlp_gain, places=places, starts=starts), dict(x=x, gate=gate, up=up, down=down), {},
        dict(
            all_gains=shape32(depth, 8, attn_gain.shape[1]),
            normed=shape16(across, *own),
        ),
        dict(
            bias=shape16(across, length, 2 * own[0]), cosine=shape32(across, own[0], HEAD_DIM),
            sine=shape32(across, own[0], HEAD_DIM),
            **{f"packed_{layer}": shape16(rows, 3 * units) for layer in range(layers)},
        ),
        dict(
            gains=pltpu.VMEM((8, attn_gain.shape[1]), jnp.float32),
            all_places=pltpu.VMEM((across, *places.shape), places.dtype),
            full=pltpu.VMEM((across, *own), jnp.bfloat16), turned=pltpu.VMEM((layers, units, rows), jnp.bfloat16),
            load=pltpu.SemaphoreType.DMA((3 + 3 * layers,)), **sems("gain", depth), **sems("place", across),
            **sems("ag", 6),
        ),
    )


def planned(
    tokens, positions, valid, piece_starts, d_out,
    attn_gain, w_query, w_key, w_value, w_out, mlp_gain, w_gate, w_up, w_down,
):
    seq_count, rows, width = tokens.shape
    layers = attn_gain.shape[0]
    ctx_count = lax.axis_size(CTX)
    tp_count = lax.axis_size(TP)
    me = lax.axis_index(CTX)
    side = lax.axis_index(TP)
    length = rows * ctx_count
    heads_q = HEADS // tp_count // ctx_count
    heads_k = KV_HEADS // tp_count // ctx_count
    cols_q = heads_q * HEAD_DIM
    cols_k = heads_k * HEAD_DIM
    units = w_gate.shape[2] // ctx_count

    def own(a):
        return lax.dynamic_index_in_dim(a, side, 0, keepdims=False)

    def cut(w, axis, count):
        return lax.dynamic_slice_in_dim(w, me * count, count, axis)

    def whole(w):
        return lax.all_gather(w, (TP, FSDP), axis=0, tiled=True).reshape(
            tp_count, width, w.shape[1]
        )

    def pack(*pieces):
        return with_layout_constraint(jnp.concatenate(pieces, axis=1), Layout(major_to_minor=(0, 1)))

    def pack_attn(layer, w_query, w_key, w_value, w_out):
        return pack(
            cut(w_query[layer], 1, cols_q),
            cut(w_key[layer], 1, cols_k),
            cut(w_value[layer], 1, cols_k),
            cut(w_out[layer], 0, cols_q).T,
            jnp.zeros((w_query.shape[1], 64), w_query.dtype),
        )

    attn_w = [whole(pack_attn(0, w_query, w_key, w_value, w_out))]
    seq_pos, valid_f = own(positions), own(valid).astype(jnp.float32)[:, None]
    half_dim = HEAD_DIM // 2
    freqs = rope_base ** (-(jnp.arange(half_dim).astype(jnp.float32) * 2.0 / HEAD_DIM))
    angles = seq_pos.astype(jnp.float32)[:, None] * freqs
    begun = start_step(
        attn_gain, mlp_gain,
        jnp.concatenate([jnp.cos(angles), jnp.sin(angles), valid_f, jnp.zeros((rows, 127 - HEAD_DIM), jnp.float32)], axis=1),
        piece_starts, tokens, w_gate, w_up, w_down,
    )
    normed, bias = begun.normed, begun.bias
    packed_mlp = [getattr(begun, f"packed_{layer}") for layer in range(layers)]
    gains = begun.all_gains.swapaxes(0, 1).reshape(8, width)
    cosine, sine_t = begun.cosine, begun.sine
    gain_a = [gains[layer][None] for layer in range(layers)]
    gain_m = [gains[layers + layer][None] for layer in range(layers)]
    grad = (d_out,)
    mlp_w = [whole(packed_mlp[0])]

    streams, attends, mlps = [(tokens,)], [], []
    for layer in range(layers):
        kept = attend_step(
            normed, streams[layer], gain_m[layer], valid_f, attn_w[layer], cosine, sine_t, bias,
            None if layer else d_out,
        )
        if layer == 0:
            grad_all, kept.full = kept.full, normed
        attends.append(kept)
        if layer + 1 < layers:
            normed_m, w_query, w_key, w_value, w_out, packed_mlp[layer + 1] = lax.optimization_barrier(
                (kept.normed_next, w_query, w_key, w_value, w_out, packed_mlp[layer + 1])
            )
            attn_w.append(whole(pack_attn(layer + 1, w_query, w_key, w_value, w_out)))
            mlp_w.append(whole(packed_mlp[layer + 1]))
            mlps.append(mlp_step(normed_m, kept.middle, gain_a[layer + 1], valid_f, mlp_w[layer]))
            streams.append(mlps[layer].stream)
            normed = mlps[layer].normed_next

    def reduced(g):
        return lax.psum_scatter(g, FSDP, scatter_dimension=0, tiled=True)

    down_rows = None
    attn_gains, mlp_gains = [], []
    for layer in reversed(range(layers)):
        kept = attends[layer]
        if layer + 1 == layers:
            came = mlp_back_step(kept.normed_next, kept.middle, gain_m[layer], grad, mlp_w[layer], grad_all=grad_all)
            end = [came.part_out, kept.middle, valid_f]
        else:
            came = mlp_back_step(
                down_rows, kept.middle, gain_m[layer], grad, mlp_w[layer], kept=mlps[layer], share=shares[0]
            )
        mlp_share = reduced(came.summed)
        mlp_gains.insert(0, came.gain_rows)
        back = attend_back_step(
            came.grad_rows, streams[layer], gain_a[layer], came.grad_new, attn_w[layer], cosine, sine_t, bias,
            kept, kept.full, None if layer else shares, end if layer else None,
        )
        attn_gains.insert(0, back.gain_rows)
        if layer:
            grad, output = back.grad_new, back.out
            down_rows, mlp_share, summed = lax.optimization_barrier((back.grad_rows, mlp_share, back.summed))
            shares = [mlp_share, reduced(summed)]
            last_stats = back.stats
    ended = tail_step(
        back.summed, mlp_share, [kept.stats for kept in attends], [kept.stats for kept in mlps] + [last_stats],
        attn_gains + mlp_gains,
    )
    input_grad = back.grad_new
    mlp_all = [[ended.gathered], [came.gathered, back.gathered_a]]
    attn_all = [[ended.last_0, ended.last_1], [back.gathered_b]]
    base = cols_q + 2 * cols_k
    placed = place_outs(
        attn_all, mlp_all,
        [(0, cols_q, False), (cols_q, cols_k, False), (cols_q + cols_k, cols_k, False), (base, cols_q, True)],
        [(0, units, False), (units, units, False), (2 * units, units, True)],
        [output, input_grad], [ended.gains, ended.all_stats],
    )
    return (*placed[7:9], placed[9], *placed[:4], placed[10], *placed[4:7], placed[11])


def place_kernel(moves, count, more, *refs):
    refs = list(refs)
    gains, stats = refs[:2]
    del refs[:2]
    outs_count = 1 + max(out for _, _, pieces in moves for _, _, _, out in pieces)
    ins, outs = refs[: count + more], refs[count + more : count + outs_count + 2 * more]
    del refs[: count + outs_count + 2 * more]
    attn_gain, mlp_gain, roots = refs[:3]
    del refs[:3]
    layers = attn_gain.shape[0]
    attn_gain[...] = gains[0:layers, :]
    mlp_gain[...] = gains[layers : 2 * layers, :]
    for layer in range(layers):
        roots[layer : layer + 1, :] = stats[0:1, 3 * layer : 3 * layer + 3]
    held, laid = refs[: count + more], refs[count + more : -2]
    in_sems, out_sems = refs[-2:]
    loads = [pltpu.make_async_copy(ins[n], held[n], in_sems.at[n]) for n in range(count + more)]
    for load in loads[:2]:
        load.start()
    stores = []
    for n, (layer, first, pieces) in enumerate(moves):
        loads[n].wait()
        if n + 2 < len(loads):
            loads[n + 2].start()
        rows = held[n].shape[1]
        for start, size, flip, out in pieces:
            for c in range(held[n].shape[0]):
                block = held[n][c, :, start : start + size].astype(jnp.float32)
                if flip:
                    laid[out][layer, c * size : (c + 1) * size, first : first + rows] = block.T
                else:
                    laid[out][layer, first : first + rows, c * size : (c + 1) * size] = block
            if any(layer == l and out == o for l, _, more in moves[n + 1 :] for _, _, _, o in more):
                continue
            store = pltpu.make_async_copy(laid[out].at[layer], outs[out].at[layer], out_sems.at[len(stores)])
            store.start()
            stores.append(store)
    for n in range(more):
        if len(moves) + 2 <= count + n:
            loads[count + n].start()
        loads[count + n].wait()
        store = pltpu.make_async_copy(held[count + n], outs[outs_count + n], out_sems.at[len(stores)])
        store.start()
        stores.append(store)
    for store in stores:
        store.wait()


def place_outs(attn_all, mlp_all, attn_pieces, mlp_pieces, handed, small):
    layers = len(attn_all)
    shapes = []
    for came, pieces in ((attn_all, attn_pieces), (mlp_all, mlp_pieces)):
        ctx_count = came[0][0].shape[0]
        depth = sum(a.shape[1] for a in came[0])
        for _, size, flip in pieces:
            wide = ctx_count * size
            shapes.append((layers, wide, depth) if flip else (layers, depth, wide))
    ins, moves = [], []
    for layer in reversed(range(layers)):
        for came, pieces, base in ((mlp_all, mlp_pieces, len(attn_pieces)), (attn_all, attn_pieces, 0)):
            first = 0
            for a in came[layer]:
                ins.append(a)
                moves.append((layer, first, [(*piece, base + n) for n, piece in enumerate(pieces)]))
                first += a.shape[1]
    hbm, vmem = pl.BlockSpec(memory_space=pl.ANY), pl.BlockSpec(memory_space=pltpu.VMEM)
    return pl.pallas_call(
        functools.partial(place_kernel, moves, len(ins), len(handed)),
        out_shape=[jax.ShapeDtypeStruct(s, jnp.float32) for s in shapes]
        + [jax.ShapeDtypeStruct(a.shape, a.dtype) for a in handed]
        + [shape32(layers, small[0].shape[1])] * 2 + [shape32(layers, 3)],
        in_specs=[vmem] * 2 + [hbm] * (len(ins) + len(handed)),
        out_specs=[hbm] * (len(shapes) + len(handed)) + [vmem] * 3,
        scratch_shapes=[pltpu.VMEM(a.shape, a.dtype) for a in ins + handed]
        + [pltpu.VMEM(s, jnp.float32) for s in shapes]
        + [pltpu.SemaphoreType.DMA((len(ins) + len(handed),)),
           pltpu.SemaphoreType.DMA((layers * len(shapes) + len(handed),))],
        compiler_params=pltpu.CompilerParams(vmem_limit_bytes=60 << 20),
    )(*small, *ins, *handed)


def fits(mesh):
    tp_count, ctx_count = mesh.shape[TP], mesh.shape[CTX]
    return ctx_count == 4 and tp_count == 2


def solution(mesh):
    in_specs = (
        P(FSDP, CTX, None),
        P(FSDP, CTX),
        P(FSDP, CTX),
        P(FSDP, None),
        P(FSDP, CTX, None),
        P(None, FSDP),
        P(None, FSDP, TP),
        P(None, FSDP, TP),
        P(None, FSDP, TP),
        P(None, TP, FSDP),
        P(None, FSDP),
        P(None, FSDP, TP),
        P(None, FSDP, TP),
        P(None, TP, FSDP),
    )
    out_specs = (
        P(FSDP, CTX, None),
        P(FSDP, CTX, None),
        P(None, FSDP),
        P(None, FSDP, TP),
        P(None, FSDP, TP),
        P(None, FSDP, TP),
        P(None, TP, FSDP),
        P(None, FSDP),
        P(None, FSDP, TP),
        P(None, FSDP, TP),
        P(None, TP, FSDP),
        P(),
    )
    return jax.shard_map(planned if fits(mesh) else general, mesh=mesh, in_specs=in_specs, out_specs=out_specs, check_vma=False)
```

```python
import functools

import jax
import jax.numpy as jnp
from jax import lax
from jax.experimental import pallas as pl
from jax.experimental.layout import Layout, with_layout_constraint
from jax.experimental.pallas import tpu as pltpu
from jax.sharding import PartitionSpec as P

MESH = pl.DeviceIdType.MESH
FSDP, CTX, TP = "fsdp", "ctx", "tp"

HEADS = 16
KV_HEADS = 8
HEAD_DIM = 96
PIECE_LEN = 256


epsilon = 1e-05
rope_base = 100000.0
neg_big = -1e30


def rope_tables(positions, head_dim):
    half_dim = head_dim // 2
    freqs = rope_base ** (-(jnp.arange(half_dim).astype(jnp.float32) * 2.0 / head_dim))
    angles = positions.astype(jnp.float32)[..., None] * freqs
    return (jnp.cos(angles)[:, :, None, :], jnp.sin(angles)[:, :, None, :])


def rotate(values, cosine, sine_t):
    half_dim = values.shape[-1] // 2
    lead_part = values[..., :half_dim]
    tail_part = values[..., half_dim:]
    return jnp.concatenate(
        [lead_part * cosine - tail_part * sine_t, tail_part * cosine + lead_part * sine_t], axis=-1
    )


def normalize(stream, gain_vec):
    inv_rms = lax.rsqrt(jnp.mean(stream * stream, axis=-1, keepdims=True) + epsilon)
    return stream * inv_rms * gain_vec.astype(jnp.float32)


def norm_back(stream, gain_vec, grad_out):
    inv_rms = lax.rsqrt(jnp.mean(stream * stream, axis=-1, keepdims=True) + epsilon)
    scaled_grad = gain_vec.astype(jnp.float32) * grad_out
    grad_in = inv_rms * scaled_grad - stream * inv_rms**3 * jnp.mean(
        scaled_grad * stream, axis=-1, keepdims=True
    )
    grad_gain = jnp.sum(grad_out * stream * inv_rms, axis=0)
    return (grad_in, grad_gain)


def score_block(query_b, key_heads, allowed, score_scale):
    raw_scores = (
        jnp.einsum("sckgd,snkd->skgcn", query_b, key_heads, preferred_element_type=jnp.float32)
        * score_scale
    )
    return jnp.where(allowed[:, None, None], raw_scores, neg_big)


def general(
    tokens,
    positions,
    valid,
    piece_starts,
    d_out,
    attn_gain,
    w_query,
    w_key,
    w_value,
    w_out,
    mlp_gain,
    w_gate,
    w_up,
    w_down,
):
    seq_count, shard_len, model_width = tokens.shape
    tok_rows = seq_count * shard_len
    tp_count = lax.axis_size(TP)
    local_heads = HEADS // tp_count
    local_kv = KV_HEADS // tp_count
    group_size = HEADS // KV_HEADS
    score_scale = HEAD_DIM ** (-0.5)
    seq_length = shard_len * lax.axis_size(CTX)
    start_tok = lax.axis_index(CTX) * shard_len
    query_index = start_tok + jnp.arange(shard_len, dtype=jnp.int32)
    key_index = jnp.arange(seq_length, dtype=jnp.int32)
    cosine, sine_t = rope_tables(positions, HEAD_DIM)
    valid_flat = valid.astype(jnp.float32).reshape(tok_rows)
    in_query = (query_index[None, None, :] >= piece_starts[:, :, None]) & (
        query_index[None, None, :] < piece_starts[:, :, None] + PIECE_LEN
    )
    in_key = (key_index[None, None, :] >= piece_starts[:, :, None]) & (
        key_index[None, None, :] < piece_starts[:, :, None] + PIECE_LEN
    )
    same_piece = jnp.any(in_query[:, :, :, None] & in_key[:, :, None, :], axis=1)
    causal = key_index[None, :] <= query_index[:, None]
    diagonal = key_index[None, :] == query_index[:, None]
    layer_count = attn_gain.shape[0]
    stream = tokens.astype(jnp.float32).reshape(tok_rows, model_width)
    saved = []
    stat_rows = []
    for layer_no in range(layer_count):
        weights = (
            lax.all_gather(attn_gain[layer_no], FSDP, axis=0, tiled=True),
            lax.all_gather(w_query[layer_no], FSDP, axis=0, tiled=True),
            lax.all_gather(w_key[layer_no], FSDP, axis=0, tiled=True),
            lax.all_gather(w_value[layer_no], FSDP, axis=0, tiled=True),
            lax.all_gather(w_out[layer_no], FSDP, axis=1, tiled=True),
            lax.all_gather(mlp_gain[layer_no], FSDP, axis=0, tiled=True),
            lax.all_gather(w_gate[layer_no], FSDP, axis=0, tiled=True),
            lax.all_gather(w_up[layer_no], FSDP, axis=0, tiled=True),
            lax.all_gather(w_down[layer_no], FSDP, axis=1, tiled=True),
        )
        gain_a, w_q, w_k, w_v, w_o, gain_m, w_g, w_u, w_d = weights
        normed_a = normalize(stream, gain_a).astype(jnp.bfloat16)
        query_heads = jnp.dot(normed_a, w_q, preferred_element_type=jnp.float32).reshape(
            seq_count, shard_len, local_heads, HEAD_DIM
        )
        query_b = (
            rotate(query_heads, cosine, sine_t)
            .astype(jnp.bfloat16)
            .reshape(seq_count, shard_len, local_kv, group_size, HEAD_DIM)
        )
        key_local = jnp.dot(normed_a, w_k, preferred_element_type=jnp.float32).reshape(
            seq_count, shard_len, local_kv, HEAD_DIM
        )
        key_local = (
            rotate(key_local, cosine, sine_t)
            .astype(jnp.bfloat16)
            .reshape(seq_count, shard_len, local_kv * HEAD_DIM)
        )
        value_local = (
            jnp.dot(normed_a, w_v, preferred_element_type=jnp.float32)
            .astype(jnp.bfloat16)
            .reshape(seq_count, shard_len, local_kv * HEAD_DIM)
        )
        key_all, value_all, valid_all = (
            lax.all_gather(key_local, CTX, axis=1, tiled=True),
            lax.all_gather(value_local, CTX, axis=1, tiled=True),
            lax.all_gather(valid.astype(jnp.bfloat16), CTX, axis=1, tiled=True),
        )
        allowed = (causal[None] | same_piece) & ((valid_all[:, None, :] > 0.5) | diagonal[None])
        key_heads = key_all.reshape(seq_count, seq_length, local_kv, HEAD_DIM)
        value_heads = value_all.reshape(seq_count, seq_length, local_kv, HEAD_DIM)
        raw_scores = score_block(query_b, key_heads, allowed, score_scale)
        row_max = jnp.max(raw_scores, axis=-1, keepdims=True)
        log_total = row_max + jnp.log(
            jnp.sum(jnp.exp(raw_scores - row_max), axis=-1, keepdims=True)
        )
        softmax_b = jnp.exp(raw_scores - log_total).astype(jnp.bfloat16)
        mixed_heads = jnp.einsum(
            "skgcn,snkd->sckgd", softmax_b, value_heads, preferred_element_type=jnp.float32
        )
        mixed_b = mixed_heads.astype(jnp.bfloat16).reshape(tok_rows, local_heads * HEAD_DIM)
        attn_branch = lax.psum(
            jnp.dot(mixed_b, w_o, preferred_element_type=jnp.float32).astype(jnp.bfloat16), TP
        ).astype(jnp.float32)
        middle = stream + attn_branch
        normed_m = normalize(middle, gain_m).astype(jnp.bfloat16)
        gate_act = jnp.dot(normed_m, w_g, preferred_element_type=jnp.float32)
        up_act = jnp.dot(normed_m, w_u, preferred_element_type=jnp.float32)
        hidden = (jax.nn.silu(gate_act) * up_act).astype(jnp.bfloat16)
        mlp_branch = lax.psum(
            jnp.dot(hidden, w_d, preferred_element_type=jnp.float32).astype(jnp.bfloat16), TP
        ).astype(jnp.float32)
        stat_rows.append(
            jnp.stack(
                [
                    jnp.sum(valid_flat[:, None] * stream * stream),
                    jnp.sum(valid_flat[:, None] * attn_branch * attn_branch),
                    jnp.sum(valid_flat[:, None] * mlp_branch * mlp_branch),
                ]
            )
        )
        kept_weights = None
        saved.append(
            (
                stream,
                normed_a,
                query_b,
                key_heads,
                value_heads,
                allowed,
                log_total,
                mixed_b,
                middle,
                normed_m,
                gate_act,
                up_act,
                hidden,
                kept_weights,
            )
        )
        stream = middle + mlp_branch
    output = stream.astype(jnp.bfloat16).reshape(seq_count, shard_len, model_width)
    total_squares, total_count = lax.psum(
        (jnp.stack(stat_rows), jnp.sum(valid_flat)), (FSDP, CTX)
    )
    rms_stats = jnp.sqrt(total_squares / (total_count * model_width))
    grad_stream = d_out.astype(jnp.float32).reshape(tok_rows, model_width)
    results = [None] * layer_count
    for layer_no in reversed(range(layer_count)):
        (
            stream_in,
            normed_a,
            query_b,
            key_heads,
            value_heads,
            allowed,
            log_total,
            mixed_b,
            middle,
            normed_m,
            gate_act,
            up_act,
            hidden,
            kept_weights,
        ) = saved[layer_no]
        weights = (
            lax.all_gather(attn_gain[layer_no], FSDP, axis=0, tiled=True),
            lax.all_gather(w_query[layer_no], FSDP, axis=0, tiled=True),
            lax.all_gather(w_key[layer_no], FSDP, axis=0, tiled=True),
            lax.all_gather(w_value[layer_no], FSDP, axis=0, tiled=True),
            lax.all_gather(w_out[layer_no], FSDP, axis=1, tiled=True),
            lax.all_gather(mlp_gain[layer_no], FSDP, axis=0, tiled=True),
            lax.all_gather(w_gate[layer_no], FSDP, axis=0, tiled=True),
            lax.all_gather(w_up[layer_no], FSDP, axis=0, tiled=True),
            lax.all_gather(w_down[layer_no], FSDP, axis=1, tiled=True),
        )
        gain_a, w_q, w_k, w_v, w_o, gain_m, w_g, w_u, w_d = weights
        grad_mlp = grad_stream.astype(jnp.bfloat16)
        grad_hidden = jnp.einsum("rd,fd->rf", grad_mlp, w_d, preferred_element_type=jnp.float32)
        g_down = jnp.einsum("rf,rd->fd", hidden, grad_mlp, preferred_element_type=jnp.float32)
        sigmoid_g = jax.nn.sigmoid(gate_act)
        grad_gate = (
            grad_hidden * up_act * sigmoid_g * (1.0 + gate_act * (1.0 - sigmoid_g))
        ).astype(jnp.bfloat16)
        grad_up = (grad_hidden * gate_act * sigmoid_g).astype(jnp.bfloat16)
        grad_normed_m = lax.psum(
            (
                jnp.einsum("rf,df->rd", grad_gate, w_g, preferred_element_type=jnp.float32)
                + jnp.einsum("rf,df->rd", grad_up, w_u, preferred_element_type=jnp.float32)
            ).astype(jnp.bfloat16),
            TP,
        ).astype(jnp.float32)
        g_gate = jnp.einsum("rd,rf->df", normed_m, grad_gate, preferred_element_type=jnp.float32)
        g_up = jnp.einsum("rd,rf->df", normed_m, grad_up, preferred_element_type=jnp.float32)
        grad_from_norm, g_gain_m = norm_back(middle, gain_m, grad_normed_m)
        grad_middle = grad_stream + grad_from_norm
        grad_attn = grad_middle.astype(jnp.bfloat16)
        grad_heads = jnp.einsum(
            "rd,hd->rh", grad_attn, w_o, preferred_element_type=jnp.float32
        ).astype(jnp.bfloat16)
        g_out = jnp.einsum("rh,rd->hd", mixed_b, grad_attn, preferred_element_type=jnp.float32)
        grad_heads = grad_heads.reshape(seq_count, shard_len, local_kv, group_size, HEAD_DIM)
        raw_scores = score_block(query_b, key_heads, allowed, score_scale)
        softmax_p = jnp.exp(raw_scores - log_total)
        grad_probs = jnp.einsum(
            "sckgd,snkd->skgcn", grad_heads, value_heads, preferred_element_type=jnp.float32
        )
        row_dots = jnp.sum(softmax_p * grad_probs, axis=-1, keepdims=True)
        grad_scores = (softmax_p * (grad_probs - row_dots)).astype(jnp.bfloat16)
        grad_query = (
            jnp.einsum(
                "skgcn,snkd->sckgd", grad_scores, key_heads, preferred_element_type=jnp.float32
            )
            * score_scale
        )
        grad_key_all = (
            jnp.einsum(
                "skgcn,sckgd->snkd", grad_scores, query_b, preferred_element_type=jnp.float32
            )
            * score_scale
        )
        grad_value_all = jnp.einsum(
            "skgcn,sckgd->snkd",
            softmax_p.astype(jnp.bfloat16),
            grad_heads,
            preferred_element_type=jnp.float32,
        )
        grad_key, grad_value = (
            lax.psum_scatter(
                grad_key_all.reshape(seq_count, seq_length, local_kv * HEAD_DIM).astype(
                    jnp.bfloat16
                ),
                CTX,
                scatter_dimension=1,
                tiled=True,
            ).astype(jnp.float32),
            lax.psum_scatter(
                grad_value_all.reshape(seq_count, seq_length, local_kv * HEAD_DIM).astype(
                    jnp.bfloat16
                ),
                CTX,
                scatter_dimension=1,
                tiled=True,
            ).astype(jnp.float32),
        )
        grad_query_b = rotate(
            grad_query.reshape(seq_count, shard_len, local_heads, HEAD_DIM), cosine, -sine_t
        )
        grad_query_b = grad_query_b.astype(jnp.bfloat16).reshape(tok_rows, local_heads * HEAD_DIM)
        grad_key_b = rotate(
            grad_key.reshape(seq_count, shard_len, local_kv, HEAD_DIM), cosine, -sine_t
        )
        grad_key_b = grad_key_b.astype(jnp.bfloat16).reshape(tok_rows, local_kv * HEAD_DIM)
        grad_value_b = grad_value.astype(jnp.bfloat16).reshape(tok_rows, local_kv * HEAD_DIM)
        grad_normed_a = lax.psum(
            (
                jnp.einsum("rh,dh->rd", grad_query_b, w_q, preferred_element_type=jnp.float32)
                + jnp.einsum("rh,dh->rd", grad_key_b, w_k, preferred_element_type=jnp.float32)
                + jnp.einsum("rh,dh->rd", grad_value_b, w_v, preferred_element_type=jnp.float32)
            ).astype(jnp.bfloat16),
            TP,
        ).astype(jnp.float32)
        g_query = jnp.einsum(
            "rd,rh->dh", normed_a, grad_query_b, preferred_element_type=jnp.float32
        )
        g_key = jnp.einsum("rd,rh->dh", normed_a, grad_key_b, preferred_element_type=jnp.float32)
        g_value = jnp.einsum(
            "rd,rh->dh", normed_a, grad_value_b, preferred_element_type=jnp.float32
        )
        grad_from_attn_norm, g_gain_a = norm_back(stream_in, gain_a, grad_normed_a)
        grad_stream = grad_middle + grad_from_attn_norm
        grad_terms = (g_gain_a, g_query, g_key, g_value, g_out, g_gain_m, g_gate, g_up, g_down)
        shares = (
            lax.psum_scatter(grad_terms[0], (FSDP, CTX), scatter_dimension=0, tiled=True),
            lax.psum_scatter(grad_terms[1], (FSDP, CTX), scatter_dimension=0, tiled=True),
            lax.psum_scatter(grad_terms[2], (FSDP, CTX), scatter_dimension=0, tiled=True),
            lax.psum_scatter(grad_terms[3], (FSDP, CTX), scatter_dimension=0, tiled=True),
            lax.psum_scatter(grad_terms[4], (FSDP, CTX), scatter_dimension=1, tiled=True),
            lax.psum_scatter(grad_terms[5], (FSDP, CTX), scatter_dimension=0, tiled=True),
            lax.psum_scatter(grad_terms[6], (FSDP, CTX), scatter_dimension=0, tiled=True),
            lax.psum_scatter(grad_terms[7], (FSDP, CTX), scatter_dimension=0, tiled=True),
            lax.psum_scatter(grad_terms[8], (FSDP, CTX), scatter_dimension=1, tiled=True),
        )
        results[layer_no] = (
            lax.all_gather(shares[0].astype(jnp.bfloat16), CTX, axis=0, tiled=True).astype(
                jnp.float32
            ),
            lax.all_gather(shares[1].astype(jnp.bfloat16), CTX, axis=0, tiled=True).astype(
                jnp.float32
            ),
            lax.all_gather(shares[2].astype(jnp.bfloat16), CTX, axis=0, tiled=True).astype(
                jnp.float32
            ),
            lax.all_gather(shares[3].astype(jnp.bfloat16), CTX, axis=0, tiled=True).astype(
                jnp.float32
            ),
            lax.all_gather(shares[4].astype(jnp.bfloat16), CTX, axis=1, tiled=True).astype(
                jnp.float32
            ),
            lax.all_gather(shares[5].astype(jnp.bfloat16), CTX, axis=0, tiled=True).astype(
                jnp.float32
            ),
            lax.all_gather(shares[6].astype(jnp.bfloat16), CTX, axis=0, tiled=True).astype(
                jnp.float32
            ),
            lax.all_gather(shares[7].astype(jnp.bfloat16), CTX, axis=0, tiled=True).astype(
                jnp.float32
            ),
            lax.all_gather(shares[8].astype(jnp.bfloat16), CTX, axis=1, tiled=True).astype(
                jnp.float32
            ),
        )
    stacked = [
        jnp.stack([results[layer_no][member] for layer_no in range(layer_count)])
        for member in range(9)
    ]
    input_grad = grad_stream.reshape(seq_count, shard_len, model_width)
    return (
        output,
        input_grad,
        stacked[0],
        stacked[1],
        stacked[2],
        stacked[3],
        stacked[4],
        stacked[5],
        stacked[6],
        stacked[7],
        stacked[8],
        rms_stats,
    )


def partners():
    me = lax.axis_index(CTX)
    return me, me ^ 1, me ^ 2, me ^ 3


def greet(*places):
    barrier = pltpu.get_barrier_semaphore()
    for place in places:
        pl.semaphore_signal(barrier, inc=1, device_id=place, device_id_type=MESH)
    pl.semaphore_wait(barrier, len(places))


def send(src, dst, sems, slot, place):
    copy = pltpu.make_async_remote_copy(
        src_ref=src,
        dst_ref=dst,
        send_sem=sems[0].at[slot],
        recv_sem=sems[1].at[slot],
        device_id=place,
        device_id_type=MESH,
    )
    copy.start()
    return copy


def run(steps, work=()):
    for n, _ in enumerate(steps):
        if n < len(work):
            work[n]()


def gather_rows(full, sems, place, own):
    me, side_x, side_y, _ = place
    to_x, to_y = {CTX: side_x}, {CTX: side_y}
    half = full.shape[1] // 2
    top, low = pl.ds(0, half), pl.ds(half, half)
    first = [
        send(own.at[top], full.at[me, top], sems, 0, to_x),
        send(own.at[low], full.at[me, low], sems, 1, to_y),
    ]
    rest = [
        send(own.at[top], full.at[me, top], sems, 2, to_y),
        send(own.at[low], full.at[me, low], sems, 3, to_x),
    ]
    yield
    first[0].wait_recv()
    rest.append(send(full.at[side_x, top], full.at[side_x, top], sems, 4, to_y))
    first[1].wait_recv()
    rest.append(send(full.at[side_y, low], full.at[side_y, low], sems, 5, to_x))
    yield
    rest[0].wait_recv()
    rest[1].wait_recv()
    yield
    rest[2].wait_recv()
    rest[3].wait_recv()
    for copy in first + rest:
        copy.wait_send()


def dot32(a, b, dims):
    return lax.dot_general(a, b, (dims, ((), ())), preferred_element_type=jnp.float32)


def start_kernel(r):
    place = partners()
    me, side_x, side_y, across = place
    groups = (
        (FSDP, r.gains, r.all_gains, (r.gain_send, r.gain_recv)),
        (CTX, r.places, r.all_places, (r.place_send, r.place_recv)),
    )
    peers = []
    for axis, _, _, _ in groups:
        count = lax.axis_size(axis)
        peers.append([lax.rem(lax.axis_index(axis) + step, count) for step in range(1, count)])
    layers = r.attn_gain.shape[0]
    r.gains[...] = jnp.zeros_like(r.gains)
    r.gains[0:layers, :] = r.attn_gain[...].astype(jnp.float32)
    r.gains[layers : 2 * layers, :] = r.mlp_gain[...].astype(jnp.float32)
    full = r.full
    own = pltpu.make_async_copy(r.x.at[lax.axis_index(TP)], full.at[me], r.load.at[0])
    own.start()
    greet(*[{groups[n][0]: peer} for n in range(2) for peer in peers[n]])
    copies = []
    for n, (axis, src, dst, sems) in enumerate(groups):
        mine = pltpu.make_async_copy(src, dst.at[lax.axis_index(axis)], r.load.at[1 + n])
        mine.start()
        for step, peer in enumerate(peers[n]):
            copies.append(send(src, dst.at[lax.axis_index(axis)], sems, step, {axis: peer}))
        copies.append(mine)
    steps = gather_rows(full, (r.ag_send, r.ag_recv), place, r.x.at[lax.axis_index(TP)])
    next(steps)
    packed = [getattr(r, f"packed_{layer}") for layer in range(r.gate.shape[0])]
    layers, units = len(packed), r.turned.shape[1]
    loads = []
    for layer in range(layers):
        cut = pl.ds(pl.multiple_of(me * units, units), units)
        for n, (src, dst) in enumerate((
            (r.gate.at[layer, :, cut], packed[layer].at[:, pl.ds(0, units)]),
            (r.up.at[layer, :, cut], packed[layer].at[:, pl.ds(units, units)]),
            (r.down.at[layer, cut], r.turned.at[layer]),
        )):
            loads.append(pltpu.make_async_copy(src, dst, r.load.at[3 + 3 * layer + n]))
    for load in loads:
        load.start()
    own.wait()
    for copy in copies:
        copy.wait()
    gain = jnp.concatenate([r.all_gains[n, 0:1, :] for n in range(lax.axis_size(FSDP))], axis=1)
    rows = full.shape[1]
    half = rows // 2
    step = 16

    def norm(top_of, low_of):
        for part_no, owner in enumerate((top_of, low_of)):
            @pl.loop(0, half // step)
            def _(i):
                here = pl.ds(pl.multiple_of(part_no * half + i * step, step), step)
                row = full[owner, here, :].astype(jnp.float32)
                inv_rms = lax.rsqrt(jnp.mean(row * row, axis=-1, keepdims=True) + epsilon)
                r.normed[owner, here, :] = (row * inv_rms * gain).astype(jnp.bfloat16)

    def mask():
        length = r.bias.shape[1]
        block = 96
        query = lax.broadcasted_iota(jnp.int32, (1, length), 1)
        here = r.starts[pl.ds(lax.axis_index(TP), 1), :]
        firsts = [here[:, n : n + 1] for n in range(r.starts.shape[1])]
        in_query = [jnp.where((query >= f) & (query < f + PIECE_LEN), 1.0, 0.0) for f in firsts]
        for owner in range(r.all_places.shape[0]):
            @pl.loop(0, rows // block)
            def _(i):
                here = pl.ds(pl.multiple_of(i * block, block), block)
                key = owner * rows + i * block + lax.broadcasted_iota(jnp.int32, (block, 1), 0)
                valid = r.all_places[owner, here, HEAD_DIM : HEAD_DIM + 1]
                seen = 0
                for f, row in zip(firsts, in_query):
                    seen += jnp.where((key >= f) & (key < f + PIECE_LEN), 1.0, 0.0) * row
                seen = jnp.where(key <= query, 1.0, seen) * valid
                seen = jnp.where(key == query, 1.0, seen)
                added = jnp.where(seen > 0, 0.0, neg_big).astype(jnp.bfloat16)
                keys = pl.ds(pl.multiple_of(owner * rows + i * block, block), block)
                for n in range(r.all_places.shape[0]):
                    one = added[:, n * rows : (n + 1) * rows]
                    r.bias[n, keys, :] = jnp.concatenate([one, one], axis=1)

    norm(me, me)
    mask()
    r.keep("bias")
    half_dim = HEAD_DIM // 2
    for owner in range(r.all_places.shape[0]):
        table = r.all_places[owner]
        cos_b, sin_b = table[:, :half_dim], table[:, half_dim:HEAD_DIM]
        r.cosine[owner] = jnp.concatenate([cos_b, cos_b], axis=1)
        r.sine[owner] = jnp.concatenate([-sin_b, sin_b], axis=1)
    r.keep("cosine", "sine")
    next(steps)
    norm(side_x, side_y)
    for load in loads:
        load.wait()
    for layer in range(layers):
        packed[layer][:, 2 * units :] = r.turned[layer].astype(jnp.float32).T.astype(jnp.bfloat16)
        r.keep(f"packed_{layer}")
    next(steps)
    norm(side_y, side_x)
    run(steps)
    norm(across, across)


def stat_steps(r, place):
    depth = lax.axis_size(FSDP)
    level = lax.axis_index(FSDP)
    others = [{FSDP: lax.rem(level + step, depth)} for step in range(1, depth)]
    here = (r.stat_send, r.stat_recv)
    layers = len(r.attn_stats)
    lane = lax.broadcasted_iota(jnp.int32, (8, 128), 1)
    tile = jnp.zeros((8, 128), jnp.float32)
    wanted = [(3 * layers, r.attn_stats[0], 2)]
    for layer in range(layers):
        wanted += [(3 * layer, r.attn_stats[layer], 1), (3 * layer + 1, r.attn_stats[layer], 0)]
        wanted.append((3 * layer + 2, r.mlp_stats[layer], 0))
    for to, ref, at in wanted:
        row = jnp.sum(ref[...], axis=0, keepdims=True)
        value = jnp.sum(jnp.where(lane[0:1] == at, row, 0.0), axis=1, keepdims=True)
        tile += jnp.where(lane == to, value, 0.0)
    width = r.width
    r.stat_sent[0, :, pl.ds(width, 128)] = tile
    r.stat_sent[0, :, pl.ds(0, width)] = jnp.zeros((8, width), jnp.float32)
    for n, ref in enumerate(r.gain_rows):
        r.stat_sent[0, n : n + 1, pl.ds(0, width)] = jnp.sum(ref[...], axis=0, keepdims=True)
    for n, peer in enumerate((sibling(), {CTX: place[1]}, {CTX: place[2]})):
        copy = send(r.stat_sent.at[n], r.stat_came.at[n], here, n, peer)
        yield
        copy.wait()
        r.stat_sent[n + 1] = r.stat_sent[n] + r.stat_came[n]
    r.stat_z[level] = r.stat_sent[3]
    copies = [send(r.stat_z.at[level], r.stat_z.at[level], here, 3 + n, peer) for n, peer in enumerate(others)]
    yield
    for copy in copies:
        copy.wait()
    part = width // depth
    here = pl.ds(pl.multiple_of(level * part, 128), part)
    gains, held = r.stat_z[0, :, here], r.stat_z[0, :, pl.ds(width, 128)]
    for n in range(1, depth):
        gains += r.stat_z[n, :, here]
        held += r.stat_z[n, :, pl.ds(width, 128)]
    r.gains[...] = gains
    count = jnp.sum(jnp.where(lane[0:1] == 3 * layers, held[0:1], 0.0), axis=1, keepdims=True)
    r.all_stats[...] = jnp.sqrt(held / (count * r.width))


def tail_kernel(width, r):
    r.width = width
    place = partners()
    me = place[0]
    depth = lax.axis_size(FSDP)
    level = lax.axis_index(FSDP)
    peers = [lax.rem(level + step, depth) for step in range(1, depth)]
    mine = pltpu.make_async_copy(r.share, r.gathered.at[me], r.load.at[0])
    mine.start()
    rows = r.share.shape[0]
    half = rows // 2
    own = pltpu.make_async_copy(r.summed.at[pl.ds(pl.multiple_of(level * rows, rows), rows)], r.own, r.load.at[1])
    own.start()
    greet_near(place, sibling(), *[{FSDP: peer} for peer in peers])
    r.gain_rows = [r.gain_rows_0, r.gain_rows_1, r.gain_rows_2, r.gain_rows_3]
    r.attn_stats = [r.attn_stats_0, r.attn_stats_1]
    r.mlp_stats = [r.mlp_stats_0, r.mlp_stats_1]
    copies = []
    for part_no in range(2):
        copies.append([])
        for step, peer in enumerate(peers):
            block = r.summed.at[pl.ds(pl.multiple_of(peer * rows + part_no * half, half), half)]
            copies[part_no].append(
                send(block, r.z_came.at[part_no, level], (r.z_send, r.z_recv), part_no * depth + step, {FSDP: peer})
            )
    first = gather_rows(r.gathered, (r.ag_send, r.ag_recv), place, r.share)
    next(first)
    counts = stat_steps(r, place)
    r.need(*list(r.loads))
    next(counts)
    next(counts)
    next(first)
    own.wait()
    step = 48
    lasts = (r.last_0, r.last_1)
    steps = []
    for part_no in range(2):
        for copy in copies[part_no]:
            copy.wait_recv()

        @pl.loop(0, half // step)
        def _(i):
            here = pl.ds(pl.multiple_of(i * step, step), step)
            start = pl.multiple_of(part_no * half + i * step, step)
            total = r.own[pl.ds(start, step), :].astype(jnp.float32)
            for peer in peers:
                total += r.z_came[part_no, peer, here, :].astype(jnp.float32)
            lasts[part_no][me, here, :] = total.astype(jnp.bfloat16)

        steps.append(gather_rows(lasts[part_no], ((r.l0_send, r.l0_recv), (r.l1_send, r.l1_recv))[part_no], place, lasts[part_no].at[me]))
        next(steps[part_no])
        if part_no == 0:
            next(counts)
    next(steps[0])
    next(counts)
    next(steps[1])
    run(first)
    mine.wait()
    r.keep("gathered")
    run(steps[0])
    run(steps[1])
    run(counts)
    for copy in copies[0] + copies[1]:
        copy.wait_send()


class Scatter:
    def __init__(self, part, buffers, sems, place):
        self.part, self.sems, self.place = part, sems, place
        self.from_x, self.from_y, self.passed, self.last = buffers
        self.half = part.shape[1] // 2
        self.copies = {}

    def send(self, slot, src, dst, axis_peer):
        self.copies[slot] = send(src, dst, self.sems, slot, {CTX: axis_peer})

    def across(self):
        _, side_x, side_y, far = self.place
        self.send(0, self.part.at[far, pl.ds(0, self.half)], self.from_x.at[1], side_x)
        self.send(1, self.part.at[far, pl.ds(self.half, self.half)], self.from_y.at[1], side_y)

    def x_out(self, some=None):
        side_x = self.place[1]
        slot, rows = self.cut(some)
        self.send(slot, self.part.at[side_x, rows], self.from_x.at[0, rows], side_x)

    def y_out(self, some=None):
        side_y = self.place[2]
        slot, rows = self.cut(some)
        below = pl.ds(self.half + rows.start, rows.size)
        self.send(slot + 1, self.part.at[side_y, below], self.from_y.at[0, rows], side_y)

    def cut(self, some):
        if some is None:
            return 2, pl.ds(0, self.half)
        first = self.half // 48 * 16
        return (2, pl.ds(0, first)) if some == 0 else (6, pl.ds(first, self.half - first))

    def pieces(self):
        first = self.half // 32 * 16
        return (0, first), (first, self.half - first)

    def pass_on(self, side, owner, came, axis_peer):
        self.copies[side].wait_recv()
        step = 16
        for n, (first, count) in enumerate(self.pieces()):
            @pl.loop(0, count // step)
            def _(i):
                rows = pl.ds(pl.multiple_of(first + i * step, step), step)
                mine = self.part[owner, pl.ds(pl.multiple_of(side * self.half + first + i * step, step), step), :]
                total = mine.astype(jnp.float32) + came[1, rows, :].astype(jnp.float32)
                self.passed[side, rows, :] = total.astype(self.passed.dtype)

            piece = pl.ds(first, count)
            self.send(4 + side + 4 * n, self.passed.at[side, piece], self.last.at[side, piece], axis_peer)

    def forward(self):
        _, side_x, side_y, _ = self.place
        self.pass_on(0, side_y, self.from_x, side_y)
        self.pass_on(1, side_x, self.from_y, side_x)

    def finish(self):
        for slot in self.copies:
            if 1 < slot < 8:
                self.copies[slot].wait_recv()

    def each_row(self, work, step=16):
        me = self.place[0]
        for n, (first, count) in enumerate(self.pieces()):
            for side in range(2):
                if n == 1:
                    self.copies[8 + side].wait_recv()
                came = self.from_x if side == 0 else self.from_y

                @pl.loop(0, count // step)
                def _(i):
                    rows = pl.ds(pl.multiple_of(first + i * step, step), step)
                    whole = pl.ds(pl.multiple_of(side * self.half + first + i * step, step), step)
                    total = self.part[me, whole, :].astype(jnp.float32)
                    total += came[0, rows, :].astype(jnp.float32)
                    work(whole, total + self.last[side, rows, :].astype(jnp.float32))
        for copy in self.copies.values():
            copy.wait_send()


def scatter_steps(scatter):
    scatter.across()
    scatter.x_out()
    scatter.y_out()
    yield
    scatter.forward()
    yield
    scatter.finish()


class WeightGrads:
    def __init__(self, lefts, rights, sent, came, summed, sems):
        self.lefts, self.rights, self.sent, self.came, self.summed, self.sems = lefts, rights, sent, came, summed, sems
        self.sizes = [r.shape[-1] for r in rights]
        self.side = lax.axis_index(TP)
        self.copies = []

    def product(self, p, t, put):
        block = 768
        left, right = self.lefts[p], self.rights[p]
        width = left.shape[-1]

        @pl.loop(0, width // block)
        def _(i):
            cols = pl.ds(pl.multiple_of(i * block, block), block)
            one = left[:, :, cols].reshape(-1, block)
            put(cols, dot32(one, right[t].reshape(one.shape[0], -1), ((0,), (0,))).astype(jnp.bfloat16))

    def theirs(self, p):
        def put(rows, value):
            self.sent[p][rows, : self.sizes[p]] = value

        self.product(p, 1 - self.side, put)
        self.copies.append(send(self.sent[p], self.came[p], self.sems, p, {TP: 1 - self.side}))

    def cols(self, p):
        start = sum(self.sizes[:p])
        return slice(start, start + self.sizes[p])

    def ours(self, p):
        def put(rows, value):
            self.summed[rows, self.cols(p)] = value

        self.product(p, self.side, put)

    def add_up(self):
        step = 64
        for p, copy in enumerate(self.copies):
            copy.wait_recv()

            @pl.loop(0, self.summed.shape[0] // step)
            def _(i):
                rows = pl.ds(pl.multiple_of(i * step, step), step)
                total = self.summed[rows, self.cols(p)].astype(jnp.float32) + self.came[p][rows, : self.sizes[p]].astype(jnp.float32)
                self.summed[rows, self.cols(p)] = total.astype(jnp.bfloat16)

    def close(self):
        for copy in self.copies:
            copy.wait_send()


def add_stats(stats, valid, *values):
    lane = lax.broadcasted_iota(jnp.int32, stats.shape, 1)
    total = stats[...] + jnp.where(lane == 2, valid, 0.0)
    for n, value in enumerate(values):
        total += jnp.where(lane == n, valid * jnp.sum(value * value, axis=-1, keepdims=True), 0.0)
    stats[...] = total


def norm_sum(scatter, stream, gain, valid, middle, normed, stats):
    stats[...] = jnp.zeros_like(stats)

    def work(rows, branch):
        before = stream[rows, :].astype(jnp.float32)
        total = before + branch
        middle[rows, :] = total
        inv_rms = lax.rsqrt(jnp.mean(total * total, axis=-1, keepdims=True) + epsilon)
        normed[rows, :] = (total * inv_rms * gain[...]).astype(normed.dtype)
        add_stats(stats, valid[rows, :], branch, before)

    scatter.each_row(work)


def norm_sum_back(scatter, stream, gain, grad, gain_rows, put):
    gain_rows[...] = jnp.zeros_like(gain_rows)

    def work(rows, got):
        x = stream[rows, :].astype(jnp.float32)
        inv_rms = lax.rsqrt(jnp.mean(x * x, axis=-1, keepdims=True) + epsilon)
        scaled = gain[...] * got
        along = jnp.mean(scaled * x, axis=-1, keepdims=True)
        put(rows, grad[rows, :].astype(jnp.float32) + inv_rms * scaled - x * (inv_rms * inv_rms * inv_rms * along))
        gain_rows[...] += got * x * inv_rms

    scatter.each_row(work)


def rows_of(ref, lead, top_of, low_of):
    half = ref.shape[-2] // 2
    return jnp.concatenate([ref[(*lead, top_of, pl.ds(0, half))], ref[(*lead, low_of, pl.ds(half, half))]], axis=0)


def put_rows(ref, lead, top_of, low_of, value):
    half = ref.shape[-2] // 2
    ref[(*lead, top_of, pl.ds(0, half))] = value[:half].astype(ref.dtype)
    ref[(*lead, low_of, pl.ds(half, half))] = value[half:].astype(ref.dtype)


def greet_near(place, *more):
    greet({CTX: place[1]}, {CTX: place[2]}, *more)


def sibling():
    return {TP: 1 - lax.axis_index(TP)}


def mlp_rows(r, top_of, low_of, back):
    units = r.hidden.shape[-1]
    x = rows_of(r.full, (), top_of, low_of)
    total, g_total = 0.0, 0.0
    for t in range(r.weights.shape[0]):
        gate_act = dot32(x, r.weights[t, :, :units], ((1,), (0,)))
        up_act = dot32(x, r.weights[t, :, units : 2 * units], ((1,), (0,)))
        sig = jax.nn.sigmoid(gate_act)
        unit = (gate_act * sig * up_act).astype(jnp.bfloat16)
        put_rows(r.hidden, (t,), top_of, low_of, unit)
        total += dot32(unit, r.weights[t, :, 2 * units :], ((1,), (1,)))
        if back:
            g_total += mlp_back_rows(r, rows_of(r.grad_all, (), top_of, low_of), t, top_of, low_of, gate_act, up_act, sig)
        else:
            put_rows(r.gate, (t,), top_of, low_of, gate_act)
            put_rows(r.up, (t,), top_of, low_of, up_act)
    put_rows(r.part_out if back else r.part, (), top_of, low_of, total)
    if back:
        put_rows(r.part, (), top_of, low_of, g_total)


def mlp_back_rows(r, grad, t, top_of, low_of, gate_act, up_act, sig):
    units = r.grad_gate.shape[-1]
    g_hidden = dot32(grad, r.weights[t, :, 2 * units :], ((1,), (0,)))
    g_gate = (g_hidden * up_act * sig * (1.0 + gate_act * (1.0 - sig))).astype(jnp.bfloat16)
    g_up = (g_hidden * gate_act * sig).astype(jnp.bfloat16)
    put_rows(r.grad_gate, (t,), top_of, low_of, g_gate)
    put_rows(r.grad_up, (t,), top_of, low_of, g_up)
    total = dot32(g_gate, r.weights[t, :, :units], ((1,), (1,)))
    return total + dot32(g_up, r.weights[t, :, units : 2 * units], ((1,), (1,)))


def gathered_work(r, place, scatter, work, rows_own, own, cut=True):
    me, side_x, side_y, across = place
    steps = gather_rows(r.full, (r.ag_send, r.ag_recv), place, rows_own)
    next(steps)
    own.wait()
    work(me, me)
    next(steps)
    work(side_x, side_y)
    next(steps)
    work(side_y, side_x)
    scatter.x_out(0 if cut else None)
    scatter.y_out(0 if cut else None)
    run(steps)
    work(across, across)
    scatter.across()
    if cut:
        scatter.x_out(1)
        scatter.y_out(1)


def mlp_kernel(r):
    place = partners()
    me = place[0]
    own = pltpu.make_async_copy(r.normed, r.full.at[me], r.load.at[0])
    own.start()
    greet_near(place)
    scatter = Scatter(r.part, (r.from_x, r.from_y, r.passed, r.last), (r.rs_send, r.rs_recv), place)

    def work(top_of, low_of):
        r.need("weights")
        mlp_rows(r, top_of, low_of, False)

    gathered_work(r, place, scatter, work, r.normed, own)
    r.keep("full", "hidden", "gate", "up")
    scatter.forward()
    scatter.finish()
    r.need("middle")
    norm_sum(scatter, r.middle, r.gain, r.valid, r.stream, r.normed_next, r.stats)


def mlp_back_kernel(both, r):
    place = partners()
    me = place[0]
    own = pltpu.make_async_copy(r.rows_own, r.full.at[me], r.load.at[0])
    own.start()
    greet_near(place, sibling())
    scatter = Scatter(r.part, (r.from_x, r.from_y, r.passed, r.last), (r.rs_send, r.rs_recv), place)

    def both_rows(top_of, low_of):
        r.need("weights", "grad_all")
        mlp_rows(r, top_of, low_of, True)

    def back_rows(top_of, low_of):
        r.need("weights", "grad_gate", "grad_up")
        total = 0.0
        grad = rows_of(r.full, (), top_of, low_of)
        for t in range(r.weights.shape[0]):
            gate_act = rows_of(r.grad_gate, (t,), top_of, low_of).astype(jnp.float32)
            up_act = rows_of(r.grad_up, (t,), top_of, low_of).astype(jnp.float32)
            total += mlp_back_rows(r, grad, t, top_of, low_of, gate_act, up_act, jax.nn.sigmoid(gate_act))
        put_rows(r.part, (), top_of, low_of, total)

    gathered_work(r, place, scatter, both_rows if both else back_rows, r.rows_own, own, not both)
    if both:
        r.keep("part_out")
    normed, grad = (r.full, r.grad_all) if both else (r.normed, r.full)
    r.need("normed", "hidden")
    units = r.hidden.shape[-1]
    sent = [r.weights.at[0, :, pl.ds(p * units, units)] for p in range(3)]
    sums = WeightGrads(
        [normed, normed, grad], [r.grad_gate, r.grad_up, r.hidden], sent, [r.came_0, r.came_1, r.came_2],
        r.summed, (r.tp_send, r.tp_recv),
    )
    sums.theirs(0)
    sums.theirs(1)
    scatter.forward()
    job = None if both else gather_part(r.share, 0, r.gathered, r.load.at[1], r.ja_send, r.ja_recv, place)
    if job:
        next(job)
    sums.theirs(2)
    sums.ours(0)
    sums.ours(1)
    sums.ours(2)
    sums.add_up()
    r.keep("summed")
    scatter.finish()
    r.need("middle", "grad")

    def put(rows, total):
        r.grad_new[rows, :] = total
        r.grad_rows[rows, :] = total.astype(r.grad_rows.dtype)

    if job:
        next(job)
    norm_sum_back(scatter, r.middle, r.gain, r.grad, r.gain_rows, put)
    if job:
        run(job)
        r.keep("gathered")
    sums.close()


LOG2E = 1.4426950408889634


def turn(x, cos_row, sin_row):
    half_dim = HEAD_DIM // 2
    swapped = jnp.concatenate([x[:, half_dim:], x[:, :half_dim]], axis=1)
    return x * cos_row + swapped * sin_row


def project_rows(r, full, top_of, low_of):
    cols_q, base = 2 * HEAD_DIM, 4 * HEAD_DIM
    x = rows_of(full, (), top_of, low_of)
    cos_b, sin_b = rows_of(r.cosine, (), top_of, low_of), rows_of(r.sine, (), top_of, low_of)
    for t in range(r.weights.shape[0]):
        flat = dot32(x, r.weights[t, :, :base], ((1,), (0,)))
        for g in range(2):
            put_rows(r.query, (t, g), top_of, low_of, turn(flat[:, g * HEAD_DIM : (g + 1) * HEAD_DIM], cos_b, sin_b))
        put_rows(r.key, (t,), top_of, low_of, turn(flat[:, cols_q : cols_q + HEAD_DIM], cos_b, sin_b))
        put_rows(r.value, (t,), top_of, low_of, flat[:, cols_q + HEAD_DIM : base])


def attend_rows(r, owner):
    base = 4 * HEAD_DIM
    pairs, _, rows, _ = r.key.shape
    factor = HEAD_DIM ** (-0.5) * LOG2E

    for t in range(pairs):
        key = r.key[t].reshape(-1, HEAD_DIM)
        value = r.value[t].reshape(-1, HEAD_DIM)
        query = jnp.concatenate([r.query[t, 0, owner], r.query[t, 1, owner]], axis=0)
        raw = dot32(key, query, ((1,), (1,)))
        raw = raw * factor + r.bias[owner].astype(jnp.float32)
        top = jnp.max(raw, axis=0, keepdims=True)
        probs = jnp.exp2(raw - top)
        total = jnp.sum(probs, axis=0, keepdims=True)
        out = dot32(value, probs.astype(jnp.bfloat16), ((0,), (0,))) * (1.0 / total)
        fill = -out.shape[1] % 128
        out = jnp.concatenate([out, jnp.zeros((HEAD_DIM, fill), jnp.float32)], axis=1).T.astype(jnp.bfloat16)
        r.lse[t, owner] = top + jnp.log2(total)
        for g in range(2):
            r.mixed[t, owner, :, g * HEAD_DIM : (g + 1) * HEAD_DIM] = out[g * rows : (g + 1) * rows]

    total = 0.0
    for t in range(pairs):
        total += dot32(r.mixed[t, owner], r.weights[t, :, base : base + 2 * HEAD_DIM], ((1,), (1,)))
    r.part[owner] = total.astype(r.part.dtype)


def attend_kernel(first, r):
    place = partners()
    me, side_x, side_y, across = place
    rows_own = r.share.at[lax.axis_index(TP)] if first else r.normed
    own = pltpu.make_async_copy(rows_own, r.full.at[me], r.load.at[0])
    own.start()
    greet_near(place)
    steps = gather_rows(r.full, (r.ag_send, r.ag_recv), place, rows_own)
    next(steps)
    own.wait()
    rows = r.normed if first else r.full
    r.need("weights", "cosine", "sine", "normed")
    if first:
        for owner in range(4):
            project_rows(r, rows, owner, owner)
    else:
        project_rows(r, rows, me, me)
        next(steps)
        project_rows(r, rows, side_x, side_y)
        next(steps)
        project_rows(r, rows, side_y, side_x)
        run(steps)
        project_rows(r, rows, across, across)
        r.keep("full")
    r.keep("query", "key", "value")
    scatter = Scatter(r.part, (r.from_x, r.from_y, r.passed, r.last), (r.rs_send, r.rs_recv), place)
    r.need("bias")
    attend_rows(r, across)
    scatter.across()
    if first:
        next(steps)
    attend_rows(r, side_x)
    scatter.x_out()
    attend_rows(r, side_y)
    scatter.y_out()
    scatter.forward()
    attend_rows(r, me)
    r.keep("lse", "mixed")
    if first:
        run(steps)
        r.keep("full")
    scatter.finish()
    r.need("stream")
    norm_sum(scatter, r.stream, r.gain, r.valid, r.middle, r.normed_next, r.stats)


def attend_back_kernel(last, r):
    place = partners()
    me, side_x, side_y, across = place
    own = pltpu.make_async_copy(r.rows_own, r.full.at[me], r.load.at[0])
    own.start()
    greet_near(place, sibling())
    cols_q, base = 2 * HEAD_DIM, 4 * HEAD_DIM
    pairs = r.weights.shape[0]
    rows = r.full.shape[1]
    scale = HEAD_DIM ** (-0.5)
    factor = scale * LOG2E
    order = (me, side_x, side_y, across)
    masks = [pltpu.make_async_copy(r.bias_in.at[owner], r.bias.at[n % 2], r.bias_load.at[n]) for n, owner in enumerate(order)]
    masks[0].start()
    masks[1].start()
    r.g_key[...] = jnp.zeros_like(r.g_key)
    r.g_value[...] = jnp.zeros_like(r.g_value)

    def project(top_of, low_of):
        r.need("weights")
        x = rows_of(r.full, (), top_of, low_of)
        for t in range(pairs):
            flat = dot32(x, r.weights[t, :, base : base + cols_q], ((1,), (0,)))
            for g in range(2):
                put_rows(r.heads, (t, g), top_of, low_of, flat[:, g * HEAD_DIM : (g + 1) * HEAD_DIM])

    def two(ref, t, owner):
        return jnp.concatenate([ref[t, 0, owner], ref[t, 1, owner]], axis=0)

    def queries_back(n):
        owner = order[n]
        masks[n].wait()
        for t in range(pairs):
            query, heads = two(r.query, t, owner), two(r.heads, t, owner)
            mixed = r.mixed[t, owner].astype(jnp.float32)
            mixed = jnp.concatenate([mixed[:, :HEAD_DIM], mixed[:, HEAD_DIM:]], axis=0)
            along = lax.dot_general(
                jnp.ones((8, HEAD_DIM), jnp.float32), heads.astype(jnp.float32) * mixed, (((1,), (1,)), ((), ())),
                precision=lax.Precision.HIGHEST, preferred_element_type=jnp.float32,
            )[0:1]
            lse = r.lse[t, owner]
            r.g_query[...] = jnp.zeros_like(r.g_query)

            @pl.loop(0, jnp.minimum(owner + 2, 4))
            def _(kept):
                here = pl.ds(pl.multiple_of(kept * rows, 16), rows)
                key, value = r.key[t, kept], r.value[t, kept]
                raw = dot32(key, query, ((1,), (1,)))
                probs = jnp.exp2(raw * factor + r.bias[n % 2, here, :].astype(jnp.float32) - lse)
                g_probs = dot32(value, heads, ((1,), (1,)))
                g_scores = (probs * (g_probs - along)).astype(jnp.bfloat16)
                r.g_value[t, kept] += dot32(probs.astype(jnp.bfloat16), heads, ((1,), (0,)))
                r.g_key[t, kept] += dot32(g_scores, query, ((1,), (0,)))
                r.g_query[...] += dot32(key, g_scores, ((0,), (0,)))

            fill = jnp.zeros((HEAD_DIM, -2 * rows % 128), jnp.float32)
            g_query = jnp.concatenate([r.g_query[...], fill], axis=1).T * scale
            for g in range(2):
                r.grad_qkv[t, owner, :, g * HEAD_DIM : (g + 1) * HEAD_DIM] = turn(
                    g_query[g * rows : (g + 1) * rows], r.cosine[owner], -r.sine[owner]
                ).astype(jnp.bfloat16)
        if n + 2 < 4:
            masks[n + 2].start()

    steps = gather_rows(r.full, (r.ag_send, r.ag_recv), place, r.rows_own)
    next(steps)
    own.wait()
    project(me, me)
    r.need("key", "value", "query", "lse", "mixed", "cosine", "sine")
    queries_back(0)
    next(steps)
    jobs = [
        gather_part(r.share_a, 1, r.gathered_a, r.load.at[1], r.ja_send, r.ja_recv, place),
        gather_part(r.share_b, None, r.gathered_b, r.load.at[2], r.jb_send, r.jb_recv, place),
    ] if last else [end_steps(r, place)]
    for job in jobs:
        next(job)
    project(side_x, side_y)
    next(steps)
    project(side_y, side_x)
    queries_back(1)
    queries_back(2)
    run(steps)
    project(across, across)
    queries_back(3)

    @pl.loop(0, 4)
    def _(owner):
        for t in range(pairs):
            r.grad_qkv[t, owner, :, cols_q : cols_q + HEAD_DIM] = turn(
                r.g_key[t, owner] * scale, r.cosine[owner], -r.sine[owner]
            ).astype(jnp.bfloat16)
            r.grad_qkv[t, owner, :, cols_q + HEAD_DIM :] = r.g_value[t, owner].astype(jnp.bfloat16)

    def branch(owner):
        total = 0.0
        for t in range(pairs):
            total += dot32(r.grad_qkv[t, owner], r.weights[t, :, :base], ((1,), (1,)))
        r.part[owner] = total.astype(r.part.dtype)

    scatter = Scatter(r.part, (r.from_x, r.from_y, r.passed, r.last), (r.rs_send, r.rs_recv), place)
    if not last:
        for job in jobs:
            next(job)
    branch(across)
    scatter.across()
    branch(side_x)
    scatter.x_out()
    branch(side_y)
    scatter.y_out()
    branch(me)
    r.need("normed")
    sums = WeightGrads(
        [r.normed, r.full], [r.grad_qkv, r.mixed],
        [r.weights.at[0, :, pl.ds(0, base)], r.weights.at[1, :, pl.ds(0, r.came_1.shape[1])]], [r.came_0, r.came_1],
        r.summed, (r.tp_send, r.tp_recv),
    )
    sums.theirs(0)
    scatter.forward()
    if last:
        for job in jobs:
            next(job)
    sums.theirs(1)
    sums.ours(0)
    sums.ours(1)
    r.summed[:, base + cols_q :] = jnp.zeros((r.summed.shape[0], r.summed.shape[1] - base - cols_q), jnp.bfloat16)
    sums.add_up()
    r.keep("summed")
    if not last:
        for job in jobs:
            run(job)
        r.keep("out")
    scatter.finish()
    r.need("stream", "grad")
    side = lax.axis_index(TP)

    def put(here, total):
        if last:
            r.grad_new[side, here, :] = total
        else:
            r.grad_new[here, :] = total
            r.grad_rows[here, :] = total.astype(r.grad_rows.dtype)

    norm_sum_back(scatter, r.stream, r.gain, r.grad, r.gain_rows, put)
    handed = []
    if last:
        handed.append(send(r.grad_new.at[side], r.grad_new.at[side], (r.tp_send, r.tp_recv), 2, sibling()))
    if last:
        for job in jobs:
            run(job)
        r.keep("gathered_a", "gathered_b")
    for copy in handed:
        copy.wait()
    sums.close()


def end_steps(r, place):
    side = lax.axis_index(TP)
    r.need("end_part")
    scatter = Scatter(
        r.end_part, (r.end_from_x, r.end_from_y, r.end_passed, r.end_last), (r.end_send, r.end_recv), place
    )
    yield from scatter_steps(scatter)

    r.stats[...] = jnp.zeros_like(r.stats)

    def work(rows, branch):
        r.out[side, rows, :] = (r.end_middle[rows, :] + branch).astype(r.out.dtype)
        add_stats(r.stats, r.valid[rows, :], branch)

    r.need("end_middle")
    scatter.each_row(work)
    send(r.out.at[side], r.out.at[side], (r.out_send, r.out_recv), 0, sibling()).wait()


def gather_part(share, part_no, full, local_sem, send_sems, recv_sems, place):
    rows = full.shape[1]
    src = share if part_no is None else share.at[pl.ds(part_no * rows, rows)]
    copy = pltpu.make_async_copy(src, full.at[place[0]], local_sem)
    copy.start()
    yield from gather_rows(full, (send_sems, recv_sems), place, src)
    copy.wait()


class Refs:
    def need(self, *names):
        for name in names:
            if name in self.loads:
                self.loads.pop(name).wait()

    def keep(self, *names):
        for name in names:
            src, dst, sem = self.late[name]
            store = pltpu.make_async_copy(src, dst, sem)
            store.start()
            self.stores.append(store)


def linked(kernel, number, micros, near, far, lazy, outs, late, scratch):
    names = [*near, *far, *lazy, *outs, *late, *scratch]
    halves = [name for name, value in lazy.items() if isinstance(value, tuple)]
    lazy = {name: value[0] if name in halves else value for name, value in lazy.items()}
    lazy_rooms = [pltpu.VMEM(v.shape[1:] if name in halves else v.shape, v.dtype) for name, v in lazy.items()]
    lazy_names, late_names = list(lazy), list(late)

    def body(*refs):
        r = Refs()
        count = len(names)
        rest = list(refs[count:])
        by_name = dict(zip(names, refs))
        r.loads, r.late, r.stores = {}, {}, []
        held = rest[: len(lazy) + len(late)]
        for n, name in enumerate(lazy_names):
            src = by_name[name].at[lax.axis_index(TP)] if name in halves else by_name[name]
            r.loads[name] = pltpu.make_async_copy(src, held[n], rest[-2].at[n])
            by_name[name] = held[n]
        for n, name in enumerate(late_names):
            r.late[name] = (held[len(lazy) + n], by_name[name], rest[-1].at[n])
            by_name[name] = held[len(lazy) + n]
        for name, ref in by_name.items():
            setattr(r, name, ref)
        for load in r.loads.values():
            load.start()
        kernel(r)
        r.need(*lazy_names)
        for store in r.stores:
            store.wait()

    vmem = pl.BlockSpec(memory_space=pltpu.VMEM)
    hbm = pl.BlockSpec(memory_space=pl.ANY)
    came = pl.pallas_call(
        body,
        out_shape=[*outs.values(), *late.values()],
        in_specs=[vmem] * len(near) + [hbm] * (len(far) + len(lazy)),
        out_specs=[vmem] * len(outs) + [hbm] * len(late),
        scratch_shapes=[
            *scratch.values(), *lazy_rooms, *map(room, late.values()),
            pltpu.SemaphoreType.DMA((max(1, len(lazy)),)), pltpu.SemaphoreType.DMA((max(1, len(late)),)),
        ],
        compiler_params=pltpu.CompilerParams(
            collective_id=number, has_side_effects=True, vmem_limit_bytes=61 << 20
        ),
        cost_estimate=pl.CostEstimate(flops=0, bytes_accessed=int(micros * 3.6e6), transcendentals=0),
    )(*near.values(), *far.values(), *lazy.values())
    result = Refs()
    for name, value in zip([*outs, *late], came):
        setattr(result, name, value)
    return result


def sems(name, count):
    return {f"{name}_send": pltpu.SemaphoreType.DMA((count,)), f"{name}_recv": pltpu.SemaphoreType.DMA((count,))}


def sum_room(rows, width, prefix=""):
    names = ("from_x", "from_y", "passed", "last")
    return {prefix + name: pltpu.VMEM((2, rows // 2, width), jnp.bfloat16) for name in names}


def shape16(*dims):
    return jax.ShapeDtypeStruct(dims, jnp.bfloat16)


def shape32(*dims):
    return jax.ShapeDtypeStruct(dims, jnp.float32)


def room(like):
    return pltpu.VMEM(like.shape, like.dtype)


def mlp_step(normed, middle, gain, valid, weights):
    rows, width = middle.shape
    pairs, units = weights.shape[0], weights.shape[2] // 3
    kept = shape16(pairs, 4, rows, units)
    return linked(
        mlp_kernel, 12, 75,
        dict(gain=gain, valid=valid), dict(normed=normed), dict(weights=weights, middle=middle),
        dict(stream=shape32(rows, width), normed_next=shape16(rows, width), stats=shape32(16, 128)),
        dict(full=shape16(4, rows, width), hidden=kept, gate=kept, up=kept),
        dict(
            part=pltpu.VMEM((4, rows, width), jnp.bfloat16), load=pltpu.SemaphoreType.DMA((1,)),
            **sum_room(rows, width), **sems("ag", 6), **sems("rs", 10),
        ),
    )


def mlp_back_step(rows_own, middle, gain, grad, weights, grad_all=None, kept=None, share=None):
    rows, width = middle.shape
    pairs, units = weights.shape[0], weights.shape[2] // 3
    both = grad_all is not None
    whole, unit = shape16(4, rows, width), shape16(pairs, 4, rows, units)
    far = dict(rows_own=rows_own)
    lazy = dict(weights=weights)
    late = dict(summed=shape16(width, 3 * units))
    scratch = dict(
        full=room(whole), part=room(whole), load=pltpu.SemaphoreType.DMA((2,)),
        **{f"came_{p}": pltpu.VMEM((width, units), jnp.bfloat16) for p in range(3)},
        **sum_room(rows, width), **sems("ag", 6), **sems("rs", 10), **sems(TP, 3),
    )
    if both:
        lazy["grad_all"] = grad_all
        late["part_out"] = whole
        scratch.update(grad_gate=room(unit), grad_up=room(unit), hidden=room(unit))
    else:
        far["share"] = share
        lazy.update(grad_gate=kept.gate, grad_up=kept.up, hidden=kept.hidden, normed=kept.full)
        late["gathered"] = shape16(4, share.shape[0] // 2, share.shape[1])
        scratch.update(**sems("ja", 6))
    lazy.update(middle=middle, grad=grad)
    return linked(
        functools.partial(mlp_back_kernel, both), 13 if both else 5, 85,
        dict(gain=gain), far, lazy,
        dict(grad_new=shape32(rows, width), grad_rows=shape16(rows, width), gain_rows=shape32(16, width)),
        late, scratch,
    )


def attend_step(normed, stream, gain, valid, weights, cosine, sine, bias, share=None):
    first = share is not None
    rows, width = stream[0].shape[1:] if first else stream.shape
    pairs = weights.shape[0]
    far, lazy = {}, dict(weights=weights, cosine=cosine, sine=sine)
    if first:
        far["share"] = share
        lazy["normed"] = normed
    else:
        far["normed"] = normed
    lazy.update(bias=bias, stream=stream)
    return linked(
        functools.partial(attend_kernel, first), 11 if first else 9, 75,
        dict(gain=gain, valid=valid), far, lazy,
        dict(middle=shape32(rows, width), normed_next=shape16(rows, width), stats=shape32(16, 128)),
        dict(
            full=shape16(4, rows, width), query=shape16(pairs, 2, 4, rows, HEAD_DIM),
            key=shape16(pairs, 4, rows, HEAD_DIM), value=shape16(pairs, 4, rows, HEAD_DIM),
            lse=shape32(pairs, 4, 1, 2 * rows), mixed=shape16(pairs, 4, rows, 2 * HEAD_DIM),
        ),
        dict(
            part=pltpu.VMEM((4, rows, width), jnp.bfloat16), load=pltpu.SemaphoreType.DMA((1,)),
            **sum_room(rows, width), **sems("ag", 6), **sems("rs", 10),
        ),
    )


def attend_back_step(
    rows_own, stream, gain, grad, weights, cosine, sine, bias, kept, normed, shares=None, end=None
):
    rows, width = rows_own.shape
    pairs = weights.shape[0]
    length = 4 * rows
    last = shares is not None
    whole = shape16(4, rows, width)
    near = dict(gain=gain)
    far = dict(rows_own=rows_own, bias_in=bias)
    lazy = dict(
        weights=weights, key=kept.key, value=kept.value, query=kept.query, lse=kept.lse, mixed=kept.mixed,
        cosine=cosine, sine=sine, normed=normed, stream=stream, grad=grad,
    )
    sizes = (4 * HEAD_DIM, 2 * HEAD_DIM)
    total = sum(sizes) + 64
    outs = dict(gain_rows=shape32(16, width))
    late = dict(summed=shape16(width, total))
    scratch = dict(
        full=room(whole), part=room(whole),
        heads=room(kept.query), g_key=pltpu.VMEM(kept.key.shape, jnp.float32),
        g_value=pltpu.VMEM(kept.key.shape, jnp.float32), g_query=pltpu.VMEM((HEAD_DIM, 2 * rows), jnp.float32),
        grad_qkv=pltpu.VMEM((pairs, 4, rows, sizes[0]), jnp.bfloat16),
        bias=pltpu.VMEM((2, length, 2 * rows), jnp.bfloat16), bias_load=pltpu.SemaphoreType.DMA((4,)),
        came_0=pltpu.VMEM((width, sizes[0]), jnp.bfloat16), came_1=pltpu.VMEM((width, 256), jnp.bfloat16),
        load=pltpu.SemaphoreType.DMA((3,)),
        **sum_room(rows, width), **sems("ag", 6), **sems("rs", 10), **sems(TP, 4),
    )
    if last:
        far.update(share_a=shares[0], share_b=shares[1])
        outs.update(grad_new=shape32(2, rows, width))
        late.update(
            gathered_a=shape16(4, shares[0].shape[0] // 2, shares[0].shape[1]),
            gathered_b=shape16(4, *shares[1].shape),
        )
        scratch.update(**sems("ja", 6), **sems("jb", 6))
    else:
        lazy = dict(end_part=end[0], **lazy, end_middle=end[1])
        near["valid"] = end[2]
        outs.update(grad_new=shape32(rows, width), grad_rows=shape16(rows, width), stats=shape32(16, 128))
        late["out"] = shape16(2, rows, width)
        scratch.update(**sum_room(rows, width, "end_"), **sems("end", 10), **sems("out", 1))
    return linked(
        functools.partial(attend_back_kernel, last), 7 if last else 6, 100, near, far, lazy, outs, late, scratch,
    )


def tail_step(summed, share, attn_stats, mlp_stats, gain_rows):
    depth = lax.axis_size(FSDP)
    half, cols = share.shape[0] // 2, summed.shape[1]
    last = shape16(4, half, cols)
    wide = summed.shape[0] + 128
    return linked(
        functools.partial(tail_kernel, summed.shape[0]), 10, 60,
        {}, dict(share=share, summed=summed),
        dict(
            **{f"attn_stats_{layer}": a for layer, a in enumerate(attn_stats)},
            **{f"mlp_stats_{layer}": a for layer, a in enumerate(mlp_stats)},
            **{f"gain_rows_{n}": a for n, a in enumerate(gain_rows)},
        ),
        dict(last_0=last, last_1=last, all_stats=shape32(8, 128), gains=shape32(8, summed.shape[0] // depth)), dict(gathered=shape16(4, *share.shape)),
        dict(
            z_came=pltpu.VMEM((2, depth, half, cols), jnp.bfloat16), stat_sent=pltpu.VMEM((4, 8, wide), jnp.float32),
            stat_came=pltpu.VMEM((3, 8, wide), jnp.float32), stat_z=pltpu.VMEM((depth, 8, wide), jnp.float32),
            own=pltpu.VMEM((share.shape[0], cols), jnp.bfloat16),
            load=pltpu.SemaphoreType.DMA((2,)), **sems("z", 2 * depth), **sems("ag", 6), **sems("stat", 3 + depth),
            **sems("l0", 6), **sems("l1", 6),
        ),
    )


def start_step(attn_gain, mlp_gain, places, starts, x, gate, up, down):
    depth, across = lax.axis_size(FSDP), lax.axis_size(CTX)
    layers, rows = gate.shape[:2]
    units = gate.shape[2] // across
    own = x.shape[1:]
    length = across * own[0]
    return linked(
        start_kernel, 8, 38,
        dict(attn_gain=attn_gain, mlp_gain=mlp_gain, places=places, starts=starts), dict(x=x, gate=gate, up=up, down=down), {},
        dict(
            all_gains=shape32(depth, 8, attn_gain.shape[1]),
            normed=shape16(across, *own),
        ),
        dict(
            bias=shape16(across, length, 2 * own[0]), cosine=shape32(across, own[0], HEAD_DIM),
            sine=shape32(across, own[0], HEAD_DIM),
            **{f"packed_{layer}": shape16(rows, 3 * units) for layer in range(layers)},
        ),
        dict(
            gains=pltpu.VMEM((8, attn_gain.shape[1]), jnp.float32),
            all_places=pltpu.VMEM((across, *places.shape), places.dtype),
            full=pltpu.VMEM((across, *own), jnp.bfloat16), turned=pltpu.VMEM((layers, units, rows), jnp.bfloat16),
            load=pltpu.SemaphoreType.DMA((3 + 3 * layers,)), **sems("gain", depth), **sems("place", across),
            **sems("ag", 6),
        ),
    )


def planned(
    tokens, positions, valid, piece_starts, d_out,
    attn_gain, w_query, w_key, w_value, w_out, mlp_gain, w_gate, w_up, w_down,
):
    seq_count, rows, width = tokens.shape
    layers = attn_gain.shape[0]
    ctx_count = lax.axis_size(CTX)
    tp_count = lax.axis_size(TP)
    me = lax.axis_index(CTX)
    side = lax.axis_index(TP)
    length = rows * ctx_count
    heads_q = HEADS // tp_count // ctx_count
    heads_k = KV_HEADS // tp_count // ctx_count
    cols_q = heads_q * HEAD_DIM
    cols_k = heads_k * HEAD_DIM
    units = w_gate.shape[2] // ctx_count

    def own(a):
        return lax.dynamic_index_in_dim(a, side, 0, keepdims=False)

    def cut(w, axis, count):
        return lax.dynamic_slice_in_dim(w, me * count, count, axis)

    def whole(w):
        return lax.all_gather(w, (TP, FSDP), axis=0, tiled=True).reshape(
            tp_count, width, w.shape[1]
        )

    def pack(*pieces):
        return with_layout_constraint(jnp.concatenate(pieces, axis=1), Layout(major_to_minor=(0, 1)))

    def pack_attn(layer, w_query, w_key, w_value, w_out):
        return pack(
            cut(w_query[layer], 1, cols_q),
            cut(w_key[layer], 1, cols_k),
            cut(w_value[layer], 1, cols_k),
            cut(w_out[layer], 0, cols_q).T,
            jnp.zeros((w_query.shape[1], 64), w_query.dtype),
        )

    attn_w = [whole(pack_attn(0, w_query, w_key, w_value, w_out))]
    seq_pos, valid_f = own(positions), own(valid).astype(jnp.float32)[:, None]
    half_dim = HEAD_DIM // 2
    freqs = rope_base ** (-(jnp.arange(half_dim).astype(jnp.float32) * 2.0 / HEAD_DIM))
    angles = seq_pos.astype(jnp.float32)[:, None] * freqs
    begun = start_step(
        attn_gain, mlp_gain,
        jnp.concatenate([jnp.cos(angles), jnp.sin(angles), valid_f, jnp.zeros((rows, 127 - HEAD_DIM), jnp.float32)], axis=1),
        piece_starts, tokens, w_gate, w_up, w_down,
    )
    normed, bias = begun.normed, begun.bias
    packed_mlp = [getattr(begun, f"packed_{layer}") for layer in range(layers)]
    gains = begun.all_gains.swapaxes(0, 1).reshape(8, width)
    cosine, sine_t = begun.cosine, begun.sine
    gain_a = [gains[layer][None] for layer in range(layers)]
    gain_m = [gains[layers + layer][None] for layer in range(layers)]
    grad = (d_out,)
    mlp_w = [whole(packed_mlp[0])]

    streams, attends, mlps = [(tokens,)], [], []
    for layer in range(layers):
        kept = attend_step(
            normed, streams[layer], gain_m[layer], valid_f, attn_w[layer], cosine, sine_t, bias,
            None if layer else d_out,
        )
        if layer == 0:
            grad_all, kept.full = kept.full, normed
        attends.append(kept)
        if layer + 1 < layers:
            normed_m, w_query, w_key, w_value, w_out, packed_mlp[layer + 1] = lax.optimization_barrier(
                (kept.normed_next, w_query, w_key, w_value, w_out, packed_mlp[layer + 1])
            )
            attn_w.append(whole(pack_attn(layer + 1, w_query, w_key, w_value, w_out)))
            mlp_w.append(whole(packed_mlp[layer + 1]))
            mlps.append(mlp_step(normed_m, kept.middle, gain_a[layer + 1], valid_f, mlp_w[layer]))
            streams.append(mlps[layer].stream)
            normed = mlps[layer].normed_next

    def reduced(g):
        return lax.psum_scatter(g, FSDP, scatter_dimension=0, tiled=True)

    down_rows = None
    attn_gains, mlp_gains = [], []
    for layer in reversed(range(layers)):
        kept = attends[layer]
        if layer + 1 == layers:
            came = mlp_back_step(kept.normed_next, kept.middle, gain_m[layer], grad, mlp_w[layer], grad_all=grad_all)
            end = [came.part_out, kept.middle, valid_f]
        else:
            came = mlp_back_step(
                down_rows, kept.middle, gain_m[layer], grad, mlp_w[layer], kept=mlps[layer], share=shares[0]
            )
        mlp_share = reduced(came.summed)
        mlp_gains.insert(0, came.gain_rows)
        back = attend_back_step(
            came.grad_rows, streams[layer], gain_a[layer], came.grad_new, attn_w[layer], cosine, sine_t, bias,
            kept, kept.full, None if layer else shares, end if layer else None,
        )
        attn_gains.insert(0, back.gain_rows)
        if layer:
            grad, output = back.grad_new, back.out
            down_rows, mlp_share, summed = lax.optimization_barrier((back.grad_rows, mlp_share, back.summed))
            shares = [mlp_share, reduced(summed)]
            last_stats = back.stats
    ended = tail_step(
        back.summed, mlp_share, [kept.stats for kept in attends], [kept.stats for kept in mlps] + [last_stats],
        attn_gains + mlp_gains,
    )
    input_grad = back.grad_new
    mlp_all = [[ended.gathered], [came.gathered, back.gathered_a]]
    attn_all = [[ended.last_0, ended.last_1], [back.gathered_b]]
    base = cols_q + 2 * cols_k
    placed = place_outs(
        attn_all, mlp_all,
        [(0, cols_q, False), (cols_q, cols_k, False), (cols_q + cols_k, cols_k, False), (base, cols_q, True)],
        [(0, units, False), (units, units, False), (2 * units, units, True)],
        [output, input_grad], [ended.gains, ended.all_stats],
    )
    return (*placed[7:9], placed[9], *placed[:4], placed[10], *placed[4:7], placed[11])


def place_kernel(moves, count, more, *refs):
    refs = list(refs)
    gains, stats = refs[:2]
    del refs[:2]
    outs_count = 1 + max(out for _, _, pieces in moves for _, _, _, out in pieces)
    ins, outs = refs[: count + more], refs[count + more : count + outs_count + 2 * more]
    del refs[: count + outs_count + 2 * more]
    attn_gain, mlp_gain, roots = refs[:3]
    del refs[:3]
    layers = attn_gain.shape[0]
    attn_gain[...] = gains[0:layers, :]
    mlp_gain[...] = gains[layers : 2 * layers, :]
    for layer in range(layers):
        roots[layer : layer + 1, :] = stats[0:1, 3 * layer : 3 * layer + 3]
    held, laid = refs[: count + more], refs[count + more : -2]
    in_sems, out_sems = refs[-2:]
    loads = [pltpu.make_async_copy(ins[n], held[n], in_sems.at[n]) for n in range(count + more)]
    for load in loads[:2]:
        load.start()
    stores = []
    for n, (layer, first, pieces) in enumerate(moves):
        loads[n].wait()
        if n + 2 < len(loads):
            loads[n + 2].start()
        rows = held[n].shape[1]
        for start, size, flip, out in pieces:
            for c in range(held[n].shape[0]):
                block = held[n][c, :, start : start + size].astype(jnp.float32)
                if flip:
                    laid[out][layer, c * size : (c + 1) * size, first : first + rows] = block.T
                else:
                    laid[out][layer, first : first + rows, c * size : (c + 1) * size] = block
            if any(layer == l and out == o for l, _, more in moves[n + 1 :] for _, _, _, o in more):
                continue
            store = pltpu.make_async_copy(laid[out].at[layer], outs[out].at[layer], out_sems.at[len(stores)])
            store.start()
            stores.append(store)
    for n in range(more):
        if len(moves) + 2 <= count + n:
            loads[count + n].start()
        loads[count + n].wait()
        store = pltpu.make_async_copy(held[count + n], outs[outs_count + n], out_sems.at[len(stores)])
        store.start()
        stores.append(store)
    for store in stores:
        store.wait()


def place_outs(attn_all, mlp_all, attn_pieces, mlp_pieces, handed, small):
    layers = len(attn_all)
    shapes = []
    for came, pieces in ((attn_all, attn_pieces), (mlp_all, mlp_pieces)):
        ctx_count = came[0][0].shape[0]
        depth = sum(a.shape[1] for a in came[0])
        for _, size, flip in pieces:
            wide = ctx_count * size
            shapes.append((layers, wide, depth) if flip else (layers, depth, wide))
    ins, moves = [], []
    for layer in reversed(range(layers)):
        for came, pieces, base in ((mlp_all, mlp_pieces, len(attn_pieces)), (attn_all, attn_pieces, 0)):
            first = 0
            for a in came[layer]:
                ins.append(a)
                moves.append((layer, first, [(*piece, base + n) for n, piece in enumerate(pieces)]))
                first += a.shape[1]
    hbm, vmem = pl.BlockSpec(memory_space=pl.ANY), pl.BlockSpec(memory_space=pltpu.VMEM)
    return pl.pallas_call(
        functools.partial(place_kernel, moves, len(ins), len(handed)),
        out_shape=[jax.ShapeDtypeStruct(s, jnp.float32) for s in shapes]
        + [jax.ShapeDtypeStruct(a.shape, a.dtype) for a in handed]
        + [shape32(layers, small[0].shape[1])] * 2 + [shape32(layers, 3)],
        in_specs=[vmem] * 2 + [hbm] * (len(ins) + len(handed)),
        out_specs=[hbm] * (len(shapes) + len(handed)) + [vmem] * 3,
        scratch_shapes=[pltpu.VMEM(a.shape, a.dtype) for a in ins + handed]
        + [pltpu.VMEM(s, jnp.float32) for s in shapes]
        + [pltpu.SemaphoreType.DMA((len(ins) + len(handed),)),
           pltpu.SemaphoreType.DMA((layers * len(shapes) + len(handed),))],
        compiler_params=pltpu.CompilerParams(vmem_limit_bytes=60 << 20),
    )(*small, *ins, *handed)


def fits(mesh):
    tp_count, ctx_count = mesh.shape[TP], mesh.shape[CTX]
    return ctx_count == 4 and tp_count == 2


def solution(mesh):
    in_specs = (
        P(FSDP, CTX, None),
        P(FSDP, CTX),
        P(FSDP, CTX),
        P(FSDP, None),
        P(FSDP, CTX, None),
        P(None, FSDP),
        P(None, FSDP, TP),
        P(None, FSDP, TP),
        P(None, FSDP, TP),
        P(None, TP, FSDP),
        P(None, FSDP),
        P(None, FSDP, TP),
        P(None, FSDP, TP),
        P(None, TP, FSDP),
    )
    out_specs = (
        P(FSDP, CTX, None),
        P(FSDP, CTX, None),
        P(None, FSDP),
        P(None, FSDP, TP),
        P(None, FSDP, TP),
        P(None, FSDP, TP),
        P(None, TP, FSDP),
        P(None, FSDP),
        P(None, FSDP, TP),
        P(None, FSDP, TP),
        P(None, TP, FSDP),
        P(),
    )
    return jax.shard_map(planned if fits(mesh) else general, mesh=mesh, in_specs=in_specs, out_specs=out_specs, check_vma=False)
```
